32 devices in a mesh: tm: 2 (over x), pair: 16 (over z, y, core).
Axes of the slice: x: 2, y: 2, z: 4, core: 2. Of those that a mesh axis runs over, the one named last changes fastest.
Arguments:
- traces: float32 [4, 2048, 1024], P('tm', 'pair'), may hold values from -6 to 6
- owner: int32 [16], replicated, may hold values from 0 to 15, each once
- tiles: int32 [48, 2], P('pair'), may hold values from 0 to 15, as said below
- counts: int32 [16], P('pair'), may hold values from 1 to 3, as said below
Outputs:
- stacks: float32 [48, 128, 16384], P('pair', None, 'tm')
The draws below stay inside these ranges and needn't reach their ends.
Inputs may be any that keep to these rules, and one draw needn't show every extreme that they name: `tiles`: each row names fiber blocks a <= b with b - a at most 6. `counts`: the first that many of an index's 3 slots are live; some index has all 3 live.
All inputs are finite; a program needn't handle non-finite values.
Results may differ from the reference program's by a relative error of at most 0.0038.
Values may be sent and summed in bfloat16 or wider, within the bound.
No kernel may reach another device: no remote copies, remote signals or barrier semaphores. Data moves between devices by JAX's collectives and lax.ppermute only.
A program may use at most 128 MiB of HBM per device.

```python
import math
import jax
import jax.numpy as jnp
from jax import lax

BLOCK = 128
NT = 1024
NF = 128
LOW_BIN = 8
LAGS = 128
REACH = 6
PMAX = 3
NBLK = 16
CHANNELS = 2048
SEGMENTS = 4
SLOTS = 48


def draw_tiles(key, part):
    first = jax.random.randint(jax.random.fold_in(key, 11), (SLOTS, 1), 0, NBLK)
    offset = jax.random.randint(jax.random.fold_in(key, 12), (SLOTS, 1), 0, REACH + 1)
    second = jnp.minimum(first + offset, NBLK - 1)
    return jnp.concatenate([first, second], axis=1).astype(jnp.int32)


def draw_counts(key, part):
    base = jax.random.randint(jax.random.fold_in(key, 21), (NBLK,), 1, PMAX + 1)
    fullest = jax.random.randint(jax.random.fold_in(key, 22), (), 0, NBLK)
    return jnp.where(jnp.arange(NBLK) == fullest, PMAX, base).astype(jnp.int32)


def block_levels(stream_key, dims, shards, low, largest):
    def one(dim, blocks):
        steps = jax.random.uniform(jax.random.fold_in(jax.random.fold_in(stream_key, 6), dim), (blocks,), jnp.float32, low / len(shards), largest / len(shards))
        return jnp.repeat(jnp.exp(steps), dims[dim] // blocks).reshape((-1,) + (1,) * (len(dims) - dim - 1))

    loudness = one(*shards[0])
    for cut in shards[1:]:
        loudness = loudness * one(*cut)
    return loudness


def normal_values(key, shape, spread, bound, shards=(), kind=jnp.bfloat16):
    factor_of = block_levels(key, shape, shards, -0.22, 0.18) if shards else 1.0
    array = jax.random.normal(key, shape, jnp.float32) * spread * factor_of
    return jnp.minimum(jnp.maximum(array, -bound), bound).astype(kind)


def setup_inputs(seed: int = 0) -> dict:
    key_of = jax.random.split(jax.random.key(seed), 5)
    return {
        "traces": normal_values(key_of[0], (SEGMENTS, CHANNELS, NT), 1.0, 6.0, ((0, 2), (1, 16)), jnp.float32),
        "owner": jax.random.permutation(key_of[1], NBLK).astype(jnp.int32),
        "tiles": draw_tiles(jax.random.fold_in(key_of[4], 71), 0),
        "counts": draw_counts(jax.random.fold_in(key_of[4], 71), 0),
    }


def forward_table():
    samples = jnp.arange(NT, dtype=jnp.int32)
    bins = LOW_BIN + jnp.arange(NF, dtype=jnp.int32)
    phase = samples[:, None] * bins[None, :] % NT
    angle = phase.astype(jnp.float32) * (2.0 * math.pi / NT)
    return jnp.concatenate([jnp.cos(angle), -jnp.sin(angle)], axis=1)

def inverse_table():
    shifts = jnp.arange(LAGS, dtype=jnp.int32) - LAGS // 2
    bins = LOW_BIN + jnp.arange(NF, dtype=jnp.int32)
    phase = jnp.mod(shifts[:, None] * bins[None, :], NT)
    angle = phase.astype(jnp.float32) * (2.0 * math.pi / NT)
    return (jnp.cos(angle), -jnp.sin(angle))

def window_sum(values):
    widths = [(0, 0)] * (values.ndim - 1) + [(2, 2)]
    padded = jnp.pad(values, widths)
    total = padded[..., 0:NF]
    for offset in range(1, 5):
        total = total + padded[..., offset:offset + NF]
    return total

def whiten(spectrum):
    real_part = spectrum[..., :NF]
    imag_part = spectrum[..., NF:]
    power = real_part * real_part + imag_part * imag_part
    counted = window_sum(jnp.ones((NF,), jnp.float32))
    smooth = window_sum(power) / counted
    level = lax.optimization_barrier(jnp.mean(power, axis=-1, keepdims=True))
    factor = lax.rsqrt(smooth + 0.05 * level + 1e-06)
    return jnp.concatenate([real_part * factor, imag_part * factor], axis=-1).astype(jnp.bfloat16)

def reference(traces, owner, tiles, counts):
    rows = traces.reshape(SEGMENTS * CHANNELS, NT)
    spectrum = jnp.dot(rows, forward_table(), precision=lax.Precision.HIGHEST)
    white = whiten(spectrum).reshape(SEGMENTS, NBLK, BLOCK, 2 * NF)
    onehot = tiles[:, :, None] == jnp.arange(NBLK, dtype=jnp.int32)[None, None, :]
    stored = lax.optimization_barrier(jnp.sum(jnp.where(onehot, owner[None, None, :], 0), axis=2)).astype(jnp.int32)
    slot_rank = jnp.arange(SLOTS, dtype=jnp.int32) % PMAX
    holder = jnp.arange(SLOTS, dtype=jnp.int32) // PMAX
    live = (slot_rank < counts[holder]).astype(jnp.float32)
    cos_part, sin_part = inverse_table()
    scale = 1.0 / math.sqrt(SEGMENTS * NF)

    def one_tile(item):
        pair_ids, alive = item
        left = lax.dynamic_index_in_dim(white, pair_ids[0], axis=1, keepdims=False).astype(jnp.float32)
        right = lax.dynamic_index_in_dim(white, pair_ids[1], axis=1, keepdims=False).astype(jnp.float32)
        left_real, left_imag = (left[..., :NF], left[..., NF:])
        right_real, right_imag = (right[..., :NF], right[..., NF:])
        cross_real = jnp.einsum('sif,sjf->fij', left_real, right_real) + jnp.einsum('sif,sjf->fij', left_imag, right_imag)
        cross_imag = jnp.einsum('sif,sjf->fij', left_real, right_imag) - jnp.einsum('sif,sjf->fij', left_imag, right_real)
        cross_real = cross_real.reshape(NF, BLOCK * BLOCK)
        cross_imag = cross_imag.reshape(NF, BLOCK * BLOCK)
        lagged = jnp.dot(cos_part, cross_real, precision=lax.Precision.HIGHEST)
        lagged = lagged + jnp.dot(sin_part, cross_imag, precision=lax.Precision.HIGHEST)
        return lagged * scale * alive
    return lax.map(one_tile, (stored, live))
```

```python
import functools
import math

import jax
import jax.numpy as jnp
import ml_dtypes
import numpy as np
from jax import lax
from jax.experimental import pallas as pl
from jax.experimental.pallas import tpu as pltpu
from jax.sharding import PartitionSpec as P

NT = 1024
NF = 128
LOW_BIN = 8
LAGS = 128


def split_bf16(table):
    high = table.astype(ml_dtypes.bfloat16)
    low = (table - high.astype(np.float64)).astype(ml_dtypes.bfloat16)
    return high, low


def forward_table():
    phase = (LOW_BIN + np.arange(NF))[:, None] * np.arange(NT)[None, :] % NT
    angle = phase * (2.0 * math.pi / NT)
    return split_bf16(np.concatenate([np.cos(angle), -np.sin(angle)], axis=0))


def inverse_table(segments):
    shifts = np.arange(LAGS) - LAGS // 2
    phase = shifts[:, None] * (LOW_BIN + np.arange(NF))[None, :] % NT
    angle = phase * (2.0 * math.pi / NT)
    scale = 1.0 / math.sqrt(segments * NF)
    table = np.concatenate([np.cos(angle), -np.sin(angle)], axis=1) * scale
    return table.astype(ml_dtypes.bfloat16)


def nt_dot(a, b):
    return lax.dot_general(a, b, (((1,), (1,)), ((), ())), preferred_element_type=jnp.float32)


def whiten_kernel(bins, x_ref, high_ref, low_ref, out_ref, pad_ref):
    segments, block, _ = x_ref.shape
    columns = segments * block
    x = x_ref[...].reshape(columns, NT)
    x_high = x.astype(jnp.bfloat16)
    x_low = (x - x_high.astype(jnp.float32)).astype(jnp.bfloat16)
    high = high_ref[...]
    spectrum = nt_dot(high, x_high) + (nt_dot(high, x_low) + nt_dot(low_ref[...], x_high))
    real_part = spectrum[:NF]
    imag_part = spectrum[NF:]
    power = real_part * real_part + imag_part * imag_part
    edge = jnp.zeros((8, columns), jnp.float32)
    pad_ref[0:8, :] = edge
    pad_ref[8 + NF : 16 + NF, :] = edge
    pad_ref[8 : 8 + NF, :] = power
    total = pad_ref[6 : 6 + NF, :]
    for offset in range(7, 11):
        total = total + pad_ref[offset : offset + NF, :]
    bin_id = lax.broadcasted_iota(jnp.int32, (NF, columns), 0)
    counted = (jnp.minimum(bin_id + 2, NF - 1) - jnp.maximum(bin_id - 2, 0) + 1).astype(jnp.float32)
    smooth = total / counted
    level = jnp.mean(power, axis=0, keepdims=True)
    factor = lax.rsqrt(smooth + 0.05 * level + 1e-06)
    parts = ((real_part * factor).astype(jnp.bfloat16), (imag_part * factor).astype(jnp.bfloat16))
    for group in range(NF // bins):
        for segment in range(segments):
            for c in range(2):
                row = (segment * 2 + c) * bins
                out_ref[group, row : row + bins, :] = parts[c][
                    group * bins : (group + 1) * bins, segment * block : (segment + 1) * block
                ]


def pick_kernel(owner_ref, tiles_ref, left_ref, right_ref, left_out, right_out):
    _, groups, rows, block = left_ref.shape
    times, share = left_out.shape[1:3]
    flat = left_ref[...].reshape(groups * rows, block).astype(jnp.float32)
    turned = flat.T.astype(jnp.bfloat16)
    for part in range(times):
        left_out[0, part] = turned[part * share : (part + 1) * share, :]
    right_out[...] = right_ref[...]


def stack_kernel(bins, chunk, counts_ref, left_ref, right_ref, table_ref, out_ref, left_all, right_all, cross_ref):
    slot = pl.program_id(0)
    part = pl.program_id(1)
    times, _, share, _ = left_ref.shape
    _, _, groups, rows, block = right_ref.shape
    wide = times * rows
    live = slot < counts_ref[0]

    @pl.when(live & (part == 0))
    def _():
        for group in range(groups):
            for step in range(times):
                left_all[:, group * wide + step * rows : group * wide + (step + 1) * rows] = left_ref[
                    step, 0, :, group * rows : (group + 1) * rows
                ].astype(jnp.float32)
                for pair in range(rows // (2 * bins)):
                    row = pair * 2 * bins
                    at = group * wide + step * rows + row
                    real_part = right_ref[step, 0, group, row : row + bins, :]
                    imag_part = right_ref[step, 0, group, row + bins : row + 2 * bins, :]
                    right_all[at : at + bins, :block] = real_part
                    right_all[at : at + bins, block:] = imag_part
                    right_all[at + bins : at + 2 * bins, :block] = imag_part
                    right_all[at + bins : at + 2 * bins, block:] = -real_part

    @pl.when(live)
    def _():
        column = lax.broadcasted_iota(jnp.int32, (bins, wide), 1) % bins
        row = lax.broadcasted_iota(jnp.int32, (bins, wide), 0)
        keep = column == row
        first = part * chunk
        several = 4 if chunk % 4 == 0 else 2
        for group in range(groups):
            weights = right_all[group * wide : (group + 1) * wide, :]
            for start in range(0, chunk, several):
                pieces = []
                for i in range(several):
                    line = left_all[pl.ds(first + start + i, 1), group * wide : (group + 1) * wide]
                    pieces.append(jnp.where(keep, jnp.broadcast_to(line, (bins, wide)), 0.0).astype(jnp.bfloat16))
                product = jnp.dot(jnp.concatenate(pieces, axis=0), weights, preferred_element_type=jnp.float32)
                product = product.astype(jnp.bfloat16)
                for i in range(several):
                    at = start + i
                    lanes = slice(at % 2 * block, (at % 2 + 1) * block)
                    piece = product[i * bins : (i + 1) * bins]
                    cross_ref[at // 2, group * bins : (group + 1) * bins, lanes] = piece[:, :block]
                    cross_ref[at // 2, NF + group * bins : NF + (group + 1) * bins, lanes] = piece[:, block:]
        table = table_ref[...]
        for pair in range(chunk // 2):
            out_ref[0, :, pair * 2 * block : (pair + 1) * 2 * block] = jnp.dot(
                table, cross_ref[pair], preferred_element_type=jnp.float32
            )

    @pl.when(jnp.logical_not(live))
    def _():
        out_ref[...] = jnp.zeros_like(out_ref)


def shards(traces, owner, tiles, counts):
    seg_count, block, _ = traces.shape
    times = lax.axis_size("tm")
    segments = seg_count * times
    share = block // times
    slots = tiles.shape[0]
    bins = max(16, 128 // segments)
    groups = NF // bins
    rows = seg_count * 2 * bins
    wide = rows * times
    high, low = forward_table()
    white = pl.pallas_call(
        functools.partial(whiten_kernel, bins),
        out_shape=jax.ShapeDtypeStruct((groups, rows, block), jnp.bfloat16),
        scratch_shapes=[pltpu.VMEM((NF + 16, seg_count * block), jnp.float32)],
        compiler_params=pltpu.CompilerParams(vmem_limit_bytes=32 << 20),
        name="whiten",
    )(traces, jnp.asarray(high), jnp.asarray(low))

    every = lax.all_gather(white, "pair", axis=0)

    def fetch(side):
        return lambda q, own, til: (own[til[q, side]], 0, 0, 0)

    left, right = pl.pallas_call(
        pick_kernel,
        grid_spec=pltpu.PrefetchScalarGridSpec(
            num_scalar_prefetch=2,
            grid=(slots,),
            in_specs=[
                pl.BlockSpec((1, groups, rows, block), fetch(0)),
                pl.BlockSpec((1, groups, rows, block), fetch(1)),
            ],
            out_specs=[
                pl.BlockSpec((1, times, share, groups * rows), lambda q, own, til: (q, 0, 0, 0)),
                pl.BlockSpec((1, groups, rows, block), lambda q, own, til: (q, 0, 0, 0)),
            ],
        ),
        out_shape=[
            jax.ShapeDtypeStruct((slots, times, share, groups * rows), jnp.bfloat16),
            jax.ShapeDtypeStruct((slots, groups, rows, block), jnp.bfloat16),
        ],
        compiler_params=pltpu.CompilerParams(vmem_limit_bytes=32 << 20),
        name="pick",
    )(owner, tiles, every, every)

    me = lax.axis_index("tm")
    lefts = []
    rights = []
    for step in range(times):
        mine = lax.dynamic_index_in_dim(left, (me + step) % times, axis=1, keepdims=False)
        if step:
            moves = [(t, (t + step) % times) for t in range(times)]
            lefts.append(lax.ppermute(mine, "tm", moves))
            rights.append(lax.ppermute(right, "tm", moves))
        else:
            lefts.append(mine)
            rights.append(right)
    left_all = jnp.stack(lefts)
    right_all = jnp.stack(rights)

    parts = 2 if share % 4 == 0 else 1
    chunk = share // parts
    return pl.pallas_call(
        functools.partial(stack_kernel, bins, chunk),
        grid_spec=pltpu.PrefetchScalarGridSpec(
            num_scalar_prefetch=1,
            grid=(slots, parts),
            in_specs=[
                pl.BlockSpec((times, 1, share, groups * rows), lambda q, k, cnt: (0, q, 0, 0)),
                pl.BlockSpec((times, 1, groups, rows, block), lambda q, k, cnt: (0, q, 0, 0, 0)),
                pl.BlockSpec((LAGS, 2 * NF), lambda q, k, cnt: (0, 0)),
            ],
            out_specs=pl.BlockSpec((1, LAGS, chunk * block), lambda q, k, cnt: (q, 0, k)),
            scratch_shapes=[
                pltpu.VMEM((share, groups * wide), jnp.float32),
                pltpu.VMEM((groups * wide, 2 * block), jnp.bfloat16),
                pltpu.VMEM((chunk // 2, 2 * NF, 2 * block), jnp.bfloat16),
            ],
        ),
        out_shape=jax.ShapeDtypeStruct((slots, LAGS, share * block), jnp.float32),
        compiler_params=pltpu.CompilerParams(vmem_limit_bytes=48 << 20),
        name="stack",
    )(counts, left_all, right_all, jnp.asarray(inverse_table(segments)))


def solution(mesh):
    placed = (P("tm", "pair", None), P(), P("pair", None), P("pair"))
    return jax.shard_map(
        shards, mesh=mesh, in_specs=placed, out_specs=P("pair", None, "tm"), check_vma=False
    )
```

```python
import functools
import math

import jax
import jax.numpy as jnp
import ml_dtypes
import numpy as np
from jax import lax
from jax.experimental import pallas as pl
from jax.experimental.pallas import tpu as pltpu
from jax.sharding import PartitionSpec as P

NT = 1024
NF = 128
LOW_BIN = 8
LAGS = 128


def split_bf16(table):
    high = table.astype(ml_dtypes.bfloat16)
    low = (table - high.astype(np.float64)).astype(ml_dtypes.bfloat16)
    return high, low


def forward_table():
    phase = (LOW_BIN + np.arange(NF))[:, None] * np.arange(NT)[None, :] % NT
    angle = phase * (2.0 * math.pi / NT)
    return split_bf16(np.concatenate([np.cos(angle), -np.sin(angle)], axis=0))


def inverse_table(segments):
    shifts = np.arange(LAGS) - LAGS // 2
    phase = shifts[:, None] * (LOW_BIN + np.arange(NF))[None, :] % NT
    angle = phase * (2.0 * math.pi / NT)
    scale = 1.0 / math.sqrt(segments * NF)
    table = np.concatenate([np.cos(angle), -np.sin(angle)], axis=1) * scale
    return table.astype(ml_dtypes.bfloat16)


def nt_dot(a, b):
    return lax.dot_general(a, b, (((1,), (1,)), ((), ())), preferred_element_type=jnp.float32)


def whiten_kernel(bins, x_ref, high_ref, low_ref, out_ref, pad_ref):
    segments, block, _ = x_ref.shape
    columns = segments * block
    x = x_ref[...].reshape(columns, NT)
    x_high = x.astype(jnp.bfloat16)
    x_low = (x - x_high.astype(jnp.float32)).astype(jnp.bfloat16)
    high = high_ref[...]
    spectrum = nt_dot(high, x_high) + (nt_dot(high, x_low) + nt_dot(low_ref[...], x_high))
    real_part = spectrum[:NF]
    imag_part = spectrum[NF:]
    power = real_part * real_part + imag_part * imag_part
    edge = jnp.zeros((8, columns), jnp.float32)
    pad_ref[0:8, :] = edge
    pad_ref[8 + NF : 16 + NF, :] = edge
    pad_ref[8 : 8 + NF, :] = power
    total = pad_ref[6 : 6 + NF, :]
    for offset in range(7, 11):
        total = total + pad_ref[offset : offset + NF, :]
    bin_id = lax.broadcasted_iota(jnp.int32, (NF, columns), 0)
    counted = (jnp.minimum(bin_id + 2, NF - 1) - jnp.maximum(bin_id - 2, 0) + 1).astype(jnp.float32)
    smooth = total / counted
    level = jnp.mean(power, axis=0, keepdims=True)
    factor = lax.rsqrt(smooth + 0.05 * level + 1e-06)
    parts = ((real_part * factor).astype(jnp.bfloat16), (imag_part * factor).astype(jnp.bfloat16))
    for group in range(NF // bins):
        for segment in range(segments):
            for c in range(2):
                row = (segment * 2 + c) * bins
                out_ref[group, row : row + bins, :] = parts[c][
                    group * bins : (group + 1) * bins, segment * block : (segment + 1) * block
                ]


def pick_kernel(dims, first_rows, count, me_ref, owner_ref, tiles_ref, *refs):
    depth, height, cores = dims
    slots = tiles_ref.shape[0]
    sources, refs = refs[:count], refs[count:]
    own_ref, sends, (held, turned, sems) = refs[0], refs[1:-3], refs[-3:]
    _, _, rows, block = held.shape
    at = me_ref[0]
    time = me_ref[1]
    z, y, c = at // (height * cores), at // cores % height, at % cores

    def copies(slot, side):
        stored = owner_ref[tiles_ref[slot, side]]
        dz = (z + depth - stored // (height * cores)) % depth
        dy = (y + height - stored // cores % height) % height
        dc = (c + cores - stored % cores) % cores
        index = 0
        for low, high, outer, inner, outers in ((0, first_rows, dy, dz, height), (first_rows, rows, dz, dy, depth)):
            if high == low:
                continue
            part = 0 if low == 0 else 1
            sem = sems.at[slot, side, part]
            for core in range(cores):
                for step in range(outers):
                    yield (dc == core) & (outer == step), pltpu.make_async_copy(
                        sources[index].at[inner], held.at[slot, side, low:high], sem
                    )
                    index += 1

    def wait(slot, side):
        for part, (low, high) in enumerate(((0, first_rows), (first_rows, rows))):
            if high > low:
                view = held.at[slot, side, low:high]
                pltpu.make_async_copy(view, view, sems.at[slot, side, part]).wait()

    for slot in range(slots):
        for side in range(2):
            for wanted, copy in copies(slot, side):
                pl.when(wanted)(copy.start)
    times = 1 + sends[0].shape[0]
    share = block // times
    for slot in range(slots):
        wait(slot, 0)
        turned[...] = held[slot, 0].astype(jnp.float32).T.astype(jnp.bfloat16)
        wait(slot, 1)
        right = held[slot, 1]
        for step in range(times):
            target = own_ref.at[slot] if step == 0 else sends[slot].at[step - 1]
            start = pl.multiple_of((time + step) % times * share, share)
            target[:rows] = right
            for piece in range(rows // block):
                low = rows + piece * share
                target[low : low + share] = turned[pl.ds(start, share), piece * block : (piece + 1) * block]


def stack_kernel(bins, chunk, rows, total, slot, times, *refs):
    counts_ref, packs, table_ref = refs[0], refs[1 : 1 + times], refs[1 + times]
    out_ref, left_all, right_all, cross_ref = refs[-4:]
    part = pl.program_id(0)
    share = left_all.shape[0]
    block = share * times
    groups = total // rows
    wide = times * rows
    live = slot < counts_ref[0]

    @pl.when(live & (part == 0))
    def _():
        for step in range(times):
            for group in range(groups):
                done = 0
                while done < rows:
                    at = group * rows + done
                    width = min(rows - done, block - at % block)
                    low = total + at // block * share
                    left_all[:, group * wide + step * rows + done : group * wide + step * rows + done + width] = packs[step][
                        low : low + share, at % block : at % block + width
                    ].astype(jnp.float32)
                    done += width
                for pair in range(rows // (2 * bins)):
                    row = group * rows + pair * 2 * bins
                    at = group * wide + step * rows + pair * 2 * bins
                    real_part = packs[step][row : row + bins, :]
                    imag_part = packs[step][row + bins : row + 2 * bins, :]
                    right_all[at : at + bins, :block] = real_part
                    right_all[at : at + bins, block:] = imag_part
                    right_all[at + bins : at + 2 * bins, :block] = imag_part
                    right_all[at + bins : at + 2 * bins, block:] = -real_part

    @pl.when(live)
    def _():
        column = lax.broadcasted_iota(jnp.int32, (bins, wide), 1) % bins
        row = lax.broadcasted_iota(jnp.int32, (bins, wide), 0)
        keep = column == row
        first = part * chunk
        several = 4 if chunk % 4 == 0 else 2
        for group in range(groups):
            weights = right_all[group * wide : (group + 1) * wide, :]
            for start in range(0, chunk, several):
                pieces = []
                for i in range(several):
                    line = left_all[pl.ds(first + start + i, 1), group * wide : (group + 1) * wide]
                    pieces.append(jnp.where(keep, jnp.broadcast_to(line, (bins, wide)), 0.0).astype(jnp.bfloat16))
                product = jnp.dot(jnp.concatenate(pieces, axis=0), weights, preferred_element_type=jnp.float32)
                product = product.astype(jnp.bfloat16)
                for i in range(several):
                    at = start + i
                    lanes = slice(at % 2 * block, (at % 2 + 1) * block)
                    piece = product[i * bins : (i + 1) * bins]
                    cross_ref[at // 2, group * bins : (group + 1) * bins, lanes] = piece[:, :block]
                    cross_ref[at // 2, NF + group * bins : NF + (group + 1) * bins, lanes] = piece[:, block:]
        table = table_ref[...]
        for pair in range(chunk // 2):
            out_ref[0, :, pair * 2 * block : (pair + 1) * 2 * block] = jnp.dot(
                table, cross_ref[pair], preferred_element_type=jnp.float32
            )

    @pl.when(jnp.logical_not(live))
    def _():
        out_ref[...] = jnp.zeros_like(out_ref)


def chip_dims(size):
    return {16: (4, 2, 2), 64: (16, 4, 1)}.get(size, (size, 1, 1))


def shift(value, dims, axis, by):
    if by == 0:
        return value
    count = math.prod(dims)
    moves = []
    for p in range(count):
        place = list(np.unravel_index(p, dims))
        place[axis] = (place[axis] + by) % dims[axis]
        moves.append((p, int(np.ravel_multi_index(place, dims))))
    return lax.ppermute(value, "pair", moves)


def gather_blocks(white, dims, first_rows):
    depth, height, cores = dims
    by_core = []
    column = [shift(white[:first_rows], dims, 0, dz) for dz in range(depth)]
    line = None
    if first_rows < white.shape[0]:
        line = jnp.stack([shift(white[first_rows:], dims, 1, dy) for dy in range(height)])
    column = jnp.stack(column)
    mine = [shift(column, dims, 1, dy) for dy in range(height)]
    later = [] if line is None else [shift(line, dims, 0, dz) for dz in range(depth)]
    sources = []
    for group in (mine, later):
        for core in range(cores):
            sources += [shift(part, dims, 2, core) for part in group]
    return sources


FIRST = 512


def shards(traces, owner, tiles, counts):
    seg_count, block, _ = traces.shape
    times = lax.axis_size("tm")
    segments = seg_count * times
    share = block // times
    slots = tiles.shape[0]
    bins = max(16, 128 // segments)
    groups = NF // bins
    rows = seg_count * 2 * bins
    wide = rows * times
    total = groups * rows
    high, low = forward_table()
    roomy = pltpu.CompilerParams(vmem_limit_bytes=56 << 20)
    white = pl.pallas_call(
        functools.partial(whiten_kernel, bins),
        out_shape=jax.ShapeDtypeStruct((groups, rows, block), jnp.bfloat16),
        scratch_shapes=[pltpu.VMEM((NF + 16, seg_count * block), jnp.float32)],
        compiler_params=roomy,
        name="whiten",
    )(traces, jnp.asarray(high), jnp.asarray(low))

    dims = chip_dims(lax.axis_size("pair"))
    first_rows = min(FIRST, total)
    sources = gather_blocks(white.reshape(total, block), dims, first_rows)
    pack = total + total // block * share
    place = jnp.stack([lax.axis_index("pair"), lax.axis_index("tm")]).astype(jnp.int32)
    smem = pl.BlockSpec(memory_space=pltpu.SMEM)
    hbm = pl.BlockSpec(memory_space=pl.ANY)
    own, *sends = pl.pallas_call(
        functools.partial(pick_kernel, dims, first_rows, len(sources)),
        in_specs=[smem] * 3 + [hbm] * len(sources),
        out_shape=[jax.ShapeDtypeStruct((slots, pack, block), jnp.bfloat16)]
        + [jax.ShapeDtypeStruct((times - 1, pack, block), jnp.bfloat16)] * slots,
        scratch_shapes=[
            pltpu.VMEM((slots, 2, total, block), jnp.bfloat16),
            pltpu.VMEM((block, total), jnp.bfloat16),
            pltpu.SemaphoreType.DMA((slots, 2, 2)),
        ],
        compiler_params=roomy,
        name="pick",
    )(place, owner, tiles, *sources)

    arrived = []
    for slot in range(slots):
        packs = []
        for step in range(1, times):
            moves = [(t, (t + step) % times) for t in range(times)]
            packs.append(lax.ppermute(sends[slot][step - 1], "tm", moves))
        arrived.append(packs)

    parts = 2 if share % 4 == 0 else 1
    chunk = share // parts
    table = jnp.asarray(inverse_table(segments))
    out = None
    for slot in range(slots):
        before = [] if out is None else [out]
        packs = [own[slot]] + arrived[slot]
        specs = [smem] + [pl.BlockSpec((pack, block), lambda k: (0, 0))] * times
        specs += [pl.BlockSpec((LAGS, 2 * NF), lambda k: (0, 0))] + [hbm] * len(before)
        out = pl.pallas_call(
            functools.partial(stack_kernel, bins, chunk, rows, total, slot, times),
            grid=(parts,),
            in_specs=specs,
            out_specs=pl.BlockSpec((1, LAGS, chunk * block), functools.partial(lambda slot, k: (slot, 0, k), slot)),
            scratch_shapes=[
                pltpu.VMEM((share, groups * wide), jnp.float32),
                pltpu.VMEM((groups * wide, 2 * block), jnp.bfloat16),
                pltpu.VMEM((chunk // 2, 2 * NF, 2 * block), jnp.bfloat16),
            ],
            out_shape=jax.ShapeDtypeStruct((slots, LAGS, share * block), jnp.float32),
            input_output_aliases={len(specs) - 1: 0} if before else {},
            compiler_params=roomy,
            cost_estimate=pl.CostEstimate(flops=5 << 30, bytes_accessed=LAGS * share * block * 4, transcendentals=0),
            name="stack",
        )(counts, *packs, table, *before)
    return out


def solution(mesh):
    placed = (P("tm", "pair", None), P(), P("pair", None), P("pair"))
    return jax.shard_map(
        shards, mesh=mesh, in_specs=placed, out_specs=P("pair", None, "tm"), check_vma=False
    )
```

```python
import functools
import math

import jax
import jax.numpy as jnp
import ml_dtypes
import numpy as np
from jax import lax
from jax.experimental import pallas as pl
from jax.experimental.pallas import tpu as pltpu
from jax.sharding import PartitionSpec as P

NT = 1024
NF = 128
LOW_BIN = 8
LAGS = 128


def split_bf16(table):
    high = table.astype(ml_dtypes.bfloat16)
    low = (table - high.astype(np.float64)).astype(ml_dtypes.bfloat16)
    return high, low


def forward_table():
    phase = (LOW_BIN + np.arange(NF))[:, None] * np.arange(NT)[None, :] % NT
    angle = phase * (2.0 * math.pi / NT)
    return split_bf16(np.concatenate([np.cos(angle), -np.sin(angle)], axis=0))


def inverse_table(segments):
    shifts = np.arange(LAGS) - LAGS // 2
    phase = shifts[:, None] * (LOW_BIN + np.arange(NF))[None, :] % NT
    angle = phase * (2.0 * math.pi / NT)
    scale = 1.0 / math.sqrt(segments * NF)
    table = np.concatenate([np.cos(angle), -np.sin(angle)], axis=1) * scale
    return table.astype(ml_dtypes.bfloat16)


def nt_dot(a, b):
    return lax.dot_general(a, b, (((1,), (1,)), ((), ())), preferred_element_type=jnp.float32)


def whiten_kernel(bins, x_hbm, high_hbm, low_hbm, *refs):
    outs, (x_ref, high_ref, low_ref, pad_ref, sems) = refs[:-5], refs[-5:]
    segments, block, _ = x_ref.shape
    high_copy = pltpu.make_async_copy(high_hbm, high_ref, sems.at[0])
    low_copy = pltpu.make_async_copy(low_hbm, low_ref, sems.at[1])
    x_copies = [pltpu.make_async_copy(x_hbm.at[s], x_ref.at[s], sems.at[2 + s]) for s in range(segments)]
    high_copy.start()
    x_copies[0].start()
    low_copy.start()
    for copy in x_copies[1:]:
        copy.start()
    bin_id = lax.broadcasted_iota(jnp.int32, (NF, block), 0)
    counted = (jnp.minimum(bin_id + 2, NF - 1) - jnp.maximum(bin_id - 2, 0) + 1).astype(jnp.float32)
    edge = jnp.zeros((8, block), jnp.float32)
    each = NF // bins // len(outs)
    for segment in range(segments):
        x_copies[segment].wait()
        if segment == 0:
            high_copy.wait()
        x = x_ref[segment]
        x_high = x.astype(jnp.bfloat16)
        x_low = (x - x_high.astype(jnp.float32)).astype(jnp.bfloat16)
        high = high_ref[...]
        spectrum = nt_dot(high, x_high) + nt_dot(high, x_low)
        if segment == 0:
            low_copy.wait()
        spectrum = spectrum + nt_dot(low_ref[...], x_high)
        real_part = spectrum[:NF]
        imag_part = spectrum[NF:]
        power = real_part * real_part + imag_part * imag_part
        pad_ref[segment, 0:8, :] = edge
        pad_ref[segment, 8 + NF : 16 + NF, :] = edge
        pad_ref[segment, 8 : 8 + NF, :] = power
        total = pad_ref[segment, 6 : 6 + NF, :]
        for offset in range(7, 11):
            total = total + pad_ref[segment, offset : offset + NF, :]
        smooth = total / counted
        level = jnp.mean(power, axis=0, keepdims=True)
        factor = lax.rsqrt(smooth + 0.05 * level + 1e-06)
        parts = ((real_part * factor).astype(jnp.bfloat16), (imag_part * factor).astype(jnp.bfloat16))
        for group in range(NF // bins):
            for c in range(2):
                row = ((group % each * segments + segment) * 2 + c) * bins
                outs[group // each][row : row + bins, :] = parts[c][group * bins : (group + 1) * bins]


def pick_kernel(dims, me_ref, owner_ref, tiles_ref, *refs):
    depth, height, cores = dims
    slots = tiles_ref.shape[0]
    sources, refs = refs[: height * cores], refs[height * cores :]
    outs, (held, turned, left_sems, right_sems, out_sems) = refs[:-5], refs[-5:]
    _, rows, block = held.shape
    times = len(outs)
    share = block // times
    pieces = rows // block
    at = me_ref[0]
    time = me_ref[1]
    z, y, c = at // (height * cores), at // cores % height, at % cores

    def fetch(slot, side, targets, sems):
        stored = owner_ref[tiles_ref[slot, side]]
        dz = (z + depth - stored // (height * cores)) % depth
        dy = (y + height - stored // cores % height) % height
        dc = (c + cores - stored % cores) % cores
        for core in range(cores):
            for step in range(height):

                @pl.when((dc == core) & (dy == step))
                def _():
                    for n, target in enumerate(targets):
                        pltpu.make_async_copy(sources[core * height + step].at[dz], target, sems.at[slot, n]).start()

    for slot in range(slots):
        fetch(slot, 0, [held.at[slot]], left_sems)
    rights = [[out.at[slot, :rows] for out in outs] for slot in range(slots)]
    for slot in range(slots):
        fetch(slot, 1, rights[slot], right_sems)
    copies = []
    for slot in range(slots):
        pltpu.make_async_copy(held.at[slot], held.at[slot], left_sems.at[slot, 0]).wait()
        flipped = held[slot].astype(jnp.float32).T.astype(jnp.bfloat16)
        for piece in range(pieces):
            turned[slot, piece] = flipped[:, piece * block : (piece + 1) * block]
        for step in range(times):
            start = pl.multiple_of((time + step) % times * share, share)
            for piece in range(pieces):
                copy = pltpu.make_async_copy(
                    turned.at[slot, piece, pl.ds(start, share)],
                    outs[step].at[slot, rows + piece * share : rows + (piece + 1) * share],
                    out_sems.at[slot, step, piece],
                )
                copy.start()
                copies.append(copy)
    for slot in range(slots):
        for n, target in enumerate(rights[slot]):
            pltpu.make_async_copy(target, target, right_sems.at[slot, n]).wait()
    for copy in copies:
        copy.wait()


def stack_kernel(bins, chunk, rows, spread, times, counts_ref, *refs):
    packs, table_ref = refs[: spread * times], refs[spread * times]
    out_ref, left_all, right_all, cross_ref = refs[-4:]
    slot = pl.program_id(0)
    part = pl.program_id(1)
    share = left_all.shape[0]
    block = share * times
    wide = times * rows
    groups = left_all.shape[1] // wide
    each = groups // spread
    live = slot < counts_ref[0]

    @pl.when(live & (part == 0))
    def _():
        for piece in range(spread):
            for step in range(times):
                pack = packs[piece * times + step]
                for index in range(each):
                    base = (piece * each + index) * wide + step * rows
                    done = 0
                    while done < rows:
                        at = index * rows + done
                        width = min(rows - done, block - at % block)
                        low = each * rows + at // block * share
                        left_all[:, base + done : base + done + width] = pack[
                            0, low : low + share, at % block : at % block + width
                        ].astype(jnp.float32)
                        done += width
                    for pair in range(rows // (2 * bins)):
                        row = index * rows + pair * 2 * bins
                        at = base + pair * 2 * bins
                        real_part = pack[0, row : row + bins, :]
                        imag_part = pack[0, row + bins : row + 2 * bins, :]
                        right_all[at : at + bins, :block] = real_part
                        right_all[at : at + bins, block:] = imag_part
                        right_all[at + bins : at + 2 * bins, :block] = imag_part
                        right_all[at + bins : at + 2 * bins, block:] = -real_part

    @pl.when(live)
    def _():
        column = lax.broadcasted_iota(jnp.int32, (bins, wide), 1) % bins
        row = lax.broadcasted_iota(jnp.int32, (bins, wide), 0)
        keep = column == row
        first = part * chunk
        several = 4 if chunk % 4 == 0 else 2
        for group in range(groups):
            weights = right_all[group * wide : (group + 1) * wide, :]
            for start in range(0, chunk, several):
                pieces = []
                for i in range(several):
                    line = left_all[pl.ds(first + start + i, 1), group * wide : (group + 1) * wide]
                    pieces.append(jnp.where(keep, jnp.broadcast_to(line, (bins, wide)), 0.0).astype(jnp.bfloat16))
                product = jnp.dot(jnp.concatenate(pieces, axis=0), weights, preferred_element_type=jnp.float32)
                product = product.astype(jnp.bfloat16)
                for i in range(several):
                    at = start + i
                    lanes = slice(at % 2 * block, (at % 2 + 1) * block)
                    piece = product[i * bins : (i + 1) * bins]
                    cross_ref[at // 2, group * bins : (group + 1) * bins, lanes] = piece[:, :block]
                    cross_ref[at // 2, NF + group * bins : NF + (group + 1) * bins, lanes] = piece[:, block:]
        table = table_ref[...]
        for pair in range(chunk // 2):
            out_ref[0, :, pair * 2 * block : (pair + 1) * 2 * block] = jnp.dot(
                table, cross_ref[pair], preferred_element_type=jnp.float32
            )

    @pl.when(jnp.logical_not(live))
    def _():
        out_ref[...] = jnp.zeros_like(out_ref)


def chip_dims(size):
    return {16: (4, 2, 2), 64: (16, 4, 1)}.get(size, (size, 1, 1))


def shift(value, dims, axis, by):
    if by == 0:
        return value
    count = math.prod(dims)
    moves = []
    for p in range(count):
        place = list(np.unravel_index(p, dims))
        place[axis] = (place[axis] + by) % dims[axis]
        moves.append((p, int(np.ravel_multi_index(place, dims))))
    return lax.ppermute(value, "pair", moves)


def gather_pieces(white, dims):
    depth, height, cores = dims
    gathered = []
    ready = None
    for own in white:
        if ready is not None:
            own, ready = lax.optimization_barrier((own, ready))
        column = [shift(own, dims, 0, dz) for dz in range(depth)]
        ready = column[1 % depth]
        column = jnp.stack(column)
        mine = [shift(column, dims, 1, dy) for dy in range(height)]
        gathered.append([shift(part, dims, 2, core) for core in range(cores) for part in mine])
    return gathered


PIECES = 2


def shards(traces, owner, tiles, counts):
    seg_count, block, _ = traces.shape
    times = lax.axis_size("tm")
    segments = seg_count * times
    share = block // times
    slots = tiles.shape[0]
    bins = max(16, 128 // segments)
    groups = NF // bins
    rows = seg_count * 2 * bins
    wide = rows * times
    total = groups * rows
    high, low = forward_table()
    smem = pl.BlockSpec(memory_space=pltpu.SMEM)
    hbm = pl.BlockSpec(memory_space=pltpu.HBM)
    anywhere = pl.BlockSpec(memory_space=pl.ANY)
    part_rows = total // PIECES
    white = pl.pallas_call(
        functools.partial(whiten_kernel, bins),
        in_specs=[hbm] * 3,
        out_shape=[jax.ShapeDtypeStruct((part_rows, block), jnp.bfloat16)] * PIECES,
        scratch_shapes=[
            pltpu.VMEM(traces.shape, jnp.float32),
            pltpu.VMEM(high.shape, jnp.bfloat16),
            pltpu.VMEM(low.shape, jnp.bfloat16),
            pltpu.VMEM((seg_count, NF + 16, block), jnp.float32),
            pltpu.SemaphoreType.DMA((2 + seg_count,)),
        ],
        compiler_params=pltpu.CompilerParams(vmem_limit_bytes=(64 << 20) - (384 << 10)),
        name="whiten",
    )(traces, jnp.asarray(high), jnp.asarray(low))

    dims = chip_dims(lax.axis_size("pair"))
    gathered = gather_pieces(white, dims)
    pack = part_rows + part_rows // block * share
    place = jnp.stack([lax.axis_index("pair"), lax.axis_index("tm")]).astype(jnp.int32)
    packs = []
    for sources in gathered:
        own, *sends = pl.pallas_call(
            functools.partial(pick_kernel, dims),
            in_specs=[smem] * 3 + [anywhere] * len(sources),
            out_specs=[anywhere] * times,
            out_shape=[jax.ShapeDtypeStruct((slots, pack, block), jnp.bfloat16)] * times,
            scratch_shapes=[
                pltpu.VMEM((slots, part_rows, block), jnp.bfloat16),
                pltpu.VMEM((slots, part_rows // block, block, block), jnp.bfloat16),
                pltpu.SemaphoreType.DMA((slots, 1)),
                pltpu.SemaphoreType.DMA((slots, times)),
                pltpu.SemaphoreType.DMA((slots, times, part_rows // block)),
            ],
            compiler_params=pltpu.CompilerParams(vmem_limit_bytes=8 << 20),
            name="pick",
        )(place, owner, tiles, *sources)
        packs.append(own)
        for step in range(1, times):
            moves = [(t, (t + step) % times) for t in range(times)]
            packs.append(lax.ppermute(sends[step - 1], "tm", moves))

    parts = 2 if share % 4 == 0 else 1
    chunk = share // parts
    return pl.pallas_call(
        functools.partial(stack_kernel, bins, chunk, rows, PIECES, times),
        grid_spec=pltpu.PrefetchScalarGridSpec(
            num_scalar_prefetch=1,
            grid=(slots, parts),
            in_specs=[pl.BlockSpec((1, pack, block), lambda q, k, cnt: (q, 0, 0))] * len(packs)
            + [pl.BlockSpec((LAGS, 2 * NF), lambda q, k, cnt: (0, 0))],
            out_specs=pl.BlockSpec((1, LAGS, chunk * block), lambda q, k, cnt: (q, 0, k)),
            scratch_shapes=[
                pltpu.VMEM((share, groups * wide), jnp.float32),
                pltpu.VMEM((groups * wide, 2 * block), jnp.bfloat16),
                pltpu.VMEM((chunk // 2, 2 * NF, 2 * block), jnp.bfloat16),
            ],
        ),
        out_shape=jax.ShapeDtypeStruct((slots, LAGS, share * block), jnp.float32),
        compiler_params=pltpu.CompilerParams(vmem_limit_bytes=24 << 20),
        name="stack",
    )(counts, *packs, jnp.asarray(inverse_table(segments)))


def solution(mesh):
    placed = (P("tm", "pair", None), P(), P("pair", None), P("pair"))
    return jax.shard_map(
        shards, mesh=mesh, in_specs=placed, out_specs=P("pair", None, "tm"), check_vma=False
    )
```

```python
import functools
import math

import jax
import jax.numpy as jnp
import ml_dtypes
import numpy as np
from jax import lax
from jax.experimental import pallas as pl
from jax.experimental.pallas import tpu as pltpu
from jax.sharding import PartitionSpec as P

NT = 1024
NF = 128
LOW_BIN = 8
LAGS = 128


def split_bf16(table):
    high = table.astype(ml_dtypes.bfloat16)
    low = (table - high.astype(np.float64)).astype(ml_dtypes.bfloat16)
    return high, low


def forward_table():
    phase = (LOW_BIN + np.arange(NF))[:, None] * np.arange(NT)[None, :] % NT
    angle = phase * (2.0 * math.pi / NT)
    return split_bf16(np.concatenate([np.cos(angle), -np.sin(angle)], axis=0))


def inverse_table(segments):
    shifts = np.arange(LAGS) - LAGS // 2
    phase = shifts[:, None] * (LOW_BIN + np.arange(NF))[None, :] % NT
    angle = phase * (2.0 * math.pi / NT)
    scale = 1.0 / math.sqrt(segments * NF)
    table = np.concatenate([np.cos(angle), -np.sin(angle)], axis=1) * scale
    return table.astype(ml_dtypes.bfloat16)


def nt_dot(a, b):
    return lax.dot_general(a, b, (((1,), (1,)), ((), ())), preferred_element_type=jnp.float32)


CHUNKS = 2
PIECES = 2


def whiten_kernel(bins, x_hbm, high_hbm, low_hbm, *refs):
    outs, (x_ref, high_ref, low_ref, pad_ref, sems) = refs[:-5], refs[-5:]
    _, segments, block, wide = x_ref.shape
    columns = segments * block
    copies = []
    for k in range(CHUNKS):
        span = slice(k * wide, (k + 1) * wide)
        sources = (high_hbm.at[:, span], x_hbm.at[:, :, span], low_hbm.at[:, span])
        copies.append(
            [
                pltpu.make_async_copy(source, target.at[k], sems.at[k, n])
                for n, (source, target) in enumerate(zip(sources, (high_ref, x_ref, low_ref)))
            ]
        )
        for copy in copies[-1]:
            copy.start()
    spectrum = None
    for k in range(CHUNKS):
        for copy in copies[k]:
            copy.wait()
        x = x_ref[k].reshape(columns, wide)
        x_high = x.astype(jnp.bfloat16)
        x_low = (x - x_high.astype(jnp.float32)).astype(jnp.bfloat16)
        high = high_ref[k]
        part = nt_dot(high, x_high) + nt_dot(high, x_low) + nt_dot(low_ref[k], x_high)
        spectrum = part if spectrum is None else spectrum + part
    real_part = spectrum[:NF]
    imag_part = spectrum[NF:]
    power = real_part * real_part + imag_part * imag_part
    edge = jnp.zeros((8, columns), jnp.float32)
    pad_ref[0:8, :] = edge
    pad_ref[8 + NF : 16 + NF, :] = edge
    pad_ref[8 : 8 + NF, :] = power
    total = pad_ref[6 : 6 + NF, :]
    for offset in range(7, 11):
        total = total + pad_ref[offset : offset + NF, :]
    bin_id = lax.broadcasted_iota(jnp.int32, (NF, columns), 0)
    counted = (jnp.minimum(bin_id + 2, NF - 1) - jnp.maximum(bin_id - 2, 0) + 1).astype(jnp.float32)
    smooth = total / counted
    level = jnp.mean(power, axis=0, keepdims=True)
    factor = lax.rsqrt(smooth + 0.05 * level + 1e-06)
    parts = ((real_part * factor).astype(jnp.bfloat16), (imag_part * factor).astype(jnp.bfloat16))
    each = NF // bins // len(outs)
    for group in range(NF // bins):
        for segment in range(segments):
            for c in range(2):
                row = ((group % each * segments + segment) * 2 + c) * bins
                outs[group // each][row : row + bins, :] = parts[c][
                    group * bins : (group + 1) * bins, segment * block : (segment + 1) * block
                ]


def pick_kernel(dims, layout, time_at, plan_ref, *refs):
    depth, height, cores = dims
    count = cores * (1 + max(array for array, _ in layout.values()))
    sources, refs = refs[:count], refs[count:]
    outs, (held, turned, left_sems, right_sems, out_sems) = refs[:-5], refs[-5:]
    slots, rows, block = held.shape
    times = len(outs)
    share = block // times
    pieces = rows // block
    time = plan_ref[time_at]

    def fetch(slot, side, targets, sems):
        away = plan_ref[slot * 2 + side]
        core = away % cores
        place = away // cores
        array = jnp.int32(0)
        index = jnp.int32(0)
        for (dz, dy), (where, at) in layout.items():
            here = place == dz * height + dy
            array = jnp.where(here, where, array)
            index = jnp.where(here, at, index)
        for n, source in enumerate(sources):

            @pl.when(core + cores * array == n)
            def _():
                for k, target in enumerate(targets):
                    pltpu.make_async_copy(source.at[index], target, sems.at[slot, k]).start()

    for slot in range(slots):
        fetch(slot, 0, [held.at[slot]], left_sems)
    rights = [[out.at[slot, :rows] for out in outs] for slot in range(slots)]
    for slot in range(slots):
        fetch(slot, 1, rights[slot], right_sems)
    copies = []
    for slot in range(slots):
        pltpu.make_async_copy(held.at[slot], held.at[slot], left_sems.at[slot, 0]).wait()
        flipped = held[slot].astype(jnp.float32).T.astype(jnp.bfloat16)
        for piece in range(pieces):
            turned[slot, piece] = flipped[:, piece * block : (piece + 1) * block]
        for step in range(times):
            start = pl.multiple_of((time + step) % times * share, share)
            for piece in range(pieces):
                copy = pltpu.make_async_copy(
                    turned.at[slot, piece, pl.ds(start, share)],
                    outs[step].at[slot, rows + piece * share : rows + (piece + 1) * share],
                    out_sems.at[slot, step, piece],
                )
                copy.start()
                copies.append(copy)
    for slot in range(slots):
        for n, target in enumerate(rights[slot]):
            pltpu.make_async_copy(target, target, right_sems.at[slot, n]).wait()
    for copy in copies:
        copy.wait()


def arrange(rows, bins, packs, left_all, right_all):
    times = len(packs)
    share = left_all.shape[0]
    block = share * times
    wide = times * rows
    each = left_all.shape[1] // wide
    for step, pack in enumerate(packs):
        for index in range(each):
            base = index * wide + step * rows
            done = 0
            while done < rows:
                at = index * rows + done
                width = min(rows - done, block - at % block)
                low = each * rows + at // block * share
                left_all[:, base + done : base + done + width] = pack[
                    0, low : low + share, at % block : at % block + width
                ].astype(jnp.float32)
                done += width
            for pair in range(rows // (2 * bins)):
                row = index * rows + pair * 2 * bins
                at = base + pair * 2 * bins
                real_part = pack[0, row : row + bins, :]
                imag_part = pack[0, row + bins : row + 2 * bins, :]
                right_all[at : at + bins, :block] = real_part
                right_all[at : at + bins, block:] = imag_part
                right_all[at + bins : at + 2 * bins, :block] = imag_part
                right_all[at + bins : at + 2 * bins, block:] = -real_part


def cross_spectra(bins, wide, first, chunk, left_all, right_all, cross_ref):
    each = left_all.shape[1] // wide
    block = right_all.shape[1] // 2
    half = each * bins
    column = lax.broadcasted_iota(jnp.int32, (bins, wide), 1) % bins
    row = lax.broadcasted_iota(jnp.int32, (bins, wide), 0)
    keep = column == row
    several = 4 if chunk % 4 == 0 else 2
    for group in range(each):
        weights = right_all[group * wide : (group + 1) * wide, :]
        for start in range(0, chunk, several):
            pieces = []
            for i in range(several):
                line = left_all[pl.ds(first + start + i, 1), group * wide : (group + 1) * wide]
                pieces.append(jnp.where(keep, jnp.broadcast_to(line, (bins, wide)), 0.0).astype(jnp.bfloat16))
            product = jnp.dot(jnp.concatenate(pieces, axis=0), weights, preferred_element_type=jnp.float32)
            product = product.astype(jnp.bfloat16)
            for i in range(several):
                at = start + i
                lanes = slice(at % 2 * block, (at % 2 + 1) * block)
                piece = product[i * bins : (i + 1) * bins]
                cross_ref[at // 2, group * bins : (group + 1) * bins, lanes] = piece[:, :block]
                cross_ref[at // 2, half + group * bins : half + (group + 1) * bins, lanes] = piece[:, block:]


def cross_kernel(bins, rows, times, counts_ref, *refs):
    packs, (table_ref, out_ref, kept_ref, left_all, right_all) = refs[:times], refs[times:]
    kept_ref[...] = table_ref[...]

    @pl.when(pl.program_id(0) < counts_ref[0])
    def _():
        arrange(rows, bins, packs, left_all, right_all)
        cross_spectra(bins, times * rows, 0, left_all.shape[0], left_all, right_all, out_ref.at[0])


def stack_kernel(bins, rows, times, chunk, counts_ref, *refs):
    packs, table_ref, early, refs = refs[:times], refs[times], refs[times + 1 : -4], refs[-4:]
    out_ref, left_all, right_all, cross_ref = refs
    part = pl.program_id(1)
    lanes = 2 * left_all.shape[0] * times
    live = pl.program_id(0) < counts_ref[0]

    @pl.when(live & (part == 0))
    def _():
        arrange(rows, bins, packs, left_all, right_all)

    @pl.when(live)
    def _():
        cross_spectra(bins, times * rows, part * chunk, chunk, left_all, right_all, cross_ref)
        table = table_ref[...]
        for pair in range(chunk // 2):
            cross = jnp.concatenate([ref[0, pair] for ref in early] + [cross_ref[pair]], axis=0)
            out_ref[0, :, pair * lanes : (pair + 1) * lanes] = jnp.dot(table, cross, preferred_element_type=jnp.float32)

    @pl.when(jnp.logical_not(live))
    def _():
        out_ref[...] = jnp.zeros_like(out_ref)


def chip_dims(size):
    return {16: (4, 2, 2), 64: (16, 4, 1)}.get(size, (size, 1, 1))


def swap(value, dims, axis, by):
    moves = []
    for p in range(math.prod(dims)):
        place = list(np.unravel_index(p, dims))
        place[axis] ^= by
        moves.append((p, int(np.ravel_multi_index(place, dims))))
    return lax.ppermute(value, "pair", moves)


def column_layout(dims):
    depth, height, _ = dims
    if (depth, height) == (4, 2):
        order = [[(0, 0), (0, 1)], [(1, 0), (2, 0), (3, 0)], [(1, 1), (2, 1), (3, 1)]]
    else:
        order = [[(0, 0)]]
        for axis, size in ((0, depth), (1, height)):
            bit = size // 2
            while bit:
                order[0] += [(z ^ bit, y) if axis == 0 else (z, y ^ bit) for z, y in order[0]]
                bit //= 2
    return {place: (n, at) for n, places in enumerate(order) for at, place in enumerate(places)}


def after(values, others):
    return lax.optimization_barrier(tuple(values) + tuple(others))[: len(values)]


def gather_piece(own, dims, last, sent):
    depth, height, cores = dims
    if (depth, height) == (4, 2):
        two = swap(own, dims, 0, 2)
        one = swap(own, dims, 0, 1)
        beside = swap(own, dims, 1, 1)
        one, two = after((one, two), [beside] + last)
        three = swap(two, dims, 0, 1)
        (column,) = after([jnp.stack([one, two, three])], sent)
        arrays = [jnp.stack([own, beside]), column, swap(column, dims, 1, 1)]
        ready = (column,)
    else:
        held = own[None]
        for axis, size in ((0, depth), (1, height)):
            bit = size // 2
            while bit:
                held = jnp.concatenate([held, swap(held, dims, axis, bit)])
                bit //= 2
        arrays = [held]
        ready = (held,)
    if cores == 1:
        return arrays, ready
    return [value for array in arrays for value in (array, swap(array, dims, 2, 1))], ready


def shards(traces, owner, tiles, counts):
    seg_count, block, _ = traces.shape
    times = lax.axis_size("tm")
    segments = seg_count * times
    share = block // times
    slots = tiles.shape[0]
    bins = max(16, 128 // segments)
    groups = NF // bins
    rows = seg_count * 2 * bins
    wide = rows * times
    total = groups * rows
    part_rows = total // PIECES
    dims = chip_dims(lax.axis_size("pair"))
    smem = pl.BlockSpec(memory_space=pltpu.SMEM)
    anywhere = pl.BlockSpec(memory_space=pl.ANY)
    high, low = forward_table()
    white = pl.pallas_call(
        functools.partial(whiten_kernel, bins),
        in_specs=[anywhere] * 3,
        out_shape=[jax.ShapeDtypeStruct((part_rows, block), jnp.bfloat16)] * PIECES,
        scratch_shapes=[
            pltpu.VMEM((CHUNKS, seg_count, block, NT // CHUNKS), jnp.float32),
            pltpu.VMEM((CHUNKS, 2 * NF, NT // CHUNKS), jnp.bfloat16),
            pltpu.VMEM((CHUNKS, 2 * NF, NT // CHUNKS), jnp.bfloat16),
            pltpu.VMEM((NF + 16, seg_count * block), jnp.float32),
            pltpu.SemaphoreType.DMA((CHUNKS, 3)),
        ],
        compiler_params=pltpu.CompilerParams(vmem_limit_bytes=(64 << 20) - (384 << 10)),
        name="whiten",
    )(traces, jnp.asarray(high), jnp.asarray(low))

    known = owner.shape[0]
    chosen = tiles.reshape(-1, 1) == jnp.arange(known, dtype=jnp.int32)
    stored = jnp.sum(jnp.where(chosen, owner, 0), axis=1)
    plan = jnp.concatenate([stored ^ lax.axis_index("pair"), lax.axis_index("tm")[None]]).astype(jnp.int32)

    layout = column_layout(dims)
    pack = part_rows + part_rows // block * share
    packs = []
    ready = ()
    last = []
    sends = []
    for own in white:
        if ready:
            own, plan = after((own, plan), ready)
            (plan,) = after((plan,), packs[-1][1:])
        sources, ready = gather_piece(own, dims, last, sends)
        last = [sources[-dims[2]]]
        own, *sends = pl.pallas_call(
            functools.partial(pick_kernel, dims, layout, 2 * slots),
            in_specs=[smem] + [anywhere] * len(sources),
            out_specs=[anywhere] * times,
            out_shape=[jax.ShapeDtypeStruct((slots, pack, block), jnp.bfloat16)] * times,
            scratch_shapes=[
                pltpu.VMEM((slots, part_rows, block), jnp.bfloat16),
                pltpu.VMEM((slots, part_rows // block, block, block), jnp.bfloat16),
                pltpu.SemaphoreType.DMA((slots, 1)),
                pltpu.SemaphoreType.DMA((slots, times)),
                pltpu.SemaphoreType.DMA((slots, times, part_rows // block)),
            ],
            compiler_params=pltpu.CompilerParams(vmem_limit_bytes=8 << 20),
            name="pick",
        )(plan, *sources)
        arrived = [own]
        for step in range(1, times):
            moves = [(t, (t + step) % times) for t in range(times)]
            arrived.append(lax.ppermute(sends[step - 1], "tm", moves))
        packs.append(arrived)

    parts = 2 if share % 4 == 0 else 1
    chunk = share // parts
    depth = 2 * NF // PIECES
    half = NF // PIECES
    table = inverse_table(segments)
    order = [c * NF + piece * half + k for piece in range(PIECES) for c in range(2) for k in range(half)]
    table = jnp.asarray(table[:, order])
    scratch = [
        pltpu.VMEM((share, groups // PIECES * wide), jnp.float32),
        pltpu.VMEM((groups // PIECES * wide, 2 * block), jnp.bfloat16),
    ]
    early = []
    for arrived in packs[:-1]:
        cross, table = pl.pallas_call(
            functools.partial(cross_kernel, bins, rows, times),
            grid_spec=pltpu.PrefetchScalarGridSpec(
                num_scalar_prefetch=1,
                grid=(slots,),
                in_specs=[pl.BlockSpec((1, pack, block), lambda q, cnt: (q, 0, 0))] * times
                + [pl.BlockSpec((LAGS, 2 * NF), lambda q, cnt: (0, 0))],
                out_specs=[
                    pl.BlockSpec((1, share // 2, depth, 2 * block), lambda q, cnt: (q, 0, 0, 0)),
                    pl.BlockSpec((LAGS, 2 * NF), lambda q, cnt: (0, 0)),
                ],
                scratch_shapes=scratch,
            ),
            out_shape=[
                jax.ShapeDtypeStruct((slots, share // 2, depth, 2 * block), jnp.bfloat16),
                jax.ShapeDtypeStruct((LAGS, 2 * NF), jnp.bfloat16),
            ],
            compiler_params=pltpu.CompilerParams(vmem_limit_bytes=24 << 20),
            name="cross",
        )(counts, *arrived, table)
        early.append(cross)
    return pl.pallas_call(
        functools.partial(stack_kernel, bins, rows, times, chunk),
        grid_spec=pltpu.PrefetchScalarGridSpec(
            num_scalar_prefetch=1,
            grid=(slots, parts),
            in_specs=[pl.BlockSpec((1, pack, block), lambda q, k, cnt: (q, 0, 0))] * times
            + [pl.BlockSpec((LAGS, 2 * NF), lambda q, k, cnt: (0, 0))]
            + [pl.BlockSpec((1, chunk // 2, depth, 2 * block), lambda q, k, cnt: (q, k, 0, 0))] * len(early),
            out_specs=pl.BlockSpec((1, LAGS, chunk * block), lambda q, k, cnt: (q, 0, k)),
            scratch_shapes=scratch + [pltpu.VMEM((chunk // 2, depth, 2 * block), jnp.bfloat16)],
        ),
        out_shape=jax.ShapeDtypeStruct((slots, LAGS, share * block), jnp.float32),
        compiler_params=pltpu.CompilerParams(vmem_limit_bytes=24 << 20),
        name="stack",
    )(counts, *packs[-1], table, *early)


def solution(mesh):
    placed = (P("tm", "pair", None), P(), P("pair", None), P("pair"))
    return jax.shard_map(
        shards, mesh=mesh, in_specs=placed, out_specs=P("pair", None, "tm"), check_vma=False
    )
```

```python
import functools
import math

import jax
import jax.numpy as jnp
import ml_dtypes
import numpy as np
from jax import lax
from jax.experimental import pallas as pl
from jax.experimental.pallas import tpu as pltpu
from jax.sharding import PartitionSpec as P

NT = 1024
NF = 128
LOW_BIN = 8
LAGS = 128


def forward_table():
    phase = (LOW_BIN + np.arange(NF))[:, None] * np.arange(NT)[None, :] % NT
    angle = phase * (2.0 * math.pi / NT)
    table = np.concatenate([np.cos(angle), -np.sin(angle)], axis=0)
    high = table.astype(ml_dtypes.bfloat16)
    low = (table - high.astype(np.float64)).astype(ml_dtypes.bfloat16)
    return np.stack([high, low])


def inverse_table(segments):
    shifts = np.arange(LAGS) - LAGS // 2
    phase = shifts[:, None] * (LOW_BIN + np.arange(NF))[None, :] % NT
    angle = phase * (2.0 * math.pi / NT)
    scale = 1.0 / math.sqrt(segments * NF)
    table = np.concatenate([np.cos(angle), -np.sin(angle)], axis=1) * scale
    return table.astype(ml_dtypes.bfloat16)


def nt_dot(a, b):
    return lax.dot_general(a, b, (((1,), (1,)), ((), ())), preferred_element_type=jnp.float32)


CHUNKS = 2
PIECES = 2


def whiten_kernel(bins, x_hbm, table_hbm, *refs):
    outs, (x_ref, table_ref, pad_ref, sems) = refs[:-4], refs[-4:]
    _, segments, block, wide = x_ref.shape
    columns = segments * block
    copies = []
    for k in range(CHUNKS):
        span = slice(k * wide, (k + 1) * wide)
        sources = (x_hbm.at[:, :, span], table_hbm.at[:, :, span])
        copies.append(
            [
                pltpu.make_async_copy(source, target.at[k], sems.at[k, n])
                for n, (source, target) in enumerate(zip(sources, (x_ref, table_ref)))
            ]
        )
        for copy in copies[-1]:
            copy.start()
    spectrum = None
    for k in range(CHUNKS):
        for copy in copies[k]:
            copy.wait()
        x = x_ref[k].reshape(columns, wide)
        x_high = x.astype(jnp.bfloat16)
        x_low = (x - x_high.astype(jnp.float32)).astype(jnp.bfloat16)
        high = table_ref[k, 0]
        part = nt_dot(high, x_high) + nt_dot(high, x_low) + nt_dot(table_ref[k, 1], x_high)
        spectrum = part if spectrum is None else spectrum + part
    real_part = spectrum[:NF]
    imag_part = spectrum[NF:]
    power = real_part * real_part + imag_part * imag_part
    edge = jnp.zeros((8, columns), jnp.float32)
    pad_ref[0:8, :] = edge
    pad_ref[8 + NF : 16 + NF, :] = edge
    pad_ref[8 : 8 + NF, :] = power
    total = pad_ref[6 : 6 + NF, :]
    for offset in range(7, 11):
        total = total + pad_ref[offset : offset + NF, :]
    bin_id = lax.broadcasted_iota(jnp.int32, (NF, columns), 0)
    counted = (jnp.minimum(bin_id + 2, NF - 1) - jnp.maximum(bin_id - 2, 0) + 1).astype(jnp.float32)
    smooth = total / counted
    level = jnp.mean(power, axis=0, keepdims=True)
    factor = lax.rsqrt(smooth + 0.05 * level + 1e-06)
    parts = ((real_part * factor).astype(jnp.bfloat16), (imag_part * factor).astype(jnp.bfloat16))
    each = NF // bins // len(outs)
    for group in range(NF // bins):
        for segment in range(segments):
            for c in range(2):
                row = ((group % each * segments + segment) * 2 + c) * bins
                outs[group // each][row : row + bins, :] = parts[c][
                    group * bins : (group + 1) * bins, segment * block : (segment + 1) * block
                ]


def pick_kernel(dims, layout, time_at, plan_ref, *refs):
    depth, height, cores = dims
    count = cores * (1 + max(array for array, _ in layout.values()))
    sources, outs, (held, turned) = refs[:count], refs[count:-2], refs[-2:]
    slots, rows, block = held.shape
    times = len(outs)
    share = block // times
    time = plan_ref[time_at]

    def fetch(slot, side, targets):
        away = plan_ref[slot * 2 + side]
        place = away // cores
        array = jnp.int32(0)
        index = jnp.int32(0)
        for (dz, dy), (where, at) in layout.items():
            here = place == dz * height + dy
            array = jnp.where(here, where, array)
            index = jnp.where(here, at, index)
        for n, source in enumerate(sources):

            @pl.when(away % cores + cores * array == n)
            def _():
                value = source[index]
                for target in targets:
                    target[...] = value

    for slot in range(slots):
        fetch(slot, 0, [held.at[slot]])
        fetch(slot, 1, [out.at[slot, :rows] for out in outs])
    for slot in range(slots):
        flipped = held[slot].astype(jnp.float32).T.astype(jnp.bfloat16)
        for piece in range(rows // block):
            turned[slot, piece] = flipped[:, piece * block : (piece + 1) * block]
        for step, out in enumerate(outs):
            start = pl.multiple_of((time + step) % times * share, share)
            for piece in range(rows // block):
                low = rows + piece * share
                out[slot, low : low + share] = turned[slot, piece, pl.ds(start, share)]


def arrange(rows, bins, packs, left_all, right_all):
    times = len(packs)
    share = left_all.shape[0]
    block = share * times
    wide = times * rows
    each = left_all.shape[1] // wide
    for step, pack in enumerate(packs):
        for index in range(each):
            base = index * wide + step * rows
            done = 0
            while done < rows:
                at = index * rows + done
                width = min(rows - done, block - at % block)
                low = each * rows + at // block * share
                left_all[:, base + done : base + done + width] = pack[
                    0, low : low + share, at % block : at % block + width
                ].astype(jnp.float32)
                done += width
            for pair in range(rows // (2 * bins)):
                row = index * rows + pair * 2 * bins
                at = base + pair * 2 * bins
                real_part = pack[0, row : row + bins, :]
                imag_part = pack[0, row + bins : row + 2 * bins, :]
                right_all[at : at + bins, :block] = real_part
                right_all[at : at + bins, block:] = imag_part
                right_all[at + bins : at + 2 * bins, :block] = imag_part
                right_all[at + bins : at + 2 * bins, block:] = -real_part


def cross_spectra(bins, wide, first, chunk, left_all, right_all, cross_ref):
    each = left_all.shape[1] // wide
    block = right_all.shape[1] // 2
    half = each * bins
    column = lax.broadcasted_iota(jnp.int32, (bins, wide), 1) % bins
    row = lax.broadcasted_iota(jnp.int32, (bins, wide), 0)
    keep = column == row
    several = 4 if chunk % 4 == 0 else 2
    for group in range(each):
        weights = right_all[group * wide : (group + 1) * wide, :]
        for start in range(0, chunk, several):
            pieces = []
            for i in range(several):
                line = left_all[pl.ds(first + start + i, 1), group * wide : (group + 1) * wide]
                pieces.append(jnp.where(keep, jnp.broadcast_to(line, (bins, wide)), 0.0).astype(jnp.bfloat16))
            product = jnp.dot(jnp.concatenate(pieces, axis=0), weights, preferred_element_type=jnp.float32)
            product = product.astype(jnp.bfloat16)
            for i in range(several):
                at = start + i
                lanes = slice(at % 2 * block, (at % 2 + 1) * block)
                piece = product[i * bins : (i + 1) * bins]
                cross_ref[at // 2, group * bins : (group + 1) * bins, lanes] = piece[:, :block]
                cross_ref[at // 2, half + group * bins : half + (group + 1) * bins, lanes] = piece[:, block:]


def cross_kernel(bins, rows, times, counts_ref, *refs):
    packs, (table_ref, out_ref, kept_ref, left_all, right_all) = refs[:times], refs[times:]
    kept_ref[...] = table_ref[...]

    @pl.when(pl.program_id(0) < counts_ref[0])
    def _():
        arrange(rows, bins, packs, left_all, right_all)
        cross_spectra(bins, times * rows, 0, left_all.shape[0], left_all, right_all, out_ref.at[0])


def stack_kernel(bins, rows, times, chunk, counts_ref, *refs):
    packs, table_ref, early, refs = refs[:times], refs[times], refs[times + 1 : -4], refs[-4:]
    out_ref, left_all, right_all, cross_ref = refs
    part = pl.program_id(1)
    lanes = 2 * left_all.shape[0] * times
    live = pl.program_id(0) < counts_ref[0]

    @pl.when(live & (part == 0))
    def _():
        arrange(rows, bins, packs, left_all, right_all)

    @pl.when(live)
    def _():
        cross_spectra(bins, times * rows, part * chunk, chunk, left_all, right_all, cross_ref)
        table = table_ref[...]
        for pair in range(chunk // 2):
            cross = jnp.concatenate([ref[0, pair] for ref in early] + [cross_ref[pair]], axis=0)
            out_ref[0, :, pair * lanes : (pair + 1) * lanes] = jnp.dot(table, cross, preferred_element_type=jnp.float32)

    @pl.when(jnp.logical_not(live))
    def _():
        out_ref[...] = jnp.zeros_like(out_ref)


def chip_dims(size):
    return {16: (4, 2, 2), 64: (16, 4, 1)}.get(size, (size, 1, 1))


def swap(value, dims, axis, by):
    moves = []
    for p in range(math.prod(dims)):
        place = list(np.unravel_index(p, dims))
        place[axis] ^= by
        moves.append((p, int(np.ravel_multi_index(place, dims))))
    return lax.ppermute(value, "pair", moves)


def column_layout(dims):
    depth, height, _ = dims
    order = [[(0, 0)]]
    for axis, size in ((0, depth), (1, height)):
        bit = size // 2
        while bit:
            more = [(z ^ bit, y) if axis == 0 else (z, y ^ bit) for z, y in order[0]]
            if axis == 1 and bit == 1:
                order.append(more)
            else:
                order[0] += more
            bit //= 2
    return {place: (n, at) for n, places in enumerate(order) for at, place in enumerate(places)}


def after(values, others):
    return lax.optimization_barrier(tuple(values) + tuple(others))[: len(values)]


def gather_piece(own, dims):
    depth, height, cores = dims
    held = own[None]
    arrays = [held]
    for axis, size in ((0, depth), (1, height)):
        bit = size // 2
        while bit:
            more = swap(held, dims, axis, bit)
            if axis == 1 and bit == 1:
                arrays = [held, more]
            elif held.shape[0] == 1:
                (room,) = after([jnp.concatenate([held, held])], ())
                held = lax.dynamic_update_slice(room, more, (1, 0, 0))
                arrays = [held]
            else:
                held = jnp.concatenate([held, more])
                arrays = [held]
            bit //= 2
    if cores == 1:
        return arrays
    return [value for array in arrays for value in (array, swap(array, dims, 2, 1))]


def shards(traces, owner, tiles, counts):
    seg_count, block, _ = traces.shape
    times = lax.axis_size("tm")
    segments = seg_count * times
    share = block // times
    slots = tiles.shape[0]
    bins = max(16, 128 // segments)
    groups = NF // bins
    rows = seg_count * 2 * bins
    wide = rows * times
    total = groups * rows
    part_rows = total // PIECES
    dims = chip_dims(lax.axis_size("pair"))
    smem = pl.BlockSpec(memory_space=pltpu.SMEM)
    anywhere = pl.BlockSpec(memory_space=pl.ANY)
    white = pl.pallas_call(
        functools.partial(whiten_kernel, bins),
        in_specs=[anywhere] * 2,
        out_shape=[jax.ShapeDtypeStruct((part_rows, block), jnp.bfloat16)] * PIECES,
        scratch_shapes=[
            pltpu.VMEM((CHUNKS, seg_count, block, NT // CHUNKS), jnp.float32),
            pltpu.VMEM((CHUNKS, 2, 2 * NF, NT // CHUNKS), jnp.bfloat16),
            pltpu.VMEM((NF + 16, seg_count * block), jnp.float32),
            pltpu.SemaphoreType.DMA((CHUNKS, 2)),
        ],
        compiler_params=pltpu.CompilerParams(vmem_limit_bytes=63 << 20),
        name="whiten",
    )(traces, jnp.asarray(forward_table()))

    known = owner.shape[0]
    chosen = tiles.reshape(-1, 1) == jnp.arange(known, dtype=jnp.int32)
    stored = jnp.sum(jnp.where(chosen, owner, 0), axis=1)
    plan = jnp.concatenate([stored ^ lax.axis_index("pair"), lax.axis_index("tm")[None]]).astype(jnp.int32)

    layout = column_layout(dims)
    pack = part_rows + part_rows // block * share
    packs = []
    for own in white:
        sources = gather_piece(own, dims)
        if packs:
            (plan,) = after((plan,), packs[-1][1:])
        own, *sends = pl.pallas_call(
            functools.partial(pick_kernel, dims, layout, 2 * slots),
            in_specs=[smem] + [pl.BlockSpec(memory_space=pltpu.VMEM)] * len(sources),
            out_shape=[jax.ShapeDtypeStruct((slots, pack, block), jnp.bfloat16)] * times,
            scratch_shapes=[
                pltpu.VMEM((slots, part_rows, block), jnp.bfloat16),
                pltpu.VMEM((slots, part_rows // block, block, block), jnp.bfloat16),
            ],
            compiler_params=pltpu.CompilerParams(vmem_limit_bytes=8 << 20),
            name="pick",
        )(plan, *sources)
        arrived = [own]
        for step in range(1, times):
            moves = [(t, (t + step) % times) for t in range(times)]
            arrived.append(lax.ppermute(sends[step - 1], "tm", moves))
        packs.append(arrived)

    parts = 2 if share % 4 == 0 else 1
    chunk = share // parts
    depth = 2 * NF // PIECES
    half = NF // PIECES
    table = inverse_table(segments)
    order = [c * NF + piece * half + k for piece in range(PIECES) for c in range(2) for k in range(half)]
    table = jnp.asarray(table[:, order])
    scratch = [
        pltpu.VMEM((share, groups // PIECES * wide), jnp.float32),
        pltpu.VMEM((groups // PIECES * wide, 2 * block), jnp.bfloat16),
    ]
    early = []
    for arrived in packs[:-1]:
        cross, table = pl.pallas_call(
            functools.partial(cross_kernel, bins, rows, times),
            grid_spec=pltpu.PrefetchScalarGridSpec(
                num_scalar_prefetch=1,
                grid=(slots,),
                in_specs=[pl.BlockSpec((1, pack, block), lambda q, cnt: (q, 0, 0))] * times
                + [pl.BlockSpec((LAGS, 2 * NF), lambda q, cnt: (0, 0))],
                out_specs=[
                    pl.BlockSpec((1, share // 2, depth, 2 * block), lambda q, cnt: (q, 0, 0, 0)),
                    pl.BlockSpec((LAGS, 2 * NF), lambda q, cnt: (0, 0)),
                ],
                scratch_shapes=scratch,
            ),
            out_shape=[
                jax.ShapeDtypeStruct((slots, share // 2, depth, 2 * block), jnp.bfloat16),
                jax.ShapeDtypeStruct((LAGS, 2 * NF), jnp.bfloat16),
            ],
            compiler_params=pltpu.CompilerParams(vmem_limit_bytes=24 << 20),
            name="cross",
        )(counts, *arrived, table)
        early.append(cross)
    return pl.pallas_call(
        functools.partial(stack_kernel, bins, rows, times, chunk),
        grid_spec=pltpu.PrefetchScalarGridSpec(
            num_scalar_prefetch=1,
            grid=(slots, parts),
            in_specs=[pl.BlockSpec((1, pack, block), lambda q, k, cnt: (q, 0, 0))] * times
            + [pl.BlockSpec((LAGS, 2 * NF), lambda q, k, cnt: (0, 0))]
            + [pl.BlockSpec((1, chunk // 2, depth, 2 * block), lambda q, k, cnt: (q, k, 0, 0))] * len(early),
            out_specs=pl.BlockSpec((1, LAGS, chunk * block), lambda q, k, cnt: (q, 0, k)),
            scratch_shapes=scratch + [pltpu.VMEM((chunk // 2, depth, 2 * block), jnp.bfloat16)],
        ),
        out_shape=jax.ShapeDtypeStruct((slots, LAGS, share * block), jnp.float32),
        compiler_params=pltpu.CompilerParams(vmem_limit_bytes=24 << 20),
        name="stack",
    )(counts, *packs[-1], table, *early)


def solution(mesh):
    placed = (P("tm", "pair", None), P(), P("pair", None), P("pair"))
    return jax.shard_map(
        shards, mesh=mesh, in_specs=placed, out_specs=P("pair", None, "tm"), check_vma=False
    )
```

```python
import functools
import math

import jax
import jax.numpy as jnp
import numpy as np
from jax import lax
from jax.experimental import pallas as pl
from jax.experimental.pallas import tpu as pltpu
from jax.sharding import PartitionSpec as P

NT = 1024
NF = 128
LOW_BIN = 8
LAGS = 128


def forward_table():
    phase = (LOW_BIN + np.arange(NF))[:, None] * np.arange(NT)[None, :] % NT
    angle = phase * (2.0 * math.pi / NT)
    return np.concatenate([np.cos(angle), -np.sin(angle)], axis=0).astype(np.float32)


def inverse_table(segments):
    shifts = np.arange(LAGS) - LAGS // 2
    phase = shifts[:, None] * (LOW_BIN + np.arange(NF))[None, :] % NT
    angle = phase * (2.0 * math.pi / NT)
    scale = 1.0 / math.sqrt(segments * NF)
    table = np.concatenate([np.cos(angle), -np.sin(angle)], axis=1) * scale
    return table.astype(np.float32)


def halves(value):
    high = value.astype(jnp.bfloat16)
    return high, (value - high.astype(jnp.float32)).astype(jnp.bfloat16)


def nt_dot(a, b):
    return lax.dot_general(a, b, (((1,), (1,)), ((), ())), preferred_element_type=jnp.float32)


CHUNKS = 2
PIECES = 2


def whiten_kernel(bins, x_hbm, table_hbm, *refs):
    outs, (x_ref, table_ref, pad_ref, sems) = refs[:-4], refs[-4:]
    _, segments, block, wide = x_ref.shape
    columns = segments * block
    copies = []
    for k in range(CHUNKS):
        span = slice(k * wide, (k + 1) * wide)
        sources = (x_hbm.at[:, :, span], table_hbm.at[:, span])
        copies.append(
            [
                pltpu.make_async_copy(source, target.at[k], sems.at[k, n])
                for n, (source, target) in enumerate(zip(sources, (x_ref, table_ref)))
            ]
        )
        for copy in copies[-1]:
            copy.start()
    spectrum = None
    for k in range(CHUNKS):
        for copy in copies[k]:
            copy.wait()
        x = x_ref[k].reshape(columns, wide)
        x_high, x_low = halves(x)
        high, low = halves(table_ref[k])
        part = nt_dot(high, x_high) + nt_dot(high, x_low) + nt_dot(low, x_high)
        spectrum = part if spectrum is None else spectrum + part
    real_part = spectrum[:NF]
    imag_part = spectrum[NF:]
    power = real_part * real_part + imag_part * imag_part
    edge = jnp.zeros((8, columns), jnp.float32)
    pad_ref[0:8, :] = edge
    pad_ref[8 + NF : 16 + NF, :] = edge
    pad_ref[8 : 8 + NF, :] = power
    total = pad_ref[6 : 6 + NF, :]
    for offset in range(7, 11):
        total = total + pad_ref[offset : offset + NF, :]
    bin_id = lax.broadcasted_iota(jnp.int32, (NF, columns), 0)
    counted = (jnp.minimum(bin_id + 2, NF - 1) - jnp.maximum(bin_id - 2, 0) + 1).astype(jnp.float32)
    smooth = total / counted
    level = jnp.mean(power, axis=0, keepdims=True)
    factor = lax.rsqrt(smooth + 0.05 * level + 1e-06)
    parts = ((real_part * factor).astype(jnp.bfloat16), (imag_part * factor).astype(jnp.bfloat16))
    each = NF // bins // len(outs)
    for group in range(NF // bins):
        for segment in range(segments):
            for c in range(2):
                row = ((group % each * segments + segment) * 2 + c) * bins
                outs[group // each][row : row + bins, :] = parts[c][
                    group * bins : (group + 1) * bins, segment * block : (segment + 1) * block
                ]


def pick_kernel(dims, layout, time_at, joined, plan_ref, *refs):
    depth, height, cores = dims
    count = cores * (1 + max(array for array, _ in layout.values()))
    sources, outs, (held, turned) = refs[:count], refs[count:-2], refs[-2:]
    slots, _, rows, block = held.shape
    times = len(outs)
    share = block // times
    time = plan_ref[time_at]

    def fetch(slot, side, targets):
        away = plan_ref[slot * 2 + side]
        place = away // cores
        array = jnp.int32(0)
        index = jnp.int32(0)
        for (dz, dy), (where, at) in layout.items():
            here = place == dz * height + dy
            array = jnp.where(here, where, array)
            index = jnp.where(here, at * joined, index)
        for n, source in enumerate(sources):

            @pl.when(away % cores + cores * array == n)
            def _():
                for step in range(joined):
                    value = source[index + step]
                    for target in targets[step]:
                        target[...] = value

    for slot in range(slots):
        fetch(slot, 0, [[held.at[slot, step]] for step in range(joined)])
        rights = [out.at[slot, :rows] for out in outs]
        fetch(slot, 1, [rights] if joined == 1 else [[right] for right in rights])
    for slot in range(slots):
        for source in range(joined):
            flipped = held[slot, source].astype(jnp.float32).T.astype(jnp.bfloat16)
            for piece in range(rows // block):
                turned[slot, source, piece] = flipped[:, piece * block : (piece + 1) * block]
        for step, out in enumerate(outs):
            source, part = (0, (time + step) % times) if joined == 1 else (step, time)
            start = pl.multiple_of(part * share, share)
            for piece in range(rows // block):
                low = rows + piece * share
                out[slot, low : low + share] = turned[slot, source, piece, pl.ds(start, share)]


def arrange(rows, bins, packs, left_all, right_all):
    times = len(packs)
    share = left_all.shape[0]
    block = share * times
    wide = times * rows
    each = left_all.shape[1] // wide
    for step, pack in enumerate(packs):
        for index in range(each):
            base = index * wide + step * rows
            done = 0
            while done < rows:
                at = index * rows + done
                width = min(rows - done, block - at % block)
                low = each * rows + at // block * share
                left_all[:, base + done : base + done + width] = pack[
                    0, low : low + share, at % block : at % block + width
                ].astype(jnp.float32)
                done += width
            for pair in range(rows // (2 * bins)):
                row = index * rows + pair * 2 * bins
                at = base + pair * 2 * bins
                real_part = pack[0, row : row + bins, :]
                imag_part = pack[0, row + bins : row + 2 * bins, :]
                right_all[at : at + bins, :block] = real_part
                right_all[at : at + bins, block:] = imag_part
                right_all[at + bins : at + 2 * bins, :block] = imag_part
                right_all[at + bins : at + 2 * bins, block:] = -real_part


def cross_spectra(bins, wide, first, chunk, left_all, right_all, cross_ref):
    each = left_all.shape[1] // wide
    block = right_all.shape[1] // 2
    half = each * bins
    column = lax.broadcasted_iota(jnp.int32, (bins, wide), 1) % bins
    row = lax.broadcasted_iota(jnp.int32, (bins, wide), 0)
    keep = column == row
    several = 4 if chunk % 4 == 0 else 2
    for group in range(each):
        weights = right_all[group * wide : (group + 1) * wide, :]
        for start in range(0, chunk, several):
            pieces = []
            for i in range(several):
                line = left_all[pl.ds(first + start + i, 1), group * wide : (group + 1) * wide]
                pieces.append(jnp.where(keep, jnp.broadcast_to(line, (bins, wide)), 0.0).astype(jnp.bfloat16))
            product = jnp.dot(jnp.concatenate(pieces, axis=0), weights, preferred_element_type=jnp.float32)
            product = product.astype(jnp.bfloat16)
            for i in range(several):
                at = start + i
                lanes = slice(at % 2 * block, (at % 2 + 1) * block)
                piece = product[i * bins : (i + 1) * bins]
                cross_ref[at // 2, group * bins : (group + 1) * bins, lanes] = piece[:, :block]
                cross_ref[at // 2, half + group * bins : half + (group + 1) * bins, lanes] = piece[:, block:]


def cross_kernel(bins, rows, times, counts_ref, *refs):
    packs, (table_ref, out_ref, kept_ref, left_all, right_all) = refs[:times], refs[times:]
    kept_ref[...] = table_ref[...].astype(jnp.bfloat16)

    @pl.when(pl.program_id(0) < counts_ref[0])
    def _():
        arrange(rows, bins, packs, left_all, right_all)
        cross_spectra(bins, times * rows, 0, left_all.shape[0], left_all, right_all, out_ref.at[0])


def stack_kernel(bins, rows, times, chunk, counts_ref, *refs):
    packs, table_ref, early, refs = refs[:times], refs[times], refs[times + 1 : -4], refs[-4:]
    out_ref, left_all, right_all, cross_ref = refs
    part = pl.program_id(1)
    lanes = 2 * left_all.shape[0] * times
    live = pl.program_id(0) < counts_ref[0]

    @pl.when(live & (part == 0))
    def _():
        arrange(rows, bins, packs, left_all, right_all)

    @pl.when(live)
    def _():
        cross_spectra(bins, times * rows, part * chunk, chunk, left_all, right_all, cross_ref)
        table = table_ref[...]
        for pair in range(chunk // 2):
            cross = jnp.concatenate([ref[0, pair] for ref in early] + [cross_ref[pair]], axis=0)
            out_ref[0, :, pair * lanes : (pair + 1) * lanes] = jnp.dot(table, cross, preferred_element_type=jnp.float32)

    @pl.when(jnp.logical_not(live))
    def _():
        out_ref[...] = jnp.zeros_like(out_ref)


def chip_dims(size):
    return {16: (4, 2, 2), 64: (16, 4, 1)}.get(size, (size, 1, 1))


def swap(value, dims, axis, by):
    moves = []
    for p in range(math.prod(dims)):
        place = list(np.unravel_index(p, dims))
        place[axis] ^= by
        moves.append((p, int(np.ravel_multi_index(place, dims))))
    return lax.ppermute(value, "pair", moves)


def column_layout(dims):
    depth, height, _ = dims
    order = [[(0, 0)]]
    for axis, size in ((0, depth), (1, height)):
        bit = size // 2
        while bit:
            more = [(z ^ bit, y) if axis == 0 else (z, y ^ bit) for z, y in order[0]]
            if axis == 1 and bit == 1:
                order.append(more)
            else:
                order[0] += more
            bit //= 2
    return {place: (n, at) for n, places in enumerate(order) for at, place in enumerate(places)}


def after(values, others):
    return lax.optimization_barrier(tuple(values) + tuple(others))[: len(values)]


def join(held, more):
    (room,) = after([jnp.concatenate([held, held])], ())
    return lax.dynamic_update_slice(room, more, (held.shape[0], 0, 0))


def swap_times(value, step, times):
    return lax.ppermute(value, "tm", [((t + step) % times, t) for t in range(times)])


def gather_one(own, dims):
    depth, height, _ = dims
    held = own
    arrays = [held]
    for axis, size in ((0, depth), (1, height)):
        bit = size // 2
        while bit:
            more = swap(held, dims, axis, bit)
            if axis == 1 and bit == 1:
                arrays = [held, more]
            else:
                held = join(held, more) if held.shape[0] == 1 else jnp.concatenate([held, more])
                arrays = [held]
            bit //= 2
    return arrays


def gather_two(first, second, dims):
    other = swap_times(second, 1, 2)
    first_far = swap(first, dims, 0, 2)
    pair = join(second, other)
    pair_far = swap(pair, dims, 0, 2)
    first_two = join(first, first_far)
    (first_two,) = after([first_two], [pair])
    first_near = swap(first_two, dims, 0, 1)
    first_four = jnp.concatenate([first_two, first_near])
    pair_two = jnp.concatenate([pair, pair_far])
    (first_four,) = after([first_four], [pair_two])
    first_beside = swap(first_four, dims, 1, 1)
    pair_near = swap(pair_two, dims, 0, 1)
    pair_four = jnp.concatenate([pair_two, pair_near])
    pair_beside = swap(pair_four, dims, 1, 1)
    return [first_four, first_beside], [pair_four, pair_beside]


def both_cores(arrays, dims):
    if dims[2] == 1:
        return arrays
    return [value for array in arrays for value in (array, swap(array, dims, 2, 1))]


def shards(traces, owner, tiles, counts):
    seg_count, block, _ = traces.shape
    times = lax.axis_size("tm")
    segments = seg_count * times
    share = block // times
    slots = tiles.shape[0]
    bins = max(16, 128 // segments)
    groups = NF // bins
    rows = seg_count * 2 * bins
    wide = rows * times
    total = groups * rows
    part_rows = total // PIECES
    dims = chip_dims(lax.axis_size("pair"))
    smem = pl.BlockSpec(memory_space=pltpu.SMEM)
    anywhere = pl.BlockSpec(memory_space=pl.ANY)
    white = pl.pallas_call(
        functools.partial(whiten_kernel, bins),
        in_specs=[anywhere] * 2,
        out_shape=[jax.ShapeDtypeStruct((part_rows, block), jnp.bfloat16)] * PIECES,
        scratch_shapes=[
            pltpu.VMEM((CHUNKS, seg_count, block, NT // CHUNKS), jnp.float32),
            pltpu.VMEM((CHUNKS, 2 * NF, NT // CHUNKS), jnp.float32),
            pltpu.VMEM((NF + 16, seg_count * block), jnp.float32),
            pltpu.SemaphoreType.DMA((CHUNKS, 2)),
        ],
        compiler_params=pltpu.CompilerParams(vmem_limit_bytes=63 << 20),
        name="whiten",
    )(traces, jnp.asarray(forward_table()))

    known = owner.shape[0]
    chosen = tiles.reshape(-1, 1) == jnp.arange(known, dtype=jnp.int32)
    stored = jnp.sum(jnp.where(chosen, owner, 0), axis=1)
    plan = jnp.concatenate([stored ^ lax.axis_index("pair"), lax.axis_index("tm")[None]]).astype(jnp.int32)

    layout = column_layout(dims)
    pack = part_rows + part_rows // block * share
    packs = []
    paired = times == 2 and dims == (4, 2, 2) and PIECES == 2
    blocks = [own[None] for own in white]
    gathered = gather_two(*blocks, dims) if paired else [gather_one(own, dims) for own in blocks]
    for piece, arrays in enumerate(gathered):
        joined = times if paired and piece else 1
        if packs:
            arrays[-1:] = after(arrays[-1:], packs[-1][1:])
        sources = both_cores(arrays, dims)
        arrived = list(pl.pallas_call(
            functools.partial(pick_kernel, dims, layout, 2 * slots, joined),
            in_specs=[smem] + [pl.BlockSpec(memory_space=pltpu.VMEM)] * len(sources),
            out_shape=[jax.ShapeDtypeStruct((slots, pack, block), jnp.bfloat16)] * times,
            scratch_shapes=[
                pltpu.VMEM((slots, joined, part_rows, block), jnp.bfloat16),
                pltpu.VMEM((slots, joined, part_rows // block, block, block), jnp.bfloat16),
            ],
            compiler_params=pltpu.CompilerParams(vmem_limit_bytes=8 << 20),
            cost_estimate=pl.CostEstimate(flops=1, bytes_accessed=1, transcendentals=0),
            name="pick",
        )(plan, *sources))
        if joined == 1:
            for step in range(1, times):
                moves = [(t, (t + step) % times) for t in range(times)]
                arrived[step] = lax.ppermute(arrived[step], "tm", moves)
        packs.append(arrived)

    parts = 4 if share % 32 == 0 else 2
    chunk = share // parts
    depth = 2 * NF // PIECES
    half = NF // PIECES
    table = inverse_table(segments)
    order = [c * NF + piece * half + k for piece in range(PIECES) for c in range(2) for k in range(half)]
    table = jnp.asarray(table[:, order])
    scratch = [
        pltpu.VMEM((share, groups // PIECES * wide), jnp.float32),
        pltpu.VMEM((groups // PIECES * wide, 2 * block), jnp.bfloat16),
    ]
    early = []
    for arrived in packs[:-1]:
        cross, table = pl.pallas_call(
            functools.partial(cross_kernel, bins, rows, times),
            grid_spec=pltpu.PrefetchScalarGridSpec(
                num_scalar_prefetch=1,
                grid=(slots,),
                in_specs=[pl.BlockSpec((1, pack, block), lambda q, cnt: (q, 0, 0))] * times
                + [pl.BlockSpec((LAGS, 2 * NF), lambda q, cnt: (0, 0))],
                out_specs=[
                    pl.BlockSpec((1, share // 2, depth, 2 * block), lambda q, cnt: (q, 0, 0, 0)),
                    pl.BlockSpec((LAGS, 2 * NF), lambda q, cnt: (0, 0)),
                ],
                scratch_shapes=scratch,
            ),
            out_shape=[
                jax.ShapeDtypeStruct((slots, share // 2, depth, 2 * block), jnp.bfloat16),
                jax.ShapeDtypeStruct((LAGS, 2 * NF), jnp.bfloat16),
            ],
            compiler_params=pltpu.CompilerParams(vmem_limit_bytes=24 << 20),
            name="cross",
        )(counts, *arrived, table)
        early.append(cross)
    return pl.pallas_call(
        functools.partial(stack_kernel, bins, rows, times, chunk),
        grid_spec=pltpu.PrefetchScalarGridSpec(
            num_scalar_prefetch=1,
            grid=(slots, parts),
            in_specs=[pl.BlockSpec((1, pack, block), lambda q, k, cnt: (q, 0, 0))] * times
            + [pl.BlockSpec((LAGS, 2 * NF), lambda q, k, cnt: (0, 0))]
            + [pl.BlockSpec((1, chunk // 2, depth, 2 * block), lambda q, k, cnt: (q, k, 0, 0))] * len(early),
            out_specs=pl.BlockSpec((1, LAGS, chunk * block), lambda q, k, cnt: (q, 0, k)),
            scratch_shapes=scratch + [pltpu.VMEM((chunk // 2, depth, 2 * block), jnp.bfloat16)],
        ),
        out_shape=jax.ShapeDtypeStruct((slots, LAGS, share * block), jnp.float32),
        compiler_params=pltpu.CompilerParams(vmem_limit_bytes=24 << 20),
        name="stack",
    )(counts, *packs[-1], table, *early)


def solution(mesh):
    placed = (P("tm", "pair", None), P(), P("pair", None), P("pair"))
    return jax.shard_map(
        shards, mesh=mesh, in_specs=placed, out_specs=P("pair", None, "tm"), check_vma=False
    )
```

```python
import functools
import math

import jax
import jax.numpy as jnp
import numpy as np
from jax import lax
from jax.experimental import pallas as pl
from jax.experimental.pallas import tpu as pltpu
from jax.sharding import PartitionSpec as P

NT = 1024
NF = 128
LOW_BIN = 8
LAGS = 128


def forward_table():
    phase = (LOW_BIN + np.arange(NF))[:, None] * np.arange(NT)[None, :] % NT
    angle = phase * (2.0 * math.pi / NT)
    return np.concatenate([np.cos(angle), -np.sin(angle)], axis=0).astype(np.float32)


def inverse_table(segments, sent):
    (shifts,) = after([jnp.arange(LAGS, dtype=jnp.int32) - LAGS // 2], sent)
    column = jnp.arange(2 * NF, dtype=jnp.int32)
    half = NF // PIECES
    bin_id = LOW_BIN + column // (2 * half) * half + column % half
    phase = jnp.mod(shifts[:, None] * bin_id[None, :], NT)
    angle = phase.astype(jnp.float32) * (2.0 * math.pi / NT)
    scale = 1.0 / math.sqrt(segments * NF)
    value = jnp.where(column // half % 2 == 0, jnp.cos(angle), -jnp.sin(angle)) * scale
    return value.astype(jnp.bfloat16)


def halves(value):
    high = value.astype(jnp.bfloat16)
    return high, (value - high.astype(jnp.float32)).astype(jnp.bfloat16)


def nt_dot(a, b):
    return lax.dot_general(a, b, (((1,), (1,)), ((), ())), preferred_element_type=jnp.float32)


CHUNKS = 2
PIECES = 2


def whiten_kernel(bins, x_hbm, table_hbm, *refs):
    outs, (x_ref, table_ref, pad_ref, sems) = refs[:-4], refs[-4:]
    _, segments, block, wide = x_ref.shape
    columns = segments * block
    copies = []
    for k in range(CHUNKS):
        span = slice(k * wide, (k + 1) * wide)
        sources = (x_hbm.at[:, :, span], table_hbm.at[:, span])
        copies.append(
            [
                pltpu.make_async_copy(source, target.at[k], sems.at[k, n])
                for n, (source, target) in enumerate(zip(sources, (x_ref, table_ref)))
            ]
        )
        for copy in copies[-1]:
            copy.start()
    spectrum = None
    for k in range(CHUNKS):
        for copy in copies[k]:
            copy.wait()
        x = x_ref[k].reshape(columns, wide)
        x_high, x_low = halves(x)
        high, low = halves(table_ref[k])
        part = nt_dot(high, x_high) + nt_dot(high, x_low) + nt_dot(low, x_high)
        spectrum = part if spectrum is None else spectrum + part
    real_part = spectrum[:NF]
    imag_part = spectrum[NF:]
    power = real_part * real_part + imag_part * imag_part
    edge = jnp.zeros((8, columns), jnp.float32)
    pad_ref[0:8, :] = edge
    pad_ref[8 + NF : 16 + NF, :] = edge
    pad_ref[8 : 8 + NF, :] = power
    total = pad_ref[6 : 6 + NF, :]
    for offset in range(7, 11):
        total = total + pad_ref[offset : offset + NF, :]
    bin_id = lax.broadcasted_iota(jnp.int32, (NF, columns), 0)
    counted = (jnp.minimum(bin_id + 2, NF - 1) - jnp.maximum(bin_id - 2, 0) + 1).astype(jnp.float32)
    smooth = total / counted
    level = jnp.mean(power, axis=0, keepdims=True)
    factor = lax.rsqrt(smooth + 0.05 * level + 1e-06)
    parts = ((real_part * factor).astype(jnp.bfloat16), (imag_part * factor).astype(jnp.bfloat16))
    each = NF // bins // len(outs)
    for group in range(NF // bins):
        for segment in range(segments):
            for c in range(2):
                row = ((group % each * segments + segment) * 2 + c) * bins
                outs[group // each][row : row + bins, :] = parts[c][
                    group * bins : (group + 1) * bins, segment * block : (segment + 1) * block
                ]


def pick_kernel(dims, layout, time_at, joined, plan_ref, *refs):
    depth, height, cores = dims
    count = cores * (1 + max(array for array, _ in layout.values()))
    sources, outs, (held, turned) = refs[:count], refs[count:-2], refs[-2:]
    slots, _, rows, block = held.shape
    times = len(outs)
    share = block // times
    time = plan_ref[time_at]

    def fetch(slot, side, targets):
        away = plan_ref[slot * 2 + side]
        place = away // cores
        array = jnp.int32(0)
        index = jnp.int32(0)
        for (dz, dy), (where, at) in layout.items():
            here = place == dz * height + dy
            array = jnp.where(here, where, array)
            index = jnp.where(here, at * joined, index)
        for n, source in enumerate(sources):

            @pl.when(away % cores + cores * array == n)
            def _():
                for step in range(joined):
                    value = source[index + step]
                    for target in targets[step]:
                        target[...] = value

    for slot in range(slots):
        fetch(slot, 0, [[held.at[slot, step]] for step in range(joined)])
        rights = [out.at[slot, :rows] for out in outs]
        fetch(slot, 1, [rights] if joined == 1 else [[right] for right in rights])
    for slot in range(slots):
        for source in range(joined):
            flipped = held[slot, source].astype(jnp.float32).T.astype(jnp.bfloat16)
            for piece in range(rows // block):
                turned[slot, source, piece] = flipped[:, piece * block : (piece + 1) * block]
        for step, out in enumerate(outs):
            source, part = (0, (time + step) % times) if joined == 1 else (step, time)
            start = pl.multiple_of(part * share, share)
            for piece in range(rows // block):
                low = rows + piece * share
                out[slot, low : low + share] = turned[slot, source, piece, pl.ds(start, share)]


def arrange(slot, rows, bins, packs, left_all, right_all):
    times = len(packs)
    share = left_all.shape[0]
    block = share * times
    wide = times * rows
    each = left_all.shape[1] // wide
    for step, pack in enumerate(packs):
        for index in range(each):
            base = index * wide + step * rows
            done = 0
            while done < rows:
                at = index * rows + done
                width = min(rows - done, block - at % block)
                low = each * rows + at // block * share
                left_all[:, base + done : base + done + width] = pack[
                    slot, low : low + share, at % block : at % block + width
                ].astype(jnp.float32)
                done += width
            for pair in range(rows // (2 * bins)):
                row = index * rows + pair * 2 * bins
                at = base + pair * 2 * bins
                real_part = pack[slot, row : row + bins, :]
                imag_part = pack[slot, row + bins : row + 2 * bins, :]
                right_all[at : at + bins, :block] = real_part
                right_all[at : at + bins, block:] = imag_part
                right_all[at + bins : at + 2 * bins, :block] = imag_part
                right_all[at + bins : at + 2 * bins, block:] = -real_part


def cross_spectra(bins, wide, first, chunk, left_all, right_all, cross_ref):
    each = left_all.shape[1] // wide
    block = right_all.shape[1] // 2
    half = each * bins
    column = lax.broadcasted_iota(jnp.int32, (bins, wide), 1) % bins
    row = lax.broadcasted_iota(jnp.int32, (bins, wide), 0)
    keep = column == row
    several = 4 if chunk % 4 == 0 else 2
    for group in range(each):
        weights = right_all[group * wide : (group + 1) * wide, :]
        for start in range(0, chunk, several):
            pieces = []
            for i in range(several):
                line = left_all[pl.ds(first + start + i, 1), group * wide : (group + 1) * wide]
                pieces.append(jnp.where(keep, jnp.broadcast_to(line, (bins, wide)), 0.0).astype(jnp.bfloat16))
            product = jnp.dot(jnp.concatenate(pieces, axis=0), weights, preferred_element_type=jnp.float32)
            product = product.astype(jnp.bfloat16)
            for i in range(several):
                at = start + i
                lanes = slice(at % 2 * block, (at % 2 + 1) * block)
                piece = product[i * bins : (i + 1) * bins]
                cross_ref[at // 2, group * bins : (group + 1) * bins, lanes] = piece[:, :block]
                cross_ref[at // 2, half + group * bins : half + (group + 1) * bins, lanes] = piece[:, block:]


def cross_kernel(bins, rows, times, counts_ref, *refs):
    packs, (out_ref, left_all, right_all) = refs[:times], refs[times:]
    for slot in range(out_ref.shape[0]):

        @pl.when(slot < counts_ref[0])
        def _():
            arrange(slot, rows, bins, packs, left_all, right_all)
            cross_spectra(bins, times * rows, 0, left_all.shape[0], left_all, right_all, out_ref.at[slot])


def stack_kernel(bins, rows, times, chunk, counts_ref, *refs):
    packs, table_ref, early, refs = refs[:times], refs[times], refs[times + 1 : -6], refs[-6:]
    out_ref, held, left_all, right_all, cross_ref, sems = refs
    slots = held.shape[0]
    share = left_all.shape[0]
    wide = times * rows
    lanes = 2 * share * times
    copies = []
    for slot in range(slots):
        leaving = []
        for n in range(share // chunk):
            span = slice(n * chunk // 2 * lanes, (n + 1) * chunk // 2 * lanes)
            leaving.append(pltpu.make_async_copy(held.at[slot, :, span], out_ref.at[slot, :, span], sems.at[slot, n]))
        copies += leaving

        @pl.when(slot < counts_ref[0])
        def _():
            arrange(slot, rows, bins, packs, left_all, right_all)
            table = table_ref[...]
            for n, copy in enumerate(leaving):
                cross_spectra(bins, wide, n * chunk, chunk, left_all, right_all, cross_ref.at[n % 2])
                for pair in range(chunk // 2):
                    at = n * chunk // 2 + pair
                    cross = jnp.concatenate([ref[slot, at] for ref in early] + [cross_ref[n % 2, pair]], axis=0)
                    held[slot, :, at * lanes : (at + 1) * lanes] = jnp.dot(
                        table, cross, preferred_element_type=jnp.float32
                    )
                copy.start()

        @pl.when(slot >= counts_ref[0])
        def _():
            held[slot] = jnp.zeros_like(held[slot])
            for copy in leaving:
                copy.start()

    for copy in copies:
        copy.wait()


def chip_dims(size):
    return {16: (4, 2, 2), 64: (16, 4, 1)}.get(size, (size, 1, 1))


def swap(value, dims, axis, by):
    moves = []
    for p in range(math.prod(dims)):
        place = list(np.unravel_index(p, dims))
        place[axis] ^= by
        moves.append((p, int(np.ravel_multi_index(place, dims))))
    return lax.ppermute(value, "pair", moves)


def is_paired(dims, times):
    return dims == (4, 2, 2) and times == 2 and PIECES == 2


def column_layout(dims, parts):
    depth, height, _ = dims
    order = [(0, 0)]
    for axis, size in ((0, depth), (1, height)):
        bit = size // 2
        while bit:
            order += [(z ^ bit, y) if axis == 0 else (z, y ^ bit) for z, y in order]
            bit //= 2
    spots = [(n, at) for n, part in enumerate(parts) for at in range(part)]
    return dict(zip(order, spots))


def after(values, others):
    return lax.optimization_barrier(tuple(values) + tuple(others))[: len(values)]


def join(held, more):
    (room,) = after([jnp.concatenate([held, held])], ())
    return lax.dynamic_update_slice(room, more, (held.shape[0], 0, 0))


def swap_times(value, step, times):
    return lax.ppermute(value, "tm", [((t + step) % times, t) for t in range(times)])


def gather_one(held, dims):
    depth, height, _ = dims
    for axis, size in ((0, depth), (1, height)):
        bit = size // 2
        while bit:
            held = jnp.concatenate([held, swap(held, dims, axis, bit)])
            bit //= 2
    return [held]


def gather_two(first, second, dims):
    first_far = swap(first, dims, 0, 2)
    other = swap_times(second, 1, 2)
    pair = join(second, other)
    pair_far = swap(pair, dims, 0, 2)
    (first_two,) = after([join(first, first_far)], [pair])
    first_near = swap(first_two, dims, 0, 1)
    pair_beside = swap(pair, dims, 1, 1)
    pair_two = jnp.concatenate([pair, pair_far])
    (first_near,) = after([first_near], [pair_two])
    first_four = jnp.concatenate([first_two, first_near])
    first_beside = swap(first_four, dims, 1, 1)
    (pair_two,) = after([pair_two], [pair_beside])
    pair_near = swap(pair_two, dims, 0, 1)
    pair_four = jnp.concatenate([pair_two, pair_near])
    pair_rest = swap(pair_four[2:], dims, 1, 1)
    return [first_four, first_beside], [pair_four, pair_beside, pair_rest]


def both_cores(arrays, dims):
    if dims[2] == 1:
        return arrays
    return [value for array in arrays for value in (array, swap(array, dims, 2, 1))]


def shards(traces, owner, tiles, counts):
    seg_count, block, _ = traces.shape
    times = lax.axis_size("tm")
    segments = seg_count * times
    share = block // times
    slots = tiles.shape[0]
    bins = max(16, 128 // segments)
    groups = NF // bins
    rows = seg_count * 2 * bins
    wide = rows * times
    total = groups * rows
    part_rows = total // PIECES
    dims = chip_dims(lax.axis_size("pair"))
    smem = pl.BlockSpec(memory_space=pltpu.SMEM)
    anywhere = pl.BlockSpec(memory_space=pl.ANY)
    white = pl.pallas_call(
        functools.partial(whiten_kernel, bins),
        in_specs=[anywhere] * 2,
        out_shape=[jax.ShapeDtypeStruct((part_rows, block), jnp.bfloat16)] * PIECES,
        scratch_shapes=[
            pltpu.VMEM((CHUNKS, seg_count, block, NT // CHUNKS), jnp.float32),
            pltpu.VMEM((CHUNKS, 2 * NF, NT // CHUNKS), jnp.float32),
            pltpu.VMEM((NF + 16, seg_count * block), jnp.float32),
            pltpu.SemaphoreType.DMA((CHUNKS, 2)),
        ],
        compiler_params=pltpu.CompilerParams(vmem_limit_bytes=63 << 20),
        name="whiten",
    )(traces, jnp.asarray(forward_table()))

    known = owner.shape[0]
    chosen = tiles.reshape(-1, 1) == jnp.arange(known, dtype=jnp.int32)
    stored = jnp.sum(jnp.where(chosen, owner, 0), axis=1)
    plan = jnp.concatenate([stored ^ lax.axis_index("pair"), lax.axis_index("tm")[None]]).astype(jnp.int32)

    paired = is_paired(dims, times)
    pack = part_rows + part_rows // block * share
    packs = []
    blocks = [own[None] for own in white]
    gathered = gather_two(*blocks, dims) if paired else [gather_one(own, dims) for own in blocks]
    for piece, arrays in enumerate(gathered):
        joined = times if paired and piece else 1
        if packs:
            arrays[-1:] = after(arrays[-1:], packs[-1][1:])
        sources = both_cores(arrays, dims)
        layout = column_layout(dims, [array.shape[0] // joined for array in arrays])
        arrived = list(pl.pallas_call(
            functools.partial(pick_kernel, dims, layout, 2 * slots, joined),
            in_specs=[smem] + [pl.BlockSpec(memory_space=pltpu.VMEM)] * len(sources),
            out_shape=[jax.ShapeDtypeStruct((slots, pack, block), jnp.bfloat16)] * times,
            scratch_shapes=[
                pltpu.VMEM((slots, joined, part_rows, block), jnp.bfloat16),
                pltpu.VMEM((slots, joined, part_rows // block, block, block), jnp.bfloat16),
            ],
            compiler_params=pltpu.CompilerParams(vmem_limit_bytes=8 << 20),
            cost_estimate=pl.CostEstimate(flops=1, bytes_accessed=1, transcendentals=0),
            name="pick",
        )(plan, *sources))
        if not packs:
            table = inverse_table(segments, arrived[1:])
        if joined == 1:
            for step in range(1, times):
                moves = [(t, (t + step) % times) for t in range(times)]
                arrived[step] = lax.ppermute(arrived[step], "tm", moves)
        if not packs:
            arrived[1:] = after(arrived[1:], [table])
        packs.append(arrived)

    chunk = min(share, 16)
    depth = 2 * NF // PIECES
    whole = pl.BlockSpec(memory_space=pltpu.VMEM)
    scratch = [
        pltpu.VMEM((share, groups // PIECES * wide), jnp.float32),
        pltpu.VMEM((groups // PIECES * wide, 2 * block), jnp.bfloat16),
    ]
    early = []
    for arrived in packs[:-1]:
        early.append(
            pl.pallas_call(
                functools.partial(cross_kernel, bins, rows, times),
                in_specs=[smem] + [whole] * times,
                out_shape=jax.ShapeDtypeStruct((slots, share // 2, depth, 2 * block), jnp.bfloat16),
                scratch_shapes=scratch,
                compiler_params=pltpu.CompilerParams(vmem_limit_bytes=24 << 20),
                name="cross",
            )(counts, *arrived)
        )
    return pl.pallas_call(
        functools.partial(stack_kernel, bins, rows, times, chunk),
        in_specs=[smem] + [whole] * (times + 1 + len(early)),
        out_specs=anywhere,
        out_shape=jax.ShapeDtypeStruct((slots, LAGS, share * block), jnp.float32),
        scratch_shapes=[pltpu.VMEM((slots, LAGS, share * block), jnp.float32)]
        + scratch
        + [
            pltpu.VMEM((2, chunk // 2, depth, 2 * block), jnp.bfloat16),
            pltpu.SemaphoreType.DMA((slots, share // chunk)),
        ],
        compiler_params=pltpu.CompilerParams(vmem_limit_bytes=40 << 20),
        name="stack",
    )(counts, *packs[-1], table, *early)


def solution(mesh):
    placed = (P("tm", "pair", None), P(), P("pair", None), P("pair"))
    return jax.shard_map(
        shards, mesh=mesh, in_specs=placed, out_specs=P("pair", None, "tm"), check_vma=False
    )
```

```python
import functools
import math

import jax
import jax.numpy as jnp
import numpy as np
from jax import lax
from jax.experimental import pallas as pl
from jax.experimental.pallas import tpu as pltpu
from jax.sharding import PartitionSpec as P

NT = 1024
NF = 128
LOW_BIN = 8
LAGS = 128


def forward_table():
    phase = (LOW_BIN + np.arange(NF))[:, None] * np.arange(NT)[None, :] % NT
    angle = phase * (2.0 * math.pi / NT)
    return np.concatenate([np.cos(angle), -np.sin(angle)], axis=0).astype(np.float32)


def inverse_table(segments, sent):
    (shifts,) = after([jnp.arange(LAGS, dtype=jnp.int32) - LAGS // 2], sent)
    column = jnp.arange(2 * NF, dtype=jnp.int32)
    half = NF // PIECES
    bin_id = LOW_BIN + column // (2 * half) * half + column % half
    phase = jnp.mod(shifts[:, None] * bin_id[None, :], NT)
    angle = phase.astype(jnp.float32) * (2.0 * math.pi / NT)
    scale = 1.0 / math.sqrt(segments * NF)
    value = jnp.where(column // half % 2 == 0, jnp.cos(angle), -jnp.sin(angle)) * scale
    return value.astype(jnp.bfloat16)


def halves(value):
    high = value.astype(jnp.bfloat16)
    return high, (value - high.astype(jnp.float32)).astype(jnp.bfloat16)


def nt_dot(a, b):
    return lax.dot_general(a, b, (((1,), (1,)), ((), ())), preferred_element_type=jnp.float32)


CHUNKS = 2
PIECES = 2


def whiten_kernel(bins, x_hbm, table_hbm, *refs):
    outs, (x_ref, table_ref, pad_ref, sems) = refs[:-4], refs[-4:]
    _, segments, block, wide = x_ref.shape
    columns = segments * block
    copies = []
    for k in range(CHUNKS):
        span = slice(k * wide, (k + 1) * wide)
        sources = (x_hbm.at[:, :, span], table_hbm.at[:, span])
        copies.append(
            [
                pltpu.make_async_copy(source, target.at[k], sems.at[k, n])
                for n, (source, target) in enumerate(zip(sources, (x_ref, table_ref)))
            ]
        )
        for copy in copies[-1]:
            copy.start()
    spectrum = None
    for k in range(CHUNKS):
        for copy in copies[k]:
            copy.wait()
        x = x_ref[k].reshape(columns, wide)
        x_high, x_low = halves(x)
        high, low = halves(table_ref[k])
        part = nt_dot(high, x_high) + nt_dot(high, x_low) + nt_dot(low, x_high)
        spectrum = part if spectrum is None else spectrum + part
    real_part = spectrum[:NF]
    imag_part = spectrum[NF:]
    power = real_part * real_part + imag_part * imag_part
    edge = jnp.zeros((8, columns), jnp.float32)
    pad_ref[0:8, :] = edge
    pad_ref[8 + NF : 16 + NF, :] = edge
    pad_ref[8 : 8 + NF, :] = power
    total = pad_ref[6 : 6 + NF, :]
    for offset in range(7, 11):
        total = total + pad_ref[offset : offset + NF, :]
    bin_id = lax.broadcasted_iota(jnp.int32, (NF, columns), 0)
    counted = (jnp.minimum(bin_id + 2, NF - 1) - jnp.maximum(bin_id - 2, 0) + 1).astype(jnp.float32)
    smooth = total / counted
    level = jnp.mean(power, axis=0, keepdims=True)
    factor = lax.rsqrt(smooth + 0.05 * level + 1e-06)
    parts = ((real_part * factor).astype(jnp.bfloat16), (imag_part * factor).astype(jnp.bfloat16))
    each = NF // bins // len(outs)
    for group in range(NF // bins):
        for segment in range(segments):
            for c in range(2):
                row = ((group % each * segments + segment) * 2 + c) * bins
                outs[group // each][row : row + bins, :] = parts[c][
                    group * bins : (group + 1) * bins, segment * block : (segment + 1) * block
                ]


def fetch(dims, layout, joined, plan_ref, at, sources, targets):
    _, height, cores = dims
    away = plan_ref[at]
    place = away // cores
    array = jnp.int32(0)
    index = jnp.int32(0)
    for (dz, dy), (where, spot) in layout.items():
        here = place == dz * height + dy
        array = jnp.where(here, where, array)
        index = jnp.where(here, spot * joined, index)
    for n, source in enumerate(sources):

        @pl.when(away % cores + cores * array == n)
        def _():
            for step in range(joined):
                value = source[index + step]
                for target in targets[step]:
                    target[...] = value


def pick_kernel(dims, layout, time_at, plan_ref, *refs):
    count = dims[2] * (1 + max(array for array, _ in layout.values()))
    sources, outs, (held, turned) = refs[:count], refs[count:-2], refs[-2:]
    slots, rows, block = held.shape
    times = len(outs)
    share = block // times
    time = plan_ref[time_at]
    for slot in range(slots):
        fetch(dims, layout, 1, plan_ref, 2 * slot, sources, [[held.at[slot]]])
        fetch(dims, layout, 1, plan_ref, 2 * slot + 1, sources, [[out.at[slot, :rows] for out in outs]])
    for slot in range(slots):
        flipped = held[slot].astype(jnp.float32).T.astype(jnp.bfloat16)
        for piece in range(rows // block):
            turned[slot, piece] = flipped[:, piece * block : (piece + 1) * block]
        for step, out in enumerate(outs):
            start = pl.multiple_of((time + step) % times * share, share)
            for piece in range(rows // block):
                low = rows + piece * share
                out[slot, low : low + share] = turned[slot, piece, pl.ds(start, share)]


def put_right(bins, block_ref, right_all, at, rows):
    block = block_ref.shape[1]
    for low in range(0, rows, 2 * bins):
        real_part = block_ref[low : low + bins, :]
        imag_part = block_ref[low + bins : low + 2 * bins, :]
        base = at(low)
        right_all[base : base + bins, :block] = real_part
        right_all[base : base + bins, block:] = imag_part
        right_all[base + bins : base + 2 * bins, :block] = imag_part
        right_all[base + bins : base + 2 * bins, block:] = -real_part


def cross_spectra(bins, wide, first, chunk, left_all, right_all, cross_ref):
    groups = left_all.shape[1] // wide
    each = groups // PIECES
    block = right_all.shape[1] // 2
    half = each * bins
    column = lax.broadcasted_iota(jnp.int32, (bins, wide), 1) % bins
    row = lax.broadcasted_iota(jnp.int32, (bins, wide), 0)
    keep = column == row
    several = 4 if chunk % 4 == 0 else 2
    for group in range(groups):
        weights = right_all[group * wide : (group + 1) * wide, :]
        real_at = group // each * 2 * half + group % each * bins
        imag_at = real_at + half
        for start in range(0, chunk, several):
            pieces = []
            for i in range(several):
                line = left_all[pl.ds(first + start + i, 1), group * wide : (group + 1) * wide]
                pieces.append(jnp.where(keep, jnp.broadcast_to(line, (bins, wide)), 0.0).astype(jnp.bfloat16))
            product = jnp.dot(jnp.concatenate(pieces, axis=0), weights, preferred_element_type=jnp.float32)
            product = product.astype(jnp.bfloat16)
            for i in range(several):
                at = start + i
                lanes = slice(at % 2 * block, (at % 2 + 1) * block)
                piece = product[i * bins : (i + 1) * bins]
                cross_ref[at // 2, real_at : real_at + bins, lanes] = piece[:, :block]
                cross_ref[at // 2, imag_at : imag_at + bins, lanes] = piece[:, block:]


def stack_kernel(bins, rows, times, chunk, picks, counts_ref, plan_ref, table_ref, *refs):
    out_ref, held, blocks, turned, left_all, right_all, cross_ref, sems = refs[-8:]
    slots = held.shape[0]
    share = left_all.shape[0]
    block = share * times
    wide = times * rows
    each = left_all.shape[1] // wide // PIECES
    part_rows = each * rows
    lanes = 2 * block
    copies = []
    for slot in range(slots):
        leaving = []
        for n in range(share // chunk):
            span = slice(n * chunk // 2 * lanes, (n + 1) * chunk // 2 * lanes)
            leaving.append(pltpu.make_async_copy(held.at[slot, :, span], out_ref.at[slot, :, span], sems.at[slot, n]))
        copies += leaving

        @pl.when(slot < counts_ref[0])
        def _():
            at_ref = 0
            for piece, pick in enumerate(picks):
                base = piece * each * wide
                if pick is None:
                    packs = refs[at_ref : at_ref + times]
                    at_ref += times
                else:
                    dims, layout, joined, time_at = pick
                    count = dims[2] * (1 + max(array for array, _ in layout.values()))
                    sources = refs[at_ref : at_ref + count]
                    at_ref += count
                    for side in range(2):
                        targets = [[blocks.at[side, step]] for step in range(joined)]
                        fetch(dims, layout, joined, plan_ref, 2 * slot + side, sources, targets)
                    start = pl.multiple_of(plan_ref[time_at] * share, share)
                for step in range(times):
                    at = functools.partial(lambda base, step, low: base + low // rows * wide + step * rows + low % rows, base, step)
                    if pick is None:
                        put_right(bins, packs[step].at[slot], right_all, at, part_rows)
                        for low in range(0, part_rows, block):
                            first = part_rows + low // block * share
                            value = packs[step][slot, first : first + share, :].astype(jnp.float32)
                            for inner in range(0, block, rows):
                                width = min(rows, block)
                                left_all[:, at(low + inner) : at(low + inner) + width] = value[:, inner : inner + width]
                    else:
                        put_right(bins, blocks.at[1, step], right_all, at, part_rows)
                        turned[...] = blocks[0, step].astype(jnp.float32).T
                        for low in range(0, part_rows, rows):
                            left_all[:, at(low) : at(low) + rows] = turned[pl.ds(start, share), low : low + rows]
            table = table_ref[...]
            for n, copy in enumerate(leaving):
                cross_spectra(bins, wide, n * chunk, chunk, left_all, right_all, cross_ref.at[n % 2])
                for pair in range(chunk // 2):
                    at = n * chunk // 2 + pair
                    held[slot, :, at * lanes : (at + 1) * lanes] = jnp.dot(
                        table, cross_ref[n % 2, pair], preferred_element_type=jnp.float32
                    )
                copy.start()

        @pl.when(slot >= counts_ref[0])
        def _():
            held[slot] = jnp.zeros_like(held[slot])
            for copy in leaving:
                copy.start()

    for copy in copies:
        copy.wait()


def chip_dims(size):
    return {16: (4, 2, 2), 64: (16, 4, 1)}.get(size, (size, 1, 1))


def swap(value, dims, axis, by):
    moves = []
    for p in range(math.prod(dims)):
        place = list(np.unravel_index(p, dims))
        place[axis] ^= by
        moves.append((p, int(np.ravel_multi_index(place, dims))))
    return lax.ppermute(value, "pair", moves)


def is_paired(dims, times):
    return dims == (4, 2, 2) and times == 2 and PIECES == 2


def column_layout(dims, parts):
    depth, height, _ = dims
    order = [(0, 0)]
    for axis, size in ((0, depth), (1, height)):
        bit = size // 2
        while bit:
            order += [(z ^ bit, y) if axis == 0 else (z, y ^ bit) for z, y in order]
            bit //= 2
    spots = [(n, at) for n, part in enumerate(parts) for at in range(part)]
    return dict(zip(order, spots))


def after(values, others):
    return lax.optimization_barrier(tuple(values) + tuple(others))[: len(values)]


def join(held, more):
    (room,) = after([jnp.concatenate([held, held])], ())
    return lax.dynamic_update_slice(room, more, (held.shape[0], 0, 0))


def swap_times(value, step, times):
    return lax.ppermute(value, "tm", [((t + step) % times, t) for t in range(times)])


def gather_one(held, dims):
    depth, height, _ = dims
    for axis, size in ((0, depth), (1, height)):
        bit = size // 2
        while bit:
            held = jnp.concatenate([held, swap(held, dims, axis, bit)])
            bit //= 2
    return [held]


def gather_two(first, second, dims):
    first_far = swap(first, dims, 0, 2)
    (room,) = after([jnp.concatenate([first, first])], ())
    (second,) = after([second], [room])
    other = swap_times(second, 1, 2)
    pair = join(second, other)
    pair_far = swap(pair, dims, 0, 2)
    (first_two,) = after([lax.dynamic_update_slice(room, first_far, (1, 0, 0))], [pair])
    first_near = swap(first_two, dims, 0, 1)
    pair_beside = swap(after([pair], [first_two])[0], dims, 1, 1)
    pair_two = jnp.concatenate([pair, pair_far])
    (first_near,) = after([first_near], [pair_two])
    first_four = jnp.concatenate([first_two, first_near])
    first_beside = swap(first_four, dims, 1, 1)
    (pair_two,) = after([pair_two], [pair_beside])
    pair_near = swap(pair_two, dims, 0, 1)
    pair_four = jnp.concatenate([pair_two, pair_near])
    pair_rest = swap(pair_four[2:], dims, 1, 1)
    return [first_four, first_beside], [pair_four, pair_beside, pair_rest], first_near


def both_cores(arrays, dims):
    if dims[2] == 1:
        return arrays
    return [value for array in arrays for value in (array, swap(array, dims, 2, 1))]


def shards(traces, owner, tiles, counts):
    seg_count, block, _ = traces.shape
    times = lax.axis_size("tm")
    segments = seg_count * times
    share = block // times
    slots = tiles.shape[0]
    bins = max(16, 128 // segments)
    groups = NF // bins
    rows = seg_count * 2 * bins
    wide = rows * times
    total = groups * rows
    part_rows = total // PIECES
    dims = chip_dims(lax.axis_size("pair"))
    smem = pl.BlockSpec(memory_space=pltpu.SMEM)
    anywhere = pl.BlockSpec(memory_space=pl.ANY)
    white = pl.pallas_call(
        functools.partial(whiten_kernel, bins),
        in_specs=[anywhere] * 2,
        out_shape=[jax.ShapeDtypeStruct((part_rows, block), jnp.bfloat16)] * PIECES,
        scratch_shapes=[
            pltpu.VMEM((CHUNKS, seg_count, block, NT // CHUNKS), jnp.float32),
            pltpu.VMEM((CHUNKS, 2 * NF, NT // CHUNKS), jnp.float32),
            pltpu.VMEM((NF + 16, seg_count * block), jnp.float32),
            pltpu.SemaphoreType.DMA((CHUNKS, 2)),
        ],
        compiler_params=pltpu.CompilerParams(vmem_limit_bytes=63 << 20),
        name="whiten",
    )(traces, jnp.asarray(forward_table()))

    paired = is_paired(dims, times)
    blocks = [own[None] for own in white]
    if paired:
        *gathered, near = gather_two(*blocks, dims)
        (tiles,) = after([tiles], [near])
    else:
        gathered = [gather_one(own, dims) for own in blocks]

    known = owner.shape[0]
    chosen = tiles.reshape(-1, 1) == jnp.arange(known, dtype=jnp.int32)
    stored = jnp.sum(jnp.where(chosen, owner, 0), axis=1)
    plan = jnp.concatenate([stored ^ lax.axis_index("pair"), lax.axis_index("tm")[None]]).astype(jnp.int32)

    pack = part_rows + part_rows // block * share
    inside = pl.BlockSpec(memory_space=pltpu.VMEM)
    inputs = []
    picks = []
    table = None
    for piece, arrays in enumerate(gathered):
        joined = times if paired and piece else 1
        layout = column_layout(dims, [array.shape[0] // joined for array in arrays])
        if joined > 1:
            arrays[-1:] = after(arrays[-1:], inputs[1:] + [table])
            inputs += both_cores(arrays, dims)
            picks.append((dims, layout, joined, 2 * slots))
            continue
        sources = both_cores(arrays, dims)
        arrived = list(pl.pallas_call(
            functools.partial(pick_kernel, dims, layout, 2 * slots),
            in_specs=[smem] + [inside] * len(sources),
            out_shape=[jax.ShapeDtypeStruct((slots, pack, block), jnp.bfloat16)] * times,
            scratch_shapes=[
                pltpu.VMEM((slots, part_rows, block), jnp.bfloat16),
                pltpu.VMEM((slots, part_rows // block, block, block), jnp.bfloat16),
            ],
            compiler_params=pltpu.CompilerParams(vmem_limit_bytes=8 << 20),
            cost_estimate=pl.CostEstimate(flops=1, bytes_accessed=1, transcendentals=0),
            name="pick",
        )(plan, *sources))
        if table is None:
            table = inverse_table(segments, arrived[1:])
        for step in range(1, times):
            moves = [(t, (t + step) % times) for t in range(times)]
            arrived[step] = lax.ppermute(arrived[step], "tm", moves)
        inputs += arrived
        picks.append(None)

    chunk = min(share, 16)
    return pl.pallas_call(
        functools.partial(stack_kernel, bins, rows, times, chunk, picks),
        in_specs=[smem] * 2 + [inside] * (1 + len(inputs)),
        out_specs=anywhere,
        out_shape=jax.ShapeDtypeStruct((slots, LAGS, share * block), jnp.float32),
        scratch_shapes=[
            pltpu.VMEM((slots, LAGS, share * block), jnp.float32),
            pltpu.VMEM((2, times, part_rows, block), jnp.bfloat16),
            pltpu.VMEM((block, part_rows), jnp.float32),
            pltpu.VMEM((share, groups * wide), jnp.float32),
            pltpu.VMEM((groups * wide, 2 * block), jnp.bfloat16),
            pltpu.VMEM((2, chunk // 2, 2 * NF, 2 * block), jnp.bfloat16),
            pltpu.SemaphoreType.DMA((slots, share // chunk)),
        ],
        compiler_params=pltpu.CompilerParams(vmem_limit_bytes=40 << 20),
        name="stack",
    )(counts, plan, table, *inputs)


def solution(mesh):
    placed = (P("tm", "pair", None), P(), P("pair", None), P("pair"))
    return jax.shard_map(
        shards, mesh=mesh, in_specs=placed, out_specs=P("pair", None, "tm"), check_vma=False
    )
```

```python
import functools
import math

import jax
import jax.numpy as jnp
import numpy as np
from jax import lax
from jax.experimental import pallas as pl
from jax.experimental.pallas import tpu as pltpu
from jax.sharding import PartitionSpec as P

NT = 1024
NF = 128
LOW_BIN = 8
LAGS = 128


def forward_table():
    phase = (LOW_BIN + np.arange(NF))[:, None] * np.arange(NT)[None, :] % NT
    angle = phase * (2.0 * math.pi / NT)
    return np.concatenate([np.cos(angle), -np.sin(angle)], axis=0).astype(np.float32)


def inverse_table(segments, sent):
    (shifts,) = after([jnp.arange(LAGS, dtype=jnp.int32) - LAGS // 2], sent)
    column = jnp.arange(2 * NF, dtype=jnp.int32)
    half = NF // PIECES
    bin_id = LOW_BIN + column // (2 * half) * half + column % half
    phase = jnp.mod(shifts[:, None] * bin_id[None, :], NT)
    angle = phase.astype(jnp.float32) * (2.0 * math.pi / NT)
    scale = 1.0 / math.sqrt(segments * NF)
    value = jnp.where(column // half % 2 == 0, jnp.cos(angle), -jnp.sin(angle)) * scale
    return value.astype(jnp.bfloat16)


def halves(value):
    high = value.astype(jnp.bfloat16)
    return high, (value - high.astype(jnp.float32)).astype(jnp.bfloat16)


def nt_dot(a, b):
    return lax.dot_general(a, b, (((1,), (1,)), ((), ())), preferred_element_type=jnp.float32)


CHUNKS = 2
PIECES = 2


def whiten_kernel(bins, x_hbm, table_hbm, *refs):
    outs, (x_ref, table_ref, pad_ref, sems) = refs[:-4], refs[-4:]
    _, segments, block, wide = x_ref.shape
    columns = segments * block
    copies = []
    for k in range(CHUNKS):
        span = slice(k * wide, (k + 1) * wide)
        sources = (x_hbm.at[:, :, span], table_hbm.at[:, span])
        copies.append(
            [
                pltpu.make_async_copy(source, target.at[k], sems.at[k, n])
                for n, (source, target) in enumerate(zip(sources, (x_ref, table_ref)))
            ]
        )
        for copy in copies[-1]:
            copy.start()
    spectrum = None
    for k in range(CHUNKS):
        for copy in copies[k]:
            copy.wait()
        x = x_ref[k].reshape(columns, wide)
        x_high, x_low = halves(x)
        high, low = halves(table_ref[k])
        part = nt_dot(high, x_high) + nt_dot(high, x_low) + nt_dot(low, x_high)
        spectrum = part if spectrum is None else spectrum + part
    real_part = spectrum[:NF]
    imag_part = spectrum[NF:]
    power = real_part * real_part + imag_part * imag_part
    edge = jnp.zeros((8, columns), jnp.float32)
    pad_ref[0:8, :] = edge
    pad_ref[8 + NF : 16 + NF, :] = edge
    pad_ref[8 : 8 + NF, :] = power
    total = pad_ref[6 : 6 + NF, :]
    for offset in range(7, 11):
        total = total + pad_ref[offset : offset + NF, :]
    bin_id = lax.broadcasted_iota(jnp.int32, (NF, columns), 0)
    counted = (jnp.minimum(bin_id + 2, NF - 1) - jnp.maximum(bin_id - 2, 0) + 1).astype(jnp.float32)
    smooth = total / counted
    level = jnp.mean(power, axis=0, keepdims=True)
    factor = lax.rsqrt(smooth + 0.05 * level + 1e-06)
    parts = ((real_part * factor).astype(jnp.bfloat16), (imag_part * factor).astype(jnp.bfloat16))
    each = NF // bins // len(outs)
    for group in range(NF // bins):
        for segment in range(segments):
            for c in range(2):
                row = ((group % each * segments + segment) * 2 + c) * bins
                outs[group // each][row : row + bins, :] = parts[c][
                    group * bins : (group + 1) * bins, segment * block : (segment + 1) * block
                ]


def fetch(dims, layout, joined, plan_ref, at, sources, targets):
    _, height, cores = dims
    away = plan_ref[at]
    place = away // cores
    array = jnp.int32(0)
    index = jnp.int32(0)
    for (dz, dy), (where, spot) in layout.items():
        here = place == dz * height + dy
        array = jnp.where(here, where, array)
        index = jnp.where(here, spot * joined, index)
    for n, source in enumerate(sources):

        @pl.when(away % cores + cores * array == n)
        def _():
            for step in range(joined):
                value = source[index + step]
                for target in targets[step]:
                    target[...] = value


def pick_kernel(dims, layout, time_at, plan_ref, *refs):
    count = dims[2] * (1 + max(array for array, _ in layout.values()))
    sources, outs, (held, turned) = refs[:count], refs[count:-2], refs[-2:]
    slots, rows, block = held.shape
    times = len(outs)
    share = block // times
    time = plan_ref[time_at]
    for slot in range(slots):
        fetch(dims, layout, 1, plan_ref, 2 * slot, sources, [[held.at[slot]]])
        fetch(dims, layout, 1, plan_ref, 2 * slot + 1, sources, [[out.at[slot, :rows] for out in outs]])
    for slot in range(slots):
        flipped = held[slot].astype(jnp.float32).T.astype(jnp.bfloat16)
        for piece in range(rows // block):
            turned[slot, piece] = flipped[:, piece * block : (piece + 1) * block]
        for step, out in enumerate(outs):
            start = pl.multiple_of((time + step) % times * share, share)
            for piece in range(rows // block):
                low = rows + piece * share
                out[slot, low : low + share] = turned[slot, piece, pl.ds(start, share)]


def put_right(bins, block_ref, right_all, at, rows):
    block = block_ref.shape[1]
    for low in range(0, rows, 2 * bins):
        real_part = block_ref[low : low + bins, :]
        imag_part = block_ref[low + bins : low + 2 * bins, :]
        base = at(low)
        right_all[base : base + bins, :block] = real_part
        right_all[base : base + bins, block:] = imag_part
        right_all[base + bins : base + 2 * bins, :block] = imag_part
        right_all[base + bins : base + 2 * bins, block:] = -real_part


def cross_spectra(bins, wide, first, chunk, left_all, right_all, cross_ref):
    groups = left_all.shape[1] // wide
    each = groups // PIECES
    block = right_all.shape[1] // 2
    half = each * bins
    column = lax.broadcasted_iota(jnp.int32, (bins, wide), 1) % bins
    row = lax.broadcasted_iota(jnp.int32, (bins, wide), 0)
    keep = (column == row).astype(jnp.float32).astype(jnp.bfloat16)
    several = 4 if chunk % 4 == 0 else 2
    for group in range(groups):
        weights = right_all[group * wide : (group + 1) * wide, :]
        real_at = group // each * 2 * half + group % each * bins
        imag_at = real_at + half
        for start in range(0, chunk, several):
            pieces = []
            for i in range(several):
                line = left_all[pl.ds(first + start + i, 1), group * wide : (group + 1) * wide]
                tile = jnp.broadcast_to(line, (16, wide)).astype(jnp.bfloat16)
                pieces += [tile * keep[low : low + 16] for low in range(0, bins, 16)]
            product = jnp.dot(jnp.concatenate(pieces, axis=0), weights, preferred_element_type=jnp.float32)
            product = product.astype(jnp.bfloat16)
            for i in range(several):
                at = start + i
                lanes = slice(at % 2 * block, (at % 2 + 1) * block)
                piece = product[i * bins : (i + 1) * bins]
                cross_ref[at // 2, real_at : real_at + bins, lanes] = piece[:, :block]
                cross_ref[at // 2, imag_at : imag_at + bins, lanes] = piece[:, block:]


def stack_kernel(bins, rows, times, chunk, picks, counts_ref, plan_ref, table_ref, *refs):
    out_ref, held, blocks, turned, left_all, right_all, cross_ref, sems = refs[-8:]
    slots = held.shape[0]
    share = left_all.shape[0]
    block = share * times
    wide = times * rows
    each = left_all.shape[1] // wide // PIECES
    part_rows = each * rows
    lanes = 2 * block
    parts = share // chunk
    width = chunk // 2 * lanes

    def leave(slot, n):
        span = pl.ds(pl.multiple_of(n * width, width), width)
        return pltpu.make_async_copy(held.at[slot, :, span], out_ref.at[slot, :, span], sems.at[slot, n])

    def one_slot(slot, carry):
        at_ref = 0
        for piece, pick in enumerate(picks):
            base = piece * each * wide
            if pick is None:
                packs = refs[at_ref : at_ref + times]
                at_ref += times
            else:
                dims, layout, joined, time_at = pick
                count = dims[2] * (1 + max(array for array, _ in layout.values()))
                sources = refs[at_ref : at_ref + count]
                at_ref += count
                for side in range(2):
                    targets = [[blocks.at[side, step]] for step in range(joined)]
                    fetch(dims, layout, joined, plan_ref, 2 * slot + side, sources, targets)
                start = pl.multiple_of(plan_ref[time_at] * share, share)
            for step in range(times):
                at = functools.partial(lambda base, step, low: base + low // rows * wide + step * rows + low % rows, base, step)
                if pick is None:
                    put_right(bins, packs[step].at[slot], right_all, at, part_rows)
                    for low in range(0, part_rows, block):
                        first = part_rows + low // block * share
                        value = packs[step][slot, first : first + share, :].astype(jnp.float32)
                        for inner in range(0, block, rows):
                            left_all[:, at(low + inner) : at(low + inner) + rows] = value[:, inner : inner + rows]
                else:
                    put_right(bins, blocks.at[1, step], right_all, at, part_rows)
                    turned[...] = blocks[0, step].astype(jnp.float32).T
                    for low in range(0, part_rows, rows):
                        left_all[:, at(low) : at(low) + rows] = turned[pl.ds(start, share), low : low + rows]
        table = table_ref[...]

        def one_chunk(n, carry):
            cross_spectra(bins, wide, n * chunk, chunk, left_all, right_all, cross_ref)
            for pair in range(chunk // 2):
                span = pl.ds(pl.multiple_of(n * width + pair * lanes, lanes), lanes)
                held[slot, :, span] = jnp.dot(table, cross_ref[pair], preferred_element_type=jnp.float32)
            leave(slot, n).start()
            return carry

        return lax.fori_loop(0, parts, one_chunk, carry)

    for slot in range(slots):

        @pl.when(slot >= counts_ref[0])
        def _():
            held[slot] = jnp.zeros_like(held[slot])
            for n in range(parts):
                leave(slot, n).start()

    lax.fori_loop(0, jnp.minimum(counts_ref[0], slots), one_slot, 0)
    for slot in range(slots):
        for n in range(parts):
            leave(slot, n).wait()


def chip_dims(size):
    return {16: (4, 2, 2), 64: (16, 4, 1)}.get(size, (size, 1, 1))


def swap(value, dims, axis, by):
    moves = []
    for p in range(math.prod(dims)):
        place = list(np.unravel_index(p, dims))
        place[axis] ^= by
        moves.append((p, int(np.ravel_multi_index(place, dims))))
    return lax.ppermute(value, "pair", moves)


def is_paired(dims, times):
    return dims == (4, 2, 2) and times == 2 and PIECES == 2


def column_layout(dims, parts):
    depth, height, _ = dims
    order = [(0, 0)]
    for axis, size in ((0, depth), (1, height)):
        bit = size // 2
        while bit:
            order += [(z ^ bit, y) if axis == 0 else (z, y ^ bit) for z, y in order]
            bit //= 2
    spots = [(n, at) for n, part in enumerate(parts) for at in range(part)]
    return dict(zip(order, spots))


def after(values, others):
    return lax.optimization_barrier(tuple(values) + tuple(others))[: len(values)]


def join(held, more):
    (room,) = after([jnp.concatenate([held, held])], ())
    return lax.dynamic_update_slice(room, more, (held.shape[0], 0, 0))


def swap_times(value, step, times):
    return lax.ppermute(value, "tm", [((t + step) % times, t) for t in range(times)])


def gather_one(held, dims):
    depth, height, _ = dims
    for axis, size in ((0, depth), (1, height)):
        bit = size // 2
        while bit:
            held = jnp.concatenate([held, swap(held, dims, axis, bit)])
            bit //= 2
    return [held]


def gather_two(first, second, dims):
    first_far = swap(first, dims, 0, 2)
    (room,) = after([jnp.concatenate([first, first])], ())
    (second,) = after([second], [room])
    other = swap_times(second, 1, 2)
    pair = join(second, other)
    pair_far = swap(pair, dims, 0, 2)
    (first_two,) = after([lax.dynamic_update_slice(room, first_far, (1, 0, 0))], [pair])
    first_near = swap(first_two, dims, 0, 1)
    pair_two = jnp.concatenate([pair, pair_far])
    (first_near,) = after([first_near], [pair_two])
    first_four = jnp.concatenate([first_two, first_near])
    first_beside = swap(first_four, dims, 1, 1)
    pair_near = swap(pair_two, dims, 0, 1)
    pair_four = jnp.concatenate([pair_two, pair_near])
    pair_beside = swap(pair_four, dims, 1, 1)
    return [first_four, first_beside], [pair_four, pair_beside], pair_two


def both_cores(arrays, dims):
    if dims[2] == 1:
        return arrays
    return [value for array in arrays for value in (array, swap(array, dims, 2, 1))]


def shards(traces, owner, tiles, counts):
    seg_count, block, _ = traces.shape
    times = lax.axis_size("tm")
    segments = seg_count * times
    share = block // times
    slots = tiles.shape[0]
    bins = max(16, 128 // segments)
    groups = NF // bins
    rows = seg_count * 2 * bins
    wide = rows * times
    total = groups * rows
    part_rows = total // PIECES
    dims = chip_dims(lax.axis_size("pair"))
    smem = pl.BlockSpec(memory_space=pltpu.SMEM)
    anywhere = pl.BlockSpec(memory_space=pl.ANY)
    white = pl.pallas_call(
        functools.partial(whiten_kernel, bins),
        in_specs=[anywhere] * 2,
        out_shape=[jax.ShapeDtypeStruct((part_rows, block), jnp.bfloat16)] * PIECES,
        scratch_shapes=[
            pltpu.VMEM((CHUNKS, seg_count, block, NT // CHUNKS), jnp.float32),
            pltpu.VMEM((CHUNKS, 2 * NF, NT // CHUNKS), jnp.float32),
            pltpu.VMEM((NF + 16, seg_count * block), jnp.float32),
            pltpu.SemaphoreType.DMA((CHUNKS, 2)),
        ],
        compiler_params=pltpu.CompilerParams(vmem_limit_bytes=63 << 20),
        name="whiten",
    )(traces, jnp.asarray(forward_table()))

    paired = is_paired(dims, times)
    blocks = [own[None] for own in white]
    if paired:
        *gathered, near = gather_two(*blocks, dims)
        (tiles,) = after([tiles], [near])
    else:
        gathered = [gather_one(own, dims) for own in blocks]

    known = owner.shape[0]
    chosen = tiles.reshape(-1, 1) == jnp.arange(known, dtype=jnp.int32)
    stored = jnp.sum(jnp.where(chosen, owner, 0), axis=1)
    plan = jnp.concatenate([stored ^ lax.axis_index("pair"), lax.axis_index("tm")[None]]).astype(jnp.int32)

    pack = part_rows + part_rows // block * share
    inside = pl.BlockSpec(memory_space=pltpu.VMEM)
    inputs = []
    picks = []
    table = None
    for piece, arrays in enumerate(gathered):
        joined = times if paired and piece else 1
        layout = column_layout(dims, [array.shape[0] // joined for array in arrays])
        if joined > 1:
            arrays[-1:] = after(arrays[-1:], inputs[1:] + [table])
            inputs += both_cores(arrays, dims)
            picks.append((dims, layout, joined, 2 * slots))
            continue
        sources = both_cores(arrays, dims)
        arrived = list(pl.pallas_call(
            functools.partial(pick_kernel, dims, layout, 2 * slots),
            in_specs=[smem] + [inside] * len(sources),
            out_shape=[jax.ShapeDtypeStruct((slots, pack, block), jnp.bfloat16)] * times,
            scratch_shapes=[
                pltpu.VMEM((slots, part_rows, block), jnp.bfloat16),
                pltpu.VMEM((slots, part_rows // block, block, block), jnp.bfloat16),
            ],
            compiler_params=pltpu.CompilerParams(vmem_limit_bytes=8 << 20),
            cost_estimate=pl.CostEstimate(flops=1, bytes_accessed=1, transcendentals=0),
            name="pick",
        )(plan, *sources))
        if table is None:
            table = inverse_table(segments, arrived[1:])
        for step in range(1, times):
            moves = [(t, (t + step) % times) for t in range(times)]
            arrived[step] = lax.ppermute(arrived[step], "tm", moves)
        inputs += arrived
        picks.append(None)

    chunk = min(share, 16)
    return pl.pallas_call(
        functools.partial(stack_kernel, bins, rows, times, chunk, picks),
        in_specs=[smem] * 2 + [inside] * (1 + len(inputs)),
        out_specs=anywhere,
        out_shape=jax.ShapeDtypeStruct((slots, LAGS, share * block), jnp.float32),
        scratch_shapes=[
            pltpu.VMEM((slots, LAGS, share * block), jnp.float32),
            pltpu.VMEM((2, times, part_rows, block), jnp.bfloat16),
            pltpu.VMEM((block, part_rows), jnp.float32),
            pltpu.VMEM((share, groups * wide), jnp.float32),
            pltpu.VMEM((groups * wide, 2 * block), jnp.bfloat16),
            pltpu.VMEM((chunk // 2, 2 * NF, 2 * block), jnp.bfloat16),
            pltpu.SemaphoreType.DMA((slots, share // chunk)),
        ],
        compiler_params=pltpu.CompilerParams(vmem_limit_bytes=40 << 20),
        name="stack",
    )(counts, plan, table, *inputs)


def solution(mesh):
    placed = (P("tm", "pair", None), P(), P("pair", None), P("pair"))
    return jax.shard_map(
        shards, mesh=mesh, in_specs=placed, out_specs=P("pair", None, "tm"), check_vma=False
    )
```

```python
import functools
import math

import jax
import jax.numpy as jnp
import numpy as np
from jax import lax
from jax.experimental import pallas as pl
from jax.experimental.pallas import tpu as pltpu
from jax.sharding import PartitionSpec as P

NT = 1024
NF = 128
LOW_BIN = 8
LAGS = 128


def forward_table():
    phase = (LOW_BIN + np.arange(NF))[:, None] * np.arange(NT)[None, :] % NT
    angle = phase * (2.0 * math.pi / NT)
    return np.concatenate([np.cos(angle), -np.sin(angle)], axis=0).astype(np.float32)


def inverse_table(segments, sent):
    (shifts,) = after([jnp.arange(LAGS, dtype=jnp.int32) - LAGS // 2], sent)
    column = jnp.arange(2 * NF, dtype=jnp.int32)
    half = NF // PIECES
    bin_id = LOW_BIN + column // (2 * half) * half + column % half
    phase = jnp.mod(shifts[:, None] * bin_id[None, :], NT)
    angle = phase.astype(jnp.float32) * (2.0 * math.pi / NT)
    scale = 1.0 / math.sqrt(segments * NF)
    value = jnp.where(column // half % 2 == 0, jnp.cos(angle), -jnp.sin(angle)) * scale
    return value.astype(jnp.bfloat16)


def halves(value):
    high = value.astype(jnp.bfloat16)
    return high, (value - high.astype(jnp.float32)).astype(jnp.bfloat16)


def nt_dot(a, b):
    return lax.dot_general(a, b, (((1,), (1,)), ((), ())), preferred_element_type=jnp.float32)


CHUNKS = 2
PIECES = 2


def whiten_kernel(bins, x_hbm, table_hbm, *refs):
    outs, (x_ref, table_ref, pad_ref, sems) = refs[:-4], refs[-4:]
    _, segments, block, wide = x_ref.shape
    columns = segments * block
    copies = []
    for k in range(CHUNKS):
        span = slice(k * wide, (k + 1) * wide)
        sources = (x_hbm.at[:, :, span], table_hbm.at[:, span])
        copies.append(
            [
                pltpu.make_async_copy(source, target.at[k], sems.at[k, n])
                for n, (source, target) in enumerate(zip(sources, (x_ref, table_ref)))
            ]
        )
        for copy in copies[-1]:
            copy.start()
    spectrum = None
    for k in range(CHUNKS):
        for copy in copies[k]:
            copy.wait()
        x = x_ref[k].reshape(columns, wide)
        x_high, x_low = halves(x)
        high, low = halves(table_ref[k])
        part = nt_dot(high, x_high) + nt_dot(high, x_low) + nt_dot(low, x_high)
        spectrum = part if spectrum is None else spectrum + part
    real_part = spectrum[:NF]
    imag_part = spectrum[NF:]
    power = real_part * real_part + imag_part * imag_part
    edge = jnp.zeros((8, columns), jnp.float32)
    pad_ref[0:8, :] = edge
    pad_ref[8 + NF : 16 + NF, :] = edge
    pad_ref[8 : 8 + NF, :] = power
    total = pad_ref[6 : 6 + NF, :]
    for offset in range(7, 11):
        total = total + pad_ref[offset : offset + NF, :]
    bin_id = lax.broadcasted_iota(jnp.int32, (NF, columns), 0)
    counted = (jnp.minimum(bin_id + 2, NF - 1) - jnp.maximum(bin_id - 2, 0) + 1).astype(jnp.float32)
    smooth = total / counted
    level = jnp.mean(power, axis=0, keepdims=True)
    factor = lax.rsqrt(smooth + 0.05 * level + 1e-06)
    parts = ((real_part * factor).astype(jnp.bfloat16), (imag_part * factor).astype(jnp.bfloat16))
    each = NF // bins // len(outs)
    for group in range(NF // bins):
        for segment in range(segments):
            for c in range(2):
                row = ((group % each * segments + segment) * 2 + c) * bins
                outs[group // each][row : row + bins, :] = parts[c][
                    group * bins : (group + 1) * bins, segment * block : (segment + 1) * block
                ]


def fetch(dims, layout, joined, plan_ref, at, sources, targets):
    _, height, cores = dims
    away = plan_ref[at]
    place = away // cores
    array = jnp.int32(0)
    index = jnp.int32(0)
    for (dz, dy), (where, spot) in layout.items():
        here = place == dz * height + dy
        array = jnp.where(here, where, array)
        index = jnp.where(here, spot * joined, index)
    for n, source in enumerate(sources):

        @pl.when(away % cores + cores * array == n)
        def _():
            for step in range(joined):
                value = source[index + step]
                for target in targets[step]:
                    target[...] = value


def pick_kernel(dims, layout, time_at, plan_ref, *refs):
    count = dims[2] * (1 + max(array for array, _ in layout.values()))
    sources, outs, (held, turned) = refs[:count], refs[count:-2], refs[-2:]
    slots, rows, block = held.shape
    times = len(outs)
    share = block // times
    time = plan_ref[time_at]
    for slot in range(slots):
        fetch(dims, layout, 1, plan_ref, 2 * slot, sources, [[held.at[slot]]])
        fetch(dims, layout, 1, plan_ref, 2 * slot + 1, sources, [[out.at[slot, :rows] for out in outs]])
    for slot in range(slots):
        flipped = held[slot].astype(jnp.float32).T.astype(jnp.bfloat16)
        for piece in range(rows // block):
            turned[slot, piece] = flipped[:, piece * block : (piece + 1) * block]
        for step, out in enumerate(outs):
            start = pl.multiple_of((time + step) % times * share, share)
            for piece in range(rows // block):
                low = rows + piece * share
                out[slot, low : low + share] = turned[slot, piece, pl.ds(start, share)]


def put_right(bins, block_ref, right_all, at, rows):
    block = block_ref.shape[1]
    for low in range(0, rows, 2 * bins):
        real_part = block_ref[low : low + bins, :]
        imag_part = block_ref[low + bins : low + 2 * bins, :]
        base = at(low)
        right_all[base : base + bins, :block] = real_part
        right_all[base : base + bins, block:] = imag_part
        right_all[base + bins : base + 2 * bins, :block] = imag_part
        right_all[base + bins : base + 2 * bins, block:] = -real_part


def cross_spectra(bins, wide, first, chunk, left_all, right_all, cross_ref):
    groups = left_all.shape[1] // wide
    each = groups // PIECES
    block = right_all.shape[1] // 2
    half = each * bins
    column = lax.broadcasted_iota(jnp.int32, (bins, wide), 1) % bins
    row = lax.broadcasted_iota(jnp.int32, (bins, wide), 0)
    keep = (column == row).astype(jnp.float32).astype(jnp.bfloat16)
    several = 16 if chunk % 16 == 0 else 2
    for group in range(groups):
        weights = right_all[group * wide : (group + 1) * wide, :]
        real_at = group // each * 2 * half + group % each * bins
        imag_at = real_at + half
        for start in range(0, chunk, several):
            pieces = []
            for i in range(several):
                line = left_all[pl.ds(first + start + i, 1), group * wide : (group + 1) * wide]
                tile = jnp.broadcast_to(line, (16, wide)).astype(jnp.bfloat16)
                pieces += [tile * keep[low : low + 16] for low in range(0, bins, 16)]
            product = jnp.dot(jnp.concatenate(pieces, axis=0), weights, preferred_element_type=jnp.float32)
            product = product.astype(jnp.bfloat16)
            for i in range(several):
                at = start + i
                lanes = slice(at % 2 * block, (at % 2 + 1) * block)
                piece = product[i * bins : (i + 1) * bins]
                cross_ref[at // 2, real_at : real_at + bins, lanes] = piece[:, :block]
                cross_ref[at // 2, imag_at : imag_at + bins, lanes] = piece[:, block:]


def stack_kernel(bins, rows, times, chunk, picks, counts_ref, plan_ref, table_ref, *refs):
    out_ref, held, blocks, turned, left_all, right_all, cross_ref, sems = refs[-8:]
    slots = held.shape[0]
    share = left_all.shape[0]
    block = share * times
    wide = times * rows
    each = left_all.shape[1] // wide // PIECES
    part_rows = each * rows
    lanes = 2 * block
    parts = share // chunk
    width = chunk // 2 * lanes

    def leave(slot, n):
        span = slice(n * width, (n + 1) * width)
        return pltpu.make_async_copy(held.at[slot, :, span], out_ref.at[slot, :, span], sems.at[slot, n])

    def one_slot(slot, carry):
        at_ref = 0
        for piece, pick in enumerate(picks):
            base = piece * each * wide
            if pick is None:
                packs = refs[at_ref : at_ref + times]
                at_ref += times
            else:
                dims, layout, joined, time_at = pick
                count = dims[2] * (1 + max(array for array, _ in layout.values()))
                sources = refs[at_ref : at_ref + count]
                at_ref += count
                for side in range(2):
                    targets = [[blocks.at[side, step]] for step in range(joined)]
                    fetch(dims, layout, joined, plan_ref, 2 * slot + side, sources, targets)
                start = pl.multiple_of(plan_ref[time_at] * share, share)
            for step in range(times):
                at = functools.partial(lambda base, step, low: base + low // rows * wide + step * rows + low % rows, base, step)
                if pick is None:
                    put_right(bins, packs[step].at[slot], right_all, at, part_rows)
                    for low in range(0, part_rows, block):
                        first = part_rows + low // block * share
                        value = packs[step][slot, first : first + share, :].astype(jnp.float32)
                        for inner in range(0, block, rows):
                            left_all[:, at(low + inner) : at(low + inner) + rows] = value[:, inner : inner + rows]
                else:
                    put_right(bins, blocks.at[1, step], right_all, at, part_rows)
                    turned[...] = blocks[0, step].astype(jnp.float32).T
                    for low in range(0, part_rows, rows):
                        left_all[:, at(low) : at(low) + rows] = turned[pl.ds(start, share), low : low + rows]
        table = table_ref[...]

        for n in range(parts):
            cross_spectra(bins, wide, n * chunk, chunk, left_all, right_all, cross_ref.at[n % 2])
            for pair in range(chunk // 2):
                span = slice(n * width + pair * lanes, n * width + (pair + 1) * lanes)
                held[slot, :, span] = jnp.dot(table, cross_ref[n % 2, pair], preferred_element_type=jnp.float32)
            leave(slot, n).start()
        return carry

    for slot in range(slots):

        @pl.when(slot >= counts_ref[0])
        def _():
            held[slot] = jnp.zeros_like(held[slot])
            for n in range(parts):
                leave(slot, n).start()

    lax.fori_loop(0, jnp.minimum(counts_ref[0], slots), one_slot, 0)
    for slot in range(slots):
        for n in range(parts):
            leave(slot, n).wait()


def chip_dims(size):
    return {16: (4, 2, 2), 64: (16, 4, 1)}.get(size, (size, 1, 1))


def swap(value, dims, axis, by):
    moves = []
    for p in range(math.prod(dims)):
        place = list(np.unravel_index(p, dims))
        place[axis] ^= by
        moves.append((p, int(np.ravel_multi_index(place, dims))))
    return lax.ppermute(value, "pair", moves)


def is_paired(dims, times):
    return dims == (4, 2, 2) and times == 2 and PIECES == 2


def column_layout(dims, parts):
    depth, height, _ = dims
    order = [(0, 0)]
    for axis, size in ((0, depth), (1, height)):
        bit = size // 2
        while bit:
            order += [(z ^ bit, y) if axis == 0 else (z, y ^ bit) for z, y in order]
            bit //= 2
    spots = [(n, at) for n, part in enumerate(parts) for at in range(part)]
    return dict(zip(order, spots))


def after(values, others):
    return lax.optimization_barrier(tuple(values) + tuple(others))[: len(values)]


def join(held, more):
    (room,) = after([jnp.concatenate([held, held])], ())
    return lax.dynamic_update_slice(room, more, (held.shape[0], 0, 0))


def swap_times(value, step, times):
    return lax.ppermute(value, "tm", [((t + step) % times, t) for t in range(times)])


def gather_one(held, dims):
    depth, height, _ = dims
    for axis, size in ((0, depth), (1, height)):
        bit = size // 2
        while bit:
            held = jnp.concatenate([held, swap(held, dims, axis, bit)])
            bit //= 2
    return [held]


def gather_two(first, second, dims):
    first_far = swap(first, dims, 0, 2)
    (room,) = after([jnp.concatenate([first, first])], ())
    (second,) = after([second], [room])
    other = swap_times(second, 1, 2)
    pair = join(second, other)
    pair_far = swap(pair, dims, 0, 2)
    (first_two,) = after([lax.dynamic_update_slice(room, first_far, (1, 0, 0))], [pair])
    first_near = swap(first_two, dims, 0, 1)
    pair_two = jnp.concatenate([pair, pair_far])
    (first_near,) = after([first_near], [pair_two])
    first_four = jnp.concatenate([first_two, first_near])
    first_beside = swap(first_four, dims, 1, 1)
    pair_near = swap(pair_two, dims, 0, 1)
    pair_four = jnp.concatenate([pair_two, pair_near])
    pair_beside = swap(pair_four, dims, 1, 1)
    return [first_four, first_beside], [pair_four, pair_beside], pair_two


def both_cores(arrays, dims):
    if dims[2] == 1:
        return arrays
    return [value for array in arrays for value in (array, swap(array, dims, 2, 1))]


def shards(traces, owner, tiles, counts):
    seg_count, block, _ = traces.shape
    times = lax.axis_size("tm")
    segments = seg_count * times
    share = block // times
    slots = tiles.shape[0]
    bins = max(16, 128 // segments)
    groups = NF // bins
    rows = seg_count * 2 * bins
    wide = rows * times
    total = groups * rows
    part_rows = total // PIECES
    dims = chip_dims(lax.axis_size("pair"))
    smem = pl.BlockSpec(memory_space=pltpu.SMEM)
    anywhere = pl.BlockSpec(memory_space=pl.ANY)
    white = pl.pallas_call(
        functools.partial(whiten_kernel, bins),
        in_specs=[anywhere] * 2,
        out_shape=[jax.ShapeDtypeStruct((part_rows, block), jnp.bfloat16)] * PIECES,
        scratch_shapes=[
            pltpu.VMEM((CHUNKS, seg_count, block, NT // CHUNKS), jnp.float32),
            pltpu.VMEM((CHUNKS, 2 * NF, NT // CHUNKS), jnp.float32),
            pltpu.VMEM((NF + 16, seg_count * block), jnp.float32),
            pltpu.SemaphoreType.DMA((CHUNKS, 2)),
        ],
        compiler_params=pltpu.CompilerParams(vmem_limit_bytes=63 << 20),
        name="whiten",
    )(traces, jnp.asarray(forward_table()))

    paired = is_paired(dims, times)
    blocks = [own[None] for own in white]
    if paired:
        *gathered, near = gather_two(*blocks, dims)
        (tiles,) = after([tiles], [near])
    else:
        gathered = [gather_one(own, dims) for own in blocks]

    known = owner.shape[0]
    chosen = tiles.reshape(-1, 1) == jnp.arange(known, dtype=jnp.int32)
    stored = jnp.sum(jnp.where(chosen, owner, 0), axis=1)
    plan = jnp.concatenate([stored ^ lax.axis_index("pair"), lax.axis_index("tm")[None]]).astype(jnp.int32)

    pack = part_rows + part_rows // block * share
    inside = pl.BlockSpec(memory_space=pltpu.VMEM)
    inputs = []
    picks = []
    table = None
    for piece, arrays in enumerate(gathered):
        joined = times if paired and piece else 1
        layout = column_layout(dims, [array.shape[0] // joined for array in arrays])
        if joined > 1:
            arrays[-1:] = after(arrays[-1:], inputs[1:] + [table])
            inputs += both_cores(arrays, dims)
            picks.append((dims, layout, joined, 2 * slots))
            continue
        sources = both_cores(arrays, dims)
        arrived = list(pl.pallas_call(
            functools.partial(pick_kernel, dims, layout, 2 * slots),
            in_specs=[smem] + [inside] * len(sources),
            out_shape=[jax.ShapeDtypeStruct((slots, pack, block), jnp.bfloat16)] * times,
            scratch_shapes=[
                pltpu.VMEM((slots, part_rows, block), jnp.bfloat16),
                pltpu.VMEM((slots, part_rows // block, block, block), jnp.bfloat16),
            ],
            compiler_params=pltpu.CompilerParams(vmem_limit_bytes=8 << 20),
            cost_estimate=pl.CostEstimate(flops=1, bytes_accessed=1, transcendentals=0),
            name="pick",
        )(plan, *sources))
        if table is None:
            table = inverse_table(segments, arrived[1:])
        for step in range(1, times):
            moves = [(t, (t + step) % times) for t in range(times)]
            arrived[step] = lax.ppermute(arrived[step], "tm", moves)
        inputs += arrived
        picks.append(None)

    chunk = min(share, 16)
    return pl.pallas_call(
        functools.partial(stack_kernel, bins, rows, times, chunk, picks),
        in_specs=[smem] * 2 + [inside] * (1 + len(inputs)),
        out_specs=anywhere,
        out_shape=jax.ShapeDtypeStruct((slots, LAGS, share * block), jnp.float32),
        scratch_shapes=[
            pltpu.VMEM((slots, LAGS, share * block), jnp.float32),
            pltpu.VMEM((2, times, part_rows, block), jnp.bfloat16),
            pltpu.VMEM((block, part_rows), jnp.float32),
            pltpu.VMEM((share, groups * wide), jnp.float32),
            pltpu.VMEM((groups * wide, 2 * block), jnp.bfloat16),
            pltpu.VMEM((2, chunk // 2, 2 * NF, 2 * block), jnp.bfloat16),
            pltpu.SemaphoreType.DMA((slots, share // chunk)),
        ],
        compiler_params=pltpu.CompilerParams(vmem_limit_bytes=40 << 20),
        name="stack",
    )(counts, plan, table, *inputs)


def solution(mesh):
    placed = (P("tm", "pair", None), P(), P("pair", None), P("pair"))
    return jax.shard_map(
        shards, mesh=mesh, in_specs=placed, out_specs=P("pair", None, "tm"), check_vma=False
    )
```

```python
import functools
import math

import jax
import jax.numpy as jnp
import numpy as np
from jax import lax
from jax.experimental import pallas as pl
from jax.experimental.pallas import tpu as pltpu
from jax.sharding import PartitionSpec as P

NT = 1024
NF = 128
LOW_BIN = 8
LAGS = 128


def forward_table():
    phase = (LOW_BIN + np.arange(NF))[:, None] * np.arange(NT)[None, :] % NT
    angle = phase * (2.0 * math.pi / NT)
    return np.concatenate([np.cos(angle), -np.sin(angle)], axis=0).astype(np.float32)


def inverse_table(segments, sent):
    (shifts,) = after([jnp.arange(LAGS, dtype=jnp.int32) - LAGS // 2], sent)
    column = jnp.arange(2 * NF, dtype=jnp.int32)
    half = NF // PIECES
    bin_id = LOW_BIN + column // (2 * half) * half + column % half
    phase = jnp.mod(shifts[:, None] * bin_id[None, :], NT)
    angle = phase.astype(jnp.float32) * (2.0 * math.pi / NT)
    scale = 1.0 / math.sqrt(segments * NF)
    value = jnp.where(column // half % 2 == 0, jnp.cos(angle), -jnp.sin(angle)) * scale
    return value.astype(jnp.bfloat16)


def halves(value):
    high = value.astype(jnp.bfloat16)
    return high, (value - high.astype(jnp.float32)).astype(jnp.bfloat16)


def nt_dot(a, b):
    return lax.dot_general(a, b, (((1,), (1,)), ((), ())), preferred_element_type=jnp.float32)


CHUNKS = 2
PIECES = 2


def whiten_kernel(bins, x_hbm, table_hbm, *refs):
    outs, (x_ref, table_ref, pad_ref, sems) = refs[:-4], refs[-4:]
    _, segments, block, wide = x_ref.shape
    columns = segments * block
    copies = []
    for k in range(CHUNKS):
        span = slice(k * wide, (k + 1) * wide)
        sources = (x_hbm.at[:, :, span], table_hbm.at[:, span])
        copies.append(
            [
                pltpu.make_async_copy(source, target.at[k], sems.at[k, n])
                for n, (source, target) in enumerate(zip(sources, (x_ref, table_ref)))
            ]
        )
        for copy in copies[-1]:
            copy.start()
    spectrum = None
    for k in range(CHUNKS):
        for copy in copies[k]:
            copy.wait()
        x = x_ref[k].reshape(columns, wide)
        x_high, x_low = halves(x)
        high, low = halves(table_ref[k])
        part = nt_dot(high, x_high) + nt_dot(high, x_low) + nt_dot(low, x_high)
        spectrum = part if spectrum is None else spectrum + part
    real_part = spectrum[:NF]
    imag_part = spectrum[NF:]
    power = real_part * real_part + imag_part * imag_part
    edge = jnp.zeros((8, columns), jnp.float32)
    pad_ref[0:8, :] = edge
    pad_ref[8 + NF : 16 + NF, :] = edge
    pad_ref[8 : 8 + NF, :] = power
    total = pad_ref[6 : 6 + NF, :]
    for offset in range(7, 11):
        total = total + pad_ref[offset : offset + NF, :]
    bin_id = lax.broadcasted_iota(jnp.int32, (NF, columns), 0)
    counted = (jnp.minimum(bin_id + 2, NF - 1) - jnp.maximum(bin_id - 2, 0) + 1).astype(jnp.float32)
    smooth = total / counted
    level = jnp.mean(power, axis=0, keepdims=True)
    factor = lax.rsqrt(smooth + 0.05 * level + 1e-06)
    parts = ((real_part * factor).astype(jnp.bfloat16), (imag_part * factor).astype(jnp.bfloat16))
    each = NF // bins // len(outs)
    for group in range(NF // bins):
        for segment in range(segments):
            for c in range(2):
                row = ((group % each * segments + segment) * 2 + c) * bins
                outs[group // each][row : row + bins, :] = parts[c][
                    group * bins : (group + 1) * bins, segment * block : (segment + 1) * block
                ]


def fetch(joined, plan_ref, at, wanted, sources, targets):
    index = plan_ref[wanted + at]
    for n, source in enumerate(sources):

        @pl.when(plan_ref[at] == n)
        def _():
            for step in range(joined):
                value = source[index + step]
                for target in targets[step]:
                    target[...] = value


def pick_kernel(count, plan_ref, *refs):
    sources, outs, (held, turned) = refs[:count], refs[count:-2], refs[-2:]
    slots, rows, block = held.shape
    times = len(outs)
    share = block // times
    time = plan_ref[4 * slots]
    for slot in range(slots):
        fetch(1, plan_ref, 2 * slot, 2 * slots, sources, [[held.at[slot]]])
        fetch(1, plan_ref, 2 * slot + 1, 2 * slots, sources, [[out.at[slot, :rows] for out in outs]])
    for slot in range(slots):
        flipped = held[slot].astype(jnp.float32).T.astype(jnp.bfloat16)
        for piece in range(rows // block):
            turned[slot, piece] = flipped[:, piece * block : (piece + 1) * block]
        for step, out in enumerate(outs):
            start = pl.multiple_of((time + step) % times * share, share)
            for piece in range(rows // block):
                low = rows + piece * share
                out[slot, low : low + share] = turned[slot, piece, pl.ds(start, share)]


def put_right(bins, block_ref, right_all, at, rows):
    block = block_ref.shape[1]
    for low in range(0, rows, 2 * bins):
        real_part = block_ref[low : low + bins, :]
        imag_part = block_ref[low + bins : low + 2 * bins, :]
        base = at(low)
        right_all[base : base + bins, :block] = real_part
        right_all[base : base + bins, block:] = imag_part
        right_all[base + bins : base + 2 * bins, :block] = imag_part
        right_all[base + bins : base + 2 * bins, block:] = -real_part


def put_pack(slot, rows, bins, step, times, pack, left_all, right_all):
    share = left_all.shape[0]
    block = share * times
    wide = times * rows
    part_rows = left_all.shape[1] // times
    at = functools.partial(column_of, rows, wide, step)
    put_right(bins, pack.at[slot], right_all, at, part_rows)
    for low in range(0, part_rows, block):
        first = part_rows + low // block * share
        value = pack[slot, first : first + share, :].astype(jnp.float32)
        for inner in range(0, block, rows):
            left_all[:, at(low + inner) : at(low + inner) + rows] = value[:, inner : inner + rows]


def column_of(rows, wide, step, low):
    return low // rows * wide + step * rows + low % rows


def cross_spectra(bins, wide, first, chunk, left_all, right_all, cross_ref):
    groups = left_all.shape[1] // wide
    block = right_all.shape[1] // 2
    half = groups * bins
    column = lax.broadcasted_iota(jnp.int32, (bins, wide), 1) % bins
    row = lax.broadcasted_iota(jnp.int32, (bins, wide), 0)
    keep = (column == row).astype(jnp.float32).astype(jnp.bfloat16)
    several = 16 if chunk % 16 == 0 else 2
    for group in range(groups):
        weights = right_all[group * wide : (group + 1) * wide, :]
        for start in range(0, chunk, several):
            pieces = []
            for i in range(several):
                line = left_all[pl.ds(first + start + i, 1), group * wide : (group + 1) * wide]
                tile = jnp.broadcast_to(line, (16, wide)).astype(jnp.bfloat16)
                pieces += [tile * keep[low : low + 16] for low in range(0, bins, 16)]
            product = jnp.dot(jnp.concatenate(pieces, axis=0), weights, preferred_element_type=jnp.float32)
            product = product.astype(jnp.bfloat16)
            for i in range(several):
                at = start + i
                lanes = slice(at % 2 * block, (at % 2 + 1) * block)
                piece = product[i * bins : (i + 1) * bins]
                cross_ref[at // 2, group * bins : (group + 1) * bins, lanes] = piece[:, :block]
                cross_ref[at // 2, half + group * bins : half + (group + 1) * bins, lanes] = piece[:, block:]


def cross_kernel(bins, rows, chunk, plan_ref, *refs):
    packs, (out_ref, left_all, right_all) = refs[:-3], refs[-3:]
    times = len(packs)

    def one_slot(slot, carry):
        for step, pack in enumerate(packs):
            put_pack(slot, rows, bins, step, times, pack, left_all, right_all)
        for n in range(left_all.shape[0] // chunk):
            into = out_ref.at[slot, n * chunk // 2 : (n + 1) * chunk // 2]
            cross_spectra(bins, times * rows, n * chunk, chunk, left_all, right_all, into)
        return carry

    slots = out_ref.shape[0]
    lax.fori_loop(0, jnp.minimum(plan_ref[4 * slots + 1], slots), one_slot, 0)


def stack_kernel(bins, rows, times, chunk, joined, plan_ref, table_ref, early_ref, *refs):
    sources, refs = refs[:-8], refs[-8:]
    out_ref, held, blocks, turned, left_all, right_all, cross_ref, sems = refs
    slots = held.shape[0]
    live = plan_ref[4 * slots + 1]
    share = left_all.shape[0]
    block = share * times
    wide = times * rows
    part_rows = left_all.shape[1] // times
    lanes = 2 * block
    parts = share // chunk
    width = chunk // 2 * lanes

    def leave(slot, n):
        span = slice(n * width, (n + 1) * width)
        return pltpu.make_async_copy(held.at[slot, :, span], out_ref.at[slot, :, span], sems.at[slot, n])

    def one_slot(slot, carry):
        if joined == 1:
            for step, pack in enumerate(sources):
                put_pack(slot, rows, bins, step, times, pack, left_all, right_all)
        else:
            for side in range(2):
                targets = [[blocks.at[side, step]] for step in range(joined)]
                fetch(joined, plan_ref, 2 * slot + side, 2 * slots, sources, targets)
            start = pl.multiple_of(plan_ref[4 * slots] * share, share)
            for step in range(times):
                at = functools.partial(column_of, rows, wide, step)
                put_right(bins, blocks.at[1, step], right_all, at, part_rows)
                turned[...] = blocks[0, step].astype(jnp.float32).T
                for low in range(0, part_rows, rows):
                    left_all[:, at(low) : at(low) + rows] = turned[pl.ds(start, share), low : low + rows]
        table = table_ref[...]
        for n in range(parts):
            cross_spectra(bins, wide, n * chunk, chunk, left_all, right_all, cross_ref.at[n % 2])
            for pair in range(chunk // 2):
                at = n * chunk // 2 + pair
                cross = jnp.concatenate([early_ref[slot, at], cross_ref[n % 2, pair]], axis=0)
                held[slot, :, at * lanes : (at + 1) * lanes] = jnp.dot(table, cross, preferred_element_type=jnp.float32)
            leave(slot, n).start()
        return carry

    for slot in range(slots):

        @pl.when(slot >= live)
        def _():
            held[slot] = jnp.zeros_like(held[slot])
            for n in range(parts):
                leave(slot, n).start()

    lax.fori_loop(0, jnp.minimum(live, slots), one_slot, 0)
    for slot in range(slots):
        for n in range(parts):
            leave(slot, n).wait()


def chip_dims(size):
    return {16: (4, 2, 2), 64: (16, 4, 1)}.get(size, (size, 1, 1))


def swap(value, dims, axis, by):
    moves = []
    for p in range(math.prod(dims)):
        place = list(np.unravel_index(p, dims))
        place[axis] ^= by
        moves.append((p, int(np.ravel_multi_index(place, dims))))
    return lax.ppermute(value, "pair", moves)


def is_paired(dims, times):
    return dims == (4, 2, 2) and times == 2 and PIECES == 2


def column_order(dims):
    depth, height, _ = dims
    order = [(0, 0)]
    for axis, size in ((0, depth), (1, height)):
        bit = size // 2
        while bit:
            order += [(z ^ bit, y) if axis == 0 else (z, y ^ bit) for z, y in order]
            bit //= 2
    return order


def plan_of(away, counts, dims, parts, joined):
    _, height, cores = dims
    source = jnp.zeros_like(away)
    index = jnp.zeros_like(away)
    spots = [(n, at) for n, part in enumerate(parts) for at in range(part)]
    for (z, y), (n, at) in zip(column_order(dims), spots):
        here = away // cores == z * height + y
        source = jnp.where(here, n * cores, source)
        index = jnp.where(here, at * joined, index)
    return jnp.concatenate([source + away % cores, index, lax.axis_index("tm")[None], counts]).astype(jnp.int32)


def after(values, others):
    return lax.optimization_barrier(tuple(values) + tuple(others))[: len(values)]


def join(held, more):
    (room,) = after([jnp.concatenate([held, held])], ())
    return lax.dynamic_update_slice(room, more, (held.shape[0], 0, 0))


def swap_times(value, step, times):
    return lax.ppermute(value, "tm", [((t + step) % times, t) for t in range(times)])


def gather_one(held, dims):
    depth, height, _ = dims
    for axis, size in ((0, depth), (1, height)):
        bit = size // 2
        while bit:
            held = jnp.concatenate([held, swap(held, dims, axis, bit)])
            bit //= 2
    return [held]


def gather_two(first, second, dims):
    first_far = swap(first, dims, 0, 2)
    (room,) = after([jnp.concatenate([first, first])], ())
    (second,) = after([second], [room])
    other = swap_times(second, 1, 2)
    pair = join(second, other)
    pair_far = swap(pair, dims, 0, 2)
    (first_two,) = after([lax.dynamic_update_slice(room, first_far, (1, 0, 0))], [pair])
    first_near = swap(first_two, dims, 0, 1)
    pair_two = jnp.concatenate([pair, pair_far])
    (first_near,) = after([first_near], [pair_two])
    first_four = jnp.concatenate([first_two, first_near])
    first_beside = swap(first_four, dims, 1, 1)
    pair_near = swap(pair_two, dims, 0, 1)
    pair_four = jnp.concatenate([pair_two, pair_near])
    first_core = swap(after([first_four], [pair_near])[0], dims, 2, 1)
    pair_beside = swap(pair_four, dims, 1, 1)
    return [first_four, first_beside], [pair_four, pair_beside], first_two, first_core


def both_cores(arrays, dims):
    if dims[2] == 1:
        return arrays
    return [value for array in arrays for value in (array, swap(array, dims, 2, 1))]


def shards(traces, owner, tiles, counts):
    seg_count, block, _ = traces.shape
    times = lax.axis_size("tm")
    segments = seg_count * times
    share = block // times
    slots = tiles.shape[0]
    bins = max(16, 128 // segments)
    groups = NF // bins
    rows = seg_count * 2 * bins
    wide = rows * times
    total = groups * rows
    part_rows = total // PIECES
    dims = chip_dims(lax.axis_size("pair"))
    smem = pl.BlockSpec(memory_space=pltpu.SMEM)
    anywhere = pl.BlockSpec(memory_space=pl.ANY)
    white = pl.pallas_call(
        functools.partial(whiten_kernel, bins),
        in_specs=[anywhere] * 2,
        out_shape=[jax.ShapeDtypeStruct((part_rows, block), jnp.bfloat16)] * PIECES,
        scratch_shapes=[
            pltpu.VMEM((CHUNKS, seg_count, block, NT // CHUNKS), jnp.float32),
            pltpu.VMEM((CHUNKS, 2 * NF, NT // CHUNKS), jnp.float32),
            pltpu.VMEM((NF + 16, seg_count * block), jnp.float32),
            pltpu.SemaphoreType.DMA((CHUNKS, 2)),
        ],
        compiler_params=pltpu.CompilerParams(vmem_limit_bytes=63 << 20),
        name="whiten",
    )(traces, jnp.asarray(forward_table()))

    paired = is_paired(dims, times)
    blocks = [own[None] for own in white]
    if paired:
        *gathered, near, swapped = gather_two(*blocks, dims)
        (tiles,) = after([tiles], [near])
    else:
        gathered = [gather_one(own, dims) for own in blocks]

    known = owner.shape[0]
    chosen = tiles.reshape(-1, 1) == jnp.arange(known, dtype=jnp.int32)
    stored = jnp.sum(jnp.where(chosen, owner, 0), axis=1)
    away = stored ^ lax.axis_index("pair")

    pack = part_rows + part_rows // block * share
    depth = 2 * NF // PIECES
    chunk = min(share, 16)
    inside = pl.BlockSpec(memory_space=pltpu.VMEM)
    operands = [
        pltpu.VMEM((share, groups // PIECES * wide), jnp.float32),
        pltpu.VMEM((groups // PIECES * wide, 2 * block), jnp.bfloat16),
    ]
    early = None
    for piece, arrays in enumerate(gathered):
        joined = times if paired and piece else 1
        plan = plan_of(away, counts, dims, [array.shape[0] // joined for array in arrays], joined)
        if joined > 1:
            arrays[-1:] = after(arrays[-1:], arrived[1:] + [table])
            arrived = both_cores(arrays, dims)
            continue
        sources = both_cores(arrays, dims)
        if paired:
            sources[1] = swapped
        arrived = list(pl.pallas_call(
            functools.partial(pick_kernel, len(sources)),
            in_specs=[smem] + [inside] * len(sources),
            out_shape=[jax.ShapeDtypeStruct((slots, pack, block), jnp.bfloat16)] * times,
            scratch_shapes=[
                pltpu.VMEM((slots, part_rows, block), jnp.bfloat16),
                pltpu.VMEM((slots, part_rows // block, block, block), jnp.bfloat16),
            ],
            compiler_params=pltpu.CompilerParams(vmem_limit_bytes=8 << 20),
            cost_estimate=pl.CostEstimate(flops=1, bytes_accessed=1, transcendentals=0),
            name="pick",
        )(plan, *sources))
        if not piece:
            table = inverse_table(segments, arrived[1:])
        for step in range(1, times):
            moves = [(t, (t + step) % times) for t in range(times)]
            arrived[step] = lax.ppermute(arrived[step], "tm", moves)
        if not piece:
            early = pl.pallas_call(
                functools.partial(cross_kernel, bins, rows, chunk),
                in_specs=[smem] + [inside] * times,
                out_shape=jax.ShapeDtypeStruct((slots, share // 2, depth, 2 * block), jnp.bfloat16),
                scratch_shapes=operands,
                compiler_params=pltpu.CompilerParams(vmem_limit_bytes=16 << 20),
                name="cross",
            )(plan, *arrived)

    return pl.pallas_call(
        functools.partial(stack_kernel, bins, rows, times, chunk, joined),
        in_specs=[smem] + [inside] * (2 + len(arrived)),
        out_specs=anywhere,
        out_shape=jax.ShapeDtypeStruct((slots, LAGS, share * block), jnp.float32),
        scratch_shapes=[
            pltpu.VMEM((slots, LAGS, share * block), jnp.float32),
            pltpu.VMEM((2, times, part_rows, block), jnp.bfloat16),
            pltpu.VMEM((block, part_rows), jnp.float32),
        ]
        + operands
        + [
            pltpu.VMEM((2, chunk // 2, depth, 2 * block), jnp.bfloat16),
            pltpu.SemaphoreType.DMA((slots, share // chunk)),
        ],
        compiler_params=pltpu.CompilerParams(vmem_limit_bytes=32 << 20),
        name="stack",
    )(plan, table, early, *arrived)


def solution(mesh):
    placed = (P("tm", "pair", None), P(), P("pair", None), P("pair"))
    return jax.shard_map(
        shards, mesh=mesh, in_specs=placed, out_specs=P("pair", None, "tm"), check_vma=False
    )
```

```python
import functools
import math

import jax
import jax.numpy as jnp
import numpy as np
from jax import lax
from jax.experimental import pallas as pl
from jax.experimental.pallas import tpu as pltpu
from jax.sharding import PartitionSpec as P

NT = 1024
NF = 128
LOW_BIN = 8
LAGS = 128


def forward_table():
    phase = (LOW_BIN + np.arange(NF))[:, None] * np.arange(NT)[None, :] % NT
    angle = phase * (2.0 * math.pi / NT)
    return np.concatenate([np.cos(angle), -np.sin(angle)], axis=0).astype(np.float32)


def inverse_table(segments, sent):
    (shifts,) = after([jnp.arange(LAGS, dtype=jnp.int32) - LAGS // 2], sent)
    column = jnp.arange(2 * NF, dtype=jnp.int32)
    half = NF // PIECES
    bin_id = LOW_BIN + column // (2 * half) * half + column % half
    phase = jnp.mod(shifts[:, None] * bin_id[None, :], NT)
    angle = phase.astype(jnp.float32) * (2.0 * math.pi / NT)
    scale = 1.0 / math.sqrt(segments * NF)
    value = jnp.where(column // half % 2 == 0, jnp.cos(angle), -jnp.sin(angle)) * scale
    return value.astype(jnp.bfloat16)


def halves(value):
    high = value.astype(jnp.bfloat16)
    return high, (value - high.astype(jnp.float32)).astype(jnp.bfloat16)


def nt_dot(a, b):
    return lax.dot_general(a, b, (((1,), (1,)), ((), ())), preferred_element_type=jnp.float32)


CHUNKS = 2
PIECES = 2


def whiten_kernel(bins, x_hbm, table_hbm, *refs):
    outs, (x_ref, table_ref, pad_ref, sems) = refs[:-4], refs[-4:]
    _, segments, block, wide = x_ref.shape
    columns = segments * block
    copies = []
    for k in range(CHUNKS):
        span = slice(k * wide, (k + 1) * wide)
        sources = (x_hbm.at[:, :, span], table_hbm.at[:, span])
        copies.append(
            [
                pltpu.make_async_copy(source, target.at[k], sems.at[k, n])
                for n, (source, target) in enumerate(zip(sources, (x_ref, table_ref)))
            ]
        )
        for copy in copies[-1]:
            copy.start()
    spectrum = None
    for k in range(CHUNKS):
        for copy in copies[k]:
            copy.wait()
        x = x_ref[k].reshape(columns, wide)
        x_high, x_low = halves(x)
        high, low = halves(table_ref[k])
        part = nt_dot(high, x_high) + nt_dot(high, x_low) + nt_dot(low, x_high)
        spectrum = part if spectrum is None else spectrum + part
    real_part = spectrum[:NF]
    imag_part = spectrum[NF:]
    power = real_part * real_part + imag_part * imag_part
    edge = jnp.zeros((8, columns), jnp.float32)
    pad_ref[0:8, :] = edge
    pad_ref[8 + NF : 16 + NF, :] = edge
    pad_ref[8 : 8 + NF, :] = power
    total = pad_ref[6 : 6 + NF, :]
    for offset in range(7, 11):
        total = total + pad_ref[offset : offset + NF, :]
    bin_id = lax.broadcasted_iota(jnp.int32, (NF, columns), 0)
    counted = (jnp.minimum(bin_id + 2, NF - 1) - jnp.maximum(bin_id - 2, 0) + 1).astype(jnp.float32)
    smooth = total / counted
    level = jnp.mean(power, axis=0, keepdims=True)
    factor = lax.rsqrt(smooth + 0.05 * level + 1e-06)
    parts = ((real_part * factor).astype(jnp.bfloat16), (imag_part * factor).astype(jnp.bfloat16))
    each = NF // bins // len(outs)
    for group in range(NF // bins):
        for segment in range(segments):
            for c in range(2):
                row = ((group % each * segments + segment) * 2 + c) * bins
                outs[group // each][row : row + bins, :] = parts[c][
                    group * bins : (group + 1) * bins, segment * block : (segment + 1) * block
                ]


def fetch(joined, plan_ref, at, wanted, sources, targets):
    index = plan_ref[wanted + at]
    for n, source in enumerate(sources):

        @pl.when(plan_ref[at] == n)
        def _():
            for step in range(joined):
                value = source[index + step]
                for target in targets[step]:
                    target[...] = value


def pick_kernel(count, plan_ref, *refs):
    sources, outs, (held, turned) = refs[:count], refs[count:-2], refs[-2:]
    slots, rows, block = held.shape
    times = len(outs)
    share = block // times
    time = plan_ref[4 * slots]
    for slot in range(slots):
        fetch(1, plan_ref, 2 * slot, 2 * slots, sources, [[held.at[slot]]])
        fetch(1, plan_ref, 2 * slot + 1, 2 * slots, sources, [[out.at[slot, :rows] for out in outs]])
    for slot in range(slots):
        flipped = held[slot].astype(jnp.float32).T.astype(jnp.bfloat16)
        for piece in range(rows // block):
            turned[slot, piece] = flipped[:, piece * block : (piece + 1) * block]
        for step, out in enumerate(outs):
            start = pl.multiple_of((time + step) % times * share, share)
            for piece in range(rows // block):
                low = rows + piece * share
                out[slot, low : low + share] = turned[slot, piece, pl.ds(start, share)]


def put_right(bins, block_ref, right_all, at, rows):
    block = block_ref.shape[1]
    for low in range(0, rows, 2 * bins):
        real_part = block_ref[low : low + bins, :]
        imag_part = block_ref[low + bins : low + 2 * bins, :]
        base = at(low)
        right_all[base : base + bins, :block] = real_part
        right_all[base : base + bins, block:] = imag_part
        right_all[base + bins : base + 2 * bins, :block] = imag_part
        right_all[base + bins : base + 2 * bins, block:] = -real_part


def put_pack(slot, rows, bins, step, times, pack, left_all, right_all):
    share = left_all.shape[0]
    block = share * times
    wide = times * rows
    part_rows = left_all.shape[1] // times
    at = functools.partial(column_of, rows, wide, step)
    put_right(bins, pack.at[slot], right_all, at, part_rows)
    for low in range(0, part_rows, block):
        first = part_rows + low // block * share
        value = pack[slot, first : first + share, :].astype(jnp.float32)
        for inner in range(0, block, rows):
            left_all[:, at(low + inner) : at(low + inner) + rows] = value[:, inner : inner + rows]


def column_of(rows, wide, step, low):
    return low // rows * wide + step * rows + low % rows


def cross_spectra(bins, wide, first, chunk, left_all, right_all, cross_ref):
    groups = left_all.shape[1] // wide
    block = right_all.shape[1] // 2
    half = groups * bins
    column = lax.broadcasted_iota(jnp.int32, (bins, wide), 1) % bins
    row = lax.broadcasted_iota(jnp.int32, (bins, wide), 0)
    keep = (column == row).astype(jnp.float32).astype(jnp.bfloat16)
    several = 16 if chunk % 16 == 0 else 2
    for group in range(groups):
        weights = right_all[group * wide : (group + 1) * wide, :]
        for start in range(0, chunk, several):
            pieces = []
            for i in range(several):
                line = left_all[pl.ds(first + start + i, 1), group * wide : (group + 1) * wide]
                tile = jnp.broadcast_to(line, (16, wide)).astype(jnp.bfloat16)
                pieces += [tile * keep[low : low + 16] for low in range(0, bins, 16)]
            product = jnp.dot(jnp.concatenate(pieces, axis=0), weights, preferred_element_type=jnp.float32)
            product = product.astype(jnp.bfloat16)
            for i in range(several):
                at = start + i
                lanes = slice(at % 2 * block, (at % 2 + 1) * block)
                piece = product[i * bins : (i + 1) * bins]
                cross_ref[at // 2, group * bins : (group + 1) * bins, lanes] = piece[:, :block]
                cross_ref[at // 2, half + group * bins : half + (group + 1) * bins, lanes] = piece[:, block:]


def cross_kernel(bins, rows, chunk, plan_ref, *refs):
    packs, (out_ref, left_all, right_all) = refs[:-3], refs[-3:]
    times = len(packs)

    def one_slot(slot, carry):
        for step, pack in enumerate(packs):
            put_pack(slot, rows, bins, step, times, pack, left_all, right_all)
        for n in range(left_all.shape[0] // chunk):
            into = out_ref.at[slot, n * chunk // 2 : (n + 1) * chunk // 2]
            cross_spectra(bins, times * rows, n * chunk, chunk, left_all, right_all, into)
        return carry

    slots = out_ref.shape[0]
    lax.fori_loop(0, jnp.minimum(plan_ref[4 * slots + 1], slots), one_slot, 0)


def stack_kernel(bins, rows, times, chunk, joined, plan_ref, table_ref, early_ref, *refs):
    sources, refs = refs[:-8], refs[-8:]
    out_ref, held, blocks, turned, left_all, right_all, cross_ref, sems = refs
    slots = held.shape[0]
    live = plan_ref[4 * slots + 1]
    share = left_all.shape[0]
    block = share * times
    wide = times * rows
    part_rows = left_all.shape[1] // times
    lanes = 2 * block
    parts = share // chunk
    width = chunk // 2 * lanes

    def leave(slot, n):
        span = slice(n * width, (n + 1) * width)
        return pltpu.make_async_copy(held.at[slot, :, span], out_ref.at[slot, :, span], sems.at[slot, n])

    def one_slot(slot, carry):
        if joined == 1:
            for step, pack in enumerate(sources):
                put_pack(slot, rows, bins, step, times, pack, left_all, right_all)
        else:
            for side in range(2):
                targets = [[blocks.at[side, step]] for step in range(joined)]
                fetch(joined, plan_ref, 2 * slot + side, 2 * slots, sources, targets)
            start = pl.multiple_of(plan_ref[4 * slots] * share, share)
            for step in range(times):
                at = functools.partial(column_of, rows, wide, step)
                put_right(bins, blocks.at[1, step], right_all, at, part_rows)
                turned[...] = blocks[0, step].astype(jnp.float32).T
                for low in range(0, part_rows, rows):
                    left_all[:, at(low) : at(low) + rows] = turned[pl.ds(start, share), low : low + rows]
        table = table_ref[...]
        for n in range(parts):
            cross_spectra(bins, wide, n * chunk, chunk, left_all, right_all, cross_ref.at[n % 2])
            for pair in range(chunk // 2):
                at = n * chunk // 2 + pair
                cross = jnp.concatenate([early_ref[slot, at], cross_ref[n % 2, pair]], axis=0)
                held[slot, :, at * lanes : (at + 1) * lanes] = jnp.dot(table, cross, preferred_element_type=jnp.float32)
            leave(slot, n).start()
        return carry

    for slot in range(slots):

        @pl.when(slot >= live)
        def _():
            held[slot] = jnp.zeros_like(held[slot])
            for n in range(parts):
                leave(slot, n).start()

    lax.fori_loop(0, jnp.minimum(live, slots), one_slot, 0)
    for slot in range(slots):
        for n in range(parts):
            leave(slot, n).wait()


def chip_dims(size):
    return {16: (4, 2, 2), 64: (16, 4, 1)}.get(size, (size, 1, 1))


def swap(value, dims, axis, by):
    moves = []
    for p in range(math.prod(dims)):
        place = list(np.unravel_index(p, dims))
        place[axis] ^= by
        moves.append((p, int(np.ravel_multi_index(place, dims))))
    return lax.ppermute(value, "pair", moves)


def is_paired(dims, times):
    return dims == (4, 2, 2) and times == 2 and PIECES == 2


def column_order(dims):
    depth, height, _ = dims
    order = [(0, 0)]
    for axis, size in ((0, depth), (1, height)):
        bit = size // 2
        while bit:
            order += [(z ^ bit, y) if axis == 0 else (z, y ^ bit) for z, y in order]
            bit //= 2
    return order


def plan_of(away, counts, dims, parts, joined):
    _, height, cores = dims
    source = jnp.zeros_like(away)
    index = jnp.zeros_like(away)
    spots = [(n, at) for n, part in enumerate(parts) for at in range(part)]
    for (z, y), (n, at) in zip(column_order(dims), spots):
        here = away // cores == z * height + y
        source = jnp.where(here, n * cores, source)
        index = jnp.where(here, at * joined, index)
    return jnp.concatenate([source + away % cores, index, lax.axis_index("tm")[None], counts]).astype(jnp.int32)


def after(values, others):
    return lax.optimization_barrier(tuple(values) + tuple(others))[: len(values)]


def join(held, more):
    (room,) = after([jnp.concatenate([held, held])], ())
    return lax.dynamic_update_slice(room, more, (held.shape[0], 0, 0))


def swap_times(value, step, times):
    return lax.ppermute(value, "tm", [((t + step) % times, t) for t in range(times)])


def gather_one(held, dims):
    depth, height, _ = dims
    for axis, size in ((0, depth), (1, height)):
        bit = size // 2
        while bit:
            held = jnp.concatenate([held, swap(held, dims, axis, bit)])
            bit //= 2
    return [held]


def gather_two(first, second, dims):
    first_far = swap(first, dims, 0, 2)
    (room,) = after([jnp.concatenate([first, first])], ())
    (second,) = after([second], [room])
    other = swap_times(second, 1, 2)
    pair = join(second, other)
    pair_far = swap(pair, dims, 0, 2)
    (first_two,) = after([lax.dynamic_update_slice(room, first_far, (1, 0, 0))], [pair])
    first_near = swap(first_two, dims, 0, 1)
    pair_two = jnp.concatenate([pair, pair_far])
    (first_near,) = after([first_near], [pair_two])
    first_four = jnp.concatenate([first_two, first_near])
    first_beside = swap(first_four, dims, 1, 1)
    pair_near = swap(pair_two, dims, 0, 1)
    pair_four = jnp.concatenate([pair_two, pair_near])
    pair_beside = swap(pair_four, dims, 1, 1)
    return [first_four, first_beside], [pair_four, pair_beside], first_two


def both_cores(arrays, dims):
    if dims[2] == 1:
        return arrays
    return [value for array in arrays for value in (array, swap(array, dims, 2, 1))]


def shards(traces, owner, tiles, counts):
    seg_count, block, _ = traces.shape
    times = lax.axis_size("tm")
    segments = seg_count * times
    share = block // times
    slots = tiles.shape[0]
    bins = max(16, 128 // segments)
    groups = NF // bins
    rows = seg_count * 2 * bins
    wide = rows * times
    total = groups * rows
    part_rows = total // PIECES
    dims = chip_dims(lax.axis_size("pair"))
    smem = pl.BlockSpec(memory_space=pltpu.SMEM)
    anywhere = pl.BlockSpec(memory_space=pl.ANY)
    white = pl.pallas_call(
        functools.partial(whiten_kernel, bins),
        in_specs=[anywhere] * 2,
        out_shape=[jax.ShapeDtypeStruct((part_rows, block), jnp.bfloat16)] * PIECES,
        scratch_shapes=[
            pltpu.VMEM((CHUNKS, seg_count, block, NT // CHUNKS), jnp.float32),
            pltpu.VMEM((CHUNKS, 2 * NF, NT // CHUNKS), jnp.float32),
            pltpu.VMEM((NF + 16, seg_count * block), jnp.float32),
            pltpu.SemaphoreType.DMA((CHUNKS, 2)),
        ],
        compiler_params=pltpu.CompilerParams(vmem_limit_bytes=63 << 20),
        name="whiten",
    )(traces, jnp.asarray(forward_table()))

    paired = is_paired(dims, times)
    blocks = [own[None] for own in white]
    if paired:
        *gathered, near = gather_two(*blocks, dims)
        (tiles,) = after([tiles], [near])
    else:
        gathered = [gather_one(own, dims) for own in blocks]

    known = owner.shape[0]
    chosen = tiles.reshape(-1, 1) == jnp.arange(known, dtype=jnp.int32)
    stored = jnp.sum(jnp.where(chosen, owner, 0), axis=1)
    away = stored ^ lax.axis_index("pair")

    pack = part_rows + part_rows // block * share
    depth = 2 * NF // PIECES
    chunk = min(share, 16)
    inside = pl.BlockSpec(memory_space=pltpu.VMEM)
    operands = [
        pltpu.VMEM((share, groups // PIECES * wide), jnp.float32),
        pltpu.VMEM((groups // PIECES * wide, 2 * block), jnp.bfloat16),
    ]
    early = None
    for piece, arrays in enumerate(gathered):
        joined = times if paired and piece else 1
        plan = plan_of(away, counts, dims, [array.shape[0] // joined for array in arrays], joined)
        if joined > 1:
            arrays[-1:] = after(arrays[-1:], arrived[1:] + [table])
            arrived = both_cores(arrays, dims)
            continue
        sources = both_cores(arrays, dims)
        arrived = list(pl.pallas_call(
            functools.partial(pick_kernel, len(sources)),
            in_specs=[smem] + [inside] * len(sources),
            out_shape=[jax.ShapeDtypeStruct((slots, pack, block), jnp.bfloat16)] * times,
            scratch_shapes=[
                pltpu.VMEM((slots, part_rows, block), jnp.bfloat16),
                pltpu.VMEM((slots, part_rows // block, block, block), jnp.bfloat16),
            ],
            compiler_params=pltpu.CompilerParams(vmem_limit_bytes=8 << 20),
            cost_estimate=pl.CostEstimate(flops=1, bytes_accessed=1, transcendentals=0),
            name="pick",
        )(plan, *sources))
        if not piece:
            table = inverse_table(segments, arrived[1:])
        for step in range(1, times):
            moves = [(t, (t + step) % times) for t in range(times)]
            arrived[step] = lax.ppermute(arrived[step], "tm", moves)
        if not piece:
            early = pl.pallas_call(
                functools.partial(cross_kernel, bins, rows, chunk),
                in_specs=[smem] + [inside] * times,
                out_shape=jax.ShapeDtypeStruct((slots, share // 2, depth, 2 * block), jnp.bfloat16),
                scratch_shapes=operands,
                compiler_params=pltpu.CompilerParams(vmem_limit_bytes=16 << 20),
                name="cross",
            )(plan, *arrived)

    return pl.pallas_call(
        functools.partial(stack_kernel, bins, rows, times, chunk, joined),
        in_specs=[smem] + [inside] * (2 + len(arrived)),
        out_specs=anywhere,
        out_shape=jax.ShapeDtypeStruct((slots, LAGS, share * block), jnp.float32),
        scratch_shapes=[
            pltpu.VMEM((slots, LAGS, share * block), jnp.float32),
            pltpu.VMEM((2, times, part_rows, block), jnp.bfloat16),
            pltpu.VMEM((block, part_rows), jnp.float32),
        ]
        + operands
        + [
            pltpu.VMEM((2, chunk // 2, depth, 2 * block), jnp.bfloat16),
            pltpu.SemaphoreType.DMA((slots, share // chunk)),
        ],
        compiler_params=pltpu.CompilerParams(vmem_limit_bytes=32 << 20),
        name="stack",
    )(plan, table, early, *arrived)


def solution(mesh):
    placed = (P("tm", "pair", None), P(), P("pair", None), P("pair"))
    return jax.shard_map(
        shards, mesh=mesh, in_specs=placed, out_specs=P("pair", None, "tm"), check_vma=False
    )
```

```python
import functools
import math

import jax
import jax.numpy as jnp
import numpy as np
from jax import lax
from jax.experimental import pallas as pl
from jax.experimental.pallas import tpu as pltpu
from jax.sharding import PartitionSpec as P

NT = 1024
NF = 128
LOW_BIN = 8
LAGS = 128


def forward_table():
    phase = (LOW_BIN + np.arange(NF))[:, None] * np.arange(NT)[None, :] % NT
    angle = phase * (2.0 * math.pi / NT)
    return np.concatenate([np.cos(angle), -np.sin(angle)], axis=0).astype(np.float32)


def inverse_table(segments, sent):
    (shifts,) = after([jnp.arange(LAGS, dtype=jnp.int32) - LAGS // 2], sent)
    column = jnp.arange(2 * NF, dtype=jnp.int32)
    half = NF // PIECES
    bin_id = LOW_BIN + column // (2 * half) * half + column % half
    phase = jnp.mod(shifts[:, None] * bin_id[None, :], NT)
    angle = phase.astype(jnp.float32) * (2.0 * math.pi / NT)
    scale = 1.0 / math.sqrt(segments * NF)
    value = jnp.where(column // half % 2 == 0, jnp.cos(angle), -jnp.sin(angle)) * scale
    return value.astype(jnp.bfloat16)


def halves(value):
    high = value.astype(jnp.bfloat16)
    return high, (value - high.astype(jnp.float32)).astype(jnp.bfloat16)


def nt_dot(a, b):
    return lax.dot_general(a, b, (((1,), (1,)), ((), ())), preferred_element_type=jnp.float32)


CHUNKS = 2
PIECES = 2


def whiten_kernel(bins, x_hbm, table_hbm, *refs):
    outs, (x_ref, table_ref, pad_ref, sems) = refs[:-4], refs[-4:]
    _, segments, block, wide = x_ref.shape
    columns = segments * block
    copies = []
    for k in range(CHUNKS):
        span = slice(k * wide, (k + 1) * wide)
        sources = (x_hbm.at[:, :, span], table_hbm.at[:, span])
        copies.append(
            [
                pltpu.make_async_copy(source, target.at[k], sems.at[k, n])
                for n, (source, target) in enumerate(zip(sources, (x_ref, table_ref)))
            ]
        )
        for copy in copies[-1]:
            copy.start()
    spectrum = None
    for k in range(CHUNKS):
        for copy in copies[k]:
            copy.wait()
        x = x_ref[k].reshape(columns, wide)
        x_high, x_low = halves(x)
        high, low = halves(table_ref[k])
        part = nt_dot(high, x_high) + nt_dot(high, x_low) + nt_dot(low, x_high)
        spectrum = part if spectrum is None else spectrum + part
    real_part = spectrum[:NF]
    imag_part = spectrum[NF:]
    power = real_part * real_part + imag_part * imag_part
    edge = jnp.zeros((8, columns), jnp.float32)
    pad_ref[0:8, :] = edge
    pad_ref[8 + NF : 16 + NF, :] = edge
    pad_ref[8 : 8 + NF, :] = power
    total = pad_ref[6 : 6 + NF, :]
    for offset in range(7, 11):
        total = total + pad_ref[offset : offset + NF, :]
    bin_id = lax.broadcasted_iota(jnp.int32, (NF, columns), 0)
    counted = (jnp.minimum(bin_id + 2, NF - 1) - jnp.maximum(bin_id - 2, 0) + 1).astype(jnp.float32)
    smooth = total / counted
    level = jnp.mean(power, axis=0, keepdims=True)
    factor = lax.rsqrt(smooth + 0.05 * level + 1e-06)
    parts = ((real_part * factor).astype(jnp.bfloat16), (imag_part * factor).astype(jnp.bfloat16))
    each = NF // bins // len(outs)
    for group in range(NF // bins):
        for segment in range(segments):
            for c in range(2):
                row = ((group % each * segments + segment) * 2 + c) * bins
                outs[group // each][row : row + bins, :] = parts[c][
                    group * bins : (group + 1) * bins, segment * block : (segment + 1) * block
                ]


def fetch(joined, plan_ref, at, wanted, sources, targets):
    index = plan_ref[wanted + at]
    for n, source in enumerate(sources):

        @pl.when(plan_ref[at] == n)
        def _():
            for step in range(joined):
                value = source[index + step]
                for target in targets[step]:
                    target[...] = value


def pick_kernel(count, plan_ref, *refs):
    sources, outs, (held, turned) = refs[:count], refs[count:-2], refs[-2:]
    slots, rows, block = held.shape
    times = len(outs)
    share = block // times
    time = plan_ref[4 * slots]
    for slot in range(slots):
        fetch(1, plan_ref, 2 * slot, 2 * slots, sources, [[held.at[slot]]])
        fetch(1, plan_ref, 2 * slot + 1, 2 * slots, sources, [[out.at[slot, :rows] for out in outs]])
    for slot in range(slots):
        flipped = held[slot].astype(jnp.float32).T.astype(jnp.bfloat16)
        for piece in range(rows // block):
            turned[slot, piece] = flipped[:, piece * block : (piece + 1) * block]
        for step, out in enumerate(outs):
            start = pl.multiple_of((time + step) % times * share, share)
            for piece in range(rows // block):
                low = rows + piece * share
                out[slot, low : low + share] = turned[slot, piece, pl.ds(start, share)]


def put_right(bins, block_ref, right_all, at, rows):
    block = block_ref.shape[1]
    for low in range(0, rows, 2 * bins):
        real_part = block_ref[low : low + bins, :]
        imag_part = block_ref[low + bins : low + 2 * bins, :]
        base = at(low)
        right_all[base : base + bins, :block] = real_part
        right_all[base : base + bins, block:] = imag_part
        right_all[base + bins : base + 2 * bins, :block] = imag_part
        right_all[base + bins : base + 2 * bins, block:] = -real_part


def put_pack(slot, rows, bins, step, times, pack, left_all, right_all):
    share = left_all.shape[0]
    block = share * times
    wide = times * rows
    part_rows = left_all.shape[1] // times
    at = functools.partial(column_of, rows, wide, step)
    put_right(bins, pack.at[slot], right_all, at, part_rows)
    for low in range(0, part_rows, block):
        first = part_rows + low // block * share
        value = pack[slot, first : first + share, :].astype(jnp.float32)
        for inner in range(0, block, rows):
            left_all[:, at(low + inner) : at(low + inner) + rows] = value[:, inner : inner + rows]


def column_of(rows, wide, step, low):
    return low // rows * wide + step * rows + low % rows


def cross_spectra(bins, wide, first, chunk, left_all, right_all, cross_ref):
    groups = left_all.shape[1] // wide
    block = right_all.shape[1] // 2
    half = groups * bins
    column = lax.broadcasted_iota(jnp.int32, (bins, wide), 1) % bins
    row = lax.broadcasted_iota(jnp.int32, (bins, wide), 0)
    keep = (column == row).astype(jnp.float32).astype(jnp.bfloat16)
    several = 16 if chunk % 16 == 0 else 2
    for group in range(groups):
        weights = right_all[group * wide : (group + 1) * wide, :]
        for start in range(0, chunk, several):
            pieces = []
            for i in range(several):
                line = left_all[pl.ds(first + start + i, 1), group * wide : (group + 1) * wide]
                tile = jnp.broadcast_to(line, (16, wide)).astype(jnp.bfloat16)
                pieces += [tile * keep[low : low + 16] for low in range(0, bins, 16)]
            product = jnp.dot(jnp.concatenate(pieces, axis=0), weights, preferred_element_type=jnp.float32)
            product = product.astype(jnp.bfloat16)
            for i in range(several):
                at = start + i
                lanes = slice(at % 2 * block, (at % 2 + 1) * block)
                piece = product[i * bins : (i + 1) * bins]
                cross_ref[at // 2, group * bins : (group + 1) * bins, lanes] = piece[:, :block]
                cross_ref[at // 2, half + group * bins : half + (group + 1) * bins, lanes] = piece[:, block:]


def cross_kernel(bins, rows, chunk, plan_ref, *refs):
    packs, (out_ref, left_all, right_all) = refs[:-3], refs[-3:]
    times = len(packs)

    def one_slot(slot, carry):
        for step, pack in enumerate(packs):
            put_pack(slot, rows, bins, step, times, pack, left_all, right_all)
        for n in range(left_all.shape[0] // chunk):
            into = out_ref.at[slot, n * chunk // 2 : (n + 1) * chunk // 2]
            cross_spectra(bins, times * rows, n * chunk, chunk, left_all, right_all, into)
        return carry

    slots = out_ref.shape[0]
    lax.fori_loop(0, jnp.minimum(plan_ref[4 * slots + 1], slots), one_slot, 0)


def stack_kernel(bins, rows, times, chunk, joined, plan_ref, table_ref, early_ref, *refs):
    sources, refs = refs[:-8], refs[-8:]
    out_ref, held, blocks, turned, left_all, right_all, cross_ref, sems = refs
    slots = held.shape[0]
    live = plan_ref[4 * slots + 1]
    share = left_all.shape[0]
    block = share * times
    wide = times * rows
    part_rows = left_all.shape[1] // times
    lanes = 2 * block
    parts = share // chunk
    width = chunk // 2 * lanes

    def leave(slot, n):
        span = slice(n * width, (n + 1) * width)
        return pltpu.make_async_copy(held.at[slot, :, span], out_ref.at[slot, :, span], sems.at[slot, n])

    def one_slot(slot, carry):
        if joined == 1:
            for step, pack in enumerate(sources):
                put_pack(slot, rows, bins, step, times, pack, left_all, right_all)
        else:
            for side in range(2):
                targets = [[blocks.at[side, step]] for step in range(joined)]
                fetch(joined, plan_ref, 2 * slot + side, 2 * slots, sources, targets)
            start = pl.multiple_of(plan_ref[4 * slots] * share, share)
            for step in range(times):
                at = functools.partial(column_of, rows, wide, step)
                put_right(bins, blocks.at[1, step], right_all, at, part_rows)
                turned[...] = blocks[0, step].astype(jnp.float32).T
                for low in range(0, part_rows, rows):
                    left_all[:, at(low) : at(low) + rows] = turned[pl.ds(start, share), low : low + rows]
        table = table_ref[...]
        for n in range(parts):
            cross_spectra(bins, wide, n * chunk, chunk, left_all, right_all, cross_ref.at[n % 2])
            for pair in range(chunk // 2):
                at = n * chunk // 2 + pair
                cross = jnp.concatenate([early_ref[slot, at], cross_ref[n % 2, pair]], axis=0)
                held[slot, :, at * lanes : (at + 1) * lanes] = jnp.dot(table, cross, preferred_element_type=jnp.float32)
            leave(slot, n).start()
        return carry

    for slot in range(slots):

        @pl.when(slot >= live)
        def _():
            held[slot] = jnp.zeros_like(held[slot])
            for n in range(parts):
                leave(slot, n).start()

    lax.fori_loop(0, jnp.minimum(live, slots), one_slot, 0)
    for slot in range(slots):
        for n in range(parts):
            leave(slot, n).wait()


def chip_dims(size):
    return {16: (4, 2, 2), 64: (16, 4, 1)}.get(size, (size, 1, 1))


def swap(value, dims, axis, by):
    moves = []
    for p in range(math.prod(dims)):
        place = list(np.unravel_index(p, dims))
        place[axis] ^= by
        moves.append((p, int(np.ravel_multi_index(place, dims))))
    return lax.ppermute(value, "pair", moves)


def is_paired(dims, times):
    return dims == (4, 2, 2) and times == 2 and PIECES == 2


def column_order(dims):
    depth, height, _ = dims
    order = [(0, 0)]
    for axis, size in ((0, depth), (1, height)):
        bit = size // 2
        while bit:
            order += [(z ^ bit, y) if axis == 0 else (z, y ^ bit) for z, y in order]
            bit //= 2
    return order


def plan_of(away, counts, dims, parts, joined):
    _, height, cores = dims
    source = jnp.zeros_like(away)
    index = jnp.zeros_like(away)
    spots = [(n, at) for n, part in enumerate(parts) for at in range(part)]
    for (z, y), (n, at) in zip(column_order(dims), spots):
        here = away // cores == z * height + y
        source = jnp.where(here, n * cores, source)
        index = jnp.where(here, at * joined, index)
    return jnp.concatenate([source + away % cores, index, lax.axis_index("tm")[None], counts]).astype(jnp.int32)


def after(values, others):
    return lax.optimization_barrier(tuple(values) + tuple(others))[: len(values)]


def join(held, more, others=()):
    (held,) = after([held], others)
    (room,) = after([jnp.concatenate([held, held])], ())
    return lax.dynamic_update_slice(room, more, (held.shape[0], 0, 0))


def swap_times(value, step, times):
    return lax.ppermute(value, "tm", [((t + step) % times, t) for t in range(times)])


def gather_one(held, dims):
    depth, height, _ = dims
    for axis, size in ((0, depth), (1, height)):
        bit = size // 2
        while bit:
            held = jnp.concatenate([held, swap(held, dims, axis, bit)])
            bit //= 2
    return [held]


def gather_two(first, second, dims):
    first_far = swap(first, dims, 0, 2)
    other = swap_times(second, 1, 2)
    pair = join(second, other)
    pair_far = swap(pair, dims, 0, 2)
    (first_two,) = after([join(first, first_far, [pair])], [pair])
    first_near = swap(first_two, dims, 0, 1)
    pair_two = jnp.concatenate([pair, pair_far])
    (first_near,) = after([first_near], [pair_two])
    first_four = jnp.concatenate([first_two, first_near])
    first_beside = swap(first_four, dims, 1, 1)
    pair_near = swap(pair_two, dims, 0, 1)
    pair_four = jnp.concatenate([pair_two, pair_near])
    pair_beside = swap(pair_four, dims, 1, 1)
    return [first_four, first_beside], [pair_four, pair_beside], first_two


def both_cores(arrays, dims):
    if dims[2] == 1:
        return arrays
    return [value for array in arrays for value in (array, swap(array, dims, 2, 1))]


def shards(traces, owner, tiles, counts):
    seg_count, block, _ = traces.shape
    times = lax.axis_size("tm")
    segments = seg_count * times
    share = block // times
    slots = tiles.shape[0]
    bins = max(16, 128 // segments)
    groups = NF // bins
    rows = seg_count * 2 * bins
    wide = rows * times
    total = groups * rows
    part_rows = total // PIECES
    dims = chip_dims(lax.axis_size("pair"))
    smem = pl.BlockSpec(memory_space=pltpu.SMEM)
    anywhere = pl.BlockSpec(memory_space=pl.ANY)
    white = pl.pallas_call(
        functools.partial(whiten_kernel, bins),
        in_specs=[anywhere] * 2,
        out_shape=[jax.ShapeDtypeStruct((part_rows, block), jnp.bfloat16)] * PIECES,
        scratch_shapes=[
            pltpu.VMEM((CHUNKS, seg_count, block, NT // CHUNKS), jnp.float32),
            pltpu.VMEM((CHUNKS, 2 * NF, NT // CHUNKS), jnp.float32),
            pltpu.VMEM((NF + 16, seg_count * block), jnp.float32),
            pltpu.SemaphoreType.DMA((CHUNKS, 2)),
        ],
        compiler_params=pltpu.CompilerParams(vmem_limit_bytes=63 << 20),
        name="whiten",
    )(traces, jnp.asarray(forward_table()))

    paired = is_paired(dims, times)
    blocks = [own[None] for own in white]
    if paired:
        *gathered, near = gather_two(*blocks, dims)
        tiles, counts = after([tiles, counts], [near])
    else:
        gathered = [gather_one(own, dims) for own in blocks]

    known = owner.shape[0]
    chosen = tiles.reshape(-1, 1) == jnp.arange(known, dtype=jnp.int32)
    stored = jnp.sum(jnp.where(chosen, owner, 0), axis=1)
    away = stored ^ lax.axis_index("pair")

    pack = part_rows + part_rows // block * share
    depth = 2 * NF // PIECES
    chunk = min(share, 16)
    inside = pl.BlockSpec(memory_space=pltpu.VMEM)
    operands = [
        pltpu.VMEM((share, groups // PIECES * wide), jnp.float32),
        pltpu.VMEM((groups // PIECES * wide, 2 * block), jnp.bfloat16),
    ]
    early = None
    for piece, arrays in enumerate(gathered):
        joined = times if paired and piece else 1
        plan = plan_of(away, counts, dims, [array.shape[0] // joined for array in arrays], joined)
        if joined > 1:
            arrays[-1:] = after(arrays[-1:], arrived[1:] + [table])
            arrived = both_cores(arrays, dims)
            continue
        sources = both_cores(arrays, dims)
        arrived = list(pl.pallas_call(
            functools.partial(pick_kernel, len(sources)),
            in_specs=[smem] + [inside] * len(sources),
            out_shape=[jax.ShapeDtypeStruct((slots, pack, block), jnp.bfloat16)] * times,
            scratch_shapes=[
                pltpu.VMEM((slots, part_rows, block), jnp.bfloat16),
                pltpu.VMEM((slots, part_rows // block, block, block), jnp.bfloat16),
            ],
            compiler_params=pltpu.CompilerParams(vmem_limit_bytes=8 << 20),
            cost_estimate=pl.CostEstimate(flops=1, bytes_accessed=1, transcendentals=0),
            name="pick",
        )(plan, *sources))
        if not piece:
            table = inverse_table(segments, arrived[1:])
        for step in range(1, times):
            moves = [(t, (t + step) % times) for t in range(times)]
            arrived[step] = lax.ppermute(arrived[step], "tm", moves)
        if not piece:
            early = pl.pallas_call(
                functools.partial(cross_kernel, bins, rows, chunk),
                in_specs=[smem] + [inside] * times,
                out_shape=jax.ShapeDtypeStruct((slots, share // 2, depth, 2 * block), jnp.bfloat16),
                scratch_shapes=operands,
                compiler_params=pltpu.CompilerParams(vmem_limit_bytes=16 << 20),
                name="cross",
            )(plan, *arrived)

    return pl.pallas_call(
        functools.partial(stack_kernel, bins, rows, times, chunk, joined),
        in_specs=[smem] + [inside] * (2 + len(arrived)),
        out_specs=anywhere,
        out_shape=jax.ShapeDtypeStruct((slots, LAGS, share * block), jnp.float32),
        scratch_shapes=[
            pltpu.VMEM((slots, LAGS, share * block), jnp.float32),
            pltpu.VMEM((2, times, part_rows, block), jnp.bfloat16),
            pltpu.VMEM((block, part_rows), jnp.float32),
        ]
        + operands
        + [
            pltpu.VMEM((2, chunk // 2, depth, 2 * block), jnp.bfloat16),
            pltpu.SemaphoreType.DMA((slots, share // chunk)),
        ],
        compiler_params=pltpu.CompilerParams(vmem_limit_bytes=32 << 20),
        name="stack",
    )(plan, table, early, *arrived)


def solution(mesh):
    placed = (P("tm", "pair", None), P(), P("pair", None), P("pair"))
    return jax.shard_map(
        shards, mesh=mesh, in_specs=placed, out_specs=P("pair", None, "tm"), check_vma=False
    )
```

```python
import functools
import math

import jax
import jax.numpy as jnp
import numpy as np
from jax import lax
from jax.experimental import pallas as pl
from jax.experimental.pallas import tpu as pltpu
from jax.sharding import PartitionSpec as P

NT = 1024
NF = 128
LOW_BIN = 8
LAGS = 128


def forward_table():
    phase = (LOW_BIN + np.arange(NF))[:, None] * np.arange(NT)[None, :] % NT
    angle = phase * (2.0 * math.pi / NT)
    return np.concatenate([np.cos(angle), -np.sin(angle)], axis=0).astype(np.float32)


def inverse_table(segments, sent):
    (shifts,) = after([jnp.arange(LAGS, dtype=jnp.int32) - LAGS // 2], sent)
    column = jnp.arange(2 * NF, dtype=jnp.int32)
    half = NF // PIECES
    bin_id = LOW_BIN + column // (2 * half) * half + column % half
    phase = jnp.mod(shifts[:, None] * bin_id[None, :], NT)
    angle = phase.astype(jnp.float32) * (2.0 * math.pi / NT)
    scale = 1.0 / math.sqrt(segments * NF)
    value = jnp.where(column // half % 2 == 0, jnp.cos(angle), -jnp.sin(angle)) * scale
    return value.astype(jnp.bfloat16)


def halves(value):
    high = value.astype(jnp.bfloat16)
    return high, (value - high.astype(jnp.float32)).astype(jnp.bfloat16)


def nt_dot(a, b):
    return lax.dot_general(a, b, (((1,), (1,)), ((), ())), preferred_element_type=jnp.float32)


CHUNKS = 2
PIECES = 2


def whiten_kernel(bins, x_hbm, table_hbm, *refs):
    outs, (x_ref, table_ref, pad_ref, sems) = refs[:-4], refs[-4:]
    _, segments, block, wide = x_ref.shape
    columns = segments * block
    copies = []
    for k in range(CHUNKS):
        span = slice(k * wide, (k + 1) * wide)
        sources = (x_hbm.at[:, :, span], table_hbm.at[:, span])
        copies.append(
            [
                pltpu.make_async_copy(source, target.at[k], sems.at[k, n])
                for n, (source, target) in enumerate(zip(sources, (x_ref, table_ref)))
            ]
        )
        for copy in copies[-1]:
            copy.start()
    spectrum = None
    for k in range(CHUNKS):
        for copy in copies[k]:
            copy.wait()
        x = x_ref[k].reshape(columns, wide)
        x_high, x_low = halves(x)
        high, low = halves(table_ref[k])
        part = nt_dot(high, x_high) + nt_dot(high, x_low) + nt_dot(low, x_high)
        spectrum = part if spectrum is None else spectrum + part
    real_part = spectrum[:NF]
    imag_part = spectrum[NF:]
    power = real_part * real_part + imag_part * imag_part
    edge = jnp.zeros((8, columns), jnp.float32)
    pad_ref[0:8, :] = edge
    pad_ref[8 + NF : 16 + NF, :] = edge
    pad_ref[8 : 8 + NF, :] = power
    total = pad_ref[6 : 6 + NF, :]
    for offset in range(7, 11):
        total = total + pad_ref[offset : offset + NF, :]
    bin_id = lax.broadcasted_iota(jnp.int32, (NF, columns), 0)
    counted = (jnp.minimum(bin_id + 2, NF - 1) - jnp.maximum(bin_id - 2, 0) + 1).astype(jnp.float32)
    smooth = total / counted
    level = jnp.mean(power, axis=0, keepdims=True)
    factor = lax.rsqrt(smooth + 0.05 * level + 1e-06)
    parts = ((real_part * factor).astype(jnp.bfloat16), (imag_part * factor).astype(jnp.bfloat16))
    each = NF // bins // len(outs)
    for group in range(NF // bins):
        for segment in range(segments):
            for c in range(2):
                row = ((group % each * segments + segment) * 2 + c) * bins
                outs[group // each][row : row + bins, :] = parts[c][
                    group * bins : (group + 1) * bins, segment * block : (segment + 1) * block
                ]


def fetch(joined, plan_ref, at, wanted, sources, targets):
    index = plan_ref[wanted + at]
    for n, source in enumerate(sources):

        @pl.when(plan_ref[at] == n)
        def _():
            for step in range(joined):
                value = source[index + step]
                for target in targets[step]:
                    target[...] = value


def pick_kernel(count, plan_ref, *refs):
    sources, outs, (held, turned) = refs[:count], refs[count:-2], refs[-2:]
    slots, rows, block = held.shape
    times = len(outs)
    share = block // times
    time = plan_ref[4 * slots]
    for slot in range(slots):
        fetch(1, plan_ref, 2 * slot, 2 * slots, sources, [[held.at[slot]]])
        fetch(1, plan_ref, 2 * slot + 1, 2 * slots, sources, [[out.at[slot, :rows] for out in outs]])
    for slot in range(slots):
        flipped = held[slot].astype(jnp.float32).T.astype(jnp.bfloat16)
        for piece in range(rows // block):
            turned[slot, piece] = flipped[:, piece * block : (piece + 1) * block]
        for step, out in enumerate(outs):
            start = pl.multiple_of((time + step) % times * share, share)
            for piece in range(rows // block):
                low = rows + piece * share
                out[slot, low : low + share] = turned[slot, piece, pl.ds(start, share)]


def put_right(bins, block_ref, right_all, at, rows):
    block = block_ref.shape[1]
    for low in range(0, rows, 2 * bins):
        real_part = block_ref[low : low + bins, :]
        imag_part = block_ref[low + bins : low + 2 * bins, :]
        base = at(low)
        right_all[base : base + bins, :block] = real_part
        right_all[base : base + bins, block:] = imag_part
        right_all[base + bins : base + 2 * bins, :block] = imag_part
        right_all[base + bins : base + 2 * bins, block:] = -real_part


def put_pack(slot, rows, bins, step, times, pack, left_all, right_all):
    share = left_all.shape[0]
    block = share * times
    wide = times * rows
    part_rows = left_all.shape[1] // times
    at = functools.partial(column_of, rows, wide, step)
    put_right(bins, pack.at[slot], right_all, at, part_rows)
    for low in range(0, part_rows, block):
        first = part_rows + low // block * share
        value = pack[slot, first : first + share, :].astype(jnp.float32)
        for inner in range(0, block, rows):
            left_all[:, at(low + inner) : at(low + inner) + rows] = value[:, inner : inner + rows]


def column_of(rows, wide, step, low):
    return low // rows * wide + step * rows + low % rows


def cross_spectra(bins, wide, first, chunk, left_all, right_all, cross_ref):
    groups = left_all.shape[1] // wide
    block = right_all.shape[1] // 2
    half = groups * bins
    column = lax.broadcasted_iota(jnp.int32, (bins, wide), 1) % bins
    row = lax.broadcasted_iota(jnp.int32, (bins, wide), 0)
    keep = (column == row).astype(jnp.float32).astype(jnp.bfloat16)
    several = 16 if chunk % 16 == 0 else 2
    for group in range(groups):
        weights = right_all[group * wide : (group + 1) * wide, :]
        for start in range(0, chunk, several):
            pieces = []
            for i in range(several):
                line = left_all[pl.ds(first + start + i, 1), group * wide : (group + 1) * wide]
                tile = jnp.broadcast_to(line, (16, wide)).astype(jnp.bfloat16)
                pieces += [tile * keep[low : low + 16] for low in range(0, bins, 16)]
            product = jnp.dot(jnp.concatenate(pieces, axis=0), weights, preferred_element_type=jnp.float32)
            product = product.astype(jnp.bfloat16)
            for i in range(several):
                at = start + i
                lanes = slice(at % 2 * block, (at % 2 + 1) * block)
                piece = product[i * bins : (i + 1) * bins]
                cross_ref[at // 2, group * bins : (group + 1) * bins, lanes] = piece[:, :block]
                cross_ref[at // 2, half + group * bins : half + (group + 1) * bins, lanes] = piece[:, block:]


def cross_kernel(bins, rows, chunk, plan_ref, *refs):
    packs, (out_ref, left_all, right_all) = refs[:-3], refs[-3:]
    times = len(packs)

    def one_slot(slot, carry):
        for step, pack in enumerate(packs):
            put_pack(slot, rows, bins, step, times, pack, left_all, right_all)
        for n in range(left_all.shape[0] // chunk):
            into = out_ref.at[slot, n * chunk // 2 : (n + 1) * chunk // 2]
            cross_spectra(bins, times * rows, n * chunk, chunk, left_all, right_all, into)
        return carry

    slots = out_ref.shape[0]
    lax.fori_loop(0, jnp.minimum(plan_ref[4 * slots + 1], slots), one_slot, 0)


def stack_kernel(bins, rows, times, chunk, joined, plan_ref, table_ref, early_ref, *refs):
    sources, refs = refs[:-8], refs[-8:]
    out_ref, held, blocks, turned, left_all, right_all, cross_ref, sems = refs
    slots = held.shape[0]
    live = plan_ref[4 * slots + 1]
    share = left_all.shape[0]
    block = share * times
    wide = times * rows
    part_rows = left_all.shape[1] // times
    lanes = 2 * block
    parts = share // chunk
    width = chunk // 2 * lanes

    def leave(slot, n):
        span = slice(n * width, (n + 1) * width)
        return pltpu.make_async_copy(held.at[slot, :, span], out_ref.at[slot, :, span], sems.at[slot, n])

    def one_slot(slot, carry):
        if joined == 1:
            for step, pack in enumerate(sources):
                put_pack(slot, rows, bins, step, times, pack, left_all, right_all)
        else:
            for side in range(2):
                targets = [[blocks.at[side, step]] for step in range(joined)]
                fetch(joined, plan_ref, 2 * slot + side, 2 * slots, sources, targets)
            start = pl.multiple_of(plan_ref[4 * slots] * share, share)
            for step in range(times):
                at = functools.partial(column_of, rows, wide, step)
                put_right(bins, blocks.at[1, step], right_all, at, part_rows)
                turned[...] = blocks[0, step].astype(jnp.float32).T
                for low in range(0, part_rows, rows):
                    left_all[:, at(low) : at(low) + rows] = turned[pl.ds(start, share), low : low + rows]
        table = table_ref[...]
        for n in range(parts):
            cross_spectra(bins, wide, n * chunk, chunk, left_all, right_all, cross_ref.at[n % 2])
            for pair in range(chunk // 2):
                at = n * chunk // 2 + pair
                cross = jnp.concatenate([early_ref[slot, at], cross_ref[n % 2, pair]], axis=0)
                held[slot, :, at * lanes : (at + 1) * lanes] = jnp.dot(table, cross, preferred_element_type=jnp.float32)
            leave(slot, n).start()
        return carry

    for slot in range(slots):

        @pl.when(slot >= live)
        def _():
            held[slot] = jnp.zeros_like(held[slot])
            for n in range(parts):
                leave(slot, n).start()

    lax.fori_loop(0, jnp.minimum(live, slots), one_slot, 0)
    for slot in range(slots):
        for n in range(parts):
            leave(slot, n).wait()


def chip_dims(size):
    return {16: (4, 2, 2), 64: (16, 4, 1)}.get(size, (size, 1, 1))


def swap(value, dims, axis, by):
    moves = []
    for p in range(math.prod(dims)):
        place = list(np.unravel_index(p, dims))
        place[axis] ^= by
        moves.append((p, int(np.ravel_multi_index(place, dims))))
    return lax.ppermute(value, "pair", moves)


def is_paired(dims, times):
    return dims == (4, 2, 2) and times == 2 and PIECES == 2


def column_order(dims):
    depth, height, _ = dims
    order = [(0, 0)]
    for axis, size in ((0, depth), (1, height)):
        bit = size // 2
        while bit:
            order += [(z ^ bit, y) if axis == 0 else (z, y ^ bit) for z, y in order]
            bit //= 2
    return order


def plan_of(away, counts, dims, parts, joined):
    _, height, cores = dims
    source = jnp.zeros_like(away)
    index = jnp.zeros_like(away)
    spots = [(n, at) for n, part in enumerate(parts) for at in range(part)]
    for (z, y), (n, at) in zip(column_order(dims), spots):
        here = away // cores == z * height + y
        source = jnp.where(here, n * cores, source)
        index = jnp.where(here, at * joined, index)
    return jnp.concatenate([source + away % cores, index, lax.axis_index("tm")[None], counts]).astype(jnp.int32)


def after(values, others):
    return lax.optimization_barrier(tuple(values) + tuple(others))[: len(values)]


def join(held, more, others=()):
    (held,) = after([held], others)
    (room,) = after([jnp.concatenate([held, held])], ())
    return lax.dynamic_update_slice(room, more, (held.shape[0], 0, 0))


def swap_times(value, step, times):
    return lax.ppermute(value, "tm", [((t + step) % times, t) for t in range(times)])


def gather_one(held, dims):
    depth, height, _ = dims
    for axis, size in ((0, depth), (1, height)):
        bit = size // 2
        while bit:
            held = jnp.concatenate([held, swap(held, dims, axis, bit)])
            bit //= 2
    return [held]


def gather_two(first, second, dims):
    first_far = swap(first, dims, 0, 2)
    (room,) = after([jnp.concatenate([first, first])], ())
    (second,) = after([second], [room])
    other = swap_times(second, 1, 2)
    first_two = lax.dynamic_update_slice(room, first_far, (1, 0, 0))
    first_near = swap(first_two, dims, 0, 1)
    (pair,) = after([join(second, other)], [first_two])
    pair_beside = swap(pair, dims, 1, 1)
    pair_far = swap(pair, dims, 0, 2)
    first_four = jnp.concatenate([first_two, first_near])
    first_beside = swap(first_four, dims, 1, 1)
    first_core = swap(after([first_four], [pair_beside])[0], dims, 2, 1)
    pair_two = join(pair, pair_far, [first_four])
    pair_near = swap(pair_two, dims, 0, 1)
    pair_four = jnp.concatenate([pair_two, pair_near])
    pair_rest = swap(pair_four[2:], dims, 1, 1)
    return [first_four, first_beside], [pair_four, pair_beside, pair_rest], first_two, first_core


def both_cores(arrays, dims):
    if dims[2] == 1:
        return arrays
    return [value for array in arrays for value in (array, swap(array, dims, 2, 1))]


def shards(traces, owner, tiles, counts):
    seg_count, block, _ = traces.shape
    times = lax.axis_size("tm")
    segments = seg_count * times
    share = block // times
    slots = tiles.shape[0]
    bins = max(16, 128 // segments)
    groups = NF // bins
    rows = seg_count * 2 * bins
    wide = rows * times
    total = groups * rows
    part_rows = total // PIECES
    dims = chip_dims(lax.axis_size("pair"))
    smem = pl.BlockSpec(memory_space=pltpu.SMEM)
    anywhere = pl.BlockSpec(memory_space=pl.ANY)
    white = pl.pallas_call(
        functools.partial(whiten_kernel, bins),
        in_specs=[anywhere] * 2,
        out_shape=[jax.ShapeDtypeStruct((part_rows, block), jnp.bfloat16)] * PIECES,
        scratch_shapes=[
            pltpu.VMEM((CHUNKS, seg_count, block, NT // CHUNKS), jnp.float32),
            pltpu.VMEM((CHUNKS, 2 * NF, NT // CHUNKS), jnp.float32),
            pltpu.VMEM((NF + 16, seg_count * block), jnp.float32),
            pltpu.SemaphoreType.DMA((CHUNKS, 2)),
        ],
        compiler_params=pltpu.CompilerParams(vmem_limit_bytes=63 << 20),
        name="whiten",
    )(traces, jnp.asarray(forward_table()))

    paired = is_paired(dims, times)
    blocks = [own[None] for own in white]
    if paired:
        *gathered, near, swapped = gather_two(*blocks, dims)
        tiles, counts = after([tiles, counts], [near])
    else:
        gathered = [gather_one(own, dims) for own in blocks]

    known = owner.shape[0]
    chosen = tiles.reshape(-1, 1) == jnp.arange(known, dtype=jnp.int32)
    stored = jnp.sum(jnp.where(chosen, owner, 0), axis=1)
    away = stored ^ lax.axis_index("pair")

    pack = part_rows + part_rows // block * share
    depth = 2 * NF // PIECES
    chunk = min(share, 16)
    inside = pl.BlockSpec(memory_space=pltpu.VMEM)
    operands = [
        pltpu.VMEM((share, groups // PIECES * wide), jnp.float32),
        pltpu.VMEM((groups // PIECES * wide, 2 * block), jnp.bfloat16),
    ]
    early = None
    for piece, arrays in enumerate(gathered):
        joined = times if paired and piece else 1
        plan = plan_of(away, counts, dims, [array.shape[0] // joined for array in arrays], joined)
        if joined > 1:
            arrays[-1:] = after(arrays[-1:], arrived[1:] + [table])
            arrived = both_cores(arrays, dims)
            continue
        sources = both_cores(arrays, dims)
        if paired:
            sources[1] = swapped
        arrived = list(pl.pallas_call(
            functools.partial(pick_kernel, len(sources)),
            in_specs=[smem] + [inside] * len(sources),
            out_shape=[jax.ShapeDtypeStruct((slots, pack, block), jnp.bfloat16)] * times,
            scratch_shapes=[
                pltpu.VMEM((slots, part_rows, block), jnp.bfloat16),
                pltpu.VMEM((slots, part_rows // block, block, block), jnp.bfloat16),
            ],
            compiler_params=pltpu.CompilerParams(vmem_limit_bytes=8 << 20),
            cost_estimate=pl.CostEstimate(flops=1, bytes_accessed=1, transcendentals=0),
            name="pick",
        )(plan, *sources))
        if not piece:
            table = inverse_table(segments, arrived[1:])
        for step in range(1, times):
            moves = [(t, (t + step) % times) for t in range(times)]
            arrived[step] = lax.ppermute(arrived[step], "tm", moves)
        if not piece:
            early = pl.pallas_call(
                functools.partial(cross_kernel, bins, rows, chunk),
                in_specs=[smem] + [inside] * times,
                out_shape=jax.ShapeDtypeStruct((slots, share // 2, depth, 2 * block), jnp.bfloat16),
                scratch_shapes=operands,
                compiler_params=pltpu.CompilerParams(vmem_limit_bytes=16 << 20),
                name="cross",
            )(plan, *arrived)

    return pl.pallas_call(
        functools.partial(stack_kernel, bins, rows, times, chunk, joined),
        in_specs=[smem] + [inside] * (2 + len(arrived)),
        out_specs=anywhere,
        out_shape=jax.ShapeDtypeStruct((slots, LAGS, share * block), jnp.float32),
        scratch_shapes=[
            pltpu.VMEM((slots, LAGS, share * block), jnp.float32),
            pltpu.VMEM((2, times, part_rows, block), jnp.bfloat16),
            pltpu.VMEM((block, part_rows), jnp.float32),
        ]
        + operands
        + [
            pltpu.VMEM((2, chunk // 2, depth, 2 * block), jnp.bfloat16),
            pltpu.SemaphoreType.DMA((slots, share // chunk)),
        ],
        compiler_params=pltpu.CompilerParams(vmem_limit_bytes=32 << 20),
        name="stack",
    )(plan, table, early, *arrived)


def solution(mesh):
    placed = (P("tm", "pair", None), P(), P("pair", None), P("pair"))
    return jax.shard_map(
        shards, mesh=mesh, in_specs=placed, out_specs=P("pair", None, "tm"), check_vma=False
    )
```

```python
import functools
import math

import jax
import jax.numpy as jnp
import numpy as np
from jax import lax
from jax.experimental import pallas as pl
from jax.experimental.pallas import tpu as pltpu
from jax.sharding import PartitionSpec as P

NT = 1024
NF = 128
LOW_BIN = 8
LAGS = 128


def forward_table():
    phase = (LOW_BIN + np.arange(NF))[:, None] * np.arange(NT)[None, :] % NT
    angle = phase * (2.0 * math.pi / NT)
    return np.concatenate([np.cos(angle), -np.sin(angle)], axis=0).astype(np.float32)


def inverse_table(segments, sent):
    (shifts,) = after([jnp.arange(LAGS, dtype=jnp.int32) - LAGS // 2], sent)
    column = jnp.arange(2 * NF, dtype=jnp.int32)
    half = NF // PIECES
    bin_id = LOW_BIN + column // (2 * half) * half + column % half
    phase = jnp.mod(shifts[:, None] * bin_id[None, :], NT)
    angle = phase.astype(jnp.float32) * (2.0 * math.pi / NT)
    scale = 1.0 / math.sqrt(segments * NF)
    value = jnp.where(column // half % 2 == 0, jnp.cos(angle), -jnp.sin(angle)) * scale
    return value.astype(jnp.bfloat16)


def halves(value):
    high = value.astype(jnp.bfloat16)
    return high, (value - high.astype(jnp.float32)).astype(jnp.bfloat16)


def nt_dot(a, b):
    return lax.dot_general(a, b, (((1,), (1,)), ((), ())), preferred_element_type=jnp.float32)


CHUNKS = 4
PIECES = 2


def whiten_kernel(bins, x_hbm, table_hbm, *refs):
    outs, (x_ref, table_ref, pad_ref, sems) = refs[:-4], refs[-4:]
    _, segments, block, wide = x_ref.shape
    columns = segments * block
    copies = []
    for k in range(CHUNKS):
        span = slice(k * wide, (k + 1) * wide)
        sources = (x_hbm.at[:, :, span], table_hbm.at[:, span])
        copies.append(
            [
                pltpu.make_async_copy(source, target.at[k], sems.at[k, n])
                for n, (source, target) in enumerate(zip(sources, (x_ref, table_ref)))
            ]
        )
        for copy in copies[-1]:
            copy.start()
    spectrum = None
    for k in range(CHUNKS):
        for copy in copies[k]:
            copy.wait()
        x = x_ref[k].reshape(columns, wide)
        x_high, x_low = halves(x)
        high, low = halves(table_ref[k])
        part = nt_dot(high, x_high) + nt_dot(high, x_low) + nt_dot(low, x_high)
        spectrum = part if spectrum is None else spectrum + part
    real_part = spectrum[:NF]
    imag_part = spectrum[NF:]
    power = real_part * real_part + imag_part * imag_part
    edge = jnp.zeros((8, columns), jnp.float32)
    pad_ref[0:8, :] = edge
    pad_ref[8 + NF : 16 + NF, :] = edge
    pad_ref[8 : 8 + NF, :] = power
    total = pad_ref[6 : 6 + NF, :]
    for offset in range(7, 11):
        total = total + pad_ref[offset : offset + NF, :]
    bin_id = lax.broadcasted_iota(jnp.int32, (NF, columns), 0)
    counted = (jnp.minimum(bin_id + 2, NF - 1) - jnp.maximum(bin_id - 2, 0) + 1).astype(jnp.float32)
    smooth = total / counted
    level = jnp.mean(power, axis=0, keepdims=True)
    factor = lax.rsqrt(smooth + 0.05 * level + 1e-06)
    parts = ((real_part * factor).astype(jnp.bfloat16), (imag_part * factor).astype(jnp.bfloat16))
    each = NF // bins // len(outs)
    for group in range(NF // bins):
        for segment in range(segments):
            for c in range(2):
                row = ((group % each * segments + segment) * 2 + c) * bins
                outs[group // each][row : row + bins, :] = parts[c][
                    group * bins : (group + 1) * bins, segment * block : (segment + 1) * block
                ]


def fetch(joined, plan_ref, at, wanted, sources, targets):
    index = plan_ref[wanted + at]
    for n, source in enumerate(sources):

        @pl.when(plan_ref[at] == n)
        def _():
            for step in range(joined):
                value = source[index + step]
                for target in targets[step]:
                    target[...] = value


def pick_kernel(count, plan_ref, *refs):
    sources, outs, (held, turned) = refs[:count], refs[count:-2], refs[-2:]
    slots, rows, block = held.shape
    times = len(outs)
    share = block // times
    time = plan_ref[4 * slots]
    for slot in range(slots):
        fetch(1, plan_ref, 2 * slot, 2 * slots, sources, [[held.at[slot]]])
        fetch(1, plan_ref, 2 * slot + 1, 2 * slots, sources, [[out.at[slot, :rows] for out in outs]])
    for slot in range(slots):
        flipped = held[slot].astype(jnp.float32).T.astype(jnp.bfloat16)
        for piece in range(rows // block):
            turned[slot, piece] = flipped[:, piece * block : (piece + 1) * block]
        for step, out in enumerate(outs):
            start = pl.multiple_of((time + step) % times * share, share)
            for piece in range(rows // block):
                low = rows + piece * share
                out[slot, low : low + share] = turned[slot, piece, pl.ds(start, share)]


def put_right(bins, block_ref, right_all, at, rows):
    block = block_ref.shape[1]
    for low in range(0, rows, 2 * bins):
        real_part = block_ref[low : low + bins, :]
        imag_part = block_ref[low + bins : low + 2 * bins, :]
        base = at(low)
        right_all[base : base + bins, :block] = real_part
        right_all[base : base + bins, block:] = imag_part
        right_all[base + bins : base + 2 * bins, :block] = imag_part
        right_all[base + bins : base + 2 * bins, block:] = -real_part


def put_pack(slot, rows, bins, step, times, pack, left_all, right_all):
    share = left_all.shape[0]
    block = share * times
    wide = times * rows
    part_rows = left_all.shape[1] // times
    at = functools.partial(column_of, rows, wide, step)
    put_right(bins, pack.at[slot], right_all, at, part_rows)
    for low in range(0, part_rows, block):
        first = part_rows + low // block * share
        value = pack[slot, first : first + share, :].astype(jnp.float32)
        for inner in range(0, block, rows):
            left_all[:, at(low + inner) : at(low + inner) + rows] = value[:, inner : inner + rows]


def column_of(rows, wide, step, low):
    return low // rows * wide + step * rows + low % rows


def cross_spectra(bins, wide, first, chunk, left_all, right_all, cross_ref):
    groups = left_all.shape[1] // wide
    block = right_all.shape[1] // 2
    half = groups * bins
    column = lax.broadcasted_iota(jnp.int32, (bins, wide), 1) % bins
    row = lax.broadcasted_iota(jnp.int32, (bins, wide), 0)
    keep = (column == row).astype(jnp.float32).astype(jnp.bfloat16)
    several = 16 if chunk % 16 == 0 else 2
    for group in range(groups):
        weights = right_all[group * wide : (group + 1) * wide, :]
        for start in range(0, chunk, several):
            pieces = []
            for i in range(several):
                line = left_all[pl.ds(first + start + i, 1), group * wide : (group + 1) * wide]
                tile = jnp.broadcast_to(line, (16, wide)).astype(jnp.bfloat16)
                pieces += [tile * keep[low : low + 16] for low in range(0, bins, 16)]
            product = jnp.dot(jnp.concatenate(pieces, axis=0), weights, preferred_element_type=jnp.float32)
            product = product.astype(jnp.bfloat16)
            for i in range(several):
                at = start + i
                lanes = slice(at % 2 * block, (at % 2 + 1) * block)
                piece = product[i * bins : (i + 1) * bins]
                cross_ref[at // 2, group * bins : (group + 1) * bins, lanes] = piece[:, :block]
                cross_ref[at // 2, half + group * bins : half + (group + 1) * bins, lanes] = piece[:, block:]


def cross_kernel(bins, rows, chunk, plan_ref, *refs):
    packs, (out_ref, left_all, right_all) = refs[:-3], refs[-3:]
    times = len(packs)

    def one_slot(slot, carry):
        for step, pack in enumerate(packs):
            put_pack(slot, rows, bins, step, times, pack, left_all, right_all)
        for n in range(left_all.shape[0] // chunk):
            into = out_ref.at[slot, n * chunk // 2 : (n + 1) * chunk // 2]
            cross_spectra(bins, times * rows, n * chunk, chunk, left_all, right_all, into)
        return carry

    slots = out_ref.shape[0]
    lax.fori_loop(0, jnp.minimum(plan_ref[4 * slots + 1], slots), one_slot, 0)


def stack_kernel(bins, rows, times, chunk, joined, plan_ref, table_ref, early_ref, *refs):
    sources, refs = refs[:-8], refs[-8:]
    out_ref, held, blocks, turned, left_all, right_all, cross_ref, sems = refs
    slots = held.shape[0]
    live = plan_ref[4 * slots + 1]
    share = left_all.shape[0]
    block = share * times
    wide = times * rows
    part_rows = left_all.shape[1] // times
    lanes = 2 * block
    parts = share // chunk
    width = chunk // 2 * lanes

    def leave(slot, n):
        span = slice(n * width, (n + 1) * width)
        return pltpu.make_async_copy(held.at[slot, :, span], out_ref.at[slot, :, span], sems.at[slot, n])

    def one_slot(slot, carry):
        if joined == 1:
            for step, pack in enumerate(sources):
                put_pack(slot, rows, bins, step, times, pack, left_all, right_all)
        else:
            for side in range(2):
                targets = [[blocks.at[side, step]] for step in range(joined)]
                fetch(joined, plan_ref, 2 * slot + side, 2 * slots, sources, targets)
            start = pl.multiple_of(plan_ref[4 * slots] * share, share)
            for step in range(times):
                at = functools.partial(column_of, rows, wide, step)
                put_right(bins, blocks.at[1, step], right_all, at, part_rows)
                turned[...] = blocks[0, step].astype(jnp.float32).T
                for low in range(0, part_rows, rows):
                    left_all[:, at(low) : at(low) + rows] = turned[pl.ds(start, share), low : low + rows]
        table = table_ref[...]
        for n in range(parts):
            cross_spectra(bins, wide, n * chunk, chunk, left_all, right_all, cross_ref.at[n % 2])
            for pair in range(chunk // 2):
                at = n * chunk // 2 + pair
                cross = jnp.concatenate([early_ref[slot, at], cross_ref[n % 2, pair]], axis=0)
                held[slot, :, at * lanes : (at + 1) * lanes] = jnp.dot(table, cross, preferred_element_type=jnp.float32)
            leave(slot, n).start()
        return carry

    for slot in range(slots):

        @pl.when(slot >= live)
        def _():
            held[slot] = jnp.zeros_like(held[slot])
            for n in range(parts):
                leave(slot, n).start()

    lax.fori_loop(0, jnp.minimum(live, slots), one_slot, 0)
    for slot in range(slots):
        for n in range(parts):
            leave(slot, n).wait()


def chip_dims(size):
    return {16: (4, 2, 2), 64: (16, 4, 1)}.get(size, (size, 1, 1))


def swap(value, dims, axis, by):
    moves = []
    for p in range(math.prod(dims)):
        place = list(np.unravel_index(p, dims))
        place[axis] ^= by
        moves.append((p, int(np.ravel_multi_index(place, dims))))
    return lax.ppermute(value, "pair", moves)


def is_paired(dims, times):
    return dims == (4, 2, 2) and times == 2 and PIECES == 2


def column_order(dims):
    depth, height, _ = dims
    order = [(0, 0)]
    for axis, size in ((0, depth), (1, height)):
        bit = size // 2
        while bit:
            order += [(z ^ bit, y) if axis == 0 else (z, y ^ bit) for z, y in order]
            bit //= 2
    return order


def plan_of(away, counts, dims, parts, joined):
    _, height, cores = dims
    source = jnp.zeros_like(away)
    index = jnp.zeros_like(away)
    spots = [(n, at) for n, part in enumerate(parts) for at in range(part)]
    for (z, y), (n, at) in zip(column_order(dims), spots):
        here = away // cores == z * height + y
        source = jnp.where(here, n * cores, source)
        index = jnp.where(here, at * joined, index)
    return jnp.concatenate([source + away % cores, index, lax.axis_index("tm")[None], counts]).astype(jnp.int32)


def after(values, others):
    return lax.optimization_barrier(tuple(values) + tuple(others))[: len(values)]


def join(held, more, others=()):
    (held,) = after([held], others)
    (room,) = after([jnp.concatenate([held, held])], ())
    return lax.dynamic_update_slice(room, more, (held.shape[0], 0, 0))


def swap_times(value, step, times):
    return lax.ppermute(value, "tm", [((t + step) % times, t) for t in range(times)])


def gather_one(held, dims):
    depth, height, _ = dims
    for axis, size in ((0, depth), (1, height)):
        bit = size // 2
        while bit:
            held = jnp.concatenate([held, swap(held, dims, axis, bit)])
            bit //= 2
    return [held]


def gather_two(first, second, dims):
    first_far = swap(first, dims, 0, 2)
    (room,) = after([jnp.concatenate([first, first])], ())
    (second,) = after([second], [room])
    other = swap_times(second, 1, 2)
    first_two = lax.dynamic_update_slice(room, first_far, (1, 0, 0))
    first_near = swap(first_two, dims, 0, 1)
    (pair,) = after([join(second, other)], [first_two])
    pair_beside = swap(pair, dims, 1, 1)
    pair_far = swap(pair, dims, 0, 2)
    first_four = jnp.concatenate([first_two, first_near])
    first_beside = swap(first_four, dims, 1, 1)
    first_core = swap(after([first_four], [pair_beside])[0], dims, 2, 1)
    pair_two = join(pair, pair_far, [first_four, pair_beside])
    pair_near = swap(pair_two, dims, 0, 1)
    pair_four = jnp.concatenate([pair_two, pair_near])
    pair_rest = swap(pair_four[2:], dims, 1, 1)
    return [first_four, first_beside], [pair_four, pair_beside, pair_rest], first_four, first_core


def both_cores(arrays, dims):
    if dims[2] == 1:
        return arrays
    return [value for array in arrays for value in (array, swap(array, dims, 2, 1))]


def shards(traces, owner, tiles, counts):
    seg_count, block, _ = traces.shape
    times = lax.axis_size("tm")
    segments = seg_count * times
    share = block // times
    slots = tiles.shape[0]
    bins = max(16, 128 // segments)
    groups = NF // bins
    rows = seg_count * 2 * bins
    wide = rows * times
    total = groups * rows
    part_rows = total // PIECES
    dims = chip_dims(lax.axis_size("pair"))
    smem = pl.BlockSpec(memory_space=pltpu.SMEM)
    anywhere = pl.BlockSpec(memory_space=pl.ANY)
    white = pl.pallas_call(
        functools.partial(whiten_kernel, bins),
        in_specs=[anywhere] * 2,
        out_shape=[jax.ShapeDtypeStruct((part_rows, block), jnp.bfloat16)] * PIECES,
        scratch_shapes=[
            pltpu.VMEM((CHUNKS, seg_count, block, NT // CHUNKS), jnp.float32),
            pltpu.VMEM((CHUNKS, 2 * NF, NT // CHUNKS), jnp.float32),
            pltpu.VMEM((NF + 16, seg_count * block), jnp.float32),
            pltpu.SemaphoreType.DMA((CHUNKS, 2)),
        ],
        compiler_params=pltpu.CompilerParams(vmem_limit_bytes=63 << 20),
        name="whiten",
    )(traces, jnp.asarray(forward_table()))

    paired = is_paired(dims, times)
    blocks = [own[None] for own in white]
    if paired:
        *gathered, near, swapped = gather_two(*blocks, dims)
        tiles, counts = after([tiles, counts], [near])
    else:
        gathered = [gather_one(own, dims) for own in blocks]

    known = owner.shape[0]
    chosen = tiles.reshape(-1, 1) == jnp.arange(known, dtype=jnp.int32)
    stored = jnp.sum(jnp.where(chosen, owner, 0), axis=1)
    away = stored ^ lax.axis_index("pair")

    pack = part_rows + part_rows // block * share
    depth = 2 * NF // PIECES
    chunk = min(share, 16)
    inside = pl.BlockSpec(memory_space=pltpu.VMEM)
    operands = [
        pltpu.VMEM((share, groups // PIECES * wide), jnp.float32),
        pltpu.VMEM((groups // PIECES * wide, 2 * block), jnp.bfloat16),
    ]
    early = None
    for piece, arrays in enumerate(gathered):
        joined = times if paired and piece else 1
        plan = plan_of(away, counts, dims, [array.shape[0] // joined for array in arrays], joined)
        if joined > 1:
            early_sources = both_cores(arrays[:-1], dims)
            arrays[-1:] = after(arrays[-1:], arrived[1:] + [table] + early_sources[3:])
            arrived = early_sources + both_cores(arrays[-1:], dims)
            continue
        sources = both_cores(arrays, dims)
        if paired:
            sources[1] = swapped
        arrived = list(pl.pallas_call(
            functools.partial(pick_kernel, len(sources)),
            in_specs=[smem] + [inside] * len(sources),
            out_shape=[jax.ShapeDtypeStruct((slots, pack, block), jnp.bfloat16)] * times,
            scratch_shapes=[
                pltpu.VMEM((slots, part_rows, block), jnp.bfloat16),
                pltpu.VMEM((slots, part_rows // block, block, block), jnp.bfloat16),
            ],
            compiler_params=pltpu.CompilerParams(vmem_limit_bytes=8 << 20),
            cost_estimate=pl.CostEstimate(flops=1, bytes_accessed=1, transcendentals=0),
            name="pick",
        )(plan, *sources))
        if not piece:
            table = inverse_table(segments, arrived[1:])
        for step in range(1, times):
            moves = [(t, (t + step) % times) for t in range(times)]
            arrived[step] = lax.ppermute(arrived[step], "tm", moves)
        if not piece:
            early = pl.pallas_call(
                functools.partial(cross_kernel, bins, rows, chunk),
                in_specs=[smem] + [inside] * times,
                out_shape=jax.ShapeDtypeStruct((slots, share // 2, depth, 2 * block), jnp.bfloat16),
                scratch_shapes=operands,
                compiler_params=pltpu.CompilerParams(vmem_limit_bytes=16 << 20),
                name="cross",
            )(plan, *arrived)

    return pl.pallas_call(
        functools.partial(stack_kernel, bins, rows, times, chunk, joined),
        in_specs=[smem] + [inside] * (2 + len(arrived)),
        out_specs=anywhere,
        out_shape=jax.ShapeDtypeStruct((slots, LAGS, share * block), jnp.float32),
        scratch_shapes=[
            pltpu.VMEM((slots, LAGS, share * block), jnp.float32),
            pltpu.VMEM((2, times, part_rows, block), jnp.bfloat16),
            pltpu.VMEM((block, part_rows), jnp.float32),
        ]
        + operands
        + [
            pltpu.VMEM((2, chunk // 2, depth, 2 * block), jnp.bfloat16),
            pltpu.SemaphoreType.DMA((slots, share // chunk)),
        ],
        compiler_params=pltpu.CompilerParams(vmem_limit_bytes=32 << 20),
        name="stack",
    )(plan, table, early, *arrived)


def solution(mesh):
    placed = (P("tm", "pair", None), P(), P("pair", None), P("pair"))
    return jax.shard_map(
        shards, mesh=mesh, in_specs=placed, out_specs=P("pair", None, "tm"), check_vma=False
    )
```

```python
import functools
import math

import jax
import jax.numpy as jnp
import numpy as np
from jax import lax
from jax.experimental import pallas as pl
from jax.experimental.pallas import tpu as pltpu
from jax.sharding import PartitionSpec as P

NT = 1024
NF = 128
LOW_BIN = 8
LAGS = 128


def forward_table():
    phase = (LOW_BIN + np.arange(NF))[:, None] * np.arange(NT)[None, :] % NT
    angle = phase * (2.0 * math.pi / NT)
    return np.concatenate([np.cos(angle), -np.sin(angle)], axis=0).astype(np.float32)


def inverse_table(segments, sent):
    (shifts,) = after([jnp.arange(LAGS, dtype=jnp.int32) - LAGS // 2], sent)
    column = jnp.arange(2 * NF, dtype=jnp.int32)
    half = NF // PIECES
    bin_id = LOW_BIN + column // (2 * half) * half + column % half
    phase = jnp.mod(shifts[:, None] * bin_id[None, :], NT)
    angle = phase.astype(jnp.float32) * (2.0 * math.pi / NT)
    scale = 1.0 / math.sqrt(segments * NF)
    value = jnp.where(column // half % 2 == 0, jnp.cos(angle), -jnp.sin(angle)) * scale
    return value.astype(jnp.bfloat16)


def halves(value):
    high = value.astype(jnp.bfloat16)
    return high, (value - high.astype(jnp.float32)).astype(jnp.bfloat16)


def nt_dot(a, b):
    return lax.dot_general(a, b, (((1,), (1,)), ((), ())), preferred_element_type=jnp.float32)


CHUNKS = 2
PIECES = 2


def whiten_kernel(bins, x_hbm, table_hbm, *refs):
    outs, (x_ref, table_ref, pad_ref, sems) = refs[:-4], refs[-4:]
    _, segments, block, wide = x_ref.shape
    columns = segments * block
    copies = []
    for k in range(CHUNKS):
        span = slice(k * wide, (k + 1) * wide)
        sources = (x_hbm.at[:, :, span], table_hbm.at[:, span])
        copies.append(
            [
                pltpu.make_async_copy(source, target.at[k], sems.at[k, n])
                for n, (source, target) in enumerate(zip(sources, (x_ref, table_ref)))
            ]
        )
        for copy in copies[-1]:
            copy.start()
    spectrum = None
    for k in range(CHUNKS):
        for copy in copies[k]:
            copy.wait()
        x = x_ref[k].reshape(columns, wide)
        x_high, x_low = halves(x)
        high, low = halves(table_ref[k])
        part = nt_dot(high, x_high) + nt_dot(high, x_low) + nt_dot(low, x_high)
        spectrum = part if spectrum is None else spectrum + part
    real_part = spectrum[:NF]
    imag_part = spectrum[NF:]
    power = real_part * real_part + imag_part * imag_part
    edge = jnp.zeros((8, columns), jnp.float32)
    pad_ref[0:8, :] = edge
    pad_ref[8 + NF : 16 + NF, :] = edge
    pad_ref[8 : 8 + NF, :] = power
    total = pad_ref[6 : 6 + NF, :]
    for offset in range(7, 11):
        total = total + pad_ref[offset : offset + NF, :]
    bin_id = lax.broadcasted_iota(jnp.int32, (NF, columns), 0)
    counted = (jnp.minimum(bin_id + 2, NF - 1) - jnp.maximum(bin_id - 2, 0) + 1).astype(jnp.float32)
    smooth = total / counted
    level = jnp.mean(power, axis=0, keepdims=True)
    factor = lax.rsqrt(smooth + 0.05 * level + 1e-06)
    parts = ((real_part * factor).astype(jnp.bfloat16), (imag_part * factor).astype(jnp.bfloat16))
    each = NF // bins // len(outs)
    for group in range(NF // bins):
        for segment in range(segments):
            for c in range(2):
                row = ((group % each * segments + segment) * 2 + c) * bins
                outs[group // each][row : row + bins, :] = parts[c][
                    group * bins : (group + 1) * bins, segment * block : (segment + 1) * block
                ]


def fetch(joined, plan_ref, at, wanted, sources, targets):
    index = plan_ref[wanted + at]
    for n, source in enumerate(sources):

        @pl.when(plan_ref[at] == n)
        def _():
            for step in range(joined):
                value = source[index + step]
                for target in targets[step]:
                    target[...] = value


def pick_kernel(count, plan_ref, *refs):
    sources, outs, (held, turned) = refs[:count], refs[count:-2], refs[-2:]
    slots, rows, block = held.shape
    times = len(outs)
    share = block // times
    time = plan_ref[4 * slots]
    for slot in range(slots):
        fetch(1, plan_ref, 2 * slot, 2 * slots, sources, [[held.at[slot]]])
        fetch(1, plan_ref, 2 * slot + 1, 2 * slots, sources, [[out.at[slot, :rows] for out in outs]])
    for slot in range(slots):
        flipped = held[slot].astype(jnp.float32).T.astype(jnp.bfloat16)
        for piece in range(rows // block):
            turned[slot, piece] = flipped[:, piece * block : (piece + 1) * block]
        for step, out in enumerate(outs):
            start = pl.multiple_of((time + step) % times * share, share)
            for piece in range(rows // block):
                low = rows + piece * share
                out[slot, low : low + share] = turned[slot, piece, pl.ds(start, share)]


def put_right(bins, block_ref, right_all, at, rows):
    block = block_ref.shape[1]
    for low in range(0, rows, 2 * bins):
        real_part = block_ref[low : low + bins, :]
        imag_part = block_ref[low + bins : low + 2 * bins, :]
        base = at(low)
        right_all[base : base + bins, :block] = real_part
        right_all[base : base + bins, block:] = imag_part
        right_all[base + bins : base + 2 * bins, :block] = imag_part
        right_all[base + bins : base + 2 * bins, block:] = -real_part


def put_pack(slot, rows, bins, step, times, pack, left_all, right_all):
    share = left_all.shape[0]
    block = share * times
    wide = times * rows
    part_rows = left_all.shape[1] // times
    at = functools.partial(column_of, rows, wide, step)
    put_right(bins, pack.at[slot], right_all, at, part_rows)
    for low in range(0, part_rows, block):
        first = part_rows + low // block * share
        value = pack[slot, first : first + share, :].astype(jnp.float32)
        for inner in range(0, block, rows):
            left_all[:, at(low + inner) : at(low + inner) + rows] = value[:, inner : inner + rows]


def column_of(rows, wide, step, low):
    return low // rows * wide + step * rows + low % rows


def cross_spectra(bins, wide, first, chunk, left_all, right_all, cross_ref):
    groups = left_all.shape[1] // wide
    block = right_all.shape[1] // 2
    half = groups * bins
    column = lax.broadcasted_iota(jnp.int32, (bins, wide), 1) % bins
    row = lax.broadcasted_iota(jnp.int32, (bins, wide), 0)
    keep = (column == row).astype(jnp.float32).astype(jnp.bfloat16)
    several = 16 if chunk % 16 == 0 else 2
    for group in range(groups):
        weights = right_all[group * wide : (group + 1) * wide, :]
        for start in range(0, chunk, several):
            pieces = []
            for i in range(several):
                line = left_all[pl.ds(first + start + i, 1), group * wide : (group + 1) * wide]
                tile = jnp.broadcast_to(line, (16, wide)).astype(jnp.bfloat16)
                pieces += [tile * keep[low : low + 16] for low in range(0, bins, 16)]
            product = jnp.dot(jnp.concatenate(pieces, axis=0), weights, preferred_element_type=jnp.float32)
            product = product.astype(jnp.bfloat16)
            for i in range(several):
                at = start + i
                lanes = slice(at % 2 * block, (at % 2 + 1) * block)
                piece = product[i * bins : (i + 1) * bins]
                cross_ref[at // 2, group * bins : (group + 1) * bins, lanes] = piece[:, :block]
                cross_ref[at // 2, half + group * bins : half + (group + 1) * bins, lanes] = piece[:, block:]


def cross_kernel(bins, rows, chunk, plan_ref, *refs):
    packs, (out_ref, left_all, right_all) = refs[:-3], refs[-3:]
    times = len(packs)

    def one_slot(slot, carry):
        for step, pack in enumerate(packs):
            put_pack(slot, rows, bins, step, times, pack, left_all, right_all)
        for n in range(left_all.shape[0] // chunk):
            into = out_ref.at[slot, n * chunk // 2 : (n + 1) * chunk // 2]
            cross_spectra(bins, times * rows, n * chunk, chunk, left_all, right_all, into)
        return carry

    slots = out_ref.shape[0]
    lax.fori_loop(0, jnp.minimum(plan_ref[4 * slots + 1], slots), one_slot, 0)


def stack_kernel(bins, rows, times, chunk, joined, plan_ref, table_ref, early_ref, *refs):
    sources, refs = refs[:-8], refs[-8:]
    out_ref, held, blocks, turned, left_all, right_all, cross_ref, sems = refs
    slots = held.shape[0]
    live = plan_ref[4 * slots + 1]
    share = left_all.shape[0]
    block = share * times
    wide = times * rows
    part_rows = left_all.shape[1] // times
    lanes = 2 * block
    parts = share // chunk
    width = chunk // 2 * lanes

    def leave(slot, n):
        span = slice(n * width, (n + 1) * width)
        return pltpu.make_async_copy(held.at[slot, :, span], out_ref.at[slot, :, span], sems.at[slot, n])

    def one_slot(slot, carry):
        if joined == 1:
            for step, pack in enumerate(sources):
                put_pack(slot, rows, bins, step, times, pack, left_all, right_all)
        else:
            for side in range(2):
                targets = [[blocks.at[side, step]] for step in range(joined)]
                fetch(joined, plan_ref, 2 * slot + side, 2 * slots, sources, targets)
            start = pl.multiple_of(plan_ref[4 * slots] * share, share)
            for step in range(times):
                at = functools.partial(column_of, rows, wide, step)
                put_right(bins, blocks.at[1, step], right_all, at, part_rows)
                turned[...] = blocks[0, step].astype(jnp.float32).T
                for low in range(0, part_rows, rows):
                    left_all[:, at(low) : at(low) + rows] = turned[pl.ds(start, share), low : low + rows]
        table = table_ref[...]
        for n in range(parts):
            cross_spectra(bins, wide, n * chunk, chunk, left_all, right_all, cross_ref.at[n % 2])
            for pair in range(chunk // 2):
                at = n * chunk // 2 + pair
                cross = jnp.concatenate([early_ref[slot, at], cross_ref[n % 2, pair]], axis=0)
                held[slot, :, at * lanes : (at + 1) * lanes] = jnp.dot(table, cross, preferred_element_type=jnp.float32)
            leave(slot, n).start()
        return carry

    for slot in range(slots):

        @pl.when(slot >= live)
        def _():
            held[slot] = jnp.zeros_like(held[slot])
            for n in range(parts):
                leave(slot, n).start()

    lax.fori_loop(0, jnp.minimum(live, slots), one_slot, 0)
    for slot in range(slots):
        for n in range(parts):
            leave(slot, n).wait()


def chip_dims(size):
    return {16: (4, 2, 2), 64: (16, 4, 1)}.get(size, (size, 1, 1))


def swap(value, dims, axis, by):
    moves = []
    for p in range(math.prod(dims)):
        place = list(np.unravel_index(p, dims))
        place[axis] ^= by
        moves.append((p, int(np.ravel_multi_index(place, dims))))
    return lax.ppermute(value, "pair", moves)


def is_paired(dims, times):
    return dims == (4, 2, 2) and times == 2 and PIECES == 2


def column_order(dims):
    depth, height, _ = dims
    order = [(0, 0)]
    for axis, size in ((0, depth), (1, height)):
        bit = size // 2
        while bit:
            order += [(z ^ bit, y) if axis == 0 else (z, y ^ bit) for z, y in order]
            bit //= 2
    return order


def plan_of(away, counts, dims, parts, joined):
    _, height, cores = dims
    source = jnp.zeros_like(away)
    index = jnp.zeros_like(away)
    spots = [(n, at) for n, part in enumerate(parts) for at in range(part)]
    for (z, y), (n, at) in zip(column_order(dims), spots):
        here = away // cores == z * height + y
        source = jnp.where(here, n * cores, source)
        index = jnp.where(here, at * joined, index)
    return jnp.concatenate([source + away % cores, index, lax.axis_index("tm")[None], counts]).astype(jnp.int32)


def after(values, others):
    return lax.optimization_barrier(tuple(values) + tuple(others))[: len(values)]


def join(held, more, others=()):
    (held,) = after([held], others)
    (room,) = after([jnp.concatenate([held, held])], ())
    return lax.dynamic_update_slice(room, more, (held.shape[0], 0, 0))


def swap_times(value, step, times):
    return lax.ppermute(value, "tm", [((t + step) % times, t) for t in range(times)])


def gather_one(held, dims):
    depth, height, _ = dims
    for axis, size in ((0, depth), (1, height)):
        bit = size // 2
        while bit:
            held = jnp.concatenate([held, swap(held, dims, axis, bit)])
            bit //= 2
    return [held]


def gather_two(first, second, dims):
    first_far = swap(first, dims, 0, 2)
    (room,) = after([jnp.concatenate([first, first])], ())
    (second,) = after([second], [room])
    other = swap_times(second, 1, 2)
    first_two = lax.dynamic_update_slice(room, first_far, (1, 0, 0))
    first_near = swap(first_two, dims, 0, 1)
    (pair,) = after([join(second, other)], [first_two])
    pair_beside = swap(pair, dims, 1, 1)
    pair_far = swap(pair, dims, 0, 2)
    first_four = jnp.concatenate([first_two, first_near])
    first_beside = swap(first_four, dims, 1, 1)
    first_core = swap(after([first_four], [pair_beside])[0], dims, 2, 1)
    pair_two = join(pair, pair_far, [first_four])
    pair_near = swap(pair_two, dims, 0, 1)
    return [first_four, first_beside], [pair_two, pair_near, pair_beside], first_two, first_core


def finish_two(pair_two, pair_near, pair_beside, dims, sent):
    pair_four = jnp.concatenate([pair_two, *after([pair_near], sent)])
    return [pair_four, pair_beside, swap(pair_four[2:], dims, 1, 1)]


def both_cores(arrays, dims):
    if dims[2] == 1:
        return arrays
    return [value for array in arrays for value in (array, swap(array, dims, 2, 1))]


def shards(traces, owner, tiles, counts):
    seg_count, block, _ = traces.shape
    times = lax.axis_size("tm")
    segments = seg_count * times
    share = block // times
    slots = tiles.shape[0]
    bins = max(16, 128 // segments)
    groups = NF // bins
    rows = seg_count * 2 * bins
    wide = rows * times
    total = groups * rows
    part_rows = total // PIECES
    dims = chip_dims(lax.axis_size("pair"))
    smem = pl.BlockSpec(memory_space=pltpu.SMEM)
    anywhere = pl.BlockSpec(memory_space=pl.ANY)
    white = pl.pallas_call(
        functools.partial(whiten_kernel, bins),
        in_specs=[anywhere] * 2,
        out_shape=[jax.ShapeDtypeStruct((part_rows, block), jnp.bfloat16)] * PIECES,
        scratch_shapes=[
            pltpu.VMEM((CHUNKS, seg_count, block, NT // CHUNKS), jnp.float32),
            pltpu.VMEM((CHUNKS, 2 * NF, NT // CHUNKS), jnp.float32),
            pltpu.VMEM((NF + 16, seg_count * block), jnp.float32),
            pltpu.SemaphoreType.DMA((CHUNKS, 2)),
        ],
        compiler_params=pltpu.CompilerParams(vmem_limit_bytes=63 << 20),
        name="whiten",
    )(traces, jnp.asarray(forward_table()))

    paired = is_paired(dims, times)
    blocks = [own[None] for own in white]
    if paired:
        *gathered, near, swapped = gather_two(*blocks, dims)
        tiles, counts = after([tiles, counts], [near])
    else:
        gathered = [gather_one(own, dims) for own in blocks]

    known = owner.shape[0]
    chosen = tiles.reshape(-1, 1) == jnp.arange(known, dtype=jnp.int32)
    stored = jnp.sum(jnp.where(chosen, owner, 0), axis=1)
    away = stored ^ lax.axis_index("pair")

    pack = part_rows + part_rows // block * share
    depth = 2 * NF // PIECES
    chunk = min(share, 16)
    inside = pl.BlockSpec(memory_space=pltpu.VMEM)
    operands = [
        pltpu.VMEM((share, groups // PIECES * wide), jnp.float32),
        pltpu.VMEM((groups // PIECES * wide, 2 * block), jnp.bfloat16),
    ]
    early = None
    for piece, arrays in enumerate(gathered):
        joined = times if paired and piece else 1
        if joined > 1:
            arrays = finish_two(*arrays, dims, picked)
        plan = plan_of(away, counts, dims, [array.shape[0] // joined for array in arrays], joined)
        if joined > 1:
            early_sources = both_cores(arrays[:-1], dims)
            arrays[-1:] = after(arrays[-1:], arrived[1:] + [table] + early_sources[3:])
            arrived = early_sources + both_cores(arrays[-1:], dims)
            continue
        sources = both_cores(arrays, dims)
        if paired:
            sources[1] = swapped
        arrived = list(pl.pallas_call(
            functools.partial(pick_kernel, len(sources)),
            in_specs=[smem] + [inside] * len(sources),
            out_shape=[jax.ShapeDtypeStruct((slots, pack, block), jnp.bfloat16)] * times,
            scratch_shapes=[
                pltpu.VMEM((slots, part_rows, block), jnp.bfloat16),
                pltpu.VMEM((slots, part_rows // block, block, block), jnp.bfloat16),
            ],
            compiler_params=pltpu.CompilerParams(vmem_limit_bytes=8 << 20),
            cost_estimate=pl.CostEstimate(flops=1, bytes_accessed=1, transcendentals=0),
            name="pick",
        )(plan, *sources))
        picked = arrived[1:]
        if not piece:
            table = inverse_table(segments, picked)
        for step in range(1, times):
            moves = [(t, (t + step) % times) for t in range(times)]
            arrived[step] = lax.ppermute(arrived[step], "tm", moves)
        if not piece:
            early = pl.pallas_call(
                functools.partial(cross_kernel, bins, rows, chunk),
                in_specs=[smem] + [inside] * times,
                out_shape=jax.ShapeDtypeStruct((slots, share // 2, depth, 2 * block), jnp.bfloat16),
                scratch_shapes=operands,
                compiler_params=pltpu.CompilerParams(vmem_limit_bytes=16 << 20),
                name="cross",
            )(plan, *arrived)

    return pl.pallas_call(
        functools.partial(stack_kernel, bins, rows, times, chunk, joined),
        in_specs=[smem] + [inside] * (2 + len(arrived)),
        out_specs=anywhere,
        out_shape=jax.ShapeDtypeStruct((slots, LAGS, share * block), jnp.float32),
        scratch_shapes=[
            pltpu.VMEM((slots, LAGS, share * block), jnp.float32),
            pltpu.VMEM((2, times, part_rows, block), jnp.bfloat16),
            pltpu.VMEM((block, part_rows), jnp.float32),
        ]
        + operands
        + [
            pltpu.VMEM((2, chunk // 2, depth, 2 * block), jnp.bfloat16),
            pltpu.SemaphoreType.DMA((slots, share // chunk)),
        ],
        compiler_params=pltpu.CompilerParams(vmem_limit_bytes=32 << 20),
        name="stack",
    )(plan, table, early, *arrived)


def solution(mesh):
    placed = (P("tm", "pair", None), P(), P("pair", None), P("pair"))
    return jax.shard_map(
        shards, mesh=mesh, in_specs=placed, out_specs=P("pair", None, "tm"), check_vma=False
    )
```

```python
import functools
import math

import jax
import jax.numpy as jnp
import numpy as np
from jax import lax
from jax.experimental import pallas as pl
from jax.experimental.pallas import tpu as pltpu
from jax.sharding import PartitionSpec as P

NT = 1024
NF = 128
LOW_BIN = 8
LAGS = 128


def forward_table():
    phase = (LOW_BIN + np.arange(NF))[:, None] * np.arange(NT)[None, :] % NT
    angle = phase * (2.0 * math.pi / NT)
    return np.concatenate([np.cos(angle), -np.sin(angle)], axis=0).astype(np.float32)


def inverse_table(segments, sent):
    (shifts,) = after([jnp.arange(LAGS, dtype=jnp.int32) - LAGS // 2], sent)
    column = jnp.arange(2 * NF, dtype=jnp.int32)
    half = NF // PIECES
    bin_id = LOW_BIN + column // (2 * half) * half + column % half
    phase = jnp.mod(shifts[:, None] * bin_id[None, :], NT)
    angle = phase.astype(jnp.float32) * (2.0 * math.pi / NT)
    scale = 1.0 / math.sqrt(segments * NF)
    value = jnp.where(column // half % 2 == 0, jnp.cos(angle), -jnp.sin(angle)) * scale
    return value.astype(jnp.bfloat16)


def halves(value):
    high = value.astype(jnp.bfloat16)
    return high, (value - high.astype(jnp.float32)).astype(jnp.bfloat16)


def nt_dot(a, b):
    return lax.dot_general(a, b, (((1,), (1,)), ((), ())), preferred_element_type=jnp.float32)


CHUNKS = 2
PIECES = 2


def whiten_kernel(bins, x_hbm, table_hbm, *refs):
    outs, (x_ref, table_ref, pad_ref, sems) = refs[:-4], refs[-4:]
    _, segments, block, wide = x_ref.shape
    columns = segments * block
    copies = []
    for k in range(CHUNKS):
        span = slice(k * wide, (k + 1) * wide)
        sources = (x_hbm.at[:, :, span], table_hbm.at[:, span])
        copies.append(
            [
                pltpu.make_async_copy(source, target.at[k], sems.at[k, n])
                for n, (source, target) in enumerate(zip(sources, (x_ref, table_ref)))
            ]
        )
        for copy in copies[-1]:
            copy.start()
    spectrum = None
    for k in range(CHUNKS):
        for copy in copies[k]:
            copy.wait()
        x = x_ref[k].reshape(columns, wide)
        x_high, x_low = halves(x)
        high, low = halves(table_ref[k])
        part = nt_dot(high, x_high) + nt_dot(high, x_low) + nt_dot(low, x_high)
        spectrum = part if spectrum is None else spectrum + part
    real_part = spectrum[:NF]
    imag_part = spectrum[NF:]
    power = real_part * real_part + imag_part * imag_part
    edge = jnp.zeros((8, columns), jnp.float32)
    pad_ref[0:8, :] = edge
    pad_ref[8 + NF : 16 + NF, :] = edge
    pad_ref[8 : 8 + NF, :] = power
    total = pad_ref[6 : 6 + NF, :]
    for offset in range(7, 11):
        total = total + pad_ref[offset : offset + NF, :]
    bin_id = lax.broadcasted_iota(jnp.int32, (NF, columns), 0)
    counted = (jnp.minimum(bin_id + 2, NF - 1) - jnp.maximum(bin_id - 2, 0) + 1).astype(jnp.float32)
    smooth = total / counted
    level = jnp.mean(power, axis=0, keepdims=True)
    factor = lax.rsqrt(smooth + 0.05 * level + 1e-06)
    parts = ((real_part * factor).astype(jnp.bfloat16), (imag_part * factor).astype(jnp.bfloat16))
    each = NF // bins // len(outs)
    for group in range(NF // bins):
        for segment in range(segments):
            for c in range(2):
                row = ((group % each * segments + segment) * 2 + c) * bins
                outs[group // each][row : row + bins, :] = parts[c][
                    group * bins : (group + 1) * bins, segment * block : (segment + 1) * block
                ]


def fetch(joined, plan_ref, at, wanted, sources, targets):
    index = plan_ref[wanted + at]
    for n, source in enumerate(sources):

        @pl.when(plan_ref[at] == n)
        def _():
            for step in range(joined):
                value = source[index + step]
                for target in targets[step]:
                    target[...] = value


def pick_kernel(count, plan_ref, *refs):
    sources, outs, (held, turned) = refs[:count], refs[count:-2], refs[-2:]
    slots, rows, block = held.shape
    times = len(outs)
    share = block // times
    time = plan_ref[4 * slots]
    for slot in range(slots):
        fetch(1, plan_ref, 2 * slot, 2 * slots, sources, [[held.at[slot]]])
        fetch(1, plan_ref, 2 * slot + 1, 2 * slots, sources, [[out.at[slot, :rows] for out in outs]])
    for slot in range(slots):
        flipped = held[slot].astype(jnp.float32).T.astype(jnp.bfloat16)
        for piece in range(rows // block):
            turned[slot, piece] = flipped[:, piece * block : (piece + 1) * block]
        for step, out in enumerate(outs):
            start = pl.multiple_of((time + step) % times * share, share)
            for piece in range(rows // block):
                low = rows + piece * share
                out[slot, low : low + share] = turned[slot, piece, pl.ds(start, share)]


def put_right(bins, block_ref, right_all, at, rows):
    block = block_ref.shape[1]
    for low in range(0, rows, 2 * bins):
        real_part = block_ref[low : low + bins, :]
        imag_part = block_ref[low + bins : low + 2 * bins, :]
        base = at(low)
        right_all[base : base + bins, :block] = real_part
        right_all[base : base + bins, block:] = imag_part
        right_all[base + bins : base + 2 * bins, :block] = imag_part
        right_all[base + bins : base + 2 * bins, block:] = -real_part


def put_pack(slot, rows, bins, step, times, pack, left_all, right_all):
    share = left_all.shape[0]
    block = share * times
    wide = times * rows
    part_rows = left_all.shape[1] // times
    at = functools.partial(column_of, rows, wide, step)
    put_right(bins, pack.at[slot], right_all, at, part_rows)
    for low in range(0, part_rows, block):
        first = part_rows + low // block * share
        value = pack[slot, first : first + share, :].astype(jnp.float32)
        for inner in range(0, block, rows):
            left_all[:, at(low + inner) : at(low + inner) + rows] = value[:, inner : inner + rows]


def column_of(rows, wide, step, low):
    return low // rows * wide + step * rows + low % rows


def cross_spectra(bins, wide, first, chunk, left_all, right_all, cross_ref):
    groups = left_all.shape[1] // wide
    block = right_all.shape[1] // 2
    half = groups * bins
    column = lax.broadcasted_iota(jnp.int32, (bins, wide), 1) % bins
    row = lax.broadcasted_iota(jnp.int32, (bins, wide), 0)
    keep = (column == row).astype(jnp.float32).astype(jnp.bfloat16)
    several = 16 if chunk % 16 == 0 else 2
    for group in range(groups):
        weights = right_all[group * wide : (group + 1) * wide, :]
        for start in range(0, chunk, several):
            pieces = []
            for i in range(several):
                line = left_all[pl.ds(first + start + i, 1), group * wide : (group + 1) * wide]
                tile = jnp.broadcast_to(line, (16, wide)).astype(jnp.bfloat16)
                pieces += [tile * keep[low : low + 16] for low in range(0, bins, 16)]
            product = jnp.dot(jnp.concatenate(pieces, axis=0), weights, preferred_element_type=jnp.float32)
            product = product.astype(jnp.bfloat16)
            for i in range(several):
                at = start + i
                lanes = slice(at % 2 * block, (at % 2 + 1) * block)
                piece = product[i * bins : (i + 1) * bins]
                cross_ref[at // 2, group * bins : (group + 1) * bins, lanes] = piece[:, :block]
                cross_ref[at // 2, half + group * bins : half + (group + 1) * bins, lanes] = piece[:, block:]


def cross_kernel(bins, rows, chunk, plan_ref, *refs):
    packs, (out_ref, left_all, right_all) = refs[:-3], refs[-3:]
    times = len(packs)
    slots = out_ref.shape[0]

    def arrange(slot):
        for step, pack in enumerate(packs):
            put_pack(slot, rows, bins, step, times, pack, left_all.at[slot % 2], right_all.at[slot % 2])

    for slot in range(slots):

        @pl.when(slot < plan_ref[4 * slots + 1])
        def _():
            if slot == 0:
                arrange(slot)
            if slot + 1 < slots:
                arrange(slot + 1)
            for n in range(left_all.shape[1] // chunk):
                into = out_ref.at[slot, n * chunk // 2 : (n + 1) * chunk // 2]
                cross_spectra(
                    bins, times * rows, n * chunk, chunk, left_all.at[slot % 2], right_all.at[slot % 2], into
                )


def stack_kernel(bins, rows, times, chunk, joined, plan_ref, table_ref, early_ref, *refs):
    sources, refs = refs[:-8], refs[-8:]
    out_ref, held, blocks, turned, left_all, right_all, cross_ref, sems = refs
    slots = held.shape[0]
    live = plan_ref[4 * slots + 1]
    share = left_all.shape[1]
    block = share * times
    wide = times * rows
    part_rows = left_all.shape[2] // times
    lanes = 2 * block
    parts = share // chunk
    width = chunk // 2 * lanes

    def leave(slot, n):
        span = slice(n * width, (n + 1) * width)
        return pltpu.make_async_copy(held.at[slot, :, span], out_ref.at[slot, :, span], sems.at[slot, n])

    def bring(slot):
        if joined > 1:
            for side in range(2):
                targets = [[blocks.at[slot % 2, side, step]] for step in range(joined)]
                fetch(joined, plan_ref, 2 * slot + side, 2 * slots, sources, targets)

    def arrange(slot):
        left, right = left_all.at[slot % 2], right_all.at[slot % 2]
        if joined == 1:
            for step, pack in enumerate(sources):
                put_pack(slot, rows, bins, step, times, pack, left, right)
            return
        start = pl.multiple_of(plan_ref[4 * slots] * share, share)
        for step in range(times):
            at = functools.partial(column_of, rows, wide, step)
            put_right(bins, blocks.at[slot % 2, 1, step], right, at, part_rows)
            turned[step] = blocks[slot % 2, 0, step].astype(jnp.float32).T
            for low in range(0, part_rows, rows):
                left[:, at(low) : at(low) + rows] = turned[step, pl.ds(start, share), low : low + rows]

    for slot in range(slots):

        @pl.when(slot >= live)
        def _():
            held[slot] = jnp.zeros_like(held[slot])
            for n in range(parts):
                leave(slot, n).start()

    for slot in range(slots):

        @pl.when(slot < live)
        def _():
            if slot == 0:
                bring(slot)
                arrange(slot)
            if slot + 1 < slots:
                bring(slot + 1)
                arrange(slot + 1)
            table = table_ref[...]
            for n in range(parts):
                cross_spectra(
                    bins, wide, n * chunk, chunk, left_all.at[slot % 2], right_all.at[slot % 2], cross_ref.at[n % 2]
                )
                for pair in range(chunk // 2):
                    at = n * chunk // 2 + pair
                    cross = jnp.concatenate([early_ref[slot, at], cross_ref[n % 2, pair]], axis=0)
                    held[slot, :, at * lanes : (at + 1) * lanes] = jnp.dot(
                        table, cross, preferred_element_type=jnp.float32
                    )
                leave(slot, n).start()

    for slot in range(slots):
        for n in range(parts):
            leave(slot, n).wait()


def chip_dims(size):
    return {16: (4, 2, 2), 64: (16, 4, 1)}.get(size, (size, 1, 1))


def swap(value, dims, axis, by):
    moves = []
    for p in range(math.prod(dims)):
        place = list(np.unravel_index(p, dims))
        place[axis] ^= by
        moves.append((p, int(np.ravel_multi_index(place, dims))))
    return lax.ppermute(value, "pair", moves)


def is_paired(dims, times):
    return dims == (4, 2, 2) and times == 2 and PIECES == 2


def column_order(dims):
    depth, height, _ = dims
    order = [(0, 0)]
    for axis, size in ((0, depth), (1, height)):
        bit = size // 2
        while bit:
            order += [(z ^ bit, y) if axis == 0 else (z, y ^ bit) for z, y in order]
            bit //= 2
    return order


def plan_of(away, counts, dims, parts, joined):
    _, height, cores = dims
    source = jnp.zeros_like(away)
    index = jnp.zeros_like(away)
    spots = [(n, at) for n, part in enumerate(parts) for at in range(part)]
    for (z, y), (n, at) in zip(column_order(dims), spots):
        here = away // cores == z * height + y
        source = jnp.where(here, n * cores, source)
        index = jnp.where(here, at * joined, index)
    return jnp.concatenate([source + away % cores, index, lax.axis_index("tm")[None], counts]).astype(jnp.int32)


def after(values, others):
    return lax.optimization_barrier(tuple(values) + tuple(others))[: len(values)]


def join(held, more, others=()):
    (held,) = after([held], others)
    (room,) = after([jnp.concatenate([held, held])], ())
    return lax.dynamic_update_slice(room, more, (held.shape[0], 0, 0))


def swap_times(value, step, times):
    return lax.ppermute(value, "tm", [((t + step) % times, t) for t in range(times)])


def gather_one(held, dims):
    depth, height, _ = dims
    for axis, size in ((0, depth), (1, height)):
        bit = size // 2
        while bit:
            held = jnp.concatenate([held, swap(held, dims, axis, bit)])
            bit //= 2
    return [held]


def gather_two(first, second, dims):
    first_far = swap(first, dims, 0, 2)
    (room,) = after([jnp.concatenate([first, first])], ())
    (second,) = after([second], [room])
    other = swap_times(second, 1, 2)
    first_two = lax.dynamic_update_slice(room, first_far, (1, 0, 0))
    first_near = swap(first_two, dims, 0, 1)
    (pair,) = after([join(second, other)], [first_two])
    pair_beside = swap(pair, dims, 1, 1)
    pair_far = swap(pair, dims, 0, 2)
    first_four = jnp.concatenate([first_two, first_near])
    first_beside = swap(first_four, dims, 1, 1)
    first_core = swap(after([first_four], [pair_beside])[0], dims, 2, 1)
    pair_two = join(pair, pair_far, [first_four])
    pair_near = swap(pair_two, dims, 0, 1)
    pair_four = jnp.concatenate([pair_two, pair_near])
    pair_rest = swap(pair_four[2:], dims, 1, 1)
    return [first_four, first_beside], [pair_four, pair_beside, pair_rest], first_two, first_core


def both_cores(arrays, dims):
    if dims[2] == 1:
        return arrays
    return [value for array in arrays for value in (array, swap(array, dims, 2, 1))]


def shards(traces, owner, tiles, counts):
    seg_count, block, _ = traces.shape
    times = lax.axis_size("tm")
    segments = seg_count * times
    share = block // times
    slots = tiles.shape[0]
    bins = max(16, 128 // segments)
    groups = NF // bins
    rows = seg_count * 2 * bins
    wide = rows * times
    total = groups * rows
    part_rows = total // PIECES
    dims = chip_dims(lax.axis_size("pair"))
    smem = pl.BlockSpec(memory_space=pltpu.SMEM)
    anywhere = pl.BlockSpec(memory_space=pl.ANY)
    white = pl.pallas_call(
        functools.partial(whiten_kernel, bins),
        in_specs=[anywhere] * 2,
        out_shape=[jax.ShapeDtypeStruct((part_rows, block), jnp.bfloat16)] * PIECES,
        scratch_shapes=[
            pltpu.VMEM((CHUNKS, seg_count, block, NT // CHUNKS), jnp.float32),
            pltpu.VMEM((CHUNKS, 2 * NF, NT // CHUNKS), jnp.float32),
            pltpu.VMEM((NF + 16, seg_count * block), jnp.float32),
            pltpu.SemaphoreType.DMA((CHUNKS, 2)),
        ],
        compiler_params=pltpu.CompilerParams(vmem_limit_bytes=63 << 20),
        name="whiten",
    )(traces, jnp.asarray(forward_table()))

    paired = is_paired(dims, times)
    blocks = [own[None] for own in white]
    if paired:
        *gathered, near, swapped = gather_two(*blocks, dims)
        tiles, counts = after([tiles, counts], [near])
    else:
        gathered = [gather_one(own, dims) for own in blocks]

    known = owner.shape[0]
    chosen = tiles.reshape(-1, 1) == jnp.arange(known, dtype=jnp.int32)
    stored = jnp.sum(jnp.where(chosen, owner, 0), axis=1)
    away = stored ^ lax.axis_index("pair")

    pack = part_rows + part_rows // block * share
    depth = 2 * NF // PIECES
    chunk = min(share, 16)
    inside = pl.BlockSpec(memory_space=pltpu.VMEM)
    operands = [
        pltpu.VMEM((2, share, groups // PIECES * wide), jnp.float32),
        pltpu.VMEM((2, groups // PIECES * wide, 2 * block), jnp.bfloat16),
    ]
    early = None
    for piece, arrays in enumerate(gathered):
        joined = times if paired and piece else 1
        plan = plan_of(away, counts, dims, [array.shape[0] // joined for array in arrays], joined)
        if joined > 1:
            early_sources = both_cores(arrays[:-1], dims)
            arrays[-1:] = after(arrays[-1:], arrived[1:] + [table] + early_sources[3:])
            arrived = early_sources + both_cores(arrays[-1:], dims)
            continue
        sources = both_cores(arrays, dims)
        if paired:
            sources[1] = swapped
        arrived = list(pl.pallas_call(
            functools.partial(pick_kernel, len(sources)),
            in_specs=[smem] + [inside] * len(sources),
            out_shape=[jax.ShapeDtypeStruct((slots, pack, block), jnp.bfloat16)] * times,
            scratch_shapes=[
                pltpu.VMEM((slots, part_rows, block), jnp.bfloat16),
                pltpu.VMEM((slots, part_rows // block, block, block), jnp.bfloat16),
            ],
            compiler_params=pltpu.CompilerParams(vmem_limit_bytes=8 << 20),
            cost_estimate=pl.CostEstimate(flops=1, bytes_accessed=1, transcendentals=0),
            name="pick",
        )(plan, *sources))
        if not piece:
            table = inverse_table(segments, arrived[1:])
        for step in range(1, times):
            moves = [(t, (t + step) % times) for t in range(times)]
            arrived[step] = lax.ppermute(arrived[step], "tm", moves)
        if not piece:
            early = pl.pallas_call(
                functools.partial(cross_kernel, bins, rows, chunk),
                in_specs=[smem] + [inside] * times,
                out_shape=jax.ShapeDtypeStruct((slots, share // 2, depth, 2 * block), jnp.bfloat16),
                scratch_shapes=operands,
                compiler_params=pltpu.CompilerParams(vmem_limit_bytes=16 << 20),
                name="cross",
            )(plan, *arrived)

    return pl.pallas_call(
        functools.partial(stack_kernel, bins, rows, times, chunk, joined),
        in_specs=[smem] + [inside] * (2 + len(arrived)),
        out_specs=anywhere,
        out_shape=jax.ShapeDtypeStruct((slots, LAGS, share * block), jnp.float32),
        scratch_shapes=[
            pltpu.VMEM((slots, LAGS, share * block), jnp.float32),
            pltpu.VMEM((2, 2, times, part_rows, block), jnp.bfloat16),
            pltpu.VMEM((times, block, part_rows), jnp.float32),
        ]
        + operands
        + [
            pltpu.VMEM((2, chunk // 2, depth, 2 * block), jnp.bfloat16),
            pltpu.SemaphoreType.DMA((slots, share // chunk)),
        ],
        compiler_params=pltpu.CompilerParams(vmem_limit_bytes=32 << 20),
        name="stack",
    )(plan, table, early, *arrived)


def solution(mesh):
    placed = (P("tm", "pair", None), P(), P("pair", None), P("pair"))
    return jax.shard_map(
        shards, mesh=mesh, in_specs=placed, out_specs=P("pair", None, "tm"), check_vma=False
    )
```

```python
import functools
import math

import jax
import jax.numpy as jnp
import numpy as np
from jax import lax
from jax.experimental import pallas as pl
from jax.experimental.pallas import tpu as pltpu
from jax.sharding import PartitionSpec as P

NT = 1024
NF = 128
LOW_BIN = 8
LAGS = 128


def forward_table():
    phase = (LOW_BIN + np.arange(NF))[:, None] * np.arange(NT)[None, :] % NT
    angle = phase * (2.0 * math.pi / NT)
    return np.concatenate([np.cos(angle), -np.sin(angle)], axis=0).astype(np.float32)


def inverse_table(segments, sent):
    (shifts,) = after([jnp.arange(LAGS, dtype=jnp.int32) - LAGS // 2], sent)
    column = jnp.arange(2 * NF, dtype=jnp.int32)
    half = NF // PIECES
    bin_id = LOW_BIN + column // (2 * half) * half + column % half
    phase = jnp.mod(shifts[:, None] * bin_id[None, :], NT)
    angle = phase.astype(jnp.float32) * (2.0 * math.pi / NT)
    scale = 1.0 / math.sqrt(segments * NF)
    value = jnp.where(column // half % 2 == 0, jnp.cos(angle), -jnp.sin(angle)) * scale
    return value.astype(jnp.bfloat16)


def halves(value):
    high = value.astype(jnp.bfloat16)
    return high, (value - high.astype(jnp.float32)).astype(jnp.bfloat16)


def nt_dot(a, b):
    return lax.dot_general(a, b, (((1,), (1,)), ((), ())), preferred_element_type=jnp.float32)


CHUNKS = 2
PIECES = 2
EARLY = 1


def whiten_kernel(bins, x_hbm, table_hbm, *refs):
    outs, (x_ref, table_ref, pad_ref, sems) = refs[:-4], refs[-4:]
    _, segments, block, wide = x_ref.shape
    columns = segments * block
    copies = []
    for k in range(CHUNKS):
        span = slice(k * wide, (k + 1) * wide)
        sources = (x_hbm.at[:, :, span], table_hbm.at[:, span])
        copies.append(
            [
                pltpu.make_async_copy(source, target.at[k], sems.at[k, n])
                for n, (source, target) in enumerate(zip(sources, (x_ref, table_ref)))
            ]
        )
        for copy in copies[-1]:
            copy.start()
    spectrum = None
    for k in range(CHUNKS):
        for copy in copies[k]:
            copy.wait()
        x = x_ref[k].reshape(columns, wide)
        x_high, x_low = halves(x)
        high, low = halves(table_ref[k])
        part = nt_dot(high, x_high) + nt_dot(high, x_low) + nt_dot(low, x_high)
        spectrum = part if spectrum is None else spectrum + part
    real_part = spectrum[:NF]
    imag_part = spectrum[NF:]
    power = real_part * real_part + imag_part * imag_part
    edge = jnp.zeros((8, columns), jnp.float32)
    pad_ref[0:8, :] = edge
    pad_ref[8 + NF : 16 + NF, :] = edge
    pad_ref[8 : 8 + NF, :] = power
    total = pad_ref[6 : 6 + NF, :]
    for offset in range(7, 11):
        total = total + pad_ref[offset : offset + NF, :]
    bin_id = lax.broadcasted_iota(jnp.int32, (NF, columns), 0)
    counted = (jnp.minimum(bin_id + 2, NF - 1) - jnp.maximum(bin_id - 2, 0) + 1).astype(jnp.float32)
    smooth = total / counted
    level = jnp.mean(power, axis=0, keepdims=True)
    factor = lax.rsqrt(smooth + 0.05 * level + 1e-06)
    parts = ((real_part * factor).astype(jnp.bfloat16), (imag_part * factor).astype(jnp.bfloat16))
    each = NF // bins // len(outs)
    for group in range(NF // bins):
        for segment in range(segments):
            for c in range(2):
                row = ((group % each * segments + segment) * 2 + c) * bins
                outs[group // each][row : row + bins, :] = parts[c][
                    group * bins : (group + 1) * bins, segment * block : (segment + 1) * block
                ]


def fetch(joined, plan_ref, at, wanted, sources, targets):
    index = plan_ref[wanted + at]
    for n, source in enumerate(sources):

        @pl.when(plan_ref[at] == n)
        def _():
            for step in range(joined):
                value = source[index + step]
                for target in targets[step]:
                    target[...] = value


def pick_kernel(count, plan_ref, *refs):
    sources, outs, (held, turned) = refs[:count], refs[count:-2], refs[-2:]
    slots, rows, block = held.shape
    times = len(outs)
    share = block // times
    time = plan_ref[4 * slots]
    for slot in range(slots):
        fetch(1, plan_ref, 2 * slot, 2 * slots, sources, [[held.at[slot]]])
        fetch(1, plan_ref, 2 * slot + 1, 2 * slots, sources, [[out.at[slot, :rows] for out in outs]])
    for slot in range(slots):
        flipped = held[slot].astype(jnp.float32).T.astype(jnp.bfloat16)
        for piece in range(rows // block):
            turned[slot, piece] = flipped[:, piece * block : (piece + 1) * block]
        for step, out in enumerate(outs):
            start = pl.multiple_of((time + step) % times * share, share)
            for piece in range(rows // block):
                low = rows + piece * share
                out[slot, low : low + share] = turned[slot, piece, pl.ds(start, share)]


def put_right(bins, block_ref, right_all, at, rows):
    block = block_ref.shape[1]
    for low in range(0, rows, 2 * bins):
        real_part = block_ref[low : low + bins, :]
        imag_part = block_ref[low + bins : low + 2 * bins, :]
        base = at(low)
        right_all[base : base + bins, :block] = real_part
        right_all[base : base + bins, block:] = imag_part
        right_all[base + bins : base + 2 * bins, :block] = imag_part
        right_all[base + bins : base + 2 * bins, block:] = -real_part


def put_pack(slot, rows, bins, step, times, pack, left_all, right_all):
    share = left_all.shape[0]
    block = share * times
    wide = times * rows
    part_rows = left_all.shape[1] // times
    at = functools.partial(column_of, rows, wide, step)
    put_right(bins, pack.at[slot], right_all, at, part_rows)
    for low in range(0, part_rows, block):
        first = part_rows + low // block * share
        value = pack[slot, first : first + share, :].astype(jnp.float32)
        for inner in range(0, block, rows):
            left_all[:, at(low + inner) : at(low + inner) + rows] = value[:, inner : inner + rows]


def column_of(rows, wide, step, low):
    return low // rows * wide + step * rows + low % rows


def cross_spectra(bins, wide, first, chunk, left_all, right_all, cross_ref):
    groups = left_all.shape[1] // wide
    block = right_all.shape[1] // 2
    half = groups * bins
    column = lax.broadcasted_iota(jnp.int32, (bins, wide), 1) % bins
    row = lax.broadcasted_iota(jnp.int32, (bins, wide), 0)
    keep = (column == row).astype(jnp.float32).astype(jnp.bfloat16)
    several = 16 if chunk % 16 == 0 else 2
    for group in range(groups):
        weights = right_all[group * wide : (group + 1) * wide, :]
        for start in range(0, chunk, several):
            pieces = []
            for i in range(several):
                line = left_all[pl.ds(first + start + i, 1), group * wide : (group + 1) * wide]
                tile = jnp.broadcast_to(line, (16, wide)).astype(jnp.bfloat16)
                pieces += [tile * keep[low : low + 16] for low in range(0, bins, 16)]
            product = jnp.dot(jnp.concatenate(pieces, axis=0), weights, preferred_element_type=jnp.float32)
            product = product.astype(jnp.bfloat16)
            for i in range(several):
                at = start + i
                lanes = slice(at % 2 * block, (at % 2 + 1) * block)
                piece = product[i * bins : (i + 1) * bins]
                cross_ref[at // 2, group * bins : (group + 1) * bins, lanes] = piece[:, :block]
                cross_ref[at // 2, half + group * bins : half + (group + 1) * bins, lanes] = piece[:, block:]


def cross_kernel(bins, rows, chunk, plan_ref, *refs):
    packs, (out_ref, left_all, right_all) = refs[:-3], refs[-3:]
    times = len(packs)
    slots = packs[0].shape[0]

    for slot in range(out_ref.shape[0]):

        @pl.when(slot < plan_ref[4 * slots + 1])
        def _():
            for step, pack in enumerate(packs):
                put_pack(slot, rows, bins, step, times, pack, left_all, right_all)
            for n in range(left_all.shape[0] // chunk):
                into = out_ref.at[slot, n * chunk // 2 : (n + 1) * chunk // 2]
                cross_spectra(bins, times * rows, n * chunk, chunk, left_all, right_all, into)


def stack_kernel(bins, rows, times, chunk, joined, plan_ref, table_ref, early_ref, *refs):
    packs, sources, refs = refs[:times], refs[times:-10], refs[-10:]
    out_ref, held, blocks, turned, left_first, right_first, left_all, right_all, cross_ref, sems = refs
    slots = held.shape[0]
    known = early_ref.shape[0]
    live = plan_ref[4 * slots + 1]
    share = left_all.shape[1]
    block = share * times
    wide = times * rows
    part_rows = left_all.shape[2] // times
    depth = cross_ref.shape[2] // 2
    lanes = 2 * block
    parts = share // chunk
    width = chunk // 2 * lanes

    def leave(slot, n):
        span = slice(n * width, (n + 1) * width)
        return pltpu.make_async_copy(held.at[slot, :, span], out_ref.at[slot, :, span], sems.at[slot, n])

    def bring(slot):
        if joined > 1:
            for side in range(2):
                targets = [[blocks.at[side, step]] for step in range(joined)]
                fetch(joined, plan_ref, 2 * slot + side, 2 * slots, sources, targets)

    def arrange(slot):
        left, right = left_all.at[slot % 2], right_all.at[slot % 2]
        if slot >= known:
            for step, pack in enumerate(packs):
                put_pack(slot, rows, bins, step, times, pack, left_first.at[slot % 2], right_first.at[slot % 2])
        if joined == 1:
            for step, pack in enumerate(sources):
                put_pack(slot, rows, bins, step, times, pack, left, right)
            return
        start = pl.multiple_of(plan_ref[4 * slots] * share, share)
        for step in range(times):
            at = functools.partial(column_of, rows, wide, step)
            put_right(bins, blocks.at[1, step], right, at, part_rows)
            turned[step] = blocks[0, step].astype(jnp.float32).T
            for low in range(0, part_rows, rows):
                left[:, at(low) : at(low) + rows] = turned[step, pl.ds(start, share), low : low + rows]

    for slot in range(slots):

        @pl.when(slot >= live)
        def _():
            held[slot] = jnp.zeros_like(held[slot])
            for n in range(parts):
                leave(slot, n).start()

    for slot in range(slots):

        @pl.when(slot < live)
        def _():
            if slot == 0:
                bring(slot)
                arrange(slot)
            table = table_ref[...]
            for n in range(parts):
                first, late = (cross_ref.at[n % 2, :, low : low + depth] for low in (0, depth))
                if slot >= known:
                    cross_spectra(bins, wide, n * chunk, chunk, left_first.at[slot % 2], right_first.at[slot % 2], first)
                cross_spectra(bins, wide, n * chunk, chunk, left_all.at[slot % 2], right_all.at[slot % 2], late)
                for pair in range(chunk // 2):
                    at = n * chunk // 2 + pair
                    if slot >= known:
                        cross = cross_ref[n % 2, pair]
                    else:
                        cross = jnp.concatenate([early_ref[slot, at], cross_ref[n % 2, pair, depth:]], axis=0)
                    held[slot, :, at * lanes : (at + 1) * lanes] = jnp.dot(
                        table, cross, preferred_element_type=jnp.float32
                    )
                leave(slot, n).start()
                if n == 0 and slot + 1 < slots:
                    bring(slot + 1)
                    arrange(slot + 1)

    for slot in range(slots):
        for n in range(parts):
            leave(slot, n).wait()


def chip_dims(size):
    return {16: (4, 2, 2), 64: (16, 4, 1)}.get(size, (size, 1, 1))


def swap(value, dims, axis, by):
    moves = []
    for p in range(math.prod(dims)):
        place = list(np.unravel_index(p, dims))
        place[axis] ^= by
        moves.append((p, int(np.ravel_multi_index(place, dims))))
    return lax.ppermute(value, "pair", moves)


def is_paired(dims, times):
    return dims == (4, 2, 2) and times == 2 and PIECES == 2


def column_order(dims):
    depth, height, _ = dims
    order = [(0, 0)]
    for axis, size in ((0, depth), (1, height)):
        bit = size // 2
        while bit:
            order += [(z ^ bit, y) if axis == 0 else (z, y ^ bit) for z, y in order]
            bit //= 2
    return order


def plan_of(away, counts, dims, parts, joined):
    _, height, cores = dims
    source = jnp.zeros_like(away)
    index = jnp.zeros_like(away)
    spots = [(n, at) for n, part in enumerate(parts) for at in range(part)]
    for (z, y), (n, at) in zip(column_order(dims), spots):
        here = away // cores == z * height + y
        source = jnp.where(here, n * cores, source)
        index = jnp.where(here, at * joined, index)
    return jnp.concatenate([source + away % cores, index, lax.axis_index("tm")[None], counts]).astype(jnp.int32)


def after(values, others):
    return lax.optimization_barrier(tuple(values) + tuple(others))[: len(values)]


def join(held, more, others=()):
    (held,) = after([held], others)
    (room,) = after([jnp.concatenate([held, held])], ())
    return lax.dynamic_update_slice(room, more, (held.shape[0], 0, 0))


def swap_times(value, step, times):
    return lax.ppermute(value, "tm", [((t + step) % times, t) for t in range(times)])


def gather_one(held, dims):
    depth, height, _ = dims
    for axis, size in ((0, depth), (1, height)):
        bit = size // 2
        while bit:
            held = jnp.concatenate([held, swap(held, dims, axis, bit)])
            bit //= 2
    return [held]


def gather_two(first, second, dims):
    first_far = swap(first, dims, 0, 2)
    (room,) = after([jnp.concatenate([first, first])], ())
    (second,) = after([second], [room])
    other = swap_times(second, 1, 2)
    first_two = lax.dynamic_update_slice(room, first_far, (1, 0, 0))
    first_near = swap(first_two, dims, 0, 1)
    (pair,) = after([join(second, other)], [first_two])
    pair_beside = swap(pair, dims, 1, 1)
    pair_far = swap(pair, dims, 0, 2)
    first_four = jnp.concatenate([first_two, first_near])
    first_beside = swap(first_four, dims, 1, 1)
    first_core = swap(after([first_four], [pair_beside])[0], dims, 2, 1)
    pair_two = join(pair, pair_far, [first_four])
    pair_near = swap(pair_two, dims, 0, 1)
    pair_four = jnp.concatenate([pair_two, pair_near])
    pair_rest = swap(pair_four[2:], dims, 1, 1)
    pair_five = jnp.concatenate([pair_four, pair_beside])
    return [first_four, first_beside], [pair_five, pair_rest], first_two, first_core


def both_cores(arrays, dims):
    if dims[2] == 1:
        return arrays
    return [value for array in arrays for value in (array, swap(array, dims, 2, 1))]


def shards(traces, owner, tiles, counts):
    seg_count, block, _ = traces.shape
    times = lax.axis_size("tm")
    segments = seg_count * times
    share = block // times
    slots = tiles.shape[0]
    bins = max(16, 128 // segments)
    groups = NF // bins
    rows = seg_count * 2 * bins
    wide = rows * times
    total = groups * rows
    part_rows = total // PIECES
    dims = chip_dims(lax.axis_size("pair"))
    smem = pl.BlockSpec(memory_space=pltpu.SMEM)
    anywhere = pl.BlockSpec(memory_space=pl.ANY)
    white = pl.pallas_call(
        functools.partial(whiten_kernel, bins),
        in_specs=[anywhere] * 2,
        out_shape=[jax.ShapeDtypeStruct((part_rows, block), jnp.bfloat16)] * PIECES,
        scratch_shapes=[
            pltpu.VMEM((CHUNKS, seg_count, block, NT // CHUNKS), jnp.float32),
            pltpu.VMEM((CHUNKS, 2 * NF, NT // CHUNKS), jnp.float32),
            pltpu.VMEM((NF + 16, seg_count * block), jnp.float32),
            pltpu.SemaphoreType.DMA((CHUNKS, 2)),
        ],
        compiler_params=pltpu.CompilerParams(vmem_limit_bytes=63 << 20),
        name="whiten",
    )(traces, jnp.asarray(forward_table()))

    paired = is_paired(dims, times)
    blocks = [own[None] for own in white]
    if paired:
        *gathered, near, swapped = gather_two(*blocks, dims)
        tiles, counts = after([tiles, counts], [near])
    else:
        gathered = [gather_one(own, dims) for own in blocks]

    known = owner.shape[0]
    chosen = tiles.reshape(-1, 1) == jnp.arange(known, dtype=jnp.int32)
    stored = jnp.sum(jnp.where(chosen, owner, 0), axis=1)
    away = stored ^ lax.axis_index("pair")

    pack = part_rows + part_rows // block * share
    depth = 2 * NF // PIECES
    chunk = min(share, 16)
    inside = pl.BlockSpec(memory_space=pltpu.VMEM)
    left_shape = (share, groups // PIECES * wide)
    right_shape = (groups // PIECES * wide, 2 * block)
    operands = [pltpu.VMEM((2,) + left_shape, jnp.float32), pltpu.VMEM((2,) + right_shape, jnp.bfloat16)]
    for piece, arrays in enumerate(gathered):
        joined = times if paired and piece else 1
        plan = plan_of(away, counts, dims, [array.shape[0] // joined for array in arrays], joined)
        if piece and joined > 1:
            column, rest = arrays
            (rest,) = after([rest], arrived[1:] + [table])
            late = [column, swap(after([column], picked)[0], dims, 2, 1), rest, swap(rest, dims, 2, 1)]
            continue
        sources = both_cores(arrays, dims)
        if paired:
            sources[1] = swapped
        arrived = list(pl.pallas_call(
            functools.partial(pick_kernel, len(sources)),
            in_specs=[smem] + [inside] * len(sources),
            out_shape=[jax.ShapeDtypeStruct((slots, pack, block), jnp.bfloat16)] * times,
            scratch_shapes=[
                pltpu.VMEM((slots, part_rows, block), jnp.bfloat16),
                pltpu.VMEM((slots, part_rows // block, block, block), jnp.bfloat16),
            ],
            compiler_params=pltpu.CompilerParams(vmem_limit_bytes=8 << 20),
            cost_estimate=pl.CostEstimate(flops=1, bytes_accessed=1, transcendentals=0),
            name="pick",
        )(plan, *sources))
        if not piece:
            picked = arrived[1:]
            table = inverse_table(segments, picked)
        for step in range(1, times):
            moves = [(t, (t + step) % times) for t in range(times)]
            arrived[step] = lax.ppermute(arrived[step], "tm", moves)
        if piece:
            late = arrived
        else:
            packs = arrived
            early = pl.pallas_call(
                functools.partial(cross_kernel, bins, rows, chunk),
                in_specs=[smem] + [inside] * times,
                out_shape=jax.ShapeDtypeStruct((min(EARLY, slots), share // 2, depth, 2 * block), jnp.bfloat16),
                scratch_shapes=[pltpu.VMEM(left_shape, jnp.float32), pltpu.VMEM(right_shape, jnp.bfloat16)],
                compiler_params=pltpu.CompilerParams(vmem_limit_bytes=16 << 20),
                name="cross",
            )(plan, *arrived)

    return pl.pallas_call(
        functools.partial(stack_kernel, bins, rows, times, chunk, joined),
        in_specs=[smem] + [inside] * (2 + len(packs) + len(late)),
        out_specs=anywhere,
        out_shape=jax.ShapeDtypeStruct((slots, LAGS, share * block), jnp.float32),
        scratch_shapes=[
            pltpu.VMEM((slots, LAGS, share * block), jnp.float32),
            pltpu.VMEM((2, times, part_rows, block), jnp.bfloat16),
            pltpu.VMEM((times, block, part_rows), jnp.float32),
        ]
        + operands
        + operands
        + [
            pltpu.VMEM((2, chunk // 2, 2 * depth, 2 * block), jnp.bfloat16),
            pltpu.SemaphoreType.DMA((slots, share // chunk)),
        ],
        compiler_params=pltpu.CompilerParams(vmem_limit_bytes=32 << 20),
        name="stack",
    )(plan, table, early, *packs, *late)


def solution(mesh):
    placed = (P("tm", "pair", None), P(), P("pair", None), P("pair"))
    return jax.shard_map(
        shards, mesh=mesh, in_specs=placed, out_specs=P("pair", None, "tm"), check_vma=False
    )
```

```python
import functools
import math

import jax
import jax.numpy as jnp
import numpy as np
from jax import lax
from jax.experimental import pallas as pl
from jax.experimental.pallas import tpu as pltpu
from jax.sharding import PartitionSpec as P

NT = 1024
NF = 128
LOW_BIN = 8
LAGS = 128


def forward_table():
    phase = (LOW_BIN + np.arange(NF))[:, None] * np.arange(NT)[None, :] % NT
    angle = phase * (2.0 * math.pi / NT)
    return np.concatenate([np.cos(angle), -np.sin(angle)], axis=0).astype(np.float32)


def inverse_table(segments, sent):
    (shifts,) = after([jnp.arange(LAGS, dtype=jnp.int32) - LAGS // 2], sent)
    column = jnp.arange(2 * NF, dtype=jnp.int32)
    half = NF // PIECES
    bin_id = LOW_BIN + column // (2 * half) * half + column % half
    phase = jnp.mod(shifts[:, None] * bin_id[None, :], NT)
    angle = phase.astype(jnp.float32) * (2.0 * math.pi / NT)
    scale = 1.0 / math.sqrt(segments * NF)
    value = jnp.where(column // half % 2 == 0, jnp.cos(angle), -jnp.sin(angle)) * scale
    return value.astype(jnp.bfloat16)


def halves(value):
    high = value.astype(jnp.bfloat16)
    return high, (value - high.astype(jnp.float32)).astype(jnp.bfloat16)


def nt_dot(a, b):
    return lax.dot_general(a, b, (((1,), (1,)), ((), ())), preferred_element_type=jnp.float32)


CHUNKS = 2
PIECES = 2


def whiten_kernel(bins, x_hbm, table_hbm, *refs):
    outs, (x_ref, table_ref, pad_ref, sems) = refs[:-4], refs[-4:]
    _, segments, block, wide = x_ref.shape
    columns = segments * block
    copies = []
    for k in range(CHUNKS):
        span = slice(k * wide, (k + 1) * wide)
        sources = (x_hbm.at[:, :, span], table_hbm.at[:, span])
        copies.append(
            [
                pltpu.make_async_copy(source, target.at[k], sems.at[k, n])
                for n, (source, target) in enumerate(zip(sources, (x_ref, table_ref)))
            ]
        )
        for copy in copies[-1]:
            copy.start()
    spectrum = None
    for k in range(CHUNKS):
        for copy in copies[k]:
            copy.wait()
        x = x_ref[k].reshape(columns, wide)
        x_high, x_low = halves(x)
        high, low = halves(table_ref[k])
        part = nt_dot(high, x_high) + nt_dot(high, x_low) + nt_dot(low, x_high)
        spectrum = part if spectrum is None else spectrum + part
    real_part = spectrum[:NF]
    imag_part = spectrum[NF:]
    power = real_part * real_part + imag_part * imag_part
    edge = jnp.zeros((8, columns), jnp.float32)
    pad_ref[0:8, :] = edge
    pad_ref[8 + NF : 16 + NF, :] = edge
    pad_ref[8 : 8 + NF, :] = power
    total = pad_ref[6 : 6 + NF, :]
    for offset in range(7, 11):
        total = total + pad_ref[offset : offset + NF, :]
    bin_id = lax.broadcasted_iota(jnp.int32, (NF, columns), 0)
    counted = (jnp.minimum(bin_id + 2, NF - 1) - jnp.maximum(bin_id - 2, 0) + 1).astype(jnp.float32)
    smooth = total / counted
    level = jnp.mean(power, axis=0, keepdims=True)
    factor = lax.rsqrt(smooth + 0.05 * level + 1e-06)
    parts = ((real_part * factor).astype(jnp.bfloat16), (imag_part * factor).astype(jnp.bfloat16))
    each = NF // bins // len(outs)
    for group in range(NF // bins):
        for segment in range(segments):
            for c in range(2):
                row = ((group % each * segments + segment) * 2 + c) * bins
                outs[group // each][row : row + bins, :] = parts[c][
                    group * bins : (group + 1) * bins, segment * block : (segment + 1) * block
                ]


def fetch(joined, plan_ref, at, wanted, sources, targets):
    index = plan_ref[wanted + at]
    for n, source in enumerate(sources):

        @pl.when(plan_ref[at] == n)
        def _():
            for step in range(joined):
                value = source[index + step]
                for target in targets[step]:
                    target[...] = value


def pick_kernel(count, plan_ref, *refs):
    sources, outs, (held, turned) = refs[:count], refs[count:-2], refs[-2:]
    slots, rows, block = held.shape
    times = len(outs)
    share = block // times
    time = plan_ref[4 * slots]
    for slot in range(slots):
        fetch(1, plan_ref, 2 * slot, 2 * slots, sources, [[held.at[slot]]])
        fetch(1, plan_ref, 2 * slot + 1, 2 * slots, sources, [[out.at[slot, :rows] for out in outs]])
    for slot in range(slots):
        flipped = held[slot].astype(jnp.float32).T.astype(jnp.bfloat16)
        for piece in range(rows // block):
            turned[slot, piece] = flipped[:, piece * block : (piece + 1) * block]
        for step, out in enumerate(outs):
            start = pl.multiple_of((time + step) % times * share, share)
            for piece in range(rows // block):
                low = rows + piece * share
                out[slot, low : low + share] = turned[slot, piece, pl.ds(start, share)]


def put_right(bins, block_ref, right_all, at, rows):
    block = block_ref.shape[1]
    for low in range(0, rows, 2 * bins):
        real_part = block_ref[low : low + bins, :]
        imag_part = block_ref[low + bins : low + 2 * bins, :]
        base = at(low)
        right_all[base : base + bins, :block] = real_part
        right_all[base : base + bins, block:] = imag_part
        right_all[base + bins : base + 2 * bins, :block] = imag_part
        right_all[base + bins : base + 2 * bins, block:] = -real_part


def put_pack(slot, rows, bins, step, times, pack, left_all, right_all):
    share = left_all.shape[0]
    block = share * times
    wide = times * rows
    part_rows = left_all.shape[1] // times
    at = functools.partial(column_of, rows, wide, step)
    put_right(bins, pack.at[slot], right_all, at, part_rows)
    for low in range(0, part_rows, block):
        first = part_rows + low // block * share
        value = pack[slot, first : first + share, :].astype(jnp.float32)
        for inner in range(0, block, rows):
            left_all[:, at(low + inner) : at(low + inner) + rows] = value[:, inner : inner + rows]


def column_of(rows, wide, step, low):
    return low // rows * wide + step * rows + low % rows


def cross_spectra(bins, wide, first, chunk, left_all, right_all, cross_ref):
    groups = left_all.shape[1] // wide
    block = right_all.shape[1] // 2
    half = groups * bins
    column = lax.broadcasted_iota(jnp.int32, (bins, wide), 1) % bins
    row = lax.broadcasted_iota(jnp.int32, (bins, wide), 0)
    keep = (column == row).astype(jnp.float32).astype(jnp.bfloat16)
    several = 16 if chunk % 16 == 0 else 2
    for group in range(groups):
        weights = right_all[group * wide : (group + 1) * wide, :]
        for start in range(0, chunk, several):
            pieces = []
            for i in range(several):
                line = left_all[pl.ds(first + start + i, 1), group * wide : (group + 1) * wide]
                tile = jnp.broadcast_to(line, (16, wide)).astype(jnp.bfloat16)
                pieces += [tile * keep[low : low + 16] for low in range(0, bins, 16)]
            product = jnp.dot(jnp.concatenate(pieces, axis=0), weights, preferred_element_type=jnp.float32)
            product = product.astype(jnp.bfloat16)
            for i in range(several):
                at = start + i
                lanes = slice(at % 2 * block, (at % 2 + 1) * block)
                piece = product[i * bins : (i + 1) * bins]
                cross_ref[at // 2, group * bins : (group + 1) * bins, lanes] = piece[:, :block]
                cross_ref[at // 2, half + group * bins : half + (group + 1) * bins, lanes] = piece[:, block:]


def cross_kernel(bins, rows, chunk, plan_ref, *refs):
    packs, (out_ref, left_all, right_all) = refs[:-3], refs[-3:]
    times = len(packs)

    def one_slot(slot, carry):
        for step, pack in enumerate(packs):
            put_pack(slot, rows, bins, step, times, pack, left_all, right_all)
        for n in range(left_all.shape[0] // chunk):
            into = out_ref.at[slot, n * chunk // 2 : (n + 1) * chunk // 2]
            cross_spectra(bins, times * rows, n * chunk, chunk, left_all, right_all, into)
        return carry

    slots = out_ref.shape[0]
    lax.fori_loop(0, jnp.minimum(plan_ref[4 * slots + 1], slots), one_slot, 0)


def stack_kernel(bins, rows, times, chunk, joined, plan_ref, table_ref, early_ref, *refs):
    sources, refs = refs[:-8], refs[-8:]
    out_ref, held, blocks, turned, left_all, right_all, cross_ref, sems = refs
    slots = held.shape[0]
    live = plan_ref[4 * slots + 1]
    share = left_all.shape[0]
    block = share * times
    wide = times * rows
    part_rows = left_all.shape[1] // times
    lanes = 2 * block
    parts = share // chunk
    width = chunk // 2 * lanes

    def leave(slot, n):
        span = slice(n * width, (n + 1) * width)
        return pltpu.make_async_copy(held.at[slot, :, span], out_ref.at[slot, :, span], sems.at[slot, n])

    def one_slot(slot, carry):
        if joined == 1:
            for step, pack in enumerate(sources):
                put_pack(slot, rows, bins, step, times, pack, left_all, right_all)
        else:
            for side in range(2):
                targets = [[blocks.at[side, step]] for step in range(joined)]
                fetch(joined, plan_ref, 2 * slot + side, 2 * slots, sources, targets)
            start = pl.multiple_of(plan_ref[4 * slots] * share, share)
            for step in range(times):
                at = functools.partial(column_of, rows, wide, step)
                put_right(bins, blocks.at[1, step], right_all, at, part_rows)
                turned[...] = blocks[0, step].astype(jnp.float32).T
                for low in range(0, part_rows, rows):
                    left_all[:, at(low) : at(low) + rows] = turned[pl.ds(start, share), low : low + rows]
        table = table_ref[...]
        for n in range(parts):
            cross_spectra(bins, wide, n * chunk, chunk, left_all, right_all, cross_ref.at[n % 2])
            for pair in range(chunk // 2):
                at = n * chunk // 2 + pair
                cross = jnp.concatenate([early_ref[slot, at], cross_ref[n % 2, pair]], axis=0)
                held[slot, :, at * lanes : (at + 1) * lanes] = jnp.dot(table, cross, preferred_element_type=jnp.float32)
            leave(slot, n).start()
        return carry

    for slot in range(slots):

        @pl.when(slot >= live)
        def _():
            held[slot] = jnp.zeros_like(held[slot])
            for n in range(parts):
                leave(slot, n).start()

    lax.fori_loop(0, jnp.minimum(live, slots), one_slot, 0)
    for slot in range(slots):
        for n in range(parts):
            leave(slot, n).wait()


def chip_dims(size):
    return {16: (4, 2, 2), 64: (16, 4, 1)}.get(size, (size, 1, 1))


def swap(value, dims, axis, by):
    moves = []
    for p in range(math.prod(dims)):
        place = list(np.unravel_index(p, dims))
        place[axis] ^= by
        moves.append((p, int(np.ravel_multi_index(place, dims))))
    return lax.ppermute(value, "pair", moves)


def is_paired(dims, times):
    return dims == (4, 2, 2) and times == 2 and PIECES == 2


def column_order(dims):
    depth, height, _ = dims
    order = [(0, 0)]
    for axis, size in ((0, depth), (1, height)):
        bit = size // 2
        while bit:
            order += [(z ^ bit, y) if axis == 0 else (z, y ^ bit) for z, y in order]
            bit //= 2
    return order


def plan_of(away, counts, dims, parts, joined):
    _, height, cores = dims
    source = jnp.zeros_like(away)
    index = jnp.zeros_like(away)
    spots = [(n, at) for n, part in enumerate(parts) for at in range(part)]
    for (z, y), (n, at) in zip(column_order(dims), spots):
        here = away // cores == z * height + y
        source = jnp.where(here, n * cores, source)
        index = jnp.where(here, at * joined, index)
    return jnp.concatenate([source + away % cores, index, lax.axis_index("tm")[None], counts]).astype(jnp.int32)


def after(values, others):
    return lax.optimization_barrier(tuple(values) + tuple(others))[: len(values)]


def join(held, more, others=()):
    (held,) = after([held], others)
    (room,) = after([jnp.concatenate([held, held])], ())
    return lax.dynamic_update_slice(room, more, (held.shape[0], 0, 0))


def swap_times(value, step, times):
    return lax.ppermute(value, "tm", [((t + step) % times, t) for t in range(times)])


def gather_one(held, dims):
    depth, height, _ = dims
    for axis, size in ((0, depth), (1, height)):
        bit = size // 2
        while bit:
            held = jnp.concatenate([held, swap(held, dims, axis, bit)])
            bit //= 2
    return [held]


def gather_two(first, second, dims):
    first_far = swap(first, dims, 0, 2)
    (room,) = after([jnp.concatenate([first, first])], ())
    (second,) = after([second], [room])
    other = swap_times(second, 1, 2)
    first_two = lax.dynamic_update_slice(room, first_far, (1, 0, 0))
    first_near = swap(first_two, dims, 0, 1)
    (pair,) = after([join(second, other)], [first_two])
    pair_beside = swap(pair, dims, 1, 1)
    pair_far = swap(pair, dims, 0, 2)
    first_four = jnp.concatenate([first_two, first_near])
    first_beside = swap(first_four, dims, 1, 1)
    first_core = swap(after([first_four], [pair_beside])[0], dims, 2, 1)
    pair_two = join(pair, pair_far, [first_four])
    pair_near = swap(pair_two, dims, 0, 1)
    pair_four = jnp.concatenate([pair_two, pair_near])
    pair_rest = swap(pair_four[2:], dims, 1, 1)
    return [first_four, first_beside], [pair_four, pair_beside, pair_rest], first_two, first_core


def both_cores(arrays, dims):
    if dims[2] == 1:
        return arrays
    return [value for array in arrays for value in (array, swap(array, dims, 2, 1))]


def shards(traces, owner, tiles, counts):
    seg_count, block, _ = traces.shape
    times = lax.axis_size("tm")
    segments = seg_count * times
    share = block // times
    slots = tiles.shape[0]
    bins = max(16, 128 // segments)
    groups = NF // bins
    rows = seg_count * 2 * bins
    wide = rows * times
    total = groups * rows
    part_rows = total // PIECES
    dims = chip_dims(lax.axis_size("pair"))
    smem = pl.BlockSpec(memory_space=pltpu.SMEM)
    anywhere = pl.BlockSpec(memory_space=pl.ANY)
    white = pl.pallas_call(
        functools.partial(whiten_kernel, bins),
        in_specs=[anywhere] * 2,
        out_shape=[jax.ShapeDtypeStruct((part_rows, block), jnp.bfloat16)] * PIECES,
        scratch_shapes=[
            pltpu.VMEM((CHUNKS, seg_count, block, NT // CHUNKS), jnp.float32),
            pltpu.VMEM((CHUNKS, 2 * NF, NT // CHUNKS), jnp.float32),
            pltpu.VMEM((NF + 16, seg_count * block), jnp.float32),
            pltpu.SemaphoreType.DMA((CHUNKS, 2)),
        ],
        compiler_params=pltpu.CompilerParams(vmem_limit_bytes=63 << 20),
        name="whiten",
    )(traces, jnp.asarray(forward_table()))

    paired = is_paired(dims, times)
    blocks = [own[None] for own in white]
    if paired:
        *gathered, near, swapped = gather_two(*blocks, dims)
        tiles, counts = after([tiles, counts], [near])
    else:
        gathered = [gather_one(own, dims) for own in blocks]

    known = owner.shape[0]
    chosen = tiles.reshape(-1, 1) == jnp.arange(known, dtype=jnp.int32)
    stored = jnp.sum(jnp.where(chosen, owner, 0), axis=1)
    away = stored ^ lax.axis_index("pair")

    pack = part_rows + part_rows // block * share
    depth = 2 * NF // PIECES
    chunk = min(share, 16)
    inside = pl.BlockSpec(memory_space=pltpu.VMEM)
    operands = [
        pltpu.VMEM((share, groups // PIECES * wide), jnp.float32),
        pltpu.VMEM((groups // PIECES * wide, 2 * block), jnp.bfloat16),
    ]
    early = None
    for piece, arrays in enumerate(gathered):
        joined = times if paired and piece else 1
        plan = plan_of(away, counts, dims, [array.shape[0] // joined for array in arrays], joined)
        if joined > 1:
            column, beside, rest = arrays
            beside_core = swap(after([beside], picked)[0], dims, 2, 1)
            (rest,) = after([rest], arrived[1:] + [table, beside_core])
            arrived = [column, swap(column, dims, 2, 1), beside, beside_core, rest, swap(rest, dims, 2, 1)]
            continue
        sources = both_cores(arrays, dims)
        if paired:
            sources[1] = swapped
        arrived = list(pl.pallas_call(
            functools.partial(pick_kernel, len(sources)),
            in_specs=[smem] + [inside] * len(sources),
            out_shape=[jax.ShapeDtypeStruct((slots, pack, block), jnp.bfloat16)] * times,
            scratch_shapes=[
                pltpu.VMEM((slots, part_rows, block), jnp.bfloat16),
                pltpu.VMEM((slots, part_rows // block, block, block), jnp.bfloat16),
            ],
            compiler_params=pltpu.CompilerParams(vmem_limit_bytes=8 << 20),
            cost_estimate=pl.CostEstimate(flops=1, bytes_accessed=1, transcendentals=0),
            name="pick",
        )(plan, *sources))
        if not piece:
            picked = arrived[1:]
            table = inverse_table(segments, picked)
        for step in range(1, times):
            moves = [(t, (t + step) % times) for t in range(times)]
            arrived[step] = lax.ppermute(arrived[step], "tm", moves)
        if not piece:
            early = pl.pallas_call(
                functools.partial(cross_kernel, bins, rows, chunk),
                in_specs=[smem] + [inside] * times,
                out_shape=jax.ShapeDtypeStruct((slots, share // 2, depth, 2 * block), jnp.bfloat16),
                scratch_shapes=operands,
                compiler_params=pltpu.CompilerParams(vmem_limit_bytes=16 << 20),
                name="cross",
            )(plan, *arrived)

    return pl.pallas_call(
        functools.partial(stack_kernel, bins, rows, times, chunk, joined),
        in_specs=[smem] + [inside] * (2 + len(arrived)),
        out_specs=anywhere,
        out_shape=jax.ShapeDtypeStruct((slots, LAGS, share * block), jnp.float32),
        scratch_shapes=[
            pltpu.VMEM((slots, LAGS, share * block), jnp.float32),
            pltpu.VMEM((2, times, part_rows, block), jnp.bfloat16),
            pltpu.VMEM((block, part_rows), jnp.float32),
        ]
        + operands
        + [
            pltpu.VMEM((2, chunk // 2, depth, 2 * block), jnp.bfloat16),
            pltpu.SemaphoreType.DMA((slots, share // chunk)),
        ],
        compiler_params=pltpu.CompilerParams(vmem_limit_bytes=32 << 20),
        name="stack",
    )(plan, table, early, *arrived)


def solution(mesh):
    placed = (P("tm", "pair", None), P(), P("pair", None), P("pair"))
    return jax.shard_map(
        shards, mesh=mesh, in_specs=placed, out_specs=P("pair", None, "tm"), check_vma=False
    )
```

```python
import functools
import math

import jax
import jax.numpy as jnp
import numpy as np
from jax import lax
from jax.experimental import pallas as pl
from jax.experimental.pallas import tpu as pltpu
from jax.sharding import PartitionSpec as P

NT = 1024
NF = 128
LOW_BIN = 8
LAGS = 128


def forward_table():
    phase = (LOW_BIN + np.arange(NF))[:, None] * np.arange(NT)[None, :] % NT
    angle = phase * (2.0 * math.pi / NT)
    return np.concatenate([np.cos(angle), -np.sin(angle)], axis=0).astype(np.float32)


def inverse_table(segments, sent):
    (shifts,) = after([jnp.arange(LAGS, dtype=jnp.int32) - LAGS // 2], sent)
    column = jnp.arange(2 * NF, dtype=jnp.int32)
    half = NF // PIECES
    bin_id = LOW_BIN + column // (2 * half) * half + column % half
    phase = jnp.mod(shifts[:, None] * bin_id[None, :], NT)
    angle = phase.astype(jnp.float32) * (2.0 * math.pi / NT)
    scale = 1.0 / math.sqrt(segments * NF)
    value = jnp.where(column // half % 2 == 0, jnp.cos(angle), -jnp.sin(angle)) * scale
    return value.astype(jnp.bfloat16)


def halves(value):
    high = value.astype(jnp.bfloat16)
    return high, (value - high.astype(jnp.float32)).astype(jnp.bfloat16)


def nt_dot(a, b):
    return lax.dot_general(a, b, (((1,), (1,)), ((), ())), preferred_element_type=jnp.float32)


CHUNKS = 2
PIECES = 2


def whiten_kernel(bins, x_hbm, table_hbm, *refs):
    outs, (x_ref, table_ref, pad_ref, sems) = refs[:-4], refs[-4:]
    _, segments, block, wide = x_ref.shape
    columns = segments * block
    copies = []
    for k in range(CHUNKS):
        span = slice(k * wide, (k + 1) * wide)
        sources = (x_hbm.at[:, :, span], table_hbm.at[:, span])
        copies.append(
            [
                pltpu.make_async_copy(source, target.at[k], sems.at[k, n])
                for n, (source, target) in enumerate(zip(sources, (x_ref, table_ref)))
            ]
        )
        for copy in copies[-1]:
            copy.start()
    spectrum = None
    for k in range(CHUNKS):
        for copy in copies[k]:
            copy.wait()
        x = x_ref[k].reshape(columns, wide)
        x_high, x_low = halves(x)
        high, low = halves(table_ref[k])
        part = nt_dot(high, x_high) + nt_dot(high, x_low) + nt_dot(low, x_high)
        spectrum = part if spectrum is None else spectrum + part
    real_part = spectrum[:NF]
    imag_part = spectrum[NF:]
    power = real_part * real_part + imag_part * imag_part
    edge = jnp.zeros((8, columns), jnp.float32)
    pad_ref[0:8, :] = edge
    pad_ref[8 + NF : 16 + NF, :] = edge
    pad_ref[8 : 8 + NF, :] = power
    total = pad_ref[6 : 6 + NF, :]
    for offset in range(7, 11):
        total = total + pad_ref[offset : offset + NF, :]
    bin_id = lax.broadcasted_iota(jnp.int32, (NF, columns), 0)
    counted = (jnp.minimum(bin_id + 2, NF - 1) - jnp.maximum(bin_id - 2, 0) + 1).astype(jnp.float32)
    smooth = total / counted
    level = jnp.mean(power, axis=0, keepdims=True)
    factor = lax.rsqrt(smooth + 0.05 * level + 1e-06)
    parts = ((real_part * factor).astype(jnp.bfloat16), (imag_part * factor).astype(jnp.bfloat16))
    each = NF // bins // len(outs)
    for group in range(NF // bins):
        for segment in range(segments):
            for c in range(2):
                row = ((group % each * segments + segment) * 2 + c) * bins
                outs[group // each][row : row + bins, :] = parts[c][
                    group * bins : (group + 1) * bins, segment * block : (segment + 1) * block
                ]


def fetch(joined, plan_ref, at, wanted, sources, targets):
    index = plan_ref[wanted + at]
    for n, source in enumerate(sources):

        @pl.when(plan_ref[at] == n)
        def _():
            for step in range(joined):
                value = source[index + step]
                for target in targets[step]:
                    target[...] = value


def slot_cuts(slots):
    return [(0, 1), (1, slots)] if slots > 1 else [(0, slots)]


def pick_kernel(count, plan_ref, *refs):
    sources, outs, (held, turned) = refs[:count], refs[count:-2], refs[-2:]
    slots, rows, block = held.shape
    cuts = slot_cuts(slots)
    times = 1 + (len(outs) - 1) // len(cuts)
    share = block // times
    time = plan_ref[4 * slots]
    targets = []
    for slot in range(slots):
        fetch(1, plan_ref, 2 * slot, 2 * slots, sources, [[held.at[slot]]])
        packs = [outs[0].at[slot]]
        for step in range(1, times):
            for n, (low, high) in enumerate(cuts):
                if low <= slot < high:
                    packs.append(outs[1 + (step - 1) * len(cuts) + n].at[slot - low])
        fetch(1, plan_ref, 2 * slot + 1, 2 * slots, sources, [[pack.at[:rows] for pack in packs]])
        targets.append(packs)
    for slot in range(slots):
        flipped = held[slot].astype(jnp.float32).T.astype(jnp.bfloat16)
        for piece in range(rows // block):
            turned[slot, piece] = flipped[:, piece * block : (piece + 1) * block]
        for step, pack in enumerate(targets[slot]):
            start = pl.multiple_of((time + step) % times * share, share)
            for piece in range(rows // block):
                low = rows + piece * share
                pack[low : low + share] = turned[slot, piece, pl.ds(start, share)]


def put_right(bins, block_ref, right_all, at, rows):
    block = block_ref.shape[1]
    for low in range(0, rows, 2 * bins):
        real_part = block_ref[low : low + bins, :]
        imag_part = block_ref[low + bins : low + 2 * bins, :]
        base = at(low)
        right_all[base : base + bins, :block] = real_part
        right_all[base : base + bins, block:] = imag_part
        right_all[base + bins : base + 2 * bins, :block] = imag_part
        right_all[base + bins : base + 2 * bins, block:] = -real_part


def put_pack(slot, rows, bins, step, times, pack, left_all, right_all):
    share = left_all.shape[0]
    block = share * times
    wide = times * rows
    part_rows = left_all.shape[1] // times
    at = functools.partial(column_of, rows, wide, step)
    put_right(bins, pack.at[slot], right_all, at, part_rows)
    for low in range(0, part_rows, block):
        first = part_rows + low // block * share
        value = pack[slot, first : first + share, :].astype(jnp.float32)
        for inner in range(0, block, rows):
            left_all[:, at(low + inner) : at(low + inner) + rows] = value[:, inner : inner + rows]


def column_of(rows, wide, step, low):
    return low // rows * wide + step * rows + low % rows


def cross_spectra(bins, wide, first, chunk, left_all, right_all, cross_ref):
    groups = left_all.shape[1] // wide
    block = right_all.shape[1] // 2
    half = groups * bins
    column = lax.broadcasted_iota(jnp.int32, (bins, wide), 1) % bins
    row = lax.broadcasted_iota(jnp.int32, (bins, wide), 0)
    keep = (column == row).astype(jnp.float32).astype(jnp.bfloat16)
    several = 16 if chunk % 16 == 0 else 2
    for group in range(groups):
        weights = right_all[group * wide : (group + 1) * wide, :]
        for start in range(0, chunk, several):
            pieces = []
            for i in range(several):
                line = left_all[pl.ds(first + start + i, 1), group * wide : (group + 1) * wide]
                tile = jnp.broadcast_to(line, (16, wide)).astype(jnp.bfloat16)
                pieces += [tile * keep[low : low + 16] for low in range(0, bins, 16)]
            product = jnp.dot(jnp.concatenate(pieces, axis=0), weights, preferred_element_type=jnp.float32)
            product = product.astype(jnp.bfloat16)
            for i in range(several):
                at = start + i
                lanes = slice(at % 2 * block, (at % 2 + 1) * block)
                piece = product[i * bins : (i + 1) * bins]
                cross_ref[at // 2, group * bins : (group + 1) * bins, lanes] = piece[:, :block]
                cross_ref[at // 2, half + group * bins : half + (group + 1) * bins, lanes] = piece[:, block:]


def cross_kernel(bins, rows, chunk, first, plan_ref, own_ref, *refs):
    packs, (out_ref, left_all, right_all) = refs[:-3], refs[-3:]
    times = 1 + len(packs)
    live = plan_ref[4 * own_ref.shape[0] + 1]

    def one_slot(slot, carry):
        put_pack(slot + first, rows, bins, 0, times, own_ref, left_all, right_all)
        for step, pack in enumerate(packs):
            put_pack(slot, rows, bins, 1 + step, times, pack, left_all, right_all)
        for n in range(left_all.shape[0] // chunk):
            into = out_ref.at[slot, n * chunk // 2 : (n + 1) * chunk // 2]
            cross_spectra(bins, times * rows, n * chunk, chunk, left_all, right_all, into)
        return carry

    lax.fori_loop(0, jnp.clip(live - first, 0, out_ref.shape[0]), one_slot, 0)


def stack_kernel(bins, rows, times, chunk, joined, plan_ref, table_ref, *refs):
    refs, (out_ref, held, blocks, turned, left_all, right_all, cross_ref, sems) = refs[:-8], refs[-8:]
    cuts = slot_cuts(held.shape[0])
    early, sources = refs[: len(cuts)], refs[len(cuts) :]
    slots = held.shape[0]
    live = plan_ref[4 * slots + 1]
    share = left_all.shape[0]
    block = share * times
    wide = times * rows
    part_rows = left_all.shape[1] // times
    lanes = 2 * block
    parts = share // chunk
    width = chunk // 2 * lanes

    def leave(slot, n):
        span = slice(n * width, (n + 1) * width)
        return pltpu.make_async_copy(held.at[slot, :, span], out_ref.at[slot, :, span], sems.at[slot, n])

    def one_slot(slot, cross_first):
        if joined == 1:
            for step, pack in enumerate(sources):
                put_pack(slot, rows, bins, step, times, pack, left_all, right_all)
        else:
            for side in range(2):
                targets = [[blocks.at[side, step]] for step in range(joined)]
                fetch(joined, plan_ref, 2 * slot + side, 2 * slots, sources, targets)
            start = pl.multiple_of(plan_ref[4 * slots] * share, share)
            for step in range(times):
                at = functools.partial(column_of, rows, wide, step)
                put_right(bins, blocks.at[1, step], right_all, at, part_rows)
                turned[...] = blocks[0, step].astype(jnp.float32).T
                for low in range(0, part_rows, rows):
                    left_all[:, at(low) : at(low) + rows] = turned[pl.ds(start, share), low : low + rows]
        table = table_ref[...]
        for n in range(parts):
            cross_spectra(bins, wide, n * chunk, chunk, left_all, right_all, cross_ref.at[n % 2])
            for pair in range(chunk // 2):
                at = n * chunk // 2 + pair
                cross = jnp.concatenate([cross_first[at], cross_ref[n % 2, pair]], axis=0)
                held[slot, :, at * lanes : (at + 1) * lanes] = jnp.dot(table, cross, preferred_element_type=jnp.float32)
            leave(slot, n).start()

    for slot in range(slots):

        @pl.when(slot >= live)
        def _():
            held[slot] = jnp.zeros_like(held[slot])
            for n in range(parts):
                leave(slot, n).start()

    for (low, high), ref in zip(cuts, early):
        for slot in range(low, high):
            pl.when(slot < live)(functools.partial(one_slot, slot, ref.at[slot - low]))

    for slot in range(slots):
        for n in range(parts):
            leave(slot, n).wait()


def chip_dims(size):
    return {16: (4, 2, 2), 64: (16, 4, 1)}.get(size, (size, 1, 1))


def swap(value, dims, axis, by):
    moves = []
    for p in range(math.prod(dims)):
        place = list(np.unravel_index(p, dims))
        place[axis] ^= by
        moves.append((p, int(np.ravel_multi_index(place, dims))))
    return lax.ppermute(value, "pair", moves)


def is_paired(dims, times):
    return dims == (4, 2, 2) and times == 2 and PIECES == 2


def column_order(dims):
    depth, height, _ = dims
    order = [(0, 0)]
    for axis, size in ((0, depth), (1, height)):
        bit = size // 2
        while bit:
            order += [(z ^ bit, y) if axis == 0 else (z, y ^ bit) for z, y in order]
            bit //= 2
    return order


def plan_of(away, counts, dims, parts, joined):
    _, height, cores = dims
    source = jnp.zeros_like(away)
    index = jnp.zeros_like(away)
    spots = [(n, at) for n, part in enumerate(parts) for at in range(part)]
    for (z, y), (n, at) in zip(column_order(dims), spots):
        here = away // cores == z * height + y
        source = jnp.where(here, n * cores, source)
        index = jnp.where(here, at * joined, index)
    return jnp.concatenate([source + away % cores, index, lax.axis_index("tm")[None], counts]).astype(jnp.int32)


def after(values, others):
    return lax.optimization_barrier(tuple(values) + tuple(others))[: len(values)]


def join(held, more, others=()):
    (held,) = after([held], others)
    (room,) = after([jnp.concatenate([held, held])], ())
    return lax.dynamic_update_slice(room, more, (held.shape[0], 0, 0))


def swap_times(value, step, times):
    return lax.ppermute(value, "tm", [((t + step) % times, t) for t in range(times)])


def gather_one(held, dims):
    depth, height, _ = dims
    for axis, size in ((0, depth), (1, height)):
        bit = size // 2
        while bit:
            held = jnp.concatenate([held, swap(held, dims, axis, bit)])
            bit //= 2
    return [held]


def gather_two(first, second, dims):
    first_far = swap(first, dims, 0, 2)
    (room,) = after([jnp.concatenate([first, first])], ())
    (second,) = after([second], [room])
    other = swap_times(second, 1, 2)
    first_two = lax.dynamic_update_slice(room, first_far, (1, 0, 0))
    first_near = swap(first_two, dims, 0, 1)
    (pair,) = after([join(second, other)], [first_two])
    pair_beside = swap(pair, dims, 1, 1)
    pair_far = swap(pair, dims, 0, 2)
    first_four = jnp.concatenate([first_two, first_near])
    first_beside = swap(first_four, dims, 1, 1)
    first_core = swap(after([first_four], [pair_beside])[0], dims, 2, 1)
    pair_two = join(pair, pair_far, [first_four])
    pair_near = swap(pair_two, dims, 0, 1)
    pair_four = jnp.concatenate([pair_two, pair_near])
    pair_rest = swap(pair_four[2:], dims, 1, 1)
    return [first_four, first_beside], [pair_four, pair_beside, pair_rest], first_two, first_core


def both_cores(arrays, dims):
    if dims[2] == 1:
        return arrays
    return [value for array in arrays for value in (array, swap(array, dims, 2, 1))]


def shards(traces, owner, tiles, counts):
    seg_count, block, _ = traces.shape
    times = lax.axis_size("tm")
    segments = seg_count * times
    share = block // times
    slots = tiles.shape[0]
    bins = max(16, 128 // segments)
    groups = NF // bins
    rows = seg_count * 2 * bins
    wide = rows * times
    total = groups * rows
    part_rows = total // PIECES
    dims = chip_dims(lax.axis_size("pair"))
    smem = pl.BlockSpec(memory_space=pltpu.SMEM)
    anywhere = pl.BlockSpec(memory_space=pl.ANY)
    white = pl.pallas_call(
        functools.partial(whiten_kernel, bins),
        in_specs=[anywhere] * 2,
        out_shape=[jax.ShapeDtypeStruct((part_rows, block), jnp.bfloat16)] * PIECES,
        scratch_shapes=[
            pltpu.VMEM((CHUNKS, seg_count, block, NT // CHUNKS), jnp.float32),
            pltpu.VMEM((CHUNKS, 2 * NF, NT // CHUNKS), jnp.float32),
            pltpu.VMEM((NF + 16, seg_count * block), jnp.float32),
            pltpu.SemaphoreType.DMA((CHUNKS, 2)),
        ],
        compiler_params=pltpu.CompilerParams(vmem_limit_bytes=63 << 20),
        name="whiten",
    )(traces, jnp.asarray(forward_table()))

    paired = is_paired(dims, times)
    blocks = [own[None] for own in white]
    if paired:
        *gathered, near, swapped = gather_two(*blocks, dims)
        tiles, counts = after([tiles, counts], [near])
    else:
        gathered = [gather_one(own, dims) for own in blocks]

    known = owner.shape[0]
    chosen = tiles.reshape(-1, 1) == jnp.arange(known, dtype=jnp.int32)
    stored = jnp.sum(jnp.where(chosen, owner, 0), axis=1)
    away = stored ^ lax.axis_index("pair")

    pack = part_rows + part_rows // block * share
    depth = 2 * NF // PIECES
    chunk = min(share, 16)
    inside = pl.BlockSpec(memory_space=pltpu.VMEM)
    operands = [
        pltpu.VMEM((share, groups // PIECES * wide), jnp.float32),
        pltpu.VMEM((groups // PIECES * wide, 2 * block), jnp.bfloat16),
    ]
    early = []
    cuts = slot_cuts(slots)
    for piece, arrays in enumerate(gathered):
        joined = times if paired and piece else 1
        plan = plan_of(away, counts, dims, [array.shape[0] // joined for array in arrays], joined)
        if joined > 1:
            column, beside, rest = arrays
            beside_core = swap(after([beside], picked)[0], dims, 2, 1)
            (rest,) = after([rest], arrived[1:] + early[:1] + [table, beside_core])
            column_core = swap(after([column], picked)[0], dims, 2, 1)
            arrived = [column, column_core, beside, beside_core, rest, swap(rest, dims, 2, 1)]
            continue
        sources = both_cores(arrays, dims)
        if paired:
            sources[1] = swapped
        arrived = list(pl.pallas_call(
            functools.partial(pick_kernel, len(sources)),
            in_specs=[smem] + [inside] * len(sources),
            out_shape=[jax.ShapeDtypeStruct((slots, pack, block), jnp.bfloat16)]
            + [jax.ShapeDtypeStruct((high - low, pack, block), jnp.bfloat16) for low, high in cuts] * (times - 1),
            scratch_shapes=[
                pltpu.VMEM((slots, part_rows, block), jnp.bfloat16),
                pltpu.VMEM((slots, part_rows // block, block, block), jnp.bfloat16),
            ],
            compiler_params=pltpu.CompilerParams(vmem_limit_bytes=8 << 20),
            cost_estimate=pl.CostEstimate(flops=1, bytes_accessed=1, transcendentals=0),
            name="pick",
        )(plan, *sources))
        if not piece:
            picked = arrived[1:]
            table = inverse_table(segments, picked)
        for step in range(1, times):
            moves = [(t, (t + step) % times) for t in range(times)]
            for n in range(len(cuts)):
                at = 1 + (step - 1) * len(cuts) + n
                arrived[at] = lax.ppermute(arrived[at], "tm", moves)
        if piece:
            own, *more = arrived
            arrived = [own] + [jnp.concatenate(more[n : n + len(cuts)]) for n in range(0, len(more), len(cuts))]
            continue
        for n, (low, high) in enumerate(cuts):
            early.append(
                pl.pallas_call(
                    functools.partial(cross_kernel, bins, rows, chunk, low),
                    in_specs=[smem] + [inside] * times,
                    out_shape=jax.ShapeDtypeStruct((high - low, share // 2, depth, 2 * block), jnp.bfloat16),
                    scratch_shapes=operands,
                    compiler_params=pltpu.CompilerParams(vmem_limit_bytes=16 << 20),
                    cost_estimate=pl.CostEstimate(flops=1, bytes_accessed=1, transcendentals=0),
                    name="cross",
                )(plan, arrived[0], *arrived[1 + n :: len(cuts)])
            )

    return pl.pallas_call(
        functools.partial(stack_kernel, bins, rows, times, chunk, joined),
        in_specs=[smem] + [inside] * (1 + len(early) + len(arrived)),
        out_specs=anywhere,
        out_shape=jax.ShapeDtypeStruct((slots, LAGS, share * block), jnp.float32),
        scratch_shapes=[
            pltpu.VMEM((slots, LAGS, share * block), jnp.float32),
            pltpu.VMEM((2, times, part_rows, block), jnp.bfloat16),
            pltpu.VMEM((block, part_rows), jnp.float32),
        ]
        + operands
        + [
            pltpu.VMEM((2, chunk // 2, depth, 2 * block), jnp.bfloat16),
            pltpu.SemaphoreType.DMA((slots, share // chunk)),
        ],
        compiler_params=pltpu.CompilerParams(vmem_limit_bytes=32 << 20),
        name="stack",
    )(plan, table, *early, *arrived)


def solution(mesh):
    placed = (P("tm", "pair", None), P(), P("pair", None), P("pair"))
    return jax.shard_map(
        shards, mesh=mesh, in_specs=placed, out_specs=P("pair", None, "tm"), check_vma=False
    )
```

```python
import functools
import math

import jax
import jax.numpy as jnp
import numpy as np
from jax import lax
from jax.experimental import pallas as pl
from jax.experimental.pallas import tpu as pltpu
from jax.sharding import PartitionSpec as P

NT = 1024
NF = 128
LOW_BIN = 8
LAGS = 128


def forward_table():
    phase = (LOW_BIN + np.arange(NF))[:, None] * np.arange(NT)[None, :] % NT
    angle = phase * (2.0 * math.pi / NT)
    return np.concatenate([np.cos(angle), -np.sin(angle)], axis=0).astype(np.float32)


def inverse_table(segments, sent):
    (shifts,) = after([jnp.arange(LAGS, dtype=jnp.int32) - LAGS // 2], sent)
    column = jnp.arange(2 * NF, dtype=jnp.int32)
    half = NF // PIECES
    bin_id = LOW_BIN + column // (2 * half) * half + column % half
    phase = jnp.mod(shifts[:, None] * bin_id[None, :], NT)
    angle = phase.astype(jnp.float32) * (2.0 * math.pi / NT)
    scale = 1.0 / math.sqrt(segments * NF)
    value = jnp.where(column // half % 2 == 0, jnp.cos(angle), -jnp.sin(angle)) * scale
    return value.astype(jnp.bfloat16)


def halves(value):
    high = value.astype(jnp.bfloat16)
    return high, (value - high.astype(jnp.float32)).astype(jnp.bfloat16)


def nt_dot(a, b):
    return lax.dot_general(a, b, (((1,), (1,)), ((), ())), preferred_element_type=jnp.float32)


CHUNKS = 2
PIECES = 2


def whiten_kernel(bins, x_hbm, table_hbm, *refs):
    outs, (x_ref, table_ref, pad_ref, sems) = refs[:-4], refs[-4:]
    _, segments, block, wide = x_ref.shape
    columns = segments * block
    copies = []
    for k in range(CHUNKS):
        span = slice(k * wide, (k + 1) * wide)
        sources = (x_hbm.at[:, :, span], table_hbm.at[:, span])
        copies.append(
            [
                pltpu.make_async_copy(source, target.at[k], sems.at[k, n])
                for n, (source, target) in enumerate(zip(sources, (x_ref, table_ref)))
            ]
        )
        for copy in copies[-1]:
            copy.start()
    spectrum = None
    for k in range(CHUNKS):
        for copy in copies[k]:
            copy.wait()
        x = x_ref[k].reshape(columns, wide)
        x_high, x_low = halves(x)
        high, low = halves(table_ref[k])
        part = nt_dot(high, x_high) + nt_dot(high, x_low) + nt_dot(low, x_high)
        spectrum = part if spectrum is None else spectrum + part
    real_part = spectrum[:NF]
    imag_part = spectrum[NF:]
    power = real_part * real_part + imag_part * imag_part
    edge = jnp.zeros((8, columns), jnp.float32)
    pad_ref[0:8, :] = edge
    pad_ref[8 + NF : 16 + NF, :] = edge
    pad_ref[8 : 8 + NF, :] = power
    total = pad_ref[6 : 6 + NF, :]
    for offset in range(7, 11):
        total = total + pad_ref[offset : offset + NF, :]
    bin_id = lax.broadcasted_iota(jnp.int32, (NF, columns), 0)
    counted = (jnp.minimum(bin_id + 2, NF - 1) - jnp.maximum(bin_id - 2, 0) + 1).astype(jnp.float32)
    smooth = total / counted
    level = jnp.mean(power, axis=0, keepdims=True)
    factor = lax.rsqrt(smooth + 0.05 * level + 1e-06)
    parts = ((real_part * factor).astype(jnp.bfloat16), (imag_part * factor).astype(jnp.bfloat16))
    each = NF // bins // len(outs)
    for group in range(NF // bins):
        for segment in range(segments):
            for c in range(2):
                row = ((group % each * segments + segment) * 2 + c) * bins
                outs[group // each][row : row + bins, :] = parts[c][
                    group * bins : (group + 1) * bins, segment * block : (segment + 1) * block
                ]


def fetch(joined, plan_ref, at, wanted, sources, targets):
    index = plan_ref[wanted + at]
    for n, source in enumerate(sources):

        @pl.when(plan_ref[at] == n)
        def _():
            for step in range(joined):
                value = source[index + step]
                for target in targets[step]:
                    target[...] = value


def slot_cuts(slots):
    return [(0, 1), (1, slots)] if slots > 1 else [(0, slots)]


def pick_kernel(count, plan_ref, *refs):
    sources, outs, (held, turned) = refs[:count], refs[count:-2], refs[-2:]
    slots, rows, block = held.shape
    cuts = slot_cuts(slots)
    times = 1 + (len(outs) - 1) // len(cuts)
    share = block // times
    time = plan_ref[4 * slots]
    targets = []
    for slot in range(slots):
        fetch(1, plan_ref, 2 * slot, 2 * slots, sources, [[held.at[slot]]])
        packs = [outs[0].at[slot]]
        for step in range(1, times):
            for n, (low, high) in enumerate(cuts):
                if low <= slot < high:
                    packs.append(outs[1 + (step - 1) * len(cuts) + n].at[slot - low])
        fetch(1, plan_ref, 2 * slot + 1, 2 * slots, sources, [[pack.at[:rows] for pack in packs]])
        targets.append(packs)
    for slot in range(slots):
        flipped = held[slot].astype(jnp.float32).T.astype(jnp.bfloat16)
        for piece in range(rows // block):
            turned[slot, piece] = flipped[:, piece * block : (piece + 1) * block]
        for step, pack in enumerate(targets[slot]):
            start = pl.multiple_of((time + step) % times * share, share)
            for piece in range(rows // block):
                low = rows + piece * share
                pack[low : low + share] = turned[slot, piece, pl.ds(start, share)]


def put_right(bins, block_ref, right_all, at, rows):
    block = block_ref.shape[1]
    for low in range(0, rows, 2 * bins):
        real_part = block_ref[low : low + bins, :]
        imag_part = block_ref[low + bins : low + 2 * bins, :]
        base = at(low)
        right_all[base : base + bins, :block] = real_part
        right_all[base : base + bins, block:] = imag_part
        right_all[base + bins : base + 2 * bins, :block] = imag_part
        right_all[base + bins : base + 2 * bins, block:] = -real_part


def put_pack(slot, rows, bins, step, times, pack, left_all, right_all):
    share = left_all.shape[0]
    block = share * times
    wide = times * rows
    part_rows = left_all.shape[1] // times
    at = functools.partial(column_of, rows, wide, step)
    put_right(bins, pack.at[slot], right_all, at, part_rows)
    for low in range(0, part_rows, block):
        first = part_rows + low // block * share
        value = pack[slot, first : first + share, :].astype(jnp.float32)
        for inner in range(0, block, rows):
            left_all[:, at(low + inner) : at(low + inner) + rows] = value[:, inner : inner + rows]


def column_of(rows, wide, step, low):
    return low // rows * wide + step * rows + low % rows


def cross_spectra(bins, wide, first, chunk, left_all, right_all, cross_ref):
    groups = left_all.shape[1] // wide
    block = right_all.shape[1] // 2
    half = groups * bins
    column = lax.broadcasted_iota(jnp.int32, (bins, wide), 1) % bins
    row = lax.broadcasted_iota(jnp.int32, (bins, wide), 0)
    keep = (column == row).astype(jnp.float32).astype(jnp.bfloat16)
    several = 16 if chunk % 16 == 0 else 2
    for group in range(groups):
        weights = right_all[group * wide : (group + 1) * wide, :]
        for start in range(0, chunk, several):
            pieces = []
            for i in range(several):
                line = left_all[pl.ds(first + start + i, 1), group * wide : (group + 1) * wide]
                tile = jnp.broadcast_to(line, (16, wide)).astype(jnp.bfloat16)
                pieces += [tile * keep[low : low + 16] for low in range(0, bins, 16)]
            product = jnp.dot(jnp.concatenate(pieces, axis=0), weights, preferred_element_type=jnp.float32)
            product = product.astype(jnp.bfloat16)
            for i in range(several):
                at = start + i
                lanes = slice(at % 2 * block, (at % 2 + 1) * block)
                piece = product[i * bins : (i + 1) * bins]
                cross_ref[at // 2, group * bins : (group + 1) * bins, lanes] = piece[:, :block]
                cross_ref[at // 2, half + group * bins : half + (group + 1) * bins, lanes] = piece[:, block:]


def cross_kernel(bins, rows, chunk, first, plan_ref, own_ref, *refs):
    packs, (out_ref, left_all, right_all) = refs[:-3], refs[-3:]
    times = 1 + len(packs)
    live = plan_ref[4 * own_ref.shape[0] + 1]

    def one_slot(slot, carry):
        put_pack(slot + first, rows, bins, 0, times, own_ref, left_all, right_all)
        for step, pack in enumerate(packs):
            put_pack(slot, rows, bins, 1 + step, times, pack, left_all, right_all)
        for n in range(left_all.shape[0] // chunk):
            into = out_ref.at[slot, n * chunk // 2 : (n + 1) * chunk // 2]
            cross_spectra(bins, times * rows, n * chunk, chunk, left_all, right_all, into)
        return carry

    lax.fori_loop(0, jnp.clip(live - first, 0, out_ref.shape[0]), one_slot, 0)


def stack_kernel(bins, rows, times, chunk, joined, plan_ref, table_ref, *refs):
    refs, (out_ref, held, blocks, turned, left_all, right_all, cross_ref, sems) = refs[:-8], refs[-8:]
    cuts = slot_cuts(held.shape[0])
    early, sources = refs[: len(cuts)], refs[len(cuts) :]
    slots = held.shape[0]
    live = plan_ref[4 * slots + 1]
    share = left_all.shape[1]
    block = share * times
    wide = times * rows
    part_rows = left_all.shape[2] // times
    lanes = 2 * block
    parts = share // chunk
    width = chunk // 2 * lanes

    def leave(slot, n):
        span = slice(n * width, (n + 1) * width)
        return pltpu.make_async_copy(held.at[slot, :, span], out_ref.at[slot, :, span], sems.at[slot, n])

    def arrange(slot):
        left, right = left_all.at[slot % 2], right_all.at[slot % 2]
        if joined == 1:
            for step, pack in enumerate(sources):
                put_pack(slot, rows, bins, step, times, pack, left, right)
            return
        for side in range(2):
            targets = [[blocks.at[side, step]] for step in range(joined)]
            fetch(joined, plan_ref, 2 * slot + side, 2 * slots, sources, targets)
        start = pl.multiple_of(plan_ref[4 * slots] * share, share)
        for step in range(times):
            at = functools.partial(column_of, rows, wide, step)
            put_right(bins, blocks.at[1, step], right, at, part_rows)
            turned[step] = blocks[0, step].astype(jnp.float32).T
            for low in range(0, part_rows, rows):
                left[:, at(low) : at(low) + rows] = turned[step, pl.ds(start, share), low : low + rows]

    def one_slot(slot, cross_first):
        if slot == 0:
            arrange(slot)
        left, right = left_all.at[slot % 2], right_all.at[slot % 2]
        table = table_ref[...]
        for n in range(parts):
            cross_spectra(bins, wide, n * chunk, chunk, left, right, cross_ref.at[n % 2])
            for pair in range(chunk // 2):
                at = n * chunk // 2 + pair
                cross = jnp.concatenate([cross_first[at], cross_ref[n % 2, pair]], axis=0)
                held[slot, :, at * lanes : (at + 1) * lanes] = jnp.dot(table, cross, preferred_element_type=jnp.float32)
            leave(slot, n).start()
            if n == 0 and slot + 1 < slots:
                arrange(slot + 1)

    for slot in range(slots):

        @pl.when(slot >= live)
        def _():
            held[slot] = jnp.zeros_like(held[slot])
            for n in range(parts):
                leave(slot, n).start()

    for (low, high), ref in zip(cuts, early):
        for slot in range(low, high):
            pl.when(slot < live)(functools.partial(one_slot, slot, ref.at[slot - low]))

    for slot in range(slots):
        for n in range(parts):
            leave(slot, n).wait()


def chip_dims(size):
    return {16: (4, 2, 2), 64: (16, 4, 1)}.get(size, (size, 1, 1))


def swap(value, dims, axis, by):
    moves = []
    for p in range(math.prod(dims)):
        place = list(np.unravel_index(p, dims))
        place[axis] ^= by
        moves.append((p, int(np.ravel_multi_index(place, dims))))
    return lax.ppermute(value, "pair", moves)


def is_paired(dims, times):
    return dims == (4, 2, 2) and times == 2 and PIECES == 2


def column_order(dims):
    depth, height, _ = dims
    order = [(0, 0)]
    for axis, size in ((0, depth), (1, height)):
        bit = size // 2
        while bit:
            order += [(z ^ bit, y) if axis == 0 else (z, y ^ bit) for z, y in order]
            bit //= 2
    return order


def plan_of(away, counts, dims, parts, joined):
    _, height, cores = dims
    source = jnp.zeros_like(away)
    index = jnp.zeros_like(away)
    spots = [(n, at) for n, part in enumerate(parts) for at in range(part)]
    for (z, y), (n, at) in zip(column_order(dims), spots):
        here = away // cores == z * height + y
        source = jnp.where(here, n * cores, source)
        index = jnp.where(here, at * joined, index)
    return jnp.concatenate([source + away % cores, index, lax.axis_index("tm")[None], counts]).astype(jnp.int32)


def after(values, others):
    return lax.optimization_barrier(tuple(values) + tuple(others))[: len(values)]


def join(held, more, others=()):
    (held,) = after([held], others)
    (room,) = after([jnp.concatenate([held, held])], ())
    return lax.dynamic_update_slice(room, more, (held.shape[0], 0, 0))


def swap_times(value, step, times):
    return lax.ppermute(value, "tm", [((t + step) % times, t) for t in range(times)])


def gather_one(held, dims):
    depth, height, _ = dims
    for axis, size in ((0, depth), (1, height)):
        bit = size // 2
        while bit:
            held = jnp.concatenate([held, swap(held, dims, axis, bit)])
            bit //= 2
    return [held]


def gather_two(first, second, dims):
    first_far = swap(first, dims, 0, 2)
    (room,) = after([jnp.concatenate([first, first])], ())
    (second,) = after([second], [room])
    other = swap_times(second, 1, 2)
    first_two = lax.dynamic_update_slice(room, first_far, (1, 0, 0))
    first_near = swap(first_two, dims, 0, 1)
    (pair,) = after([join(second, other)], [first_two])
    pair_beside = swap(pair, dims, 1, 1)
    pair_far = swap(pair, dims, 0, 2)
    first_four = jnp.concatenate([first_two, first_near])
    first_beside = swap(first_four, dims, 1, 1)
    first_core = swap(after([first_four], [pair_beside])[0], dims, 2, 1)
    pair_two = join(pair, pair_far, [first_four])
    pair_near = swap(pair_two, dims, 0, 1)
    pair_four = jnp.concatenate([pair_two, pair_near])
    pair_rest = swap(pair_four[2:], dims, 1, 1)
    return [first_four, first_beside], [pair_four, pair_beside, pair_rest], first_two, first_core


def both_cores(arrays, dims):
    if dims[2] == 1:
        return arrays
    return [value for array in arrays for value in (array, swap(array, dims, 2, 1))]


def shards(traces, owner, tiles, counts):
    seg_count, block, _ = traces.shape
    times = lax.axis_size("tm")
    segments = seg_count * times
    share = block // times
    slots = tiles.shape[0]
    bins = max(16, 128 // segments)
    groups = NF // bins
    rows = seg_count * 2 * bins
    wide = rows * times
    total = groups * rows
    part_rows = total // PIECES
    dims = chip_dims(lax.axis_size("pair"))
    smem = pl.BlockSpec(memory_space=pltpu.SMEM)
    anywhere = pl.BlockSpec(memory_space=pl.ANY)
    white = pl.pallas_call(
        functools.partial(whiten_kernel, bins),
        in_specs=[anywhere] * 2,
        out_shape=[jax.ShapeDtypeStruct((part_rows, block), jnp.bfloat16)] * PIECES,
        scratch_shapes=[
            pltpu.VMEM((CHUNKS, seg_count, block, NT // CHUNKS), jnp.float32),
            pltpu.VMEM((CHUNKS, 2 * NF, NT // CHUNKS), jnp.float32),
            pltpu.VMEM((NF + 16, seg_count * block), jnp.float32),
            pltpu.SemaphoreType.DMA((CHUNKS, 2)),
        ],
        compiler_params=pltpu.CompilerParams(vmem_limit_bytes=63 << 20),
        name="whiten",
    )(traces, jnp.asarray(forward_table()))

    paired = is_paired(dims, times)
    blocks = [own[None] for own in white]
    if paired:
        *gathered, near, swapped = gather_two(*blocks, dims)
        tiles, counts = after([tiles, counts], [near])
    else:
        gathered = [gather_one(own, dims) for own in blocks]

    known = owner.shape[0]
    chosen = tiles.reshape(-1, 1) == jnp.arange(known, dtype=jnp.int32)
    stored = jnp.sum(jnp.where(chosen, owner, 0), axis=1)
    away = stored ^ lax.axis_index("pair")

    pack = part_rows + part_rows // block * share
    depth = 2 * NF // PIECES
    chunk = min(share, 16)
    inside = pl.BlockSpec(memory_space=pltpu.VMEM)
    operands = [
        pltpu.VMEM((share, groups // PIECES * wide), jnp.float32),
        pltpu.VMEM((groups // PIECES * wide, 2 * block), jnp.bfloat16),
    ]
    early = []
    cuts = slot_cuts(slots)
    for piece, arrays in enumerate(gathered):
        joined = times if paired and piece else 1
        plan = plan_of(away, counts, dims, [array.shape[0] // joined for array in arrays], joined)
        if joined > 1:
            column, beside, rest = arrays
            beside_core = swap(after([beside], picked)[0], dims, 2, 1)
            (rest,) = after([rest], arrived[1:] + early[:1] + [table, beside_core])
            column_core = swap(after([column], picked)[0], dims, 2, 1)
            arrived = [column, column_core, beside, beside_core, rest, swap(rest, dims, 2, 1)]
            continue
        sources = both_cores(arrays, dims)
        if paired:
            sources[1] = swapped
        arrived = list(pl.pallas_call(
            functools.partial(pick_kernel, len(sources)),
            in_specs=[smem] + [inside] * len(sources),
            out_shape=[jax.ShapeDtypeStruct((slots, pack, block), jnp.bfloat16)]
            + [jax.ShapeDtypeStruct((high - low, pack, block), jnp.bfloat16) for low, high in cuts] * (times - 1),
            scratch_shapes=[
                pltpu.VMEM((slots, part_rows, block), jnp.bfloat16),
                pltpu.VMEM((slots, part_rows // block, block, block), jnp.bfloat16),
            ],
            compiler_params=pltpu.CompilerParams(vmem_limit_bytes=8 << 20),
            cost_estimate=pl.CostEstimate(flops=1, bytes_accessed=1, transcendentals=0),
            name="pick",
        )(plan, *sources))
        if not piece:
            picked = arrived[1:]
            table = inverse_table(segments, picked)
        for step in range(1, times):
            moves = [(t, (t + step) % times) for t in range(times)]
            for n in range(len(cuts)):
                at = 1 + (step - 1) * len(cuts) + n
                arrived[at] = lax.ppermute(arrived[at], "tm", moves)
        if piece:
            own, *more = arrived
            arrived = [own] + [jnp.concatenate(more[n : n + len(cuts)]) for n in range(0, len(more), len(cuts))]
            continue
        for n, (low, high) in enumerate(cuts):
            early.append(
                pl.pallas_call(
                    functools.partial(cross_kernel, bins, rows, chunk, low),
                    in_specs=[smem] + [inside] * times,
                    out_shape=jax.ShapeDtypeStruct((high - low, share // 2, depth, 2 * block), jnp.bfloat16),
                    scratch_shapes=operands,
                    compiler_params=pltpu.CompilerParams(vmem_limit_bytes=16 << 20),
                    cost_estimate=pl.CostEstimate(flops=1, bytes_accessed=1, transcendentals=0),
                    name="cross",
                )(plan, arrived[0], *arrived[1 + n :: len(cuts)])
            )

    return pl.pallas_call(
        functools.partial(stack_kernel, bins, rows, times, chunk, joined),
        in_specs=[smem] + [inside] * (1 + len(early) + len(arrived)),
        out_specs=anywhere,
        out_shape=jax.ShapeDtypeStruct((slots, LAGS, share * block), jnp.float32),
        scratch_shapes=[
            pltpu.VMEM((slots, LAGS, share * block), jnp.float32),
            pltpu.VMEM((2, times, part_rows, block), jnp.bfloat16),
            pltpu.VMEM((times, block, part_rows), jnp.float32),
        ]
        + [pltpu.VMEM((2,) + operand.shape, operand.dtype) for operand in operands]
        + [
            pltpu.VMEM((2, chunk // 2, depth, 2 * block), jnp.bfloat16),
            pltpu.SemaphoreType.DMA((slots, share // chunk)),
        ],
        compiler_params=pltpu.CompilerParams(vmem_limit_bytes=32 << 20),
        name="stack",
    )(plan, table, *early, *arrived)


def solution(mesh):
    placed = (P("tm", "pair", None), P(), P("pair", None), P("pair"))
    return jax.shard_map(
        shards, mesh=mesh, in_specs=placed, out_specs=P("pair", None, "tm"), check_vma=False
    )
```

```python
import functools
import math

import jax
import jax.numpy as jnp
import numpy as np
from jax import lax
from jax.experimental import pallas as pl
from jax.experimental.pallas import tpu as pltpu
from jax.sharding import PartitionSpec as P

NT = 1024
NF = 128
LOW_BIN = 8
LAGS = 128


def forward_table():
    phase = (LOW_BIN + np.arange(NF))[:, None] * np.arange(NT)[None, :] % NT
    angle = phase * (2.0 * math.pi / NT)
    return np.concatenate([np.cos(angle), -np.sin(angle)], axis=0).astype(np.float32)


def inverse_table(segments, sent):
    (shifts,) = after([jnp.arange(LAGS, dtype=jnp.int32) - LAGS // 2], sent)
    column = jnp.arange(2 * NF, dtype=jnp.int32)
    half = NF // PIECES
    bin_id = LOW_BIN + column // (2 * half) * half + column % half
    phase = jnp.mod(shifts[:, None] * bin_id[None, :], NT)
    angle = phase.astype(jnp.float32) * (2.0 * math.pi / NT)
    scale = 1.0 / math.sqrt(segments * NF)
    value = jnp.where(column // half % 2 == 0, jnp.cos(angle), -jnp.sin(angle)) * scale
    return value.astype(jnp.bfloat16)


def halves(value):
    high = value.astype(jnp.bfloat16)
    return high, (value - high.astype(jnp.float32)).astype(jnp.bfloat16)


def nt_dot(a, b):
    return lax.dot_general(a, b, (((1,), (1,)), ((), ())), preferred_element_type=jnp.float32)


CHUNKS = 1
PIECES = 2


def whiten_kernel(bins, x_hbm, table_hbm, *refs):
    outs, (x_ref, table_ref, pad_ref, sems) = refs[:-4], refs[-4:]
    _, segments, block, wide = x_ref.shape
    columns = segments * block
    copies = []
    for k in range(CHUNKS):
        span = slice(k * wide, (k + 1) * wide)
        sources = (x_hbm.at[:, :, span], table_hbm.at[:, span])
        copies.append(
            [
                pltpu.make_async_copy(source, target.at[k], sems.at[k, n])
                for n, (source, target) in enumerate(zip(sources, (x_ref, table_ref)))
            ]
        )
        for copy in copies[-1]:
            copy.start()
    spectrum = None
    for k in range(CHUNKS):
        for copy in copies[k]:
            copy.wait()
        x = x_ref[k].reshape(columns, wide)
        x_high, x_low = halves(x)
        high, low = halves(table_ref[k])
        part = nt_dot(high, x_high) + nt_dot(high, x_low) + nt_dot(low, x_high)
        spectrum = part if spectrum is None else spectrum + part
    real_part = spectrum[:NF]
    imag_part = spectrum[NF:]
    power = real_part * real_part + imag_part * imag_part
    edge = jnp.zeros((8, columns), jnp.float32)
    pad_ref[0:8, :] = edge
    pad_ref[8 + NF : 16 + NF, :] = edge
    pad_ref[8 : 8 + NF, :] = power
    total = pad_ref[6 : 6 + NF, :]
    for offset in range(7, 11):
        total = total + pad_ref[offset : offset + NF, :]
    bin_id = lax.broadcasted_iota(jnp.int32, (NF, columns), 0)
    counted = (jnp.minimum(bin_id + 2, NF - 1) - jnp.maximum(bin_id - 2, 0) + 1).astype(jnp.float32)
    smooth = total / counted
    level = jnp.mean(power, axis=0, keepdims=True)
    factor = lax.rsqrt(smooth + 0.05 * level + 1e-06)
    parts = ((real_part * factor).astype(jnp.bfloat16), (imag_part * factor).astype(jnp.bfloat16))
    each = NF // bins // len(outs)
    for group in range(NF // bins):
        for segment in range(segments):
            for c in range(2):
                row = ((group % each * segments + segment) * 2 + c) * bins
                outs[group // each][row : row + bins, :] = parts[c][
                    group * bins : (group + 1) * bins, segment * block : (segment + 1) * block
                ]


def fetch(joined, plan_ref, at, wanted, sources, targets):
    index = plan_ref[wanted + at]
    for n, source in enumerate(sources):

        @pl.when(plan_ref[at] == n)
        def _():
            for step in range(joined):
                value = source[index + step]
                for target in targets[step]:
                    target[...] = value


def slot_cuts(slots):
    return [(0, 1), (1, slots)] if slots > 1 else [(0, slots)]


def pick_kernel(count, plan_ref, *refs):
    sources, outs, (held, turned) = refs[:count], refs[count:-2], refs[-2:]
    slots, rows, block = held.shape
    cuts = slot_cuts(slots)
    times = 1 + (len(outs) - 1) // len(cuts)
    share = block // times
    time = plan_ref[4 * slots]
    targets = []
    for slot in range(slots):
        fetch(1, plan_ref, 2 * slot, 2 * slots, sources, [[held.at[slot]]])
        packs = [outs[0].at[slot]]
        for step in range(1, times):
            for n, (low, high) in enumerate(cuts):
                if low <= slot < high:
                    packs.append(outs[1 + (step - 1) * len(cuts) + n].at[slot - low])
        fetch(1, plan_ref, 2 * slot + 1, 2 * slots, sources, [[pack.at[:rows] for pack in packs]])
        targets.append(packs)
    for slot in range(slots):
        flipped = held[slot].astype(jnp.float32).T.astype(jnp.bfloat16)
        for piece in range(rows // block):
            turned[slot, piece] = flipped[:, piece * block : (piece + 1) * block]
        for step, pack in enumerate(targets[slot]):
            start = pl.multiple_of((time + step) % times * share, share)
            for piece in range(rows // block):
                low = rows + piece * share
                pack[low : low + share] = turned[slot, piece, pl.ds(start, share)]


def put_right(bins, block_ref, right_all, at, rows):
    block = block_ref.shape[1]
    for low in range(0, rows, 2 * bins):
        real_part = block_ref[low : low + bins, :]
        imag_part = block_ref[low + bins : low + 2 * bins, :]
        base = at(low)
        right_all[base : base + bins, :block] = real_part
        right_all[base : base + bins, block:] = imag_part
        right_all[base + bins : base + 2 * bins, :block] = imag_part
        right_all[base + bins : base + 2 * bins, block:] = -real_part


def put_pack(slot, rows, bins, step, times, pack, left_all, right_all):
    share = left_all.shape[0]
    block = share * times
    wide = times * rows
    part_rows = left_all.shape[1] // times
    at = functools.partial(column_of, rows, wide, step)
    put_right(bins, pack.at[slot], right_all, at, part_rows)
    for low in range(0, part_rows, block):
        first = part_rows + low // block * share
        value = pack[slot, first : first + share, :].astype(jnp.float32)
        for inner in range(0, block, rows):
            left_all[:, at(low + inner) : at(low + inner) + rows] = value[:, inner : inner + rows]


def column_of(rows, wide, step, low):
    return low // rows * wide + step * rows + low % rows


def cross_spectra(bins, wide, first, chunk, left_all, right_all, cross_ref):
    groups = left_all.shape[1] // wide
    block = right_all.shape[1] // 2
    half = groups * bins
    column = lax.broadcasted_iota(jnp.int32, (bins, wide), 1) % bins
    row = lax.broadcasted_iota(jnp.int32, (bins, wide), 0)
    keep = (column == row).astype(jnp.float32).astype(jnp.bfloat16)
    several = 16 if chunk % 16 == 0 else 2
    for group in range(groups):
        weights = right_all[group * wide : (group + 1) * wide, :]
        for start in range(0, chunk, several):
            pieces = []
            for i in range(several):
                line = left_all[pl.ds(first + start + i, 1), group * wide : (group + 1) * wide]
                tile = jnp.broadcast_to(line, (16, wide)).astype(jnp.bfloat16)
                pieces += [tile * keep[low : low + 16] for low in range(0, bins, 16)]
            product = jnp.dot(jnp.concatenate(pieces, axis=0), weights, preferred_element_type=jnp.float32)
            product = product.astype(jnp.bfloat16)
            for i in range(several):
                at = start + i
                lanes = slice(at % 2 * block, (at % 2 + 1) * block)
                piece = product[i * bins : (i + 1) * bins]
                cross_ref[at // 2, group * bins : (group + 1) * bins, lanes] = piece[:, :block]
                cross_ref[at // 2, half + group * bins : half + (group + 1) * bins, lanes] = piece[:, block:]


def cross_kernel(bins, rows, chunk, first, plan_ref, own_ref, *refs):
    packs, (out_ref, left_all, right_all) = refs[:-3], refs[-3:]
    times = 1 + len(packs)
    live = plan_ref[4 * own_ref.shape[0] + 1]

    def one_slot(slot, carry):
        put_pack(slot + first, rows, bins, 0, times, own_ref, left_all, right_all)
        for step, pack in enumerate(packs):
            put_pack(slot, rows, bins, 1 + step, times, pack, left_all, right_all)
        for n in range(left_all.shape[0] // chunk):
            into = out_ref.at[slot, n * chunk // 2 : (n + 1) * chunk // 2]
            cross_spectra(bins, times * rows, n * chunk, chunk, left_all, right_all, into)
        return carry

    lax.fori_loop(0, jnp.clip(live - first, 0, out_ref.shape[0]), one_slot, 0)


def stack_kernel(bins, rows, times, chunk, joined, plan_ref, table_ref, *refs):
    refs, (out_ref, held, blocks, turned, left_all, right_all, cross_ref, sems) = refs[:-8], refs[-8:]
    cuts = slot_cuts(held.shape[0])
    early, sources = refs[: len(cuts)], refs[len(cuts) :]
    slots = held.shape[0]
    live = plan_ref[4 * slots + 1]
    share = left_all.shape[0]
    block = share * times
    wide = times * rows
    part_rows = left_all.shape[1] // times
    lanes = 2 * block
    parts = share // chunk
    width = chunk // 2 * lanes

    def leave(slot, n):
        span = slice(n * width, (n + 1) * width)
        return pltpu.make_async_copy(held.at[slot, :, span], out_ref.at[slot, :, span], sems.at[slot, n])

    def one_slot(slot, cross_first):
        if joined == 1:
            for step, pack in enumerate(sources):
                put_pack(slot, rows, bins, step, times, pack, left_all, right_all)
        else:
            for side in range(2):
                targets = [[blocks.at[side, step]] for step in range(joined)]
                fetch(joined, plan_ref, 2 * slot + side, 2 * slots, sources, targets)
            start = pl.multiple_of(plan_ref[4 * slots] * share, share)
            for step in range(times):
                at = functools.partial(column_of, rows, wide, step)
                put_right(bins, blocks.at[1, step], right_all, at, part_rows)
                turned[...] = blocks[0, step].astype(jnp.float32).T
                for low in range(0, part_rows, rows):
                    left_all[:, at(low) : at(low) + rows] = turned[pl.ds(start, share), low : low + rows]
        table = table_ref[...]
        for n in range(parts):
            cross_spectra(bins, wide, n * chunk, chunk, left_all, right_all, cross_ref.at[n % 2])
            for pair in range(chunk // 2):
                at = n * chunk // 2 + pair
                cross = jnp.concatenate([cross_first[at], cross_ref[n % 2, pair]], axis=0)
                held[slot, :, at * lanes : (at + 1) * lanes] = jnp.dot(table, cross, preferred_element_type=jnp.float32)
            leave(slot, n).start()

    for slot in range(slots):

        @pl.when(slot >= live)
        def _():
            held[slot] = jnp.zeros_like(held[slot])
            for n in range(parts):
                leave(slot, n).start()

    for (low, high), ref in zip(cuts, early):
        for slot in range(low, high):
            pl.when(slot < live)(functools.partial(one_slot, slot, ref.at[slot - low]))

    for slot in range(slots):
        for n in range(parts):
            leave(slot, n).wait()


def chip_dims(size):
    return {16: (4, 2, 2), 64: (16, 4, 1)}.get(size, (size, 1, 1))


def swap(value, dims, axis, by):
    moves = []
    for p in range(math.prod(dims)):
        place = list(np.unravel_index(p, dims))
        place[axis] ^= by
        moves.append((p, int(np.ravel_multi_index(place, dims))))
    return lax.ppermute(value, "pair", moves)


def is_paired(dims, times):
    return dims == (4, 2, 2) and times == 2 and PIECES == 2


def column_order(dims):
    depth, height, _ = dims
    order = [(0, 0)]
    for axis, size in ((0, depth), (1, height)):
        bit = size // 2
        while bit:
            order += [(z ^ bit, y) if axis == 0 else (z, y ^ bit) for z, y in order]
            bit //= 2
    return order


def plan_of(away, counts, dims, parts, joined):
    _, height, cores = dims
    source = jnp.zeros_like(away)
    index = jnp.zeros_like(away)
    spots = [(n, at) for n, part in enumerate(parts) for at in range(part)]
    for (z, y), (n, at) in zip(column_order(dims), spots):
        here = away // cores == z * height + y
        source = jnp.where(here, n * cores, source)
        index = jnp.where(here, at * joined, index)
    return jnp.concatenate([source + away % cores, index, lax.axis_index("tm")[None], counts]).astype(jnp.int32)


def after(values, others):
    return lax.optimization_barrier(tuple(values) + tuple(others))[: len(values)]


def join(held, more, others=()):
    (held,) = after([held], others)
    (room,) = after([jnp.concatenate([held, held])], ())
    return lax.dynamic_update_slice(room, more, (held.shape[0], 0, 0))


def swap_times(value, step, times):
    return lax.ppermute(value, "tm", [((t + step) % times, t) for t in range(times)])


def gather_one(held, dims):
    depth, height, _ = dims
    for axis, size in ((0, depth), (1, height)):
        bit = size // 2
        while bit:
            held = jnp.concatenate([held, swap(held, dims, axis, bit)])
            bit //= 2
    return [held]


def gather_two(first, second, dims):
    first_far = swap(first, dims, 0, 2)
    (room,) = after([jnp.concatenate([first, first])], ())
    (second,) = after([second], [room])
    other = swap_times(second, 1, 2)
    first_two = lax.dynamic_update_slice(room, first_far, (1, 0, 0))
    first_near = swap(first_two, dims, 0, 1)
    (pair,) = after([join(second, other)], [first_two])
    pair_beside = swap(pair, dims, 1, 1)
    pair_far = swap(pair, dims, 0, 2)
    first_four = jnp.concatenate([first_two, first_near])
    first_beside = swap(first_four, dims, 1, 1)
    first_core = swap(after([first_four], [pair_beside])[0], dims, 2, 1)
    pair_two = join(pair, pair_far, [first_four])
    pair_near = swap(pair_two, dims, 0, 1)
    pair_four = jnp.concatenate([pair_two, pair_near])
    pair_rest = swap(pair_four[2:], dims, 1, 1)
    return [first_four, first_beside], [pair_four, pair_beside, pair_rest], first_two, first_core


def both_cores(arrays, dims):
    if dims[2] == 1:
        return arrays
    return [value for array in arrays for value in (array, swap(array, dims, 2, 1))]


def shards(traces, owner, tiles, counts):
    seg_count, block, _ = traces.shape
    times = lax.axis_size("tm")
    segments = seg_count * times
    share = block // times
    slots = tiles.shape[0]
    bins = max(16, 128 // segments)
    groups = NF // bins
    rows = seg_count * 2 * bins
    wide = rows * times
    total = groups * rows
    part_rows = total // PIECES
    dims = chip_dims(lax.axis_size("pair"))
    smem = pl.BlockSpec(memory_space=pltpu.SMEM)
    anywhere = pl.BlockSpec(memory_space=pl.ANY)
    white = pl.pallas_call(
        functools.partial(whiten_kernel, bins),
        in_specs=[anywhere] * 2,
        out_shape=[jax.ShapeDtypeStruct((part_rows, block), jnp.bfloat16)] * PIECES,
        scratch_shapes=[
            pltpu.VMEM((CHUNKS, seg_count, block, NT // CHUNKS), jnp.float32),
            pltpu.VMEM((CHUNKS, 2 * NF, NT // CHUNKS), jnp.float32),
            pltpu.VMEM((NF + 16, seg_count * block), jnp.float32),
            pltpu.SemaphoreType.DMA((CHUNKS, 2)),
        ],
        compiler_params=pltpu.CompilerParams(vmem_limit_bytes=63 << 20),
        name="whiten",
    )(traces, jnp.asarray(forward_table()))

    paired = is_paired(dims, times)
    blocks = [own[None] for own in white]
    if paired:
        *gathered, near, swapped = gather_two(*blocks, dims)
        tiles, counts = after([tiles, counts], [near])
    else:
        gathered = [gather_one(own, dims) for own in blocks]

    known = owner.shape[0]
    chosen = tiles.reshape(-1, 1) == jnp.arange(known, dtype=jnp.int32)
    stored = jnp.sum(jnp.where(chosen, owner, 0), axis=1)
    away = stored ^ lax.axis_index("pair")

    pack = part_rows + part_rows // block * share
    depth = 2 * NF // PIECES
    chunk = min(share, 16)
    inside = pl.BlockSpec(memory_space=pltpu.VMEM)
    operands = [
        pltpu.VMEM((share, groups // PIECES * wide), jnp.float32),
        pltpu.VMEM((groups // PIECES * wide, 2 * block), jnp.bfloat16),
    ]
    early = []
    cuts = slot_cuts(slots)
    for piece, arrays in enumerate(gathered):
        joined = times if paired and piece else 1
        plan = plan_of(away, counts, dims, [array.shape[0] // joined for array in arrays], joined)
        if joined > 1:
            column, beside, rest = arrays
            beside_core = swap(after([beside], picked)[0], dims, 2, 1)
            (rest,) = after([rest], arrived[1:] + early[:1] + [table, beside_core])
            column_core = swap(after([column], picked)[0], dims, 2, 1)
            arrived = [column, column_core, beside, beside_core, rest, swap(rest, dims, 2, 1)]
            continue
        sources = both_cores(arrays, dims)
        if paired:
            sources[1] = swapped
        arrived = list(pl.pallas_call(
            functools.partial(pick_kernel, len(sources)),
            in_specs=[smem] + [inside] * len(sources),
            out_shape=[jax.ShapeDtypeStruct((slots, pack, block), jnp.bfloat16)]
            + [jax.ShapeDtypeStruct((high - low, pack, block), jnp.bfloat16) for low, high in cuts] * (times - 1),
            scratch_shapes=[
                pltpu.VMEM((slots, part_rows, block), jnp.bfloat16),
                pltpu.VMEM((slots, part_rows // block, block, block), jnp.bfloat16),
            ],
            compiler_params=pltpu.CompilerParams(vmem_limit_bytes=8 << 20),
            cost_estimate=pl.CostEstimate(flops=1, bytes_accessed=1, transcendentals=0),
            name="pick",
        )(plan, *sources))
        if not piece:
            picked = arrived[1:]
            table = inverse_table(segments, picked)
        for step in range(1, times):
            moves = [(t, (t + step) % times) for t in range(times)]
            for n in range(len(cuts)):
                at = 1 + (step - 1) * len(cuts) + n
                arrived[at] = lax.ppermute(arrived[at], "tm", moves)
        if piece:
            own, *more = arrived
            arrived = [own] + [jnp.concatenate(more[n : n + len(cuts)]) for n in range(0, len(more), len(cuts))]
            continue
        for n, (low, high) in enumerate(cuts):
            early.append(
                pl.pallas_call(
                    functools.partial(cross_kernel, bins, rows, chunk, low),
                    in_specs=[smem] + [inside] * times,
                    out_shape=jax.ShapeDtypeStruct((high - low, share // 2, depth, 2 * block), jnp.bfloat16),
                    scratch_shapes=operands,
                    compiler_params=pltpu.CompilerParams(vmem_limit_bytes=16 << 20),
                    cost_estimate=pl.CostEstimate(flops=1, bytes_accessed=1, transcendentals=0),
                    name="cross",
                )(plan, arrived[0], *arrived[1 + n :: len(cuts)])
            )

    return pl.pallas_call(
        functools.partial(stack_kernel, bins, rows, times, chunk, joined),
        in_specs=[smem] + [inside] * (1 + len(early) + len(arrived)),
        out_specs=anywhere,
        out_shape=jax.ShapeDtypeStruct((slots, LAGS, share * block), jnp.float32),
        scratch_shapes=[
            pltpu.VMEM((slots, LAGS, share * block), jnp.float32),
            pltpu.VMEM((2, times, part_rows, block), jnp.bfloat16),
            pltpu.VMEM((block, part_rows), jnp.float32),
        ]
        + operands
        + [
            pltpu.VMEM((2, chunk // 2, depth, 2 * block), jnp.bfloat16),
            pltpu.SemaphoreType.DMA((slots, share // chunk)),
        ],
        compiler_params=pltpu.CompilerParams(vmem_limit_bytes=32 << 20),
        name="stack",
    )(plan, table, *early, *arrived)


def solution(mesh):
    placed = (P("tm", "pair", None), P(), P("pair", None), P("pair"))
    return jax.shard_map(
        shards, mesh=mesh, in_specs=placed, out_specs=P("pair", None, "tm"), check_vma=False
    )
```

```python
import functools
import math

import jax
import jax.numpy as jnp
import numpy as np
from jax import lax
from jax.experimental import pallas as pl
from jax.experimental.pallas import tpu as pltpu
from jax.sharding import PartitionSpec as P

NT = 1024
NF = 128
LOW_BIN = 8
LAGS = 128


def forward_table():
    phase = (LOW_BIN + np.arange(NF))[:, None] * np.arange(NT)[None, :] % NT
    angle = phase * (2.0 * math.pi / NT)
    return np.concatenate([np.cos(angle), -np.sin(angle)], axis=0).astype(np.float32)


def inverse_table(segments, sent):
    (shifts,) = after([jnp.arange(LAGS, dtype=jnp.int32) - LAGS // 2], sent)
    column = jnp.arange(2 * NF, dtype=jnp.int32)
    half = NF // PIECES
    bin_id = LOW_BIN + column // (2 * half) * half + column % half
    phase = jnp.mod(shifts[:, None] * bin_id[None, :], NT)
    angle = phase.astype(jnp.float32) * (2.0 * math.pi / NT)
    scale = 1.0 / math.sqrt(segments * NF)
    value = jnp.where(column // half % 2 == 0, jnp.cos(angle), -jnp.sin(angle)) * scale
    return value.astype(jnp.bfloat16)


def halves(value):
    high = value.astype(jnp.bfloat16)
    return high, (value - high.astype(jnp.float32)).astype(jnp.bfloat16)


def nt_dot(a, b):
    return lax.dot_general(a, b, (((1,), (1,)), ((), ())), preferred_element_type=jnp.float32)


CHUNKS = 1
PIECES = 2


def whiten_kernel(bins, x_hbm, table_hbm, *refs):
    outs, (x_ref, table_ref, pad_ref, sems) = refs[:-4], refs[-4:]
    _, segments, block, wide = x_ref.shape
    columns = segments * block
    copies = []
    for k in range(CHUNKS):
        span = slice(k * wide, (k + 1) * wide)
        sources = (x_hbm.at[:, :, span], table_hbm.at[:, span])
        copies.append(
            [
                pltpu.make_async_copy(source, target.at[k], sems.at[k, n])
                for n, (source, target) in enumerate(zip(sources, (x_ref, table_ref)))
            ]
        )
        for copy in copies[-1]:
            copy.start()
    spectrum = None
    for k in range(CHUNKS):
        for copy in copies[k]:
            copy.wait()
        x = x_ref[k].reshape(columns, wide)
        x_high, x_low = halves(x)
        high, low = halves(table_ref[k])
        part = nt_dot(high, x_high) + nt_dot(high, x_low) + nt_dot(low, x_high)
        spectrum = part if spectrum is None else spectrum + part
    real_part = spectrum[:NF]
    imag_part = spectrum[NF:]
    power = real_part * real_part + imag_part * imag_part
    edge = jnp.zeros((8, columns), jnp.float32)
    pad_ref[0:8, :] = edge
    pad_ref[8 + NF : 16 + NF, :] = edge
    pad_ref[8 : 8 + NF, :] = power
    total = pad_ref[6 : 6 + NF, :]
    for offset in range(7, 11):
        total = total + pad_ref[offset : offset + NF, :]
    bin_id = lax.broadcasted_iota(jnp.int32, (NF, columns), 0)
    counted = (jnp.minimum(bin_id + 2, NF - 1) - jnp.maximum(bin_id - 2, 0) + 1).astype(jnp.float32)
    smooth = total / counted
    level = jnp.mean(power, axis=0, keepdims=True)
    factor = lax.rsqrt(smooth + 0.05 * level + 1e-06)
    parts = ((real_part * factor).astype(jnp.bfloat16), (imag_part * factor).astype(jnp.bfloat16))
    each = NF // bins // len(outs)
    for group in range(NF // bins):
        for segment in range(segments):
            for c in range(2):
                row = ((group % each * segments + segment) * 2 + c) * bins
                outs[group // each][row : row + bins, :] = parts[c][
                    group * bins : (group + 1) * bins, segment * block : (segment + 1) * block
                ]


def fetch(joined, plan_ref, at, wanted, sources, targets):
    index = plan_ref[wanted + at]
    for n, source in enumerate(sources):

        @pl.when(plan_ref[at] == n)
        def _():
            for step in range(joined):
                value = source[index + step]
                for target in targets[step]:
                    target[...] = value


def slot_cuts(slots):
    return [(0, 1), (1, slots)] if slots > 1 else [(0, slots)]


def pick_kernel(count, plan_ref, *refs):
    sources, outs, (held, turned) = refs[:count], refs[count:-2], refs[-2:]
    slots, rows, block = held.shape
    cuts = slot_cuts(slots)
    times = 1 + (len(outs) - 1) // len(cuts)
    share = block // times
    time = plan_ref[4 * slots]
    targets = []
    for slot in range(slots):
        fetch(1, plan_ref, 2 * slot, 2 * slots, sources, [[held.at[slot]]])
        packs = [outs[0].at[slot]]
        for step in range(1, times):
            for n, (low, high) in enumerate(cuts):
                if low <= slot < high:
                    packs.append(outs[1 + (step - 1) * len(cuts) + n].at[slot - low])
        fetch(1, plan_ref, 2 * slot + 1, 2 * slots, sources, [[pack.at[:rows] for pack in packs]])
        targets.append(packs)
    for slot in range(slots):
        flipped = held[slot].astype(jnp.float32).T.astype(jnp.bfloat16)
        for piece in range(rows // block):
            turned[slot, piece] = flipped[:, piece * block : (piece + 1) * block]
        for step, pack in enumerate(targets[slot]):
            start = pl.multiple_of((time + step) % times * share, share)
            for piece in range(rows // block):
                low = rows + piece * share
                pack[low : low + share] = turned[slot, piece, pl.ds(start, share)]


def put_right(bins, block_ref, right_all, at, rows):
    block = block_ref.shape[1]
    for low in range(0, rows, 2 * bins):
        real_part = block_ref[low : low + bins, :]
        imag_part = block_ref[low + bins : low + 2 * bins, :]
        base = at(low)
        right_all[base : base + bins, :block] = real_part
        right_all[base : base + bins, block:] = imag_part
        right_all[base + bins : base + 2 * bins, :block] = imag_part
        right_all[base + bins : base + 2 * bins, block:] = -real_part


def put_pack(slot, rows, bins, step, times, pack, left_all, right_all):
    share = left_all.shape[0]
    block = share * times
    wide = times * rows
    part_rows = left_all.shape[1] // times
    at = functools.partial(column_of, rows, wide, step)
    put_right(bins, pack.at[slot], right_all, at, part_rows)
    for low in range(0, part_rows, block):
        first = part_rows + low // block * share
        value = pack[slot, first : first + share, :].astype(jnp.float32)
        for inner in range(0, block, rows):
            left_all[:, at(low + inner) : at(low + inner) + rows] = value[:, inner : inner + rows]


def column_of(rows, wide, step, low):
    return low // rows * wide + step * rows + low % rows


def cross_spectra(bins, wide, first, chunk, left_all, right_all, cross_ref):
    groups = left_all.shape[1] // wide
    block = right_all.shape[1] // 2
    half = groups * bins
    column = lax.broadcasted_iota(jnp.int32, (bins, wide), 1) % bins
    row = lax.broadcasted_iota(jnp.int32, (bins, wide), 0)
    keep = (column == row).astype(jnp.float32).astype(jnp.bfloat16)
    several = 32 if chunk % 32 == 0 else 16 if chunk % 16 == 0 else 2
    for group in range(groups):
        weights = right_all[group * wide : (group + 1) * wide, :]
        for start in range(0, chunk, several):
            pieces = []
            for i in range(several):
                line = left_all[pl.ds(first + start + i, 1), group * wide : (group + 1) * wide]
                tile = jnp.broadcast_to(line, (16, wide)).astype(jnp.bfloat16)
                pieces += [tile * keep[low : low + 16] for low in range(0, bins, 16)]
            product = jnp.dot(jnp.concatenate(pieces, axis=0), weights, preferred_element_type=jnp.float32)
            product = product.astype(jnp.bfloat16)
            for i in range(several):
                at = start + i
                lanes = slice(at % 2 * block, (at % 2 + 1) * block)
                piece = product[i * bins : (i + 1) * bins]
                cross_ref[at // 2, group * bins : (group + 1) * bins, lanes] = piece[:, :block]
                cross_ref[at // 2, half + group * bins : half + (group + 1) * bins, lanes] = piece[:, block:]


def cross_kernel(bins, rows, chunk, first, plan_ref, own_ref, *refs):
    packs, (out_ref, left_all, right_all) = refs[:-3], refs[-3:]
    times = 1 + len(packs)
    live = plan_ref[4 * own_ref.shape[0] + 1]

    def one_slot(slot, carry):
        put_pack(slot + first, rows, bins, 0, times, own_ref, left_all, right_all)
        for step, pack in enumerate(packs):
            put_pack(slot, rows, bins, 1 + step, times, pack, left_all, right_all)
        for n in range(left_all.shape[0] // chunk):
            into = out_ref.at[slot, n * chunk // 2 : (n + 1) * chunk // 2]
            cross_spectra(bins, times * rows, n * chunk, chunk, left_all, right_all, into)
        return carry

    lax.fori_loop(0, jnp.clip(live - first, 0, out_ref.shape[0]), one_slot, 0)


def stack_kernel(bins, rows, times, chunk, joined, plan_ref, table_ref, *refs):
    refs, (out_ref, held, blocks, turned, left_all, right_all, cross_ref, sems) = refs[:-8], refs[-8:]
    cuts = slot_cuts(held.shape[0])
    early, sources = refs[: len(cuts)], refs[len(cuts) :]
    slots = held.shape[0]
    live = plan_ref[4 * slots + 1]
    share = left_all.shape[0]
    block = share * times
    wide = times * rows
    part_rows = left_all.shape[1] // times
    lanes = 2 * block
    parts = share // chunk
    width = chunk // 2 * lanes

    def leave(slot, n):
        span = slice(n * width, (n + 1) * width)
        return pltpu.make_async_copy(held.at[slot, :, span], out_ref.at[slot, :, span], sems.at[slot, n])

    def one_slot(slot, cross_first):
        if joined == 1:
            for step, pack in enumerate(sources):
                put_pack(slot, rows, bins, step, times, pack, left_all, right_all)
        else:
            for side in range(2):
                targets = [[blocks.at[side, step]] for step in range(joined)]
                fetch(joined, plan_ref, 2 * slot + side, 2 * slots, sources, targets)
            start = pl.multiple_of(plan_ref[4 * slots] * share, share)
            for step in range(times):
                at = functools.partial(column_of, rows, wide, step)
                put_right(bins, blocks.at[1, step], right_all, at, part_rows)
                turned[...] = blocks[0, step].astype(jnp.float32).T
                for low in range(0, part_rows, rows):
                    left_all[:, at(low) : at(low) + rows] = turned[pl.ds(start, share), low : low + rows]
        table = table_ref[...]
        for n in range(parts):
            cross_spectra(bins, wide, n * chunk, chunk, left_all, right_all, cross_ref.at[n % 2])
            for pair in range(chunk // 2):
                at = n * chunk // 2 + pair
                cross = jnp.concatenate([cross_first[at], cross_ref[n % 2, pair]], axis=0)
                held[slot, :, at * lanes : (at + 1) * lanes] = jnp.dot(table, cross, preferred_element_type=jnp.float32)
            leave(slot, n).start()

    for slot in range(slots):

        @pl.when(slot >= live)
        def _():
            held[slot] = jnp.zeros_like(held[slot])
            for n in range(parts):
                leave(slot, n).start()

    for (low, high), ref in zip(cuts, early):
        for slot in range(low, high):
            pl.when(slot < live)(functools.partial(one_slot, slot, ref.at[slot - low]))

    for slot in range(slots):
        for n in range(parts):
            leave(slot, n).wait()


def chip_dims(size):
    return {16: (4, 2, 2), 64: (16, 4, 1)}.get(size, (size, 1, 1))


def swap(value, dims, axis, by):
    moves = []
    for p in range(math.prod(dims)):
        place = list(np.unravel_index(p, dims))
        place[axis] ^= by
        moves.append((p, int(np.ravel_multi_index(place, dims))))
    return lax.ppermute(value, "pair", moves)


def is_paired(dims, times):
    return dims == (4, 2, 2) and times == 2 and PIECES == 2


def column_order(dims):
    depth, height, _ = dims
    order = [(0, 0)]
    for axis, size in ((0, depth), (1, height)):
        bit = size // 2
        while bit:
            order += [(z ^ bit, y) if axis == 0 else (z, y ^ bit) for z, y in order]
            bit //= 2
    return order


def plan_of(away, counts, dims, parts, joined):
    _, height, cores = dims
    source = jnp.zeros_like(away)
    index = jnp.zeros_like(away)
    spots = [(n, at) for n, part in enumerate(parts) for at in range(part)]
    for (z, y), (n, at) in zip(column_order(dims), spots):
        here = away // cores == z * height + y
        source = jnp.where(here, n * cores, source)
        index = jnp.where(here, at * joined, index)
    return jnp.concatenate([source + away % cores, index, lax.axis_index("tm")[None], counts]).astype(jnp.int32)


def after(values, others):
    return lax.optimization_barrier(tuple(values) + tuple(others))[: len(values)]


def join(held, more, others=()):
    (held,) = after([held], others)
    (room,) = after([jnp.concatenate([held, held])], ())
    return lax.dynamic_update_slice(room, more, (held.shape[0], 0, 0))


def swap_times(value, step, times):
    return lax.ppermute(value, "tm", [((t + step) % times, t) for t in range(times)])


def gather_one(held, dims):
    depth, height, _ = dims
    for axis, size in ((0, depth), (1, height)):
        bit = size // 2
        while bit:
            held = jnp.concatenate([held, swap(held, dims, axis, bit)])
            bit //= 2
    return [held]


def gather_two(first, second, dims):
    first_far = swap(first, dims, 0, 2)
    (room,) = after([jnp.concatenate([first, first])], ())
    (second,) = after([second], [room])
    other = swap_times(second, 1, 2)
    first_two = lax.dynamic_update_slice(room, first_far, (1, 0, 0))
    first_near = swap(first_two, dims, 0, 1)
    (pair,) = after([join(second, other)], [first_two])
    pair_beside = swap(pair, dims, 1, 1)
    pair_far = swap(pair, dims, 0, 2)
    first_four = jnp.concatenate([first_two, first_near])
    first_beside = swap(first_four, dims, 1, 1)
    first_core = swap(after([first_four], [pair_beside])[0], dims, 2, 1)
    pair_two = join(pair, pair_far, [first_four])
    pair_near = swap(pair_two, dims, 0, 1)
    pair_four = jnp.concatenate([pair_two, pair_near])
    pair_rest = swap(pair_four[2:], dims, 1, 1)
    return [first_four, first_beside], [pair_four, pair_beside, pair_rest], first_two, first_core


def both_cores(arrays, dims):
    if dims[2] == 1:
        return arrays
    return [value for array in arrays for value in (array, swap(array, dims, 2, 1))]


def shards(traces, owner, tiles, counts):
    seg_count, block, _ = traces.shape
    times = lax.axis_size("tm")
    segments = seg_count * times
    share = block // times
    slots = tiles.shape[0]
    bins = max(16, 128 // segments)
    groups = NF // bins
    rows = seg_count * 2 * bins
    wide = rows * times
    total = groups * rows
    part_rows = total // PIECES
    dims = chip_dims(lax.axis_size("pair"))
    smem = pl.BlockSpec(memory_space=pltpu.SMEM)
    anywhere = pl.BlockSpec(memory_space=pl.ANY)
    white = pl.pallas_call(
        functools.partial(whiten_kernel, bins),
        in_specs=[anywhere] * 2,
        out_shape=[jax.ShapeDtypeStruct((part_rows, block), jnp.bfloat16)] * PIECES,
        scratch_shapes=[
            pltpu.VMEM((CHUNKS, seg_count, block, NT // CHUNKS), jnp.float32),
            pltpu.VMEM((CHUNKS, 2 * NF, NT // CHUNKS), jnp.float32),
            pltpu.VMEM((NF + 16, seg_count * block), jnp.float32),
            pltpu.SemaphoreType.DMA((CHUNKS, 2)),
        ],
        compiler_params=pltpu.CompilerParams(vmem_limit_bytes=63 << 20),
        name="whiten",
    )(traces, jnp.asarray(forward_table()))

    paired = is_paired(dims, times)
    blocks = [own[None] for own in white]
    if paired:
        *gathered, near, swapped = gather_two(*blocks, dims)
        tiles, counts = after([tiles, counts], [near])
    else:
        gathered = [gather_one(own, dims) for own in blocks]

    known = owner.shape[0]
    chosen = tiles.reshape(-1, 1) == jnp.arange(known, dtype=jnp.int32)
    stored = jnp.sum(jnp.where(chosen, owner, 0), axis=1)
    away = stored ^ lax.axis_index("pair")

    pack = part_rows + part_rows // block * share
    depth = 2 * NF // PIECES
    chunk = min(share, 16)
    inside = pl.BlockSpec(memory_space=pltpu.VMEM)
    operands = [
        pltpu.VMEM((share, groups // PIECES * wide), jnp.float32),
        pltpu.VMEM((groups // PIECES * wide, 2 * block), jnp.bfloat16),
    ]
    early = []
    cuts = slot_cuts(slots)
    for piece, arrays in enumerate(gathered):
        joined = times if paired and piece else 1
        plan = plan_of(away, counts, dims, [array.shape[0] // joined for array in arrays], joined)
        if joined > 1:
            column, beside, rest = arrays
            beside_core = swap(after([beside], picked)[0], dims, 2, 1)
            (rest,) = after([rest], arrived[1:] + early[:1] + [table, beside_core])
            column_core = swap(after([column], picked)[0], dims, 2, 1)
            arrived = [column, column_core, beside, beside_core, rest, swap(rest, dims, 2, 1)]
            continue
        sources = both_cores(arrays, dims)
        if paired:
            sources[1] = swapped
        arrived = list(pl.pallas_call(
            functools.partial(pick_kernel, len(sources)),
            in_specs=[smem] + [inside] * len(sources),
            out_shape=[jax.ShapeDtypeStruct((slots, pack, block), jnp.bfloat16)]
            + [jax.ShapeDtypeStruct((high - low, pack, block), jnp.bfloat16) for low, high in cuts] * (times - 1),
            scratch_shapes=[
                pltpu.VMEM((slots, part_rows, block), jnp.bfloat16),
                pltpu.VMEM((slots, part_rows // block, block, block), jnp.bfloat16),
            ],
            compiler_params=pltpu.CompilerParams(vmem_limit_bytes=8 << 20),
            cost_estimate=pl.CostEstimate(flops=1, bytes_accessed=1, transcendentals=0),
            name="pick",
        )(plan, *sources))
        if not piece:
            picked = arrived[1:]
            table = inverse_table(segments, picked)
        for step in range(1, times):
            moves = [(t, (t + step) % times) for t in range(times)]
            for n in range(len(cuts)):
                at = 1 + (step - 1) * len(cuts) + n
                arrived[at] = lax.ppermute(arrived[at], "tm", moves)
        if piece:
            own, *more = arrived
            arrived = [own] + [jnp.concatenate(more[n : n + len(cuts)]) for n in range(0, len(more), len(cuts))]
            continue
        for n, (low, high) in enumerate(cuts):
            early.append(
                pl.pallas_call(
                    functools.partial(cross_kernel, bins, rows, min(share, 32), low),
                    in_specs=[smem] + [inside] * times,
                    out_shape=jax.ShapeDtypeStruct((high - low, share // 2, depth, 2 * block), jnp.bfloat16),
                    scratch_shapes=operands,
                    compiler_params=pltpu.CompilerParams(vmem_limit_bytes=16 << 20),
                    cost_estimate=pl.CostEstimate(flops=1, bytes_accessed=1, transcendentals=0),
                    name="cross",
                )(plan, arrived[0], *arrived[1 + n :: len(cuts)])
            )

    return pl.pallas_call(
        functools.partial(stack_kernel, bins, rows, times, chunk, joined),
        in_specs=[smem] + [inside] * (1 + len(early) + len(arrived)),
        out_specs=anywhere,
        out_shape=jax.ShapeDtypeStruct((slots, LAGS, share * block), jnp.float32),
        scratch_shapes=[
            pltpu.VMEM((slots, LAGS, share * block), jnp.float32),
            pltpu.VMEM((2, times, part_rows, block), jnp.bfloat16),
            pltpu.VMEM((block, part_rows), jnp.float32),
        ]
        + operands
        + [
            pltpu.VMEM((2, chunk // 2, depth, 2 * block), jnp.bfloat16),
            pltpu.SemaphoreType.DMA((slots, share // chunk)),
        ],
        compiler_params=pltpu.CompilerParams(vmem_limit_bytes=32 << 20),
        name="stack",
    )(plan, table, *early, *arrived)


def solution(mesh):
    placed = (P("tm", "pair", None), P(), P("pair", None), P("pair"))
    return jax.shard_map(
        shards, mesh=mesh, in_specs=placed, out_specs=P("pair", None, "tm"), check_vma=False
    )
```
